32 devices in a mesh: batch: 4 (over y, x), expert: 8 (over z, core).
Axes of the slice: x: 2, y: 2, z: 4, core: 2. Of those that a mesh axis runs over, the one named last changes fastest.
Arguments:
- block_input: float32 [4, 1024, 1280], P('batch', 'expert'), may hold values from -6 to 6
- seq_ids: int32 [4, 1024], P('batch', 'expert'), may hold values from 0 to 1, as said below
- routes: int32 [4, 1024, 6], P('batch', 'expert'), may hold values from 0 to 15, all different within a row; in each aligned block of 128 rows (0 to 127, 128 to 255, ..., all dimensions but the last counted through in order) at most 72 rows name the same one
- cotangent: float32 [4, 1024, 1280], P('batch', 'expert'), may hold values from -6 to 6
- qkv_weight: float32 [1280, 3840], P(('batch', 'expert')), may hold values from -0.25 to 0.25
- out_weight: float32 [1280, 1280], P(('batch', 'expert')), may hold values from -1.25 to 1.25
- shared_up: float32 [1280, 1792], P(('batch', 'expert')), may hold values from -0.15625 to 0.15625
- shared_down: float32 [896, 1280], P(('batch', 'expert')), may hold values from -0.375 to 0.375
- router_weight: float32 [1280, 16], P(('batch', 'expert')), may hold values from -0.078125 to 0.078125
- gain_attn: float32 [1280], P(('batch', 'expert')), may hold values from 0.1 to 1.9
- gain_ffn: float32 [1280], P(('batch', 'expert')), may hold values from 0.1 to 1.9
- expert_up: float32 [16, 1280, 1792], P('expert', 'batch'), may hold values from -0.15625 to 0.15625
- expert_down: float32 [16, 896, 1280], P('expert', 'batch'), may hold values from -0.75 to 0.75
Outputs:
- block_output: float32 [4, 1024, 1280], P('batch', 'expert')
- input_grad: float32 [4, 1024, 1280], P('batch', 'expert')
- qkv_grad: float32 [1280, 3840], P(('batch', 'expert'))
- out_grad: float32 [1280, 1280], P(('batch', 'expert'))
- shared_up_grad: float32 [1280, 1792], P(('batch', 'expert'))
- shared_down_grad: float32 [896, 1280], P(('batch', 'expert'))
- router_grad: float32 [1280, 16], P(('batch', 'expert'))
- gain_attn_grad: float32 [1280], P(('batch', 'expert'))
- gain_ffn_grad: float32 [1280], P(('batch', 'expert'))
- expert_up_grad: float32 [16, 1280, 1792], P('expert', 'batch')
- expert_down_grad: float32 [16, 896, 1280], P('expert', 'batch')
The draws below stay inside these ranges and needn't reach their ends.
Inputs may be any that keep to these rules, and one draw needn't show every extreme that they name: `seq_ids`: in each pack the ids are 0 up to a boundary and 1 from it on; the boundary lies between 384 and 640. `routes`: each row names 6 different experts; among the rows of one device no expert is named more than 72 times, and in every draw some expert is named exactly 72 times by the rows of some device.
All inputs are finite; a program needn't handle non-finite values.
Results may differ from the reference program's by a relative error of at most 0.028.
Values may be sent and summed in bfloat16 or wider, within the bound.
A program may use at most 320 MiB of HBM per device.

```python
import math
import jax
import jax.numpy as jnp
import numpy as np
from jax import lax

D = 1280
HEADS = 10
HEAD = 128
FF = 896
SFF = 896
TOP = 6
TOK_DEV = 128
EXPERTS = 16
LEN = 1024
CAP = 72
N_BATCH = 4
N_EXPERT = 8


def draw_seq_ids(key, part):
    boundary = jax.random.randint(key, (N_BATCH, 1), LEN * 3 // 8, LEN * 5 // 8 + 1)
    positions = jnp.arange(LEN, dtype=jnp.int32)[None, :]
    return (positions >= boundary).astype(jnp.int32)


def block_levels(key, shape, split, low, high):
    factor_of, own = 1.0, jax.random.fold_in(key, 6)
    for dim, shards_of in split:
        steps = jnp.exp(jax.random.uniform(jax.random.fold_in(own, dim), (shards_of,), jnp.float32, low / len(split), high / len(split)))
        factor_of = factor_of * jnp.repeat(steps, shape[dim] // shards_of).reshape([-1 if axis == dim else 1 for axis in range(len(shape))])
    return factor_of


def assign_block(own_key, own, number, rows, number_of, top, most, lean):
    sequence = jax.random.permutation(own_key, number_of)
    heavy_load, ordinary = load_shares(number_of, rows * top, most, lean, True), load_shares(number_of, rows * top, most, lean, False)
    places = jnp.arange(number_of)

    def named(sizes, offset_by):
        used = int((sizes > 0).sum())
        fixed = max(1, used // 4)
        shifted = fixed + (places - fixed + offset_by * (used - fixed)) % max(1, number_of - fixed)
        return jnp.zeros((number_of,), jnp.int32).at[sequence[jnp.where(places < fixed, places, shifted)]].set(jnp.asarray(sizes, jnp.int32))

    sizes = jnp.where(number % 4 == 0, named(heavy_load, number // 4), named(ordinary, number - number // 4 - 1))
    mixed = jax.random.permutation(jax.random.fold_in(own, 3), number_of)
    giver, sink = mixed[0:number_of // 2 * 2:2], mixed[1:number_of // 2 * 2:2]
    slack = jnp.minimum(sizes[giver] - 1, most - sizes[sink]) // 2
    slack = jnp.where((giver == sequence[0]) | (sink == sequence[0]) | (sizes[sink] == 0), 0, jnp.maximum(slack, 0))
    shifted = jax.random.randint(jax.random.fold_in(own, 4), (number_of // 2,), 0, 1 << 20) % (slack + 1)
    sizes = sizes.at[giver].add(-shifted).at[sink].add(shifted)
    items = jnp.searchsorted(jnp.cumsum(sizes), jnp.arange(rows * top), side="right").astype(jnp.int32)
    grid = items.reshape(top, rows).T
    grid = grid[jax.random.permutation(jax.random.fold_in(own, 1), rows)]
    offset_by = jax.random.randint(jax.random.fold_in(own, 2), (rows, 1), 0, top)
    return jnp.take_along_axis(grid, (jnp.arange(top)[None, :] + offset_by) % top, axis=1)


def load_shares(number_of, total, reach, lean, full):
    portions = [(1 << 20) // math.isqrt(grade ** lean) + 1 for grade in range(1, number_of + 1)]
    largest = reach if full else min(reach, max(-(-total // number_of), total * portions[0] // sum(portions)))
    least = 1 if total - largest >= number_of - 1 else 0
    holding, surplus = [largest] + [least] * (number_of - 1), total - largest - least * (number_of - 1)
    while surplus > 0:
        movable = [i for i in range(1, number_of) if holding[i] < largest] or [i for i in range(1, number_of) if holding[i] < reach]
        pool, budget = sum([portions[i] for i in movable]), surplus
        for i in movable:
            more = min(reach - holding[i], max(1, budget * portions[i] // pool), surplus)
            holding[i] = holding[i] + more
            surplus = surplus - more
    return np.array(holding)


def gaussian(stream_key, extent, scale, limit, pieces=(), kind=jnp.bfloat16):
    factor_of = block_levels(stream_key, extent, pieces, -0.22, 0.18) if pieces else 1.0
    array = jax.random.normal(stream_key, extent, jnp.float32) * scale * factor_of
    return jnp.minimum(jnp.maximum(array, -limit), limit).astype(kind)


def setup_inputs(seed: int = 0) -> dict:
    seeds = jax.random.split(jax.random.key(seed), 14)
    block_input = gaussian(seeds[0], (N_BATCH, LEN, D), 1.0, 6.0, ((0, 4), (1, 8)), jnp.float32)
    seq_ids = draw_seq_ids(jax.random.fold_in(seeds[13], 71), 0)
    routes_keys = jax.random.split(jax.random.fold_in(seeds[2], 1), N_BATCH * LEN // TOK_DEV)
    routes_turns = jax.random.permutation(jax.random.fold_in(seeds[2], 3), N_BATCH * LEN // TOK_DEV)
    routes = jax.vmap(lambda own, number: assign_block(jax.random.fold_in(seeds[2], 2), own, number, TOK_DEV, EXPERTS, TOP, CAP, 2))(routes_keys, routes_turns).reshape((N_BATCH, LEN, TOP))
    cotangent = gaussian(seeds[3], (N_BATCH, LEN, D), 1.0, 6.0, ((0, 4), (1, 8)), jnp.float32)
    qkv_weight = gaussian(seeds[4], (D, 3 * D), (D // 2) ** -0.5, 0.25, ((0, 32),), jnp.float32)
    out_weight = gaussian(seeds[5], (D, D), (D // 64) ** -0.5, 1.25, ((0, 32),), jnp.float32)
    shared_up = gaussian(seeds[6], (D, 2 * SFF), D ** -0.5, 0.15625, ((0, 32),), jnp.float32)
    shared_down = gaussian(seeds[7], (SFF, D), (SFF // 4) ** -0.5, 0.375, ((0, 32),), jnp.float32)
    router_weight = gaussian(seeds[8], (D, EXPERTS), (4 * D) ** -0.5, 0.078125, ((0, 32),), jnp.float32)
    gain_attn = jnp.clip(1.0 + 0.18 * jax.random.normal(seeds[9], (D,), jnp.float32), 0.1, 1.9)
    gain_ffn = jnp.clip(1.0 + 0.18 * jax.random.normal(seeds[10], (D,), jnp.float32), 0.1, 1.9)
    expert_up = gaussian(seeds[11], (EXPERTS, D, 2 * FF), D ** -0.5, 0.15625, ((0, 8), (1, 4)), jnp.float32)
    expert_down = gaussian(seeds[12], (EXPERTS, FF, D), (FF // 16) ** -0.5, 0.75, ((0, 8), (1, 4)), jnp.float32)
    return dict(block_input=block_input, seq_ids=seq_ids, routes=routes, cotangent=cotangent, qkv_weight=qkv_weight, out_weight=out_weight, shared_up=shared_up, shared_down=shared_down, router_weight=router_weight, gain_attn=gain_attn, gain_ffn=gain_ffn, expert_up=expert_up, expert_down=expert_down)


@jax.custom_vjp
def low(v):
    return lax.optimization_barrier(v.astype(jnp.bfloat16)).astype(jnp.float32)

@jax.custom_vjp
def low_back(v):
    return v

def low_keep(v):
    return (low(v), None)

def low_pass(kept, grad):
    return (grad,)

def back_keep(v):
    return (v, None)

def back_low(kept, grad):
    return (low(grad),)
low.defvjp(low_keep, low_pass)
low_back.defvjp(back_keep, back_low)
EPSILON = 1e-06
NEGATIVE = -1e+30

def matmul(left, right):
    return jnp.dot(left, right, precision=lax.Precision.HIGHEST, preferred_element_type=jnp.float32)

def rotate(values, positions, sign):
    half = values.shape[-1] // 2
    frequency = 10000.0 ** (-jnp.arange(half, dtype=jnp.float32) / half)
    angle = positions.astype(jnp.float32)[:, None] * frequency[None, :]
    cosine = jnp.cos(angle)[:, None, :]
    sine = sign * jnp.sin(angle)[:, None, :]
    first = values[..., :half]
    second = values[..., half:]
    return jnp.concatenate([first * cosine - second * sine, first * sine + second * cosine], axis=-1)

def rms_norm(rows, gain):
    return rows * lax.rsqrt(lax.optimization_barrier(jnp.mean(rows * rows, axis=-1, keepdims=True)) + EPSILON) * low(gain)

def swiglu(pre, hidden_width):
    return jax.nn.silu(pre[:, :hidden_width]) * pre[:, hidden_width:]

def slot_table(route_pack):
    flat = route_pack.reshape(N_EXPERT, TOK_DEV * TOP)
    onehot = (flat[:, :, None] == jnp.arange(EXPERTS, dtype=jnp.int32)[None, None, :]).astype(jnp.int32)
    ranks = jnp.cumsum(onehot, axis=1)
    slots = lax.optimization_barrier(jnp.sum(ranks * onehot, axis=2)) - 1
    blocks = jnp.broadcast_to(jnp.arange(N_EXPERT, dtype=jnp.int32)[:, None], flat.shape)
    index = jnp.arange(LEN * TOP, dtype=jnp.int32).reshape(N_EXPERT, TOK_DEV * TOP)
    routing_table = jnp.full((EXPERTS, N_EXPERT, CAP), LEN * TOP, jnp.int32).at[flat, blocks, slots].set(index)
    return routing_table.reshape(EXPERTS, N_EXPERT * CAP)

def forward_pack(layer_parameters, rows, ids, route_pack, routing_table):
    query_key_value_weight, output_projection_weight, shared_up_matrix, shared_down_matrix, router_matrix, attention_norm_gain, feedforward_norm_gain, expert_up_matrix, expert_down_matrix = layer_parameters
    positions = jnp.arange(LEN, dtype=jnp.int32)
    input_low = low(rms_norm(rows, attention_norm_gain))
    projected = low_back(matmul(input_low, low(query_key_value_weight)))
    queries = low(rotate(projected[:, :D].reshape(LEN, HEADS, HEAD), positions, 1.0))
    keys = low(rotate(projected[:, D:2 * D].reshape(LEN, HEADS, HEAD), positions, 1.0))
    values = low(projected[:, 2 * D:].reshape(LEN, HEADS, HEAD))
    block_rows = min(512, LEN)

    def attend(block):
        start = block * block_rows
        query_block = lax.dynamic_slice_in_dim(queries, start, block_rows, 0)
        query_pos = start + jnp.arange(block_rows, dtype=jnp.int32)
        query_seq = lax.dynamic_slice_in_dim(ids, start, block_rows, 0)
        allowed = (positions[None, :] <= query_pos[:, None]) & (ids[None, :] == query_seq[:, None])
        scores = low_back(jnp.einsum('qhd,khd->hqk', query_block, keys, precision=lax.Precision.HIGHEST) * HEAD ** (-0.5))
        scores = jnp.where(allowed[None], scores, NEGATIVE)
        weights = jax.nn.softmax(scores, axis=2)
        return jnp.einsum('hqk,khd->qhd', low(weights), values, precision=lax.Precision.HIGHEST)
    attended = lax.map(jax.checkpoint(attend), jnp.arange(LEN // block_rows, dtype=jnp.int32))
    attn = low(low_back(attended.reshape(LEN, D)))
    resid = rows + low_back(matmul(attn, low(output_projection_weight)))
    ffn_low = low(rms_norm(resid, feedforward_norm_gain))
    logits = low_back(matmul(ffn_low, low(router_matrix)))
    probs = jax.nn.softmax(logits, axis=-1)
    chosen = jnp.take_along_axis(probs, route_pack, axis=1)
    gates = chosen / lax.optimization_barrier(jnp.sum(chosen, axis=1, keepdims=True))
    shared_pre = low_back(matmul(ffn_low, low(shared_up_matrix)))
    shared_hidden = low(swiglu(shared_pre, SFF))
    shared_out = low_back(matmul(shared_hidden, low(shared_down_matrix)))
    padded_rows = jnp.concatenate([ffn_low, jnp.zeros((1, D), ffn_low.dtype)], axis=0)
    padded_gates = jnp.concatenate([gates.reshape(-1), jnp.zeros((1,), gates.dtype)], axis=0)

    def single_expert_apply(packed):
        index, up_w, down_w = packed
        expert_rows = low_back(padded_rows[index // TOP])
        expert_pre = low_back(matmul(expert_rows, low(up_w)))
        expert_hidden = low(swiglu(expert_pre, FF))
        expert_out = low(low_back(matmul(expert_hidden, low(down_w))))
        return expert_out * padded_gates[index][:, None]
    gate_weighted_rows = lax.map(jax.checkpoint(single_expert_apply), (routing_table, expert_up_matrix, expert_down_matrix))
    routed = jnp.zeros((LEN + 1, D), gate_weighted_rows.dtype).at[(routing_table // TOP).reshape(-1)].add(gate_weighted_rows.reshape(-1, D))[:LEN]
    return resid + shared_out + routed

def add_trees(first, second):
    return jax.tree.map(lambda left, right: left + right, first, second)

def reference(block_input, seq_ids, routes, cotangent, qkv_weight, out_weight, shared_up, shared_down, router_weight, gain_attn, gain_ffn, expert_up, expert_down):
    layer_parameters = (qkv_weight, out_weight, shared_up, shared_down, router_weight, gain_attn, gain_ffn, expert_up, expert_down)
    tables = jax.vmap(slot_table)(routes)

    def one_pack(total, packed):
        rows, ids, route_pack, routing_table, upstream = packed

        def forward_here(weights, inputs):
            return forward_pack(weights, inputs, ids, route_pack, routing_table)
        result, pull = jax.vjp(forward_here, layer_parameters, rows)
        weight_grads, row_grads = pull(upstream)
        return (add_trees(total, weight_grads), (result, row_grads))
    zeros_tree = jax.tree.map(jnp.zeros_like, layer_parameters)
    total, (outputs, input_grads) = lax.scan(one_pack, zeros_tree, (block_input, seq_ids, routes, tables, cotangent))
    return (outputs, input_grads, total[0], total[1], total[2], total[3], total[4], total[5], total[6], total[7], total[8])
```

```python
import functools

import jax
import jax.numpy as jnp
from jax import lax
from jax.experimental import pallas as pl
from jax.experimental.pallas import tpu as pltpu
from jax.sharding import PartitionSpec as P

HEAD = 128
TOP = 6


EPSILON = 1e-06
NEGATIVE = -1e30


def rotate(values, positions, sign):
    half = values.shape[-1] // 2
    frequency = 10000.0 ** (-jnp.arange(half, dtype=jnp.float32) / half)
    angle = positions.astype(jnp.float32)[:, None] * frequency[None, :]
    cosine = jnp.cos(angle)[:, None, :]
    sine = sign * jnp.sin(angle)[:, None, :]
    first = values[..., :half]
    second = values[..., half:]
    return jnp.concatenate(
        [first * cosine - second * sine, first * sine + second * cosine], axis=-1
    )


def swiglu(pre, hidden_width):
    return jax.nn.silu(pre[..., :hidden_width]) * pre[..., hidden_width:]


def swiglu_back(pre, dhidden, hidden_width):
    gate_part = pre[..., :hidden_width]
    up_part = pre[..., hidden_width:]
    sigma = jax.nn.sigmoid(gate_part)
    dgate = dhidden * up_part * sigma * (1.0 + gate_part * (1.0 - sigma))
    dupper = dhidden * gate_part * sigma
    return jnp.concatenate([dgate, dupper], axis=-1)


def norm_back(dnormed, normed, inv_rms, gain):
    dscaled = dnormed * gain
    dinputs = inv_rms * (dscaled - normed * jnp.mean(dscaled * normed, axis=1, keepdims=True))
    return (dinputs, jnp.sum(dnormed * normed, axis=0))


def per_device(
    block_input,
    seq_ids,
    routes,
    cotangent,
    qkv_weight,
    out_weight,
    shared_up,
    shared_down,
    router_weight,
    gain_attn,
    gain_ffn,
    expert_up,
    expert_down,
):
    dense = (
        lax.all_gather(qkv_weight.astype(jnp.bfloat16), ("batch", "expert"), axis=0, tiled=True),
        lax.all_gather(out_weight.astype(jnp.bfloat16), ("batch", "expert"), axis=0, tiled=True),
        lax.all_gather(shared_up.astype(jnp.bfloat16), ("batch", "expert"), axis=0, tiled=True),
        lax.all_gather(shared_down.astype(jnp.bfloat16), ("batch", "expert"), axis=0, tiled=True),
        lax.all_gather(router_weight.astype(jnp.bfloat16), ("batch", "expert"), axis=0, tiled=True),
        lax.all_gather(gain_attn.astype(jnp.bfloat16), ("batch", "expert"), axis=0, tiled=True),
        lax.all_gather(gain_ffn.astype(jnp.bfloat16), ("batch", "expert"), axis=0, tiled=True),
    )
    full_qkv, full_out, full_sup, full_sdown, full_router, low_gain_a, low_gain_f = dense
    gain_first = low_gain_a.astype(jnp.float32)
    gain_second = low_gain_f.astype(jnp.float32)
    experts_up, experts_down = (
        lax.all_gather(expert_up.astype(jnp.bfloat16), "batch", axis=1, tiled=True),
        lax.all_gather(expert_down.astype(jnp.bfloat16), "batch", axis=1, tiled=True),
    )
    rows_in = block_input[0]
    ids_local = seq_ids[0]
    route_local = routes[0]
    upstream = cotangent[0]
    tokens_dev = rows_in.shape[0]
    model_width = rows_in.shape[1]
    heads_count = model_width // HEAD
    groups = lax.axis_size("expert")
    local_experts = experts_up.shape[0]
    experts_all = local_experts * groups
    shared_width = full_sdown.shape[0]
    hidden_width = experts_down.shape[1]
    capacity = max(2, tokens_dev * TOP * 3 // (experts_all * 2))
    score_scale = HEAD ** (-0.5)
    positions = lax.axis_index("expert") * tokens_dev + jnp.arange(tokens_dev, dtype=jnp.int32)
    key_ids = lax.all_gather(ids_local, "expert", axis=0, tiled=True)
    inv_first = lax.rsqrt(jnp.mean(rows_in * rows_in, axis=1, keepdims=True) + EPSILON)
    normed_first = rows_in * inv_first
    input_low = (normed_first * gain_first).astype(jnp.bfloat16)
    projected = jnp.dot(input_low, full_qkv, preferred_element_type=jnp.float32)
    queries = rotate(
        projected[:, :model_width].reshape(tokens_dev, heads_count, HEAD), positions, 1.0
    ).astype(jnp.bfloat16)
    keys = rotate(
        projected[:, model_width : 2 * model_width].reshape(tokens_dev, heads_count, HEAD),
        positions,
        1.0,
    ).astype(jnp.bfloat16)
    values = (
        projected[:, 2 * model_width :].reshape(tokens_dev, heads_count, HEAD).astype(jnp.bfloat16)
    )

    def key_mask(key_count):
        key_pos = jnp.arange(key_count, dtype=jnp.int32)
        return (key_pos[None, :] <= positions[:, None]) & (key_ids[None, :] == ids_local[:, None])

    run_max = jnp.full((heads_count, tokens_dev), NEGATIVE, jnp.float32)
    key_piece = lax.all_gather(keys, "expert", axis=0, tiled=True)
    value_piece = lax.all_gather(values, "expert", axis=0, tiled=True)
    allowed = key_mask(key_piece.shape[0])[None]
    scores = (
        jnp.einsum("qhd,khd->hqk", queries, key_piece, preferred_element_type=jnp.float32)
        * score_scale
    )
    scores = jnp.where(allowed, scores, NEGATIVE)
    new_max = jnp.maximum(run_max, jnp.max(scores, axis=2))
    weights = jnp.where(allowed, jnp.exp(scores - new_max[:, :, None]), 0.0)
    run_sum = jnp.sum(weights, axis=2)
    update = jnp.einsum(
        "hqk,khd->qhd",
        weights.astype(jnp.bfloat16),
        value_piece,
        preferred_element_type=jnp.float32,
    )
    run_acc = update
    run_max, run_sum, run_acc = (new_max, run_sum, run_acc)
    attn_full = run_acc / jnp.transpose(run_sum)[:, :, None]
    logsum = run_max + jnp.log(run_sum)
    attn_low = attn_full.reshape(tokens_dev, model_width).astype(jnp.bfloat16)
    resid = rows_in + jnp.dot(attn_low, full_out, preferred_element_type=jnp.float32)
    inv_second = lax.rsqrt(jnp.mean(resid * resid, axis=1, keepdims=True) + EPSILON)
    normed_second = resid * inv_second
    ffn_low = (normed_second * gain_second).astype(jnp.bfloat16)
    logits = jnp.dot(ffn_low, full_router, preferred_element_type=jnp.float32)
    probs = jax.nn.softmax(logits, axis=1)
    route_hot = route_local[:, :, None] == jnp.arange(experts_all, dtype=jnp.int32)[None, None, :]
    chosen = jnp.sum(jnp.where(route_hot, probs[:, None, :], 0.0), axis=2)
    chosen_sum = jnp.sum(chosen, axis=1, keepdims=True)
    gates = chosen / chosen_sum
    shared_pre = jnp.dot(ffn_low, full_sup, preferred_element_type=jnp.float32)
    shared_hidden = swiglu(shared_pre, shared_width).astype(jnp.bfloat16)
    shared_result = jnp.dot(shared_hidden, full_sdown, preferred_element_type=jnp.float32)
    flat_route = route_local.reshape(-1)
    flat_hot = (flat_route[:, None] == jnp.arange(experts_all, dtype=jnp.int32)[None, :]).astype(
        jnp.bfloat16
    )
    pair_count = tokens_dev * TOP
    pair_index = jnp.arange(pair_count, dtype=jnp.int32)
    earlier = (pair_index[None, :] < pair_index[:, None]).astype(jnp.bfloat16)
    counts = jnp.dot(earlier, flat_hot, preferred_element_type=jnp.float32)
    slots = jnp.sum(counts * flat_hot, axis=1).astype(jnp.int32)
    source_table = (
        jnp.full((experts_all * capacity,), pair_count, jnp.int32)
        .at[flat_route * capacity + slots]
        .set(jnp.arange(pair_count, dtype=jnp.int32))
    )
    send_table = jnp.transpose(
        source_table.reshape(groups, local_experts, capacity), (1, 0, 2)
    ).reshape(-1)
    return_pos = (
        flat_route % local_experts * (groups * capacity)
        + flat_route // local_experts * capacity
        + slots
    )
    padded_rows = jnp.concatenate([ffn_low, jnp.zeros((1, model_width), jnp.bfloat16)], axis=0)
    send_rows = padded_rows[send_table // TOP].reshape(local_experts, groups, capacity, model_width)
    received = lax.all_to_all(send_rows, "expert", split_axis=1, concat_axis=1, tiled=True)
    expert_rows = received.reshape(local_experts, groups * capacity, model_width)
    expert_pre = jnp.einsum(
        "erd,edf->erf", expert_rows, experts_up, preferred_element_type=jnp.float32
    )
    expert_hidden = swiglu(expert_pre, hidden_width).astype(jnp.bfloat16)
    expert_result = jnp.einsum(
        "erf,efd->erd", expert_hidden, experts_down, preferred_element_type=jnp.float32
    ).astype(jnp.bfloat16)
    returned = lax.all_to_all(
        expert_result.reshape(local_experts, groups, capacity, model_width),
        "expert",
        split_axis=1,
        concat_axis=1,
        tiled=True,
    )
    token_outputs = returned.reshape(-1, model_width)[return_pos].reshape(
        tokens_dev, TOP, model_width
    )
    routed = jnp.sum(gates[:, :, None] * token_outputs, axis=1)
    output_rows = resid + shared_result + routed
    shared_cot = upstream.astype(jnp.bfloat16)
    shared_down_term = jnp.dot(shared_hidden.T, shared_cot, preferred_element_type=jnp.float32)
    dshared_hidden = jnp.dot(shared_cot, full_sdown.T, preferred_element_type=jnp.float32)
    dshared_pre = swiglu_back(shared_pre, dshared_hidden, shared_width).astype(jnp.bfloat16)
    shared_up_term = jnp.dot(ffn_low.T, dshared_pre, preferred_element_type=jnp.float32)
    dnormed_second = jnp.dot(dshared_pre, full_sup.T, preferred_element_type=jnp.float32)
    token_cot = (gates[:, :, None] * upstream[:, None, :]).astype(jnp.bfloat16)
    dgates = jnp.sum(upstream[:, None, :] * token_outputs, axis=2)
    padded_cot = jnp.concatenate(
        [token_cot.reshape(-1, model_width), jnp.zeros((1, model_width), jnp.bfloat16)], axis=0
    )
    send_cot = padded_cot[send_table].reshape(local_experts, groups, capacity, model_width)
    received_cot = lax.all_to_all(
        send_cot, "expert", split_axis=1, concat_axis=1, tiled=True
    ).reshape(local_experts, groups * capacity, model_width)
    down_term = jnp.einsum(
        "erf,erd->efd", expert_hidden, received_cot, preferred_element_type=jnp.float32
    )
    dexpert_hidden = jnp.einsum(
        "erd,efd->erf", received_cot, experts_down, preferred_element_type=jnp.float32
    )
    dexpert_pre = swiglu_back(expert_pre, dexpert_hidden, hidden_width).astype(jnp.bfloat16)
    up_term = jnp.einsum(
        "erd,erf->edf", expert_rows, dexpert_pre, preferred_element_type=jnp.float32
    )
    drows = jnp.einsum(
        "erf,edf->erd", dexpert_pre, experts_up, preferred_element_type=jnp.float32
    ).astype(jnp.bfloat16)
    returned_grad = lax.all_to_all(
        drows.reshape(local_experts, groups, capacity, model_width),
        "expert",
        split_axis=1,
        concat_axis=1,
        tiled=True,
    )
    row_grads = returned_grad.reshape(-1, model_width)[return_pos].reshape(
        tokens_dev, TOP, model_width
    )
    dnormed_second = dnormed_second + jnp.sum(row_grads, axis=1, dtype=jnp.float32)
    expert_up_grad, expert_down_grad = (
        lax.psum_scatter(
            up_term.astype(jnp.bfloat16), "batch", scatter_dimension=1, tiled=True
        ).astype(jnp.float32),
        lax.psum_scatter(
            down_term.astype(jnp.bfloat16), "batch", scatter_dimension=1, tiled=True
        ).astype(jnp.float32),
    )
    dchosen = (dgates - jnp.sum(dgates * gates, axis=1, keepdims=True)) / chosen_sum
    dprobs = jnp.sum(jnp.where(route_hot, dchosen[:, :, None], 0.0), axis=1)
    dlogits = (probs * (dprobs - jnp.sum(probs * dprobs, axis=1, keepdims=True))).astype(
        jnp.bfloat16
    )
    router_term = jnp.dot(ffn_low.T, dlogits, preferred_element_type=jnp.float32)
    dnormed_second = dnormed_second + jnp.dot(
        dlogits, full_router.T, preferred_element_type=jnp.float32
    )
    dresid_norm, gain_ffn_term = norm_back(dnormed_second, normed_second, inv_second, gain_second)
    dresid = upstream + dresid_norm
    dproj = dresid.astype(jnp.bfloat16)
    out_term = jnp.dot(attn_low.T, dproj, preferred_element_type=jnp.float32)
    dattn = (
        jnp.dot(dproj, full_out.T, preferred_element_type=jnp.float32)
        .astype(jnp.bfloat16)
        .reshape(tokens_dev, heads_count, HEAD)
    )
    delta_rows = jnp.sum(dattn.astype(jnp.float32) * attn_full, axis=2)
    delta_heads = jnp.transpose(delta_rows)
    key_piece = lax.all_gather(keys, "expert", axis=0, tiled=True)
    value_piece = lax.all_gather(values, "expert", axis=0, tiled=True)
    allowed = key_mask(key_piece.shape[0])[None]
    scores = (
        jnp.einsum("qhd,khd->hqk", queries, key_piece, preferred_element_type=jnp.float32)
        * score_scale
    )
    attn_probs = jnp.where(allowed, jnp.exp(scores - logsum[:, :, None]), 0.0)
    dprob = jnp.einsum("qhd,khd->hqk", dattn, value_piece, preferred_element_type=jnp.float32)
    dscore = (attn_probs * (dprob - delta_heads[:, :, None])).astype(jnp.bfloat16)
    attn_probs, dscore = (attn_probs, dscore)
    dquery = jnp.einsum("hqk,khd->qhd", dscore, key_piece, preferred_element_type=jnp.float32)
    dkey_piece = jnp.einsum("hqk,qhd->khd", dscore, queries, preferred_element_type=jnp.float32)
    dvalue_piece = jnp.einsum(
        "hqk,qhd->khd", attn_probs.astype(jnp.bfloat16), dattn, preferred_element_type=jnp.float32
    )
    folded = (dquery, dkey_piece, dvalue_piece)
    dquery = folded[0]
    dkey, dvalue = (
        lax.psum_scatter(
            folded[1].astype(jnp.bfloat16), "expert", scatter_dimension=0, tiled=True
        ).astype(jnp.float32),
        lax.psum_scatter(
            folded[2].astype(jnp.bfloat16), "expert", scatter_dimension=0, tiled=True
        ).astype(jnp.float32),
    )
    dquery_raw = rotate(dquery * score_scale, positions, -1.0).reshape(tokens_dev, model_width)
    dkey_raw = rotate(dkey * score_scale, positions, -1.0).reshape(tokens_dev, model_width)
    dprojected = jnp.concatenate(
        [dquery_raw, dkey_raw, dvalue.reshape(tokens_dev, model_width)], axis=1
    ).astype(jnp.bfloat16)
    qkv_term = jnp.dot(input_low.T, dprojected, preferred_element_type=jnp.float32)
    dnormed_first = jnp.dot(dprojected, full_qkv.T, preferred_element_type=jnp.float32)
    dinput_norm, gain_attn_term = norm_back(dnormed_first, normed_first, inv_first, gain_first)
    input_grad = dresid + dinput_norm
    grads = (
        lax.psum_scatter(qkv_term, ("batch", "expert"), scatter_dimension=0, tiled=True),
        lax.psum_scatter(out_term, ("batch", "expert"), scatter_dimension=0, tiled=True),
        lax.psum_scatter(shared_up_term, ("batch", "expert"), scatter_dimension=0, tiled=True),
        lax.psum_scatter(shared_down_term, ("batch", "expert"), scatter_dimension=0, tiled=True),
        lax.psum_scatter(router_term, ("batch", "expert"), scatter_dimension=0, tiled=True),
        lax.psum_scatter(gain_attn_term, ("batch", "expert"), scatter_dimension=0, tiled=True),
        lax.psum_scatter(gain_ffn_term, ("batch", "expert"), scatter_dimension=0, tiled=True),
    )
    (
        qkv_grad,
        out_grad,
        shared_up_grad,
        shared_down_grad,
        router_grad,
        gain_attn_grad,
        gain_ffn_grad,
    ) = grads
    return (
        output_rows[None],
        input_grad[None],
        qkv_grad,
        out_grad,
        shared_up_grad,
        shared_down_grad,
        router_grad,
        gain_attn_grad,
        gain_ffn_grad,
        expert_up_grad,
        expert_down_grad,
    )


PAIR_OF = {0: 0, 2: 1, 3: 2, 4: 3, 6: 4}
AXES = ("batch", "expert")
F32 = jnp.float32
LOW = jnp.bfloat16


def low(values):
    return values.astype(LOW)


def dot(left, right, dims=((1,), (0,))):
    return lax.dot_general(left, right, (dims, ((), ())), preferred_element_type=F32)


def swap(values, batch_bit, expert_bit=0, only=range(8)):
    pairs = [
        (b * 8 + e, (b ^ batch_bit) * 8 + (e ^ expert_bit)) for b in range(4) for e in range(8)
    ]
    pairs = [pair for pair in pairs if pair[0] % 8 in only]
    return lax.ppermute(values, AXES, pairs)


def halves(values, axis):
    size = values.shape[axis] // 2
    return (
        lax.slice_in_dim(values, 0, size, axis=axis),
        lax.slice_in_dim(values, size, 2 * size, axis=axis),
    )


def gather_batch(piece, axis, cut):
    b = lax.axis_index("batch")
    from_x = swap(piece, 1)
    from_y = swap(piece, 2)
    far_a = swap(halves(from_x, cut)[0], 2)
    far_b = swap(halves(from_y, cut)[1], 1)
    far = jnp.concatenate([far_a, far_b], axis=cut)
    rows = piece.shape[axis]
    shape = list(piece.shape)
    shape[axis] = 4 * rows
    whole = jnp.zeros(shape, piece.dtype)
    for bit, part in enumerate((piece, from_x, from_y, far)):
        whole = lax.dynamic_update_slice_in_dim(whole, part, (b ^ bit) * rows, axis)
    return whole


def scatter_batch(whole, axis, cut):
    b = lax.axis_index("batch")
    rows = whole.shape[axis] // 4

    def block(bit):
        return lax.dynamic_slice_in_dim(whole, (b ^ bit) * rows, rows, axis)

    own_a, own_b = halves(block(0), cut)
    x_a, x_b = halves(block(1), cut)
    y_a, y_b = halves(block(2), cut)
    far_a, far_b = halves(block(3), cut)
    got_own_a = swap(low(x_a), 1).astype(F32)
    got_y_a = swap(low(far_a), 1).astype(F32)
    got_own_b = swap(low(y_b), 2).astype(F32)
    got_x_b = swap(low(far_b), 2).astype(F32)
    last_a = swap(low(y_a.astype(F32) + got_y_a), 2).astype(F32)
    last_b = swap(low(x_b.astype(F32) + got_x_b), 1).astype(F32)
    return jnp.concatenate(
        [own_a.astype(F32) + got_own_a + last_a, own_b.astype(F32) + got_own_b + last_b], axis=cut
    )


def gather_tokens(values):
    return lax.all_gather(values, "expert", axis=0, tiled=True)


def scatter_tokens(values):
    return lax.psum_scatter(values, "expert", scatter_dimension=0, tiled=True).astype(F32)


def exchange(values):
    return lax.all_to_all(values, "expert", split_axis=0, concat_axis=0, tiled=True)


def silu_parts(gate, up):
    sigma = jax.nn.sigmoid(gate)
    return gate * sigma, up * sigma * (1.0 + gate * (1.0 - sigma))


def pack_device(
    block_input,
    seq_ids,
    routes,
    cotangent,
    qkv_weight,
    out_weight,
    shared_up,
    shared_down,
    router_weight,
    gain_attn,
    gain_ffn,
    expert_up,
    expert_down,
):
    b = lax.axis_index("batch")
    e = lax.axis_index("expert")
    rows_in = block_input[0]
    upstream = cotangent[0]
    tokens, width = rows_in.shape
    length = tokens * 8
    rows_w = qkv_weight.shape[0]
    pair = 2 * HEAD
    pairs_of_heads = width // pair
    hidden = expert_up.shape[2] // 2
    experts = expert_up.shape[0] * 8
    s_rows = shared_down.shape[0]
    s_own = 4 * s_rows
    s_pad = -(-s_own // 128) * 128
    scale = HEAD ** (-0.5)

    qkv_low = low(qkv_weight).reshape(rows_w, 3, pairs_of_heads, pair)
    nothing = jnp.zeros((rows_w, 3, pair), LOW)
    columns = [qkv_low[:, :, PAIR_OF[i]] if i in PAIR_OF else nothing for i in range(8)]
    columns = jnp.stack(columns).reshape(8, rows_w, 3 * pair)
    sup_low = low(shared_up).reshape(rows_w, 2, 4, 8, s_rows).transpose(3, 0, 1, 2, 4)
    sup_low = jnp.pad(
        sup_low.reshape(8, rows_w, 2, s_own), ((0, 0), (0, 0), (0, 0), (0, s_pad - s_own))
    )
    columns = jnp.concatenate([columns, sup_low.reshape(8, rows_w, 2 * s_pad)], axis=2)
    columns = exchange(columns).reshape(8 * rows_w, 3 * pair + 2 * s_pad)
    columns = gather_batch(columns, 0, 0)
    w_qkv = columns[:, : 3 * pair]
    w_sup = columns[:, 3 * pair :]
    up_low = gather_batch(low(expert_up), 1, 1)
    down_low = gather_batch(low(expert_down), 1, 1)
    w_sdown = gather_batch(low(shared_down), 0, 1)
    w_sdown = jnp.pad(w_sdown, ((0, s_pad - s_own), (0, 0)))
    core = lax.rem(e, 2)
    out_z = gather_tokens(low(out_weight))
    half_rows = 4 * rows_w
    out_mine = lax.dynamic_slice_in_dim(out_z, core * half_rows, half_rows, 0)
    out_mine = gather_batch(out_mine, 0, 1).reshape(4, 1, half_rows, width)
    out_other = swap(out_mine, 0, 1)
    w_out = jnp.zeros((4, 2, half_rows, width), LOW)
    w_out = lax.dynamic_update_slice_in_dim(w_out, out_mine, core, 1)
    w_out = lax.dynamic_update_slice_in_dim(w_out, out_other, 1 - core, 1).reshape(width, width)

    small = jnp.concatenate([router_weight, gain_attn[:, None], gain_ffn[:, None]], axis=1)
    small = lax.all_gather(low(small), AXES, axis=0, tiled=True)
    w_router = small[:, :experts]
    gain_first = small[:, experts].astype(F32)
    gain_second = small[:, experts + 1].astype(F32)
    marks = gather_tokens(jnp.concatenate([routes[0], seq_ids[0][:, None]], axis=1))
    route_all = marks[:, :TOP]
    ids_all = marks[:, TOP]
    cot_all = gather_tokens(low(upstream))

    inv_first = lax.rsqrt(jnp.mean(rows_in * rows_in, axis=1, keepdims=True) + EPSILON)
    xhat_first = rows_in * inv_first
    n1_all = gather_tokens(low(xhat_first * gain_first))
    positions = jnp.arange(length, dtype=jnp.int32)
    projected = dot(n1_all, w_qkv)
    queries = low(rotate(projected[:, :pair].reshape(length, 2, HEAD), positions, 1.0))
    keys = low(rotate(projected[:, pair : 2 * pair].reshape(length, 2, HEAD), positions, 1.0))
    values = low(projected[:, 2 * pair :].reshape(length, 2, HEAD))
    allowed = (positions[None, :] <= positions[:, None]) & (ids_all[None, :] == ids_all[:, None])
    scores = jnp.einsum("qhd,khd->hqk", queries, keys, preferred_element_type=F32) * scale
    scores = jnp.where(allowed[None], scores, NEGATIVE)
    top = jnp.max(scores, axis=2, keepdims=True)
    attn_p = jnp.exp(scores - top)
    total = jnp.sum(attn_p, axis=2, keepdims=True)
    attn_p = attn_p / total
    attn_low = low(attn_p)
    attended = jnp.einsum("hqk,khd->qhd", attn_low, values, preferred_element_type=F32)
    attended_low = low(attended)
    arrived = exchange(attended_low.reshape(8, tokens, pair))
    attn = jnp.concatenate([arrived[i] for i in PAIR_OF], axis=1)
    resid = rows_in + dot(attn, w_out)

    inv_second = lax.rsqrt(jnp.mean(resid * resid, axis=1, keepdims=True) + EPSILON)
    xhat_second = resid * inv_second
    n2 = low(xhat_second * gain_second)
    n2_all = gather_tokens(n2)
    logits = dot(n2_all, w_router)
    hot = route_all[:, :, None] == jnp.arange(experts, dtype=jnp.int32)[None, None, :]
    routed_to = jnp.any(hot, axis=1)
    logits = jnp.where(routed_to, logits, NEGATIVE)
    gates = jnp.where(routed_to, jnp.exp(logits - jnp.max(logits, axis=1, keepdims=True)), 0.0)
    gates = gates / jnp.sum(gates, axis=1, keepdims=True)
    mine = lax.dynamic_slice_in_dim(gates, 2 * e, 2, 1)

    output_part = 0.0
    drow_part = 0.0
    dgates = []
    up_terms = []
    down_terms = []
    for k in range(2):
        gate = mine[:, k : k + 1]
        pre = dot(n2_all, up_low[k])
        silu, slope = silu_parts(pre[:, :hidden], pre[:, hidden:])
        hid = silu * pre[:, hidden:]
        back = dot(cot_all, down_low[k], ((1,), (1,)))
        dgates.append(jnp.sum(back * hid, axis=1, keepdims=True))
        hid_low = low(hid * gate)
        output_part = output_part + dot(hid_low, down_low[k])
        down_terms.append(dot(hid_low, cot_all, ((0,), (0,))))
        back = back * gate
        dpre = low(jnp.concatenate([back * slope, back * silu], axis=1))
        up_terms.append(dot(n2_all, dpre, ((0,), (0,))))
        drow_part = drow_part + dot(dpre, up_low[k], ((1,), (1,)))
    pre = dot(n2_all, w_sup)
    silu, slope = silu_parts(pre[:, :s_pad], pre[:, s_pad:])
    hid_low = low(silu * pre[:, s_pad:])
    back = dot(cot_all, w_sdown, ((1,), (1,)))
    output_part = output_part + dot(hid_low, w_sdown)
    sdown_term = dot(hid_low, cot_all, ((0,), (0,)))[:s_own]
    dpre = low(jnp.concatenate([back * slope, back * silu], axis=1))
    sup_term = dot(n2_all, dpre, ((0,), (0,)))
    drow_part = drow_part + dot(dpre, w_sup, ((1,), (1,)))
    output_rows = resid + scatter_tokens(low(output_part))
    expert_up_grad = scatter_batch(low(jnp.stack(up_terms)), 1, 1)
    expert_down_grad = scatter_batch(low(jnp.stack(down_terms)), 1, 1)
    shared_down_grad = scatter_batch(low(sdown_term), 0, 1)

    lane = jnp.arange(experts, dtype=jnp.int32)[None, :] - 2 * e
    dgate = jnp.where(lane == 0, dgates[0], 0.0) + jnp.where(lane == 1, dgates[1], 0.0)
    dgate_high = low(dgate)
    dgate_rest = low(dgate - dgate_high.astype(F32))
    spare = jnp.zeros((length, 128 - 2 * experts), LOW)
    dn2 = scatter_tokens(
        jnp.concatenate([low(drow_part), dgate_high, dgate_rest, spare], axis=1)
    )
    dgate = dn2[:, width : width + experts] + dn2[:, width + experts : width + 2 * experts]
    own_gates = lax.dynamic_slice_in_dim(gates, e * tokens, tokens, 0)
    dlogits = low(own_gates * (dgate - jnp.sum(own_gates * dgate, axis=1, keepdims=True)))
    router_term = dot(dlogits, n2, ((0,), (0,)))
    dn2 = dn2[:, :width] + dot(dlogits, w_router, ((1,), (1,)))
    dresid, gain_ffn_term = norm_back(dn2, xhat_second, inv_second, gain_second)
    dresid = upstream + dresid
    dproj = low(dresid)
    dattn = low(dot(dproj, w_out, ((1,), (1,))))
    dattn = jnp.stack(
        [
            dattn[:, PAIR_OF[i] * pair : (PAIR_OF[i] + 1) * pair]
            if i in PAIR_OF
            else jnp.zeros((tokens, pair), LOW)
            for i in range(8)
        ]
    )
    dattn = exchange(dattn).reshape(length, 2, HEAD)
    out_term = dot(attn, dproj, ((0,), (0,))).reshape(4, 2, half_rows, width)
    out_away = swap(low(lax.dynamic_slice_in_dim(out_term, 1 - core, 1, 1)), 0, 1)
    out_term = lax.dynamic_slice_in_dim(out_term, core, 1, 1) + out_away
    out_term = scatter_batch(low(out_term).reshape(4 * half_rows, width), 0, 1)
    out_pad = lax.dynamic_update_slice_in_dim(
        jnp.zeros((2 * half_rows, width), LOW), low(out_term), core * half_rows, 0
    )
    out_grad = scatter_tokens(out_pad)

    delta = jnp.sum(dattn.astype(F32) * attended, axis=2).T[:, :, None]
    dprob = jnp.einsum("qhd,khd->hqk", dattn, values, preferred_element_type=F32)
    dscore = low(attn_p * (dprob - delta))
    dquery = jnp.einsum("hqk,khd->qhd", dscore, keys, preferred_element_type=F32)
    dkey = jnp.einsum("hqk,qhd->khd", dscore, queries, preferred_element_type=F32)
    dvalue = jnp.einsum("hqk,qhd->khd", attn_low, dattn, preferred_element_type=F32)
    dprojected = low(
        jnp.concatenate(
            [
                rotate(dquery * scale, positions, -1.0).reshape(length, pair),
                rotate(dkey * scale, positions, -1.0).reshape(length, pair),
                dvalue.reshape(length, pair),
            ],
            axis=1,
        )
    )
    qkv_term = dot(n1_all, dprojected, ((0,), (0,)))
    dn1 = scatter_tokens(low(dot(dprojected, w_qkv, ((1,), (1,)))))
    dinput, gain_attn_term = norm_back(dn1, xhat_first, inv_first, gain_first)
    input_grad = dresid + dinput

    columns = scatter_batch(low(jnp.concatenate([qkv_term, sup_term], axis=1)), 0, 0)
    columns = exchange(low(columns).reshape(8, rows_w, 3 * pair + 2 * s_pad)).astype(F32)
    qkv_grad = jnp.stack([columns[i, :, : 3 * pair] for i in PAIR_OF])
    qkv_grad = qkv_grad.reshape(pairs_of_heads, rows_w, 3, pair).transpose(1, 2, 0, 3)
    qkv_grad = qkv_grad.reshape(rows_w, 3 * width)
    sup_grad = columns[:, :, 3 * pair :].reshape(8, rows_w, 2, s_pad)[..., :s_own]
    sup_grad = sup_grad.reshape(8, rows_w, 2, 4, s_rows).transpose(1, 2, 3, 0, 4)
    sup_grad = sup_grad.reshape(rows_w, shared_up.shape[1])

    small = jnp.concatenate([router_term, gain_attn_term[None], gain_ffn_term[None]], axis=0)
    small = lax.psum(small, AXES)
    small = lax.dynamic_slice_in_dim(small, (b * 8 + e) * rows_w, rows_w, 1)
    return (
        output_rows[None],
        input_grad[None],
        qkv_grad,
        out_grad,
        sup_grad,
        shared_down_grad,
        small[:experts].T,
        small[experts],
        small[experts + 1],
        expert_up_grad,
        expert_down_grad,
    )


def solution(mesh):
    in_specs = (
        P("batch", "expert", None),
        P("batch", "expert"),
        P("batch", "expert", None),
        P("batch", "expert", None),
        P(("batch", "expert"), None),
        P(("batch", "expert"), None),
        P(("batch", "expert"), None),
        P(("batch", "expert"), None),
        P(("batch", "expert"), None),
        P(("batch", "expert")),
        P(("batch", "expert")),
        P("expert", "batch", None),
        P("expert", "batch", None),
    )
    out_specs = (
        P("batch", "expert", None),
        P("batch", "expert", None),
        P(("batch", "expert"), None),
        P(("batch", "expert"), None),
        P(("batch", "expert"), None),
        P(("batch", "expert"), None),
        P(("batch", "expert"), None),
        P(("batch", "expert")),
        P(("batch", "expert")),
        P("expert", "batch", None),
        P("expert", "batch", None),
    )
    sizes = dict(mesh.shape)
    body = pack_device if sizes == {"batch": 4, "expert": 8} else per_device
    return jax.shard_map(
        body, mesh=mesh, in_specs=in_specs, out_specs=out_specs, check_vma=False
    )
```

```python
import functools

import jax
import jax.numpy as jnp
from jax import lax
from jax.experimental import pallas as pl
from jax.experimental.pallas import tpu as pltpu
from jax.sharding import PartitionSpec as P

HEAD = 128
TOP = 6


EPSILON = 1e-06
NEGATIVE = -1e30


def rotate(values, positions, sign):
    half = values.shape[-1] // 2
    frequency = 10000.0 ** (-jnp.arange(half, dtype=jnp.float32) / half)
    angle = positions.astype(jnp.float32)[:, None] * frequency[None, :]
    cosine = jnp.cos(angle)[:, None, :]
    sine = sign * jnp.sin(angle)[:, None, :]
    first = values[..., :half]
    second = values[..., half:]
    return jnp.concatenate(
        [first * cosine - second * sine, first * sine + second * cosine], axis=-1
    )


def swiglu(pre, hidden_width):
    return jax.nn.silu(pre[..., :hidden_width]) * pre[..., hidden_width:]


def swiglu_back(pre, dhidden, hidden_width):
    gate_part = pre[..., :hidden_width]
    up_part = pre[..., hidden_width:]
    sigma = jax.nn.sigmoid(gate_part)
    dgate = dhidden * up_part * sigma * (1.0 + gate_part * (1.0 - sigma))
    dupper = dhidden * gate_part * sigma
    return jnp.concatenate([dgate, dupper], axis=-1)


def norm_back(dnormed, normed, inv_rms, gain):
    dscaled = dnormed * gain
    dinputs = inv_rms * (dscaled - normed * jnp.mean(dscaled * normed, axis=1, keepdims=True))
    return (dinputs, jnp.sum(dnormed * normed, axis=0))


def per_device(
    block_input,
    seq_ids,
    routes,
    cotangent,
    qkv_weight,
    out_weight,
    shared_up,
    shared_down,
    router_weight,
    gain_attn,
    gain_ffn,
    expert_up,
    expert_down,
):
    dense = (
        lax.all_gather(qkv_weight.astype(jnp.bfloat16), ("batch", "expert"), axis=0, tiled=True),
        lax.all_gather(out_weight.astype(jnp.bfloat16), ("batch", "expert"), axis=0, tiled=True),
        lax.all_gather(shared_up.astype(jnp.bfloat16), ("batch", "expert"), axis=0, tiled=True),
        lax.all_gather(shared_down.astype(jnp.bfloat16), ("batch", "expert"), axis=0, tiled=True),
        lax.all_gather(router_weight.astype(jnp.bfloat16), ("batch", "expert"), axis=0, tiled=True),
        lax.all_gather(gain_attn.astype(jnp.bfloat16), ("batch", "expert"), axis=0, tiled=True),
        lax.all_gather(gain_ffn.astype(jnp.bfloat16), ("batch", "expert"), axis=0, tiled=True),
    )
    full_qkv, full_out, full_sup, full_sdown, full_router, low_gain_a, low_gain_f = dense
    gain_first = low_gain_a.astype(jnp.float32)
    gain_second = low_gain_f.astype(jnp.float32)
    experts_up, experts_down = (
        lax.all_gather(expert_up.astype(jnp.bfloat16), "batch", axis=1, tiled=True),
        lax.all_gather(expert_down.astype(jnp.bfloat16), "batch", axis=1, tiled=True),
    )
    rows_in = block_input[0]
    ids_local = seq_ids[0]
    route_local = routes[0]
    upstream = cotangent[0]
    tokens_dev = rows_in.shape[0]
    model_width = rows_in.shape[1]
    heads_count = model_width // HEAD
    groups = lax.axis_size("expert")
    local_experts = experts_up.shape[0]
    experts_all = local_experts * groups
    shared_width = full_sdown.shape[0]
    hidden_width = experts_down.shape[1]
    capacity = max(2, tokens_dev * TOP * 3 // (experts_all * 2))
    score_scale = HEAD ** (-0.5)
    positions = lax.axis_index("expert") * tokens_dev + jnp.arange(tokens_dev, dtype=jnp.int32)
    key_ids = lax.all_gather(ids_local, "expert", axis=0, tiled=True)
    inv_first = lax.rsqrt(jnp.mean(rows_in * rows_in, axis=1, keepdims=True) + EPSILON)
    normed_first = rows_in * inv_first
    input_low = (normed_first * gain_first).astype(jnp.bfloat16)
    projected = jnp.dot(input_low, full_qkv, preferred_element_type=jnp.float32)
    queries = rotate(
        projected[:, :model_width].reshape(tokens_dev, heads_count, HEAD), positions, 1.0
    ).astype(jnp.bfloat16)
    keys = rotate(
        projected[:, model_width : 2 * model_width].reshape(tokens_dev, heads_count, HEAD),
        positions,
        1.0,
    ).astype(jnp.bfloat16)
    values = (
        projected[:, 2 * model_width :].reshape(tokens_dev, heads_count, HEAD).astype(jnp.bfloat16)
    )

    def key_mask(key_count):
        key_pos = jnp.arange(key_count, dtype=jnp.int32)
        return (key_pos[None, :] <= positions[:, None]) & (key_ids[None, :] == ids_local[:, None])

    run_max = jnp.full((heads_count, tokens_dev), NEGATIVE, jnp.float32)
    key_piece = lax.all_gather(keys, "expert", axis=0, tiled=True)
    value_piece = lax.all_gather(values, "expert", axis=0, tiled=True)
    allowed = key_mask(key_piece.shape[0])[None]
    scores = (
        jnp.einsum("qhd,khd->hqk", queries, key_piece, preferred_element_type=jnp.float32)
        * score_scale
    )
    scores = jnp.where(allowed, scores, NEGATIVE)
    new_max = jnp.maximum(run_max, jnp.max(scores, axis=2))
    weights = jnp.where(allowed, jnp.exp(scores - new_max[:, :, None]), 0.0)
    run_sum = jnp.sum(weights, axis=2)
    update = jnp.einsum(
        "hqk,khd->qhd",
        weights.astype(jnp.bfloat16),
        value_piece,
        preferred_element_type=jnp.float32,
    )
    run_acc = update
    run_max, run_sum, run_acc = (new_max, run_sum, run_acc)
    attn_full = run_acc / jnp.transpose(run_sum)[:, :, None]
    logsum = run_max + jnp.log(run_sum)
    attn_low = attn_full.reshape(tokens_dev, model_width).astype(jnp.bfloat16)
    resid = rows_in + jnp.dot(attn_low, full_out, preferred_element_type=jnp.float32)
    inv_second = lax.rsqrt(jnp.mean(resid * resid, axis=1, keepdims=True) + EPSILON)
    normed_second = resid * inv_second
    ffn_low = (normed_second * gain_second).astype(jnp.bfloat16)
    logits = jnp.dot(ffn_low, full_router, preferred_element_type=jnp.float32)
    probs = jax.nn.softmax(logits, axis=1)
    route_hot = route_local[:, :, None] == jnp.arange(experts_all, dtype=jnp.int32)[None, None, :]
    chosen = jnp.sum(jnp.where(route_hot, probs[:, None, :], 0.0), axis=2)
    chosen_sum = jnp.sum(chosen, axis=1, keepdims=True)
    gates = chosen / chosen_sum
    shared_pre = jnp.dot(ffn_low, full_sup, preferred_element_type=jnp.float32)
    shared_hidden = swiglu(shared_pre, shared_width).astype(jnp.bfloat16)
    shared_result = jnp.dot(shared_hidden, full_sdown, preferred_element_type=jnp.float32)
    flat_route = route_local.reshape(-1)
    flat_hot = (flat_route[:, None] == jnp.arange(experts_all, dtype=jnp.int32)[None, :]).astype(
        jnp.bfloat16
    )
    pair_count = tokens_dev * TOP
    pair_index = jnp.arange(pair_count, dtype=jnp.int32)
    earlier = (pair_index[None, :] < pair_index[:, None]).astype(jnp.bfloat16)
    counts = jnp.dot(earlier, flat_hot, preferred_element_type=jnp.float32)
    slots = jnp.sum(counts * flat_hot, axis=1).astype(jnp.int32)
    source_table = (
        jnp.full((experts_all * capacity,), pair_count, jnp.int32)
        .at[flat_route * capacity + slots]
        .set(jnp.arange(pair_count, dtype=jnp.int32))
    )
    send_table = jnp.transpose(
        source_table.reshape(groups, local_experts, capacity), (1, 0, 2)
    ).reshape(-1)
    return_pos = (
        flat_route % local_experts * (groups * capacity)
        + flat_route // local_experts * capacity
        + slots
    )
    padded_rows = jnp.concatenate([ffn_low, jnp.zeros((1, model_width), jnp.bfloat16)], axis=0)
    send_rows = padded_rows[send_table // TOP].reshape(local_experts, groups, capacity, model_width)
    received = lax.all_to_all(send_rows, "expert", split_axis=1, concat_axis=1, tiled=True)
    expert_rows = received.reshape(local_experts, groups * capacity, model_width)
    expert_pre = jnp.einsum(
        "erd,edf->erf", expert_rows, experts_up, preferred_element_type=jnp.float32
    )
    expert_hidden = swiglu(expert_pre, hidden_width).astype(jnp.bfloat16)
    expert_result = jnp.einsum(
        "erf,efd->erd", expert_hidden, experts_down, preferred_element_type=jnp.float32
    ).astype(jnp.bfloat16)
    returned = lax.all_to_all(
        expert_result.reshape(local_experts, groups, capacity, model_width),
        "expert",
        split_axis=1,
        concat_axis=1,
        tiled=True,
    )
    token_outputs = returned.reshape(-1, model_width)[return_pos].reshape(
        tokens_dev, TOP, model_width
    )
    routed = jnp.sum(gates[:, :, None] * token_outputs, axis=1)
    output_rows = resid + shared_result + routed
    shared_cot = upstream.astype(jnp.bfloat16)
    shared_down_term = jnp.dot(shared_hidden.T, shared_cot, preferred_element_type=jnp.float32)
    dshared_hidden = jnp.dot(shared_cot, full_sdown.T, preferred_element_type=jnp.float32)
    dshared_pre = swiglu_back(shared_pre, dshared_hidden, shared_width).astype(jnp.bfloat16)
    shared_up_term = jnp.dot(ffn_low.T, dshared_pre, preferred_element_type=jnp.float32)
    dnormed_second = jnp.dot(dshared_pre, full_sup.T, preferred_element_type=jnp.float32)
    token_cot = (gates[:, :, None] * upstream[:, None, :]).astype(jnp.bfloat16)
    dgates = jnp.sum(upstream[:, None, :] * token_outputs, axis=2)
    padded_cot = jnp.concatenate(
        [token_cot.reshape(-1, model_width), jnp.zeros((1, model_width), jnp.bfloat16)], axis=0
    )
    send_cot = padded_cot[send_table].reshape(local_experts, groups, capacity, model_width)
    received_cot = lax.all_to_all(
        send_cot, "expert", split_axis=1, concat_axis=1, tiled=True
    ).reshape(local_experts, groups * capacity, model_width)
    down_term = jnp.einsum(
        "erf,erd->efd", expert_hidden, received_cot, preferred_element_type=jnp.float32
    )
    dexpert_hidden = jnp.einsum(
        "erd,efd->erf", received_cot, experts_down, preferred_element_type=jnp.float32
    )
    dexpert_pre = swiglu_back(expert_pre, dexpert_hidden, hidden_width).astype(jnp.bfloat16)
    up_term = jnp.einsum(
        "erd,erf->edf", expert_rows, dexpert_pre, preferred_element_type=jnp.float32
    )
    drows = jnp.einsum(
        "erf,edf->erd", dexpert_pre, experts_up, preferred_element_type=jnp.float32
    ).astype(jnp.bfloat16)
    returned_grad = lax.all_to_all(
        drows.reshape(local_experts, groups, capacity, model_width),
        "expert",
        split_axis=1,
        concat_axis=1,
        tiled=True,
    )
    row_grads = returned_grad.reshape(-1, model_width)[return_pos].reshape(
        tokens_dev, TOP, model_width
    )
    dnormed_second = dnormed_second + jnp.sum(row_grads, axis=1, dtype=jnp.float32)
    expert_up_grad, expert_down_grad = (
        lax.psum_scatter(
            up_term.astype(jnp.bfloat16), "batch", scatter_dimension=1, tiled=True
        ).astype(jnp.float32),
        lax.psum_scatter(
            down_term.astype(jnp.bfloat16), "batch", scatter_dimension=1, tiled=True
        ).astype(jnp.float32),
    )
    dchosen = (dgates - jnp.sum(dgates * gates, axis=1, keepdims=True)) / chosen_sum
    dprobs = jnp.sum(jnp.where(route_hot, dchosen[:, :, None], 0.0), axis=1)
    dlogits = (probs * (dprobs - jnp.sum(probs * dprobs, axis=1, keepdims=True))).astype(
        jnp.bfloat16
    )
    router_term = jnp.dot(ffn_low.T, dlogits, preferred_element_type=jnp.float32)
    dnormed_second = dnormed_second + jnp.dot(
        dlogits, full_router.T, preferred_element_type=jnp.float32
    )
    dresid_norm, gain_ffn_term = norm_back(dnormed_second, normed_second, inv_second, gain_second)
    dresid = upstream + dresid_norm
    dproj = dresid.astype(jnp.bfloat16)
    out_term = jnp.dot(attn_low.T, dproj, preferred_element_type=jnp.float32)
    dattn = (
        jnp.dot(dproj, full_out.T, preferred_element_type=jnp.float32)
        .astype(jnp.bfloat16)
        .reshape(tokens_dev, heads_count, HEAD)
    )
    delta_rows = jnp.sum(dattn.astype(jnp.float32) * attn_full, axis=2)
    delta_heads = jnp.transpose(delta_rows)
    key_piece = lax.all_gather(keys, "expert", axis=0, tiled=True)
    value_piece = lax.all_gather(values, "expert", axis=0, tiled=True)
    allowed = key_mask(key_piece.shape[0])[None]
    scores = (
        jnp.einsum("qhd,khd->hqk", queries, key_piece, preferred_element_type=jnp.float32)
        * score_scale
    )
    attn_probs = jnp.where(allowed, jnp.exp(scores - logsum[:, :, None]), 0.0)
    dprob = jnp.einsum("qhd,khd->hqk", dattn, value_piece, preferred_element_type=jnp.float32)
    dscore = (attn_probs * (dprob - delta_heads[:, :, None])).astype(jnp.bfloat16)
    attn_probs, dscore = (attn_probs, dscore)
    dquery = jnp.einsum("hqk,khd->qhd", dscore, key_piece, preferred_element_type=jnp.float32)
    dkey_piece = jnp.einsum("hqk,qhd->khd", dscore, queries, preferred_element_type=jnp.float32)
    dvalue_piece = jnp.einsum(
        "hqk,qhd->khd", attn_probs.astype(jnp.bfloat16), dattn, preferred_element_type=jnp.float32
    )
    folded = (dquery, dkey_piece, dvalue_piece)
    dquery = folded[0]
    dkey, dvalue = (
        lax.psum_scatter(
            folded[1].astype(jnp.bfloat16), "expert", scatter_dimension=0, tiled=True
        ).astype(jnp.float32),
        lax.psum_scatter(
            folded[2].astype(jnp.bfloat16), "expert", scatter_dimension=0, tiled=True
        ).astype(jnp.float32),
    )
    dquery_raw = rotate(dquery * score_scale, positions, -1.0).reshape(tokens_dev, model_width)
    dkey_raw = rotate(dkey * score_scale, positions, -1.0).reshape(tokens_dev, model_width)
    dprojected = jnp.concatenate(
        [dquery_raw, dkey_raw, dvalue.reshape(tokens_dev, model_width)], axis=1
    ).astype(jnp.bfloat16)
    qkv_term = jnp.dot(input_low.T, dprojected, preferred_element_type=jnp.float32)
    dnormed_first = jnp.dot(dprojected, full_qkv.T, preferred_element_type=jnp.float32)
    dinput_norm, gain_attn_term = norm_back(dnormed_first, normed_first, inv_first, gain_first)
    input_grad = dresid + dinput_norm
    grads = (
        lax.psum_scatter(qkv_term, ("batch", "expert"), scatter_dimension=0, tiled=True),
        lax.psum_scatter(out_term, ("batch", "expert"), scatter_dimension=0, tiled=True),
        lax.psum_scatter(shared_up_term, ("batch", "expert"), scatter_dimension=0, tiled=True),
        lax.psum_scatter(shared_down_term, ("batch", "expert"), scatter_dimension=0, tiled=True),
        lax.psum_scatter(router_term, ("batch", "expert"), scatter_dimension=0, tiled=True),
        lax.psum_scatter(gain_attn_term, ("batch", "expert"), scatter_dimension=0, tiled=True),
        lax.psum_scatter(gain_ffn_term, ("batch", "expert"), scatter_dimension=0, tiled=True),
    )
    (
        qkv_grad,
        out_grad,
        shared_up_grad,
        shared_down_grad,
        router_grad,
        gain_attn_grad,
        gain_ffn_grad,
    ) = grads
    return (
        output_rows[None],
        input_grad[None],
        qkv_grad,
        out_grad,
        shared_up_grad,
        shared_down_grad,
        router_grad,
        gain_attn_grad,
        gain_ffn_grad,
        expert_up_grad,
        expert_down_grad,
    )


PAIR_OF = {0: 0, 2: 1, 4: 2, 6: 3, 3: 4}
AXES = ("batch", "expert")
F32 = jnp.float32
LOW = jnp.bfloat16


def low(values):
    return values.astype(LOW)


def dot(left, right, dims=((1,), (0,))):
    return lax.dot_general(left, right, (dims, ((), ())), preferred_element_type=F32)


def swap(values, batch_bit, expert_bit=0, only=range(8)):
    pairs = [
        (b * 8 + e, (b ^ batch_bit) * 8 + (e ^ expert_bit)) for b in range(4) for e in range(8)
    ]
    pairs = [pair for pair in pairs if pair[0] % 8 in only]
    return lax.ppermute(values, AXES, pairs)


def halves(values, axis):
    size = values.shape[axis] // 2
    return (
        lax.slice_in_dim(values, 0, size, axis=axis),
        lax.slice_in_dim(values, size, 2 * size, axis=axis),
    )


def gather_near(piece):
    return piece, swap(piece, 1), swap(piece, 2)


def gather_far(near, axis, cut):
    b = lax.axis_index("batch")
    piece, from_x, from_y = near
    far_a = swap(halves(from_x, cut)[0], 2)
    far_b = swap(halves(from_y, cut)[1], 1)
    far = jnp.concatenate([far_a, far_b], axis=cut)
    rows = piece.shape[axis]
    shape = list(piece.shape)
    shape[axis] = 4 * rows
    whole = jnp.zeros(shape, piece.dtype)
    for bit, part in enumerate((piece, from_x, from_y, far)):
        whole = lax.dynamic_update_slice_in_dim(whole, part, (b ^ bit) * rows, axis)
    return whole


def after(values, *earlier):
    return lax.optimization_barrier((values, *earlier))[0]


def scatter_batch(whole, axis, cut):
    b = lax.axis_index("batch")
    rows = whole.shape[axis] // 4

    def block(bit):
        return lax.dynamic_slice_in_dim(whole, (b ^ bit) * rows, rows, axis)

    own_a, own_b = halves(block(0), cut)
    x_a, x_b = halves(block(1), cut)
    y_a, y_b = halves(block(2), cut)
    far_a, far_b = halves(block(3), cut)
    got_own_a = swap(low(x_a), 1).astype(F32)
    got_y_a = swap(low(far_a), 1).astype(F32)
    got_own_b = swap(low(y_b), 2).astype(F32)
    got_x_b = swap(low(far_b), 2).astype(F32)
    last_a = swap(low(y_a.astype(F32) + got_y_a), 2).astype(F32)
    last_b = swap(low(x_b.astype(F32) + got_x_b), 1).astype(F32)
    return jnp.concatenate(
        [own_a.astype(F32) + got_own_a + last_a, own_b.astype(F32) + got_own_b + last_b], axis=cut
    )


def z_shift(values, steps):
    pairs = [
        (b * 8 + e, b * 8 + (e + 2 * steps) % 8) for b in range(4) for e in range(8)
    ]
    return lax.ppermute(values, AXES, pairs)


def gather_z(block):
    z = lax.axis_index("expert") // 2
    whole = jnp.zeros((4, *block.shape), block.dtype)
    whole = lax.dynamic_update_index_in_dim(whole, block, z, 0)
    for steps in (1, 2, 3):
        part = z_shift(block, steps)
        whole = lax.dynamic_update_index_in_dim(whole, part, lax.rem(z + 4 - steps, 4), 0)
    return whole


def gather_pack(block):
    core = lax.rem(lax.axis_index("expert"), 2)
    mine = gather_z(block)
    other = swap(mine, 0, 1)
    first = jnp.where(core == 0, mine, other)
    second = jnp.where(core == 0, other, mine)
    return jnp.stack([first, second], axis=1).reshape(8, *block.shape)


def scatter_z(blocks):
    z = lax.axis_index("expert") // 2
    total = lax.dynamic_index_in_dim(blocks, z, 0, False).astype(F32)
    for steps in (1, 2, 3):
        block = lax.dynamic_index_in_dim(blocks, lax.rem(z + steps, 4), 0, False)
        total = total + z_shift(low(block), steps).astype(F32)
    return total


def scatter_pack(blocks):
    core = lax.rem(lax.axis_index("expert"), 2)
    pairs = blocks.reshape(4, 2, *blocks.shape[1:])
    away = lax.dynamic_index_in_dim(pairs, 1 - core, 1, False)
    mine = lax.dynamic_index_in_dim(pairs, core, 1, False)
    return scatter_z(mine.astype(F32) + swap(low(away), 0, 1).astype(F32))


def total_all(values):
    for batch_bit, expert_bit in ((0, 1), (1, 0), (2, 0), (0, 2), (0, 4)):
        values = values + swap(values, batch_bit, expert_bit)
    return values


MESH_ID = pl.DeviceIdType.MESH


def place():
    b = lax.axis_index("batch")
    e = lax.axis_index("expert")
    return b, e, e // 2, lax.rem(e, 2)


def greet(devices):
    barrier = pltpu.get_barrier_semaphore()
    for device in devices:
        pl.semaphore_signal(barrier, inc=1, device_id=device, device_id_type=MESH_ID)
    pl.semaphore_wait(barrier, len(devices))


def greet_line():
    b, e, z, core = place()
    barrier = pltpu.get_barrier_semaphore()
    pl.semaphore_signal(barrier, inc=1, device_id=(b, e ^ 1), device_id_type=MESH_ID)

    @pl.when(z > 0)
    def _():
        pl.semaphore_signal(barrier, inc=1, device_id=(b, e - 2), device_id_type=MESH_ID)

    @pl.when(z < 3)
    def _():
        pl.semaphore_signal(barrier, inc=1, device_id=(b, e + 2), device_id_type=MESH_ID)

    ends = jnp.where((z == 0) | (z == 3), 1, 0)
    pl.semaphore_wait(barrier, 3 - ends)


def pack_mates():
    b, e, _, _ = place()
    return [(b, lax.rem(e + i, 8)) for i in range(1, 8)]


def send(src, dst, send_sem, recv_sem, device):
    return pltpu.make_async_remote_copy(
        src_ref=src,
        dst_ref=dst,
        send_sem=send_sem,
        recv_sem=recv_sem,
        device_id=device,
        device_id_type=MESH_ID,
    )


GATHER_SEMS = [pltpu.SemaphoreType.DMA((3,))] * 4 + [pltpu.SemaphoreType.DMA((4,))] * 2


def line_stages(buf, up_send, up_recv, down_send, down_recv, core_send, core_recv):
    b, e, z, core = place()

    def to_core(owner_z):
        block = buf.at[2 * owner_z + core]
        return send(block, block, core_send.at[owner_z], core_recv.at[owner_z], (b, e ^ 1))

    def up(step):
        block = buf.at[jnp.maximum(2 * (z - step), 0) + core]
        return send(block, block, up_send.at[step], up_recv.at[step], (b, jnp.minimum(e + 2, 7)))

    def down(step):
        block = buf.at[jnp.minimum(2 * (z + step), 6) + core]
        return send(
            block, block, down_send.at[step], down_recv.at[step], (b, jnp.maximum(e - 2, 0))
        )

    def start(step):
        @pl.when((z >= step) & (z < 3))
        def _():
            up(step).start()

        @pl.when((z + step <= 3) & (z > 0))
        def _():
            down(step).start()

        if step == 0:
            to_core(z).start()

    def arrive(step):
        @pl.when(z - 1 - step >= 0)
        def _():
            up(step).wait_recv()

        @pl.when(z + 1 + step <= 3)
        def _():
            down(step).wait_recv()

        if step < 2:
            start(step + 1)

        @pl.when(z - 1 - step >= 0)
        def _():
            to_core(z - 1 - step).start()

        @pl.when(z + 1 + step <= 3)
        def _():
            to_core(z + 1 + step).start()

    def finish():
        for owner_z in range(4):
            to_core(owner_z).wait()
        for step in range(3):

            @pl.when((z >= step) & (z < 3))
            def _():
                up(step).wait_send()

            @pl.when((z + step <= 3) & (z > 0))
            def _():
                down(step).wait_send()

    return [lambda: start(0)] + [functools.partial(arrive, i) for i in range(3)] + [finish]


def line_gather(buf, *sems):
    for stage in line_stages(buf, *sems):
        stage()


def scatter_scratch(tokens, width):
    return [pltpu.VMEM((4, tokens, width), LOW)] + [
        pltpu.VMEM((3, tokens, width), LOW) for _ in range(4)
    ]


SCATTER_SEMS = [pltpu.SemaphoreType.DMA((3,))] * 4 + [pltpu.SemaphoreType.DMA((4,))] * 2


def line_scatter(
    part,
    from_core,
    up_out,
    up_in,
    down_out,
    down_in,
    up_send,
    up_recv,
    down_send,
    down_recv,
    core_send,
    core_recv,
):
    b, e, z, core = place()

    def to_core(target):
        return send(
            part.at[2 * target + 1 - core],
            from_core.at[target],
            core_send.at[target],
            core_recv.at[target],
            (b, e ^ 1),
        )

    def up(step):
        return send(
            up_out.at[step],
            up_in.at[step],
            up_send.at[step],
            up_recv.at[step],
            (b, jnp.minimum(e + 2, 7)),
        )

    def down(step):
        return send(
            down_out.at[step],
            down_in.at[step],
            down_send.at[step],
            down_recv.at[step],
            (b, jnp.maximum(e - 2, 0)),
        )

    def chip_sum(target):
        return part[2 * target + core].astype(F32) + from_core[target].astype(F32)

    for target in (3, 0, 2, 1):
        to_core(target).start()
    for target in range(4):
        to_core(target).wait()
    for step in range(3):
        top = 3 - step

        @pl.when(z < top)
        def _():
            @pl.when(z > 0)
            def _():
                up(step).wait_recv()
                up_out[step] = low(chip_sum(top) + up_in[step].astype(F32))

            @pl.when(z == 0)
            def _():
                up_out[step] = low(chip_sum(top))

            up(step).start()

        @pl.when(z > step)
        def _():
            @pl.when(z < 3)
            def _():
                down(step).wait_recv()
                down_out[step] = low(chip_sum(step) + down_in[step].astype(F32))

            @pl.when(z == 3)
            def _():
                down_out[step] = low(chip_sum(step))

            down(step).start()

    @pl.when(z == 0)
    def _():
        up_in[0] = jnp.zeros_like(up_in[0])

    @pl.when(z == 3)
    def _():
        down_in[0] = jnp.zeros_like(down_in[0])

    last_up = lax.rem(3 - z, 3)
    last_down = lax.rem(z, 3)

    @pl.when(z > 0)
    def _():
        up(last_up).wait_recv()

    @pl.when(z < 3)
    def _():
        down(last_down).wait_recv()

    total = chip_sum(z) + up_in[last_up].astype(F32) + down_in[last_down].astype(F32)
    for step in range(3):

        @pl.when(z < 3 - step)
        def _():
            up(step).wait_send()

        @pl.when(z > step)
        def _():
            down(step).wait_send()

    return total


def kernel_call(body, outs, args, scratch, collective_id):
    vmem = pl.BlockSpec(memory_space=pltpu.VMEM)
    return pl.pallas_call(
        body,
        out_shape=[jax.ShapeDtypeStruct(shape, dtype) for shape, dtype in outs],
        in_specs=[vmem] * len(args),
        out_specs=[vmem] * len(outs),
        scratch_shapes=scratch,
        compiler_params=pltpu.CompilerParams(
            collective_id=collective_id, has_side_effects=True, vmem_limit_bytes=48 * 2**20
        ),
    )(*args)


def opening_kernel(
    rows, small, marks, columns, w_out, n1_all, gains, small_all, marks_all, columns_all, out_all,
    *sems,
):
    (
        b_send, b_recv, s_send, s_recv, m_send, m_recv, c_send, c_recv,
        x_send, x_recv, y_send, y_recv, z_send, z_recv, o_send, o_recv, p_send, p_recv,
    ) = sems[:18]
    b, e, z, core = place()
    over = [(b ^ bit, e) for bit in (1, 2, 3)]
    mates = pack_mates()
    greet(over + mates)
    small_all[e, b] = small[...]
    marks_all[e] = marks[...]
    columns_all[b, e] = columns[e]
    out_all[core, b, z] = w_out[...]
    first = []
    for i, device in enumerate(over):
        first.append(send(small, small_all.at[e, b], b_send.at[i], b_recv.at[i], device))
        first[-1].start()
    across = []
    for i, device in enumerate(mates):
        across.append(
            send(columns.at[device[1]], columns_all.at[b, e], c_send.at[i], c_recv.at[i], device)
        )
        across[-1].start()
    along = []
    for i in range(3):
        device = (b, lax.rem(e + 2 * i + 2, 8))
        along.append(
            send(w_out, out_all.at[core, b, z], z_send.at[i], z_recv.at[i], device)
        )
        along[-1].start()
    rest = []
    for i, device in enumerate(mates):
        rest.append(send(marks, marks_all.at[e], m_send.at[i], m_recv.at[i], device))
        rest[-1].start()
    values = rows[...]
    inv = lax.rsqrt(jnp.mean(values * values, axis=1, keepdims=True) + EPSILON)
    for copy in first:
        copy.wait()
    second = []
    for i, device in enumerate(mates):
        second.append(send(small_all.at[e], small_all.at[e], s_send.at[i], s_recv.at[i], device))
        second[-1].start()
    for copy in second:
        copy.wait()

    width = rows.shape[1]
    piece = width // 32
    lane = lax.broadcasted_iota(jnp.int32, (128, width), 1)
    spread = low(jnp.where(lax.rem(lane, piece) == lax.broadcasted_iota(jnp.int32, (128, width), 0), 1.0, 0.0))
    row = lax.broadcasted_iota(jnp.int32, (32, width), 0)
    owner = lax.rem(row, 4) * 8 + row // 4
    mine = lax.broadcasted_iota(jnp.int32, (32, width), 1) // piece == owner
    for i, index in enumerate((5, 6)):
        pieces = jnp.concatenate([small_all[j, :, index, :] for j in range(8)], axis=0)
        spread_out = dot(low(pieces), spread)
        gains[i : i + 1, :] = jnp.sum(jnp.where(mine, spread_out, 0.0), axis=0, keepdims=True)
    n1_all[e] = low(values * inv * gains[0:1, :])
    stages = line_stages(n1_all, *sems[18:])
    stages[0]()

    def hop(owner, half, sems_out, sems_in, slot, device):
        block = columns_all.at[owner, pl.ds(4 * half, 4)]
        return send(block, block, sems_out.at[slot], sems_in.at[slot], device)

    def over_x(slot):
        owner, half = ((b, 0), (b, 1), (b ^ 2, 1))[slot]
        return hop(owner, half, x_send, x_recv, slot, over[0])

    def over_y(slot):
        owner, half = ((b, 1), (b, 0), (b ^ 1, 0))[slot]
        return hop(owner, half, y_send, y_recv, slot, over[1])

    def out_block(owner):
        return out_all.at[core, owner]

    for copy in across:
        copy.wait()
    for slot in range(2):
        over_x(slot).start()
        over_y(slot).start()
    for copy in along:
        copy.wait()
    beyond = []
    for i, device in enumerate(over):
        beyond.append(send(out_block(b), out_block(b), o_send.at[i], o_recv.at[i], device))
        beyond[-1].start()

    def out_pair(slot):
        block = out_block(b ^ slot)
        return send(block, block, p_send.at[slot], p_recv.at[slot], (b, e ^ 1))

    out_pair(0).start()
    stages[1]()
    over_x(0).wait_recv()
    over_y(2).start()
    over_y(0).wait_recv()
    over_x(2).start()
    stages[2]()
    stages[3]()
    for i, copy in enumerate(beyond):
        copy.wait()
        out_pair(i + 1).start()
    stages[4]()
    for slot in range(3):
        for over_one in (over_x, over_y):
            if slot > 0:
                over_one(slot).wait_recv()
            over_one(slot).wait_send()
    for copy in rest:
        copy.wait()
    for slot in range(4):
        out_pair(slot).wait()


def opening(rows, small, marks, columns, w_out):
    tokens, width = rows.shape
    sizes = (3, 3, 7, 7, 7, 7, 7, 7, 3, 3, 3, 3, 3, 3, 3, 3, 4, 4)
    return kernel_call(
        opening_kernel,
        [
            ((8, tokens, width), LOW),
            ((2, width), F32),
            ((8, 4, 8, 128), F32),
            ((8, 8, 128), F32),
            ((4, *columns.shape), LOW),
            ((2, 4, 4, *w_out.shape), LOW),
        ],
        (rows, small, marks, columns, w_out),
        [pltpu.SemaphoreType.DMA((size,)) for size in sizes] + GATHER_SEMS,
        0,
    )


def holder(e):
    return (lax.rem(e, 2) == 0) | (e == 3), jnp.where(e == 3, 4, e // 2)


def middle_kernel(
    attended, w_out, rows, gain, attn, resid, n2_all, a_send, a_recv, *sems
):
    b, e, z, core = place()
    greet(pack_mates())
    holds, pair = holder(e)

    def give(i):
        other = lax.rem(e + i, 8)
        return send(
            attended.at[other], attn.at[pair], a_send.at[i - 1], a_recv.at[pair], (b, other)
        )

    @pl.when(holds)
    def _():
        for i in range(1, 8):
            give(i).start()
        attn[pair] = attended[e]

    total = rows[...]
    for source, index in PAIR_OF.items():

        @pl.when(e != source)
        def _():
            block = attn.at[index]
            send(block, block, a_send.at[0], a_recv.at[index], (b, source)).wait_recv()

        size = attn.shape[2]
        total = total + dot(attn[index], w_out[index * size : (index + 1) * size, :])
    resid[...] = total
    inv = lax.rsqrt(jnp.mean(total * total, axis=1, keepdims=True) + EPSILON)
    n2_all[e] = low(total * inv * gain[...])
    line_gather(n2_all, *sems)

    @pl.when(holds)
    def _():
        for i in range(1, 8):
            give(i).wait_send()


def middle(attended, w_out, rows, gain):
    tokens, width = rows.shape
    pair = attended.shape[2]
    return kernel_call(
        middle_kernel,
        [
            ((width // pair, tokens, pair), LOW),
            ((tokens, width), F32),
            ((8, tokens, width), LOW),
        ],
        (attended, w_out, rows, gain),
        [pltpu.SemaphoreType.DMA((7,)), pltpu.SemaphoreType.DMA((len(PAIR_OF),))] + GATHER_SEMS,
        1,
    )


def turn_kernel(
    part,
    upstream,
    gates,
    w_router,
    resid,
    gain,
    w_out,
    dresid,
    dlogits,
    gain_term,
    darrived,
    dattn,
    a_send,
    a_recv,
    *scratch,
):
    b, e, z, core = place()
    greet(pack_mates())
    holds, pair = holder(e)
    total = line_scatter(part, *scratch)
    width = upstream.shape[1]
    experts = gates.shape[1]
    dgate = total[:, width : width + experts] + total[:, width + experts : width + 2 * experts]
    own = gates[...]
    dlog = low(own * (dgate - jnp.sum(own * dgate, axis=1, keepdims=True)))
    dlogits[...] = dlog
    dn2 = total[:, :width] + dot(dlog, w_router[...])
    rows = resid[...]
    inv = lax.rsqrt(jnp.mean(rows * rows, axis=1, keepdims=True) + EPSILON)
    xhat = rows * inv
    gain_term[...] = jnp.sum(dn2 * xhat, axis=0, keepdims=True)
    scaled = dn2 * gain[...]
    grad = upstream[...] + inv * (scaled - xhat * jnp.mean(scaled * xhat, axis=1, keepdims=True))
    dresid[...] = grad
    back = low(dot(low(grad), w_out[...], ((1,), (1,))))
    size = dattn.shape[2]

    def give(source, index):
        return send(dattn.at[index], darrived.at[e], a_send.at[index], a_recv.at[e], (b, source))

    for source, index in PAIR_OF.items():
        dattn[index] = back[:, index * size : (index + 1) * size]

        @pl.when(e != source)
        def _():
            give(source, index).start()

    @pl.when(jnp.logical_not(holds))
    def _():
        darrived[...] = jnp.zeros_like(darrived)

    @pl.when(holds)
    def _():
        darrived[e] = dattn[pair]
        for i in range(1, 8):
            other = lax.rem(e + i, 8)
            block = darrived.at[other]
            send(block, block, a_send.at[0], a_recv.at[other], (b, other)).wait_recv()

    for source, index in PAIR_OF.items():

        @pl.when(e != source)
        def _():
            give(source, index).wait_send()


def turn(part, upstream, gates, w_router, resid, gain, w_out):
    tokens, width = upstream.shape
    pair = 2 * HEAD
    count = len(PAIR_OF)
    return kernel_call(
        turn_kernel,
        [
            ((tokens, width), F32),
            (gates.shape, LOW),
            ((1, width), F32),
            ((8, tokens, pair), LOW),
        ],
        (part, upstream, gates, w_router, resid, gain, w_out),
        [
            pltpu.VMEM((count, tokens, pair), LOW),
            pltpu.SemaphoreType.DMA((count,)),
            pltpu.SemaphoreType.DMA((8,)),
        ]
        + scatter_scratch(tokens, part.shape[2])
        + SCATTER_SEMS,
        2,
    )


def closing_kernel(part, rows, gain, dresid, input_grad, *scratch):
    greet_line()
    values = rows[...]
    inv = lax.rsqrt(jnp.mean(values * values, axis=1, keepdims=True) + EPSILON)
    xhat = values * inv
    scaled = line_scatter(part, *scratch) * gain[...]
    input_grad[...] = dresid[...] + inv * (
        scaled - xhat * jnp.mean(scaled * xhat, axis=1, keepdims=True)
    )


def closing(part, rows, gain, dresid):
    tokens, width = rows.shape
    return kernel_call(
        closing_kernel,
        [((tokens, width), F32)],
        (part, rows, gain, dresid),
        scatter_scratch(tokens, width) + SCATTER_SEMS,
        3,
    )[0]


def exchange(values):
    return lax.all_to_all(values, "expert", split_axis=0, concat_axis=0, tiled=True)


def silu_parts(gate, up):
    sigma = jax.nn.sigmoid(gate)
    return gate * sigma, up * sigma * (1.0 + gate * (1.0 - sigma))


def pack_device(
    block_input,
    seq_ids,
    routes,
    cotangent,
    qkv_weight,
    out_weight,
    shared_up,
    shared_down,
    router_weight,
    gain_attn,
    gain_ffn,
    expert_up,
    expert_down,
):
    b = lax.axis_index("batch")
    e = lax.axis_index("expert")
    rows_in = block_input[0]
    upstream = cotangent[0]
    tokens, width = rows_in.shape
    length = tokens * 8
    rows_w = qkv_weight.shape[0]
    pair = 2 * HEAD
    pairs_of_heads = width // pair
    hidden = expert_up.shape[2] // 2
    experts = expert_up.shape[0] * 8
    s_rows = shared_down.shape[0]
    s_own = 4 * s_rows
    s_pad = -(-s_own // 128) * 128
    scale = HEAD ** (-0.5)

    qkv_low = low(qkv_weight).reshape(rows_w, 3, pairs_of_heads, pair)
    nothing = jnp.zeros((rows_w, 3, pair), LOW)
    columns = [qkv_low[:, :, PAIR_OF[i]] if i in PAIR_OF else nothing for i in range(8)]
    columns = jnp.stack(columns).reshape(8, rows_w, 3 * pair)
    sup_low = low(shared_up).reshape(rows_w, 2, 4, 8, s_rows).transpose(3, 0, 1, 2, 4)
    sup_low = jnp.pad(
        sup_low.reshape(8, rows_w, 2, s_own), ((0, 0), (0, 0), (0, 0), (0, s_pad - s_own))
    )
    columns = jnp.concatenate([columns, sup_low.reshape(8, rows_w, 2 * s_pad)], axis=2)
    up_near = gather_near(low(expert_up))
    down_near = gather_near(low(expert_down))
    sdown_near = gather_near(low(shared_down))
    core = lax.rem(e, 2)

    small = jnp.concatenate(
        [
            router_weight.reshape(-1, 128),
            jnp.pad(gain_attn[None], ((0, 0), (0, 128 - rows_w))),
            jnp.pad(gain_ffn[None], ((0, 0), (0, 128 - rows_w))),
            jnp.zeros((1, 128), F32),
        ]
    )
    small = low(small).astype(F32)
    marks = jnp.concatenate([routes[0].T, seq_ids], axis=0).astype(F32)
    marks = jnp.pad(marks, ((0, 7 - TOP), (0, 0)))
    n1_all, gains, small, marks, columns, w_out = opening(
        rows_in, small, marks, columns, low(out_weight)
    )
    n1_all = n1_all.reshape(length, width)
    columns = columns.reshape(width, 3 * pair + 2 * s_pad)
    w_qkv = columns[:, : 3 * pair]
    w_sup = columns[:, 3 * pair :]
    w_out = w_out.transpose(1, 2, 0, 3, 4).reshape(width, width)
    router_rows = rows_w * experts // 128
    w_router = low(small[:, :, :router_rows].transpose(1, 0, 2, 3).reshape(width, experts))
    gain_first = gains[0:1]
    gain_second = gains[1:2]
    marks = marks.astype(jnp.int32).transpose(0, 2, 1).reshape(length, 8)
    route_all = marks[:, :TOP]
    ids_all = marks[:, TOP]
    cot_all = gather_pack(after(low(upstream), n1_all)).reshape(length, width)

    positions = jnp.arange(length, dtype=jnp.int32)
    projected = dot(n1_all, w_qkv)
    queries = low(rotate(projected[:, :pair].reshape(length, 2, HEAD), positions, 1.0))
    keys = low(rotate(projected[:, pair : 2 * pair].reshape(length, 2, HEAD), positions, 1.0))
    values = low(projected[:, 2 * pair :].reshape(length, 2, HEAD))
    allowed = (positions[None, :] <= positions[:, None]) & (ids_all[None, :] == ids_all[:, None])
    scores = jnp.einsum("qhd,khd->hqk", queries, keys, preferred_element_type=F32) * scale
    scores = jnp.where(allowed[None], scores, NEGATIVE)
    top = jnp.max(scores, axis=2, keepdims=True)
    attn_p = jnp.exp(scores - top)
    total = jnp.sum(attn_p, axis=2, keepdims=True)
    attn_p = attn_p / total
    attn_low = low(attn_p)
    attended = jnp.einsum("hqk,khd->qhd", attn_low, values, preferred_element_type=F32)
    attended_low = low(attended)
    up_low = gather_far(after(up_near, attended_low), 1, 1)
    attn, resid, n2_all = middle(
        attended_low.reshape(8, tokens, pair), w_out, rows_in, gain_second
    )
    attn = attn.transpose(1, 0, 2).reshape(tokens, width)

    n2 = lax.dynamic_index_in_dim(n2_all, e, 0, False)
    n2_all = n2_all.reshape(length, width)
    down_low = gather_far(after(down_near, n2_all), 1, 1)
    w_sdown = gather_far(after(sdown_near, n2_all), 0, 1)
    w_sdown = jnp.pad(w_sdown, ((0, s_pad - s_own), (0, 0)))
    logits = dot(n2_all, w_router)
    hot = route_all[:, :, None] == jnp.arange(experts, dtype=jnp.int32)[None, None, :]
    routed_to = jnp.any(hot, axis=1)
    logits = jnp.where(routed_to, logits, NEGATIVE)
    gates = jnp.where(routed_to, jnp.exp(logits - jnp.max(logits, axis=1, keepdims=True)), 0.0)
    gates = gates / jnp.sum(gates, axis=1, keepdims=True)
    mine = lax.dynamic_slice_in_dim(gates, 2 * e, 2, 1)

    output_part = 0.0
    drow_part = 0.0
    dgates = []
    up_terms = []
    down_terms = []
    for k in range(2):
        gate = mine[:, k : k + 1]
        pre = dot(n2_all, up_low[k])
        silu, slope = silu_parts(pre[:, :hidden], pre[:, hidden:])
        hid = silu * pre[:, hidden:]
        back = dot(cot_all, down_low[k], ((1,), (1,)))
        dgates.append(jnp.sum(back * hid, axis=1, keepdims=True))
        hid_low = low(hid * gate)
        output_part = output_part + dot(hid_low, down_low[k])
        down_terms.append(dot(hid_low, cot_all, ((0,), (0,))))
        back = back * gate
        dpre = low(jnp.concatenate([back * slope, back * silu], axis=1))
        up_terms.append(dot(n2_all, dpre, ((0,), (0,))))
        drow_part = drow_part + dot(dpre, up_low[k], ((1,), (1,)))
    pre = dot(n2_all, w_sup)
    silu, slope = silu_parts(pre[:, :s_pad], pre[:, s_pad:])
    hid_low = low(silu * pre[:, s_pad:])
    back = dot(cot_all, w_sdown, ((1,), (1,)))
    output_part = output_part + dot(hid_low, w_sdown)
    sdown_term = dot(hid_low, cot_all, ((0,), (0,)))[:s_own]
    dpre = low(jnp.concatenate([back * slope, back * silu], axis=1))
    sup_term = dot(n2_all, dpre, ((0,), (0,)))
    drow_part = drow_part + dot(dpre, w_sup, ((1,), (1,)))
    expert_up_grad = scatter_batch(low(jnp.stack(up_terms)), 1, 1)
    expert_down_grad = scatter_batch(low(jnp.stack(down_terms)), 1, 1)
    shared_down_grad = scatter_batch(low(sdown_term), 0, 1)

    lane = jnp.arange(experts, dtype=jnp.int32)[None, :] - 2 * e
    dgate = jnp.where(lane == 0, dgates[0], 0.0) + jnp.where(lane == 1, dgates[1], 0.0)
    dgate_high = low(dgate)
    dgate_rest = low(dgate - dgate_high.astype(F32))
    spare = jnp.zeros((length, 128 - 2 * experts), LOW)
    part = jnp.concatenate([low(drow_part), dgate_high, dgate_rest, spare], axis=1)
    own_gates = lax.dynamic_slice_in_dim(gates, e * tokens, tokens, 0)
    dresid, dlogits, gain_ffn_term, dattn = turn(
        part.reshape(8, tokens, part.shape[1]),
        upstream,
        own_gates,
        w_router.T,
        resid,
        gain_second,
        w_out,
    )
    dattn = dattn.reshape(length, 2, HEAD)
    output_part = after(low(output_part), dresid).reshape(8, tokens, width)
    output_rows = resid + scatter_pack(output_part)
    router_term = dot(dlogits, n2, ((0,), (0,)))
    small = total_all(jnp.concatenate([router_term, gain_ffn_term], axis=0))
    small = lax.dynamic_slice_in_dim(small, (b * 8 + e) * rows_w, rows_w, 1)
    dproj = low(dresid)
    out_term = dot(attn, dproj, ((0,), (0,))).reshape(4, 4, 2, rows_w, width)
    out_away = swap(low(lax.dynamic_index_in_dim(out_term, 1 - core, 2, False)), 0, 1)
    out_term = lax.dynamic_index_in_dim(out_term, core, 2, False) + out_away
    out_term = scatter_batch(low(out_term).reshape(16 * rows_w, width), 0, 1)
    out_grad = scatter_z(out_term.reshape(4, rows_w, width))

    delta = jnp.sum(dattn.astype(F32) * attended, axis=2).T[:, :, None]
    dprob = jnp.einsum("qhd,khd->hqk", dattn, values, preferred_element_type=F32)
    dscore = low(attn_p * (dprob - delta))
    dquery = jnp.einsum("hqk,khd->qhd", dscore, keys, preferred_element_type=F32)
    dkey = jnp.einsum("hqk,qhd->khd", dscore, queries, preferred_element_type=F32)
    dvalue = jnp.einsum("hqk,qhd->khd", attn_low, dattn, preferred_element_type=F32)
    dprojected = low(
        jnp.concatenate(
            [
                rotate(dquery * scale, positions, -1.0).reshape(length, pair),
                rotate(dkey * scale, positions, -1.0).reshape(length, pair),
                dvalue.reshape(length, pair),
            ],
            axis=1,
        )
    )
    qkv_term = dot(n1_all, dprojected, ((0,), (0,)))
    dn1 = low(dot(dprojected, w_qkv, ((1,), (1,))))
    input_grad = closing(dn1.reshape(8, tokens, width), rows_in, gain_first, dresid)

    columns = scatter_batch(low(jnp.concatenate([qkv_term, sup_term], axis=1)), 0, 0)
    columns = exchange(low(columns).reshape(8, rows_w, 3 * pair + 2 * s_pad)).astype(F32)
    qkv_grad = jnp.stack([columns[i, :, : 3 * pair] for i in PAIR_OF])
    qkv_grad = qkv_grad.reshape(pairs_of_heads, rows_w, 3, pair).transpose(1, 2, 0, 3)
    qkv_grad = qkv_grad.reshape(rows_w, 3 * width)
    sup_grad = columns[:, :, 3 * pair :].reshape(8, rows_w, 2, s_pad)[..., :s_own]
    sup_grad = sup_grad.reshape(8, rows_w, 2, 4, s_rows).transpose(1, 2, 3, 0, 4)
    sup_grad = sup_grad.reshape(rows_w, shared_up.shape[1])

    own_first = low(gain_attn).astype(F32)
    gain_attn_grad = jnp.sum(low(qkv_weight).astype(F32) * qkv_grad, axis=1) / own_first
    return (
        output_rows[None],
        input_grad[None],
        qkv_grad,
        out_grad,
        sup_grad,
        shared_down_grad,
        small[:experts].T,
        gain_attn_grad,
        small[experts],
        expert_up_grad,
        expert_down_grad,
    )


def solution(mesh):
    in_specs = (
        P("batch", "expert", None),
        P("batch", "expert"),
        P("batch", "expert", None),
        P("batch", "expert", None),
        P(("batch", "expert"), None),
        P(("batch", "expert"), None),
        P(("batch", "expert"), None),
        P(("batch", "expert"), None),
        P(("batch", "expert"), None),
        P(("batch", "expert")),
        P(("batch", "expert")),
        P("expert", "batch", None),
        P("expert", "batch", None),
    )
    out_specs = (
        P("batch", "expert", None),
        P("batch", "expert", None),
        P(("batch", "expert"), None),
        P(("batch", "expert"), None),
        P(("batch", "expert"), None),
        P(("batch", "expert"), None),
        P(("batch", "expert"), None),
        P(("batch", "expert")),
        P(("batch", "expert")),
        P("expert", "batch", None),
        P("expert", "batch", None),
    )
    sizes = dict(mesh.shape)
    body = pack_device if sizes == {"batch": 4, "expert": 8} else per_device
    return jax.shard_map(
        body, mesh=mesh, in_specs=in_specs, out_specs=out_specs, check_vma=False
    )
```

```python
import functools

import jax
import jax.numpy as jnp
from jax import lax
from jax.experimental import pallas as pl
from jax.experimental.pallas import tpu as pltpu
from jax.sharding import PartitionSpec as P

HEAD = 128
TOP = 6


EPSILON = 1e-06
NEGATIVE = -1e30


def rotate(values, positions, sign):
    half = values.shape[-1] // 2
    frequency = 10000.0 ** (-jnp.arange(half, dtype=jnp.float32) / half)
    angle = positions.astype(jnp.float32)[:, None] * frequency[None, :]
    cosine = jnp.cos(angle)[:, None, :]
    sine = sign * jnp.sin(angle)[:, None, :]
    first = values[..., :half]
    second = values[..., half:]
    return jnp.concatenate(
        [first * cosine - second * sine, first * sine + second * cosine], axis=-1
    )


def swiglu(pre, hidden_width):
    return jax.nn.silu(pre[..., :hidden_width]) * pre[..., hidden_width:]


def swiglu_back(pre, dhidden, hidden_width):
    gate_part = pre[..., :hidden_width]
    up_part = pre[..., hidden_width:]
    sigma = jax.nn.sigmoid(gate_part)
    dgate = dhidden * up_part * sigma * (1.0 + gate_part * (1.0 - sigma))
    dupper = dhidden * gate_part * sigma
    return jnp.concatenate([dgate, dupper], axis=-1)


def norm_back(dnormed, normed, inv_rms, gain):
    dscaled = dnormed * gain
    dinputs = inv_rms * (dscaled - normed * jnp.mean(dscaled * normed, axis=1, keepdims=True))
    return (dinputs, jnp.sum(dnormed * normed, axis=0))


def per_device(
    block_input,
    seq_ids,
    routes,
    cotangent,
    qkv_weight,
    out_weight,
    shared_up,
    shared_down,
    router_weight,
    gain_attn,
    gain_ffn,
    expert_up,
    expert_down,
):
    dense = (
        lax.all_gather(qkv_weight.astype(jnp.bfloat16), ("batch", "expert"), axis=0, tiled=True),
        lax.all_gather(out_weight.astype(jnp.bfloat16), ("batch", "expert"), axis=0, tiled=True),
        lax.all_gather(shared_up.astype(jnp.bfloat16), ("batch", "expert"), axis=0, tiled=True),
        lax.all_gather(shared_down.astype(jnp.bfloat16), ("batch", "expert"), axis=0, tiled=True),
        lax.all_gather(router_weight.astype(jnp.bfloat16), ("batch", "expert"), axis=0, tiled=True),
        lax.all_gather(gain_attn.astype(jnp.bfloat16), ("batch", "expert"), axis=0, tiled=True),
        lax.all_gather(gain_ffn.astype(jnp.bfloat16), ("batch", "expert"), axis=0, tiled=True),
    )
    full_qkv, full_out, full_sup, full_sdown, full_router, low_gain_a, low_gain_f = dense
    gain_first = low_gain_a.astype(jnp.float32)
    gain_second = low_gain_f.astype(jnp.float32)
    experts_up, experts_down = (
        lax.all_gather(expert_up.astype(jnp.bfloat16), "batch", axis=1, tiled=True),
        lax.all_gather(expert_down.astype(jnp.bfloat16), "batch", axis=1, tiled=True),
    )
    rows_in = block_input[0]
    ids_local = seq_ids[0]
    route_local = routes[0]
    upstream = cotangent[0]
    tokens_dev = rows_in.shape[0]
    model_width = rows_in.shape[1]
    heads_count = model_width // HEAD
    groups = lax.axis_size("expert")
    local_experts = experts_up.shape[0]
    experts_all = local_experts * groups
    shared_width = full_sdown.shape[0]
    hidden_width = experts_down.shape[1]
    capacity = max(2, tokens_dev * TOP * 3 // (experts_all * 2))
    score_scale = HEAD ** (-0.5)
    positions = lax.axis_index("expert") * tokens_dev + jnp.arange(tokens_dev, dtype=jnp.int32)
    key_ids = lax.all_gather(ids_local, "expert", axis=0, tiled=True)
    inv_first = lax.rsqrt(jnp.mean(rows_in * rows_in, axis=1, keepdims=True) + EPSILON)
    normed_first = rows_in * inv_first
    input_low = (normed_first * gain_first).astype(jnp.bfloat16)
    projected = jnp.dot(input_low, full_qkv, preferred_element_type=jnp.float32)
    queries = rotate(
        projected[:, :model_width].reshape(tokens_dev, heads_count, HEAD), positions, 1.0
    ).astype(jnp.bfloat16)
    keys = rotate(
        projected[:, model_width : 2 * model_width].reshape(tokens_dev, heads_count, HEAD),
        positions,
        1.0,
    ).astype(jnp.bfloat16)
    values = (
        projected[:, 2 * model_width :].reshape(tokens_dev, heads_count, HEAD).astype(jnp.bfloat16)
    )

    def key_mask(key_count):
        key_pos = jnp.arange(key_count, dtype=jnp.int32)
        return (key_pos[None, :] <= positions[:, None]) & (key_ids[None, :] == ids_local[:, None])

    run_max = jnp.full((heads_count, tokens_dev), NEGATIVE, jnp.float32)
    key_piece = lax.all_gather(keys, "expert", axis=0, tiled=True)
    value_piece = lax.all_gather(values, "expert", axis=0, tiled=True)
    allowed = key_mask(key_piece.shape[0])[None]
    scores = (
        jnp.einsum("qhd,khd->hqk", queries, key_piece, preferred_element_type=jnp.float32)
        * score_scale
    )
    scores = jnp.where(allowed, scores, NEGATIVE)
    new_max = jnp.maximum(run_max, jnp.max(scores, axis=2))
    weights = jnp.where(allowed, jnp.exp(scores - new_max[:, :, None]), 0.0)
    run_sum = jnp.sum(weights, axis=2)
    update = jnp.einsum(
        "hqk,khd->qhd",
        weights.astype(jnp.bfloat16),
        value_piece,
        preferred_element_type=jnp.float32,
    )
    run_acc = update
    run_max, run_sum, run_acc = (new_max, run_sum, run_acc)
    attn_full = run_acc / jnp.transpose(run_sum)[:, :, None]
    logsum = run_max + jnp.log(run_sum)
    attn_low = attn_full.reshape(tokens_dev, model_width).astype(jnp.bfloat16)
    resid = rows_in + jnp.dot(attn_low, full_out, preferred_element_type=jnp.float32)
    inv_second = lax.rsqrt(jnp.mean(resid * resid, axis=1, keepdims=True) + EPSILON)
    normed_second = resid * inv_second
    ffn_low = (normed_second * gain_second).astype(jnp.bfloat16)
    logits = jnp.dot(ffn_low, full_router, preferred_element_type=jnp.float32)
    probs = jax.nn.softmax(logits, axis=1)
    route_hot = route_local[:, :, None] == jnp.arange(experts_all, dtype=jnp.int32)[None, None, :]
    chosen = jnp.sum(jnp.where(route_hot, probs[:, None, :], 0.0), axis=2)
    chosen_sum = jnp.sum(chosen, axis=1, keepdims=True)
    gates = chosen / chosen_sum
    shared_pre = jnp.dot(ffn_low, full_sup, preferred_element_type=jnp.float32)
    shared_hidden = swiglu(shared_pre, shared_width).astype(jnp.bfloat16)
    shared_result = jnp.dot(shared_hidden, full_sdown, preferred_element_type=jnp.float32)
    flat_route = route_local.reshape(-1)
    flat_hot = (flat_route[:, None] == jnp.arange(experts_all, dtype=jnp.int32)[None, :]).astype(
        jnp.bfloat16
    )
    pair_count = tokens_dev * TOP
    pair_index = jnp.arange(pair_count, dtype=jnp.int32)
    earlier = (pair_index[None, :] < pair_index[:, None]).astype(jnp.bfloat16)
    counts = jnp.dot(earlier, flat_hot, preferred_element_type=jnp.float32)
    slots = jnp.sum(counts * flat_hot, axis=1).astype(jnp.int32)
    source_table = (
        jnp.full((experts_all * capacity,), pair_count, jnp.int32)
        .at[flat_route * capacity + slots]
        .set(jnp.arange(pair_count, dtype=jnp.int32))
    )
    send_table = jnp.transpose(
        source_table.reshape(groups, local_experts, capacity), (1, 0, 2)
    ).reshape(-1)
    return_pos = (
        flat_route % local_experts * (groups * capacity)
        + flat_route // local_experts * capacity
        + slots
    )
    padded_rows = jnp.concatenate([ffn_low, jnp.zeros((1, model_width), jnp.bfloat16)], axis=0)
    send_rows = padded_rows[send_table // TOP].reshape(local_experts, groups, capacity, model_width)
    received = lax.all_to_all(send_rows, "expert", split_axis=1, concat_axis=1, tiled=True)
    expert_rows = received.reshape(local_experts, groups * capacity, model_width)
    expert_pre = jnp.einsum(
        "erd,edf->erf", expert_rows, experts_up, preferred_element_type=jnp.float32
    )
    expert_hidden = swiglu(expert_pre, hidden_width).astype(jnp.bfloat16)
    expert_result = jnp.einsum(
        "erf,efd->erd", expert_hidden, experts_down, preferred_element_type=jnp.float32
    ).astype(jnp.bfloat16)
    returned = lax.all_to_all(
        expert_result.reshape(local_experts, groups, capacity, model_width),
        "expert",
        split_axis=1,
        concat_axis=1,
        tiled=True,
    )
    token_outputs = returned.reshape(-1, model_width)[return_pos].reshape(
        tokens_dev, TOP, model_width
    )
    routed = jnp.sum(gates[:, :, None] * token_outputs, axis=1)
    output_rows = resid + shared_result + routed
    shared_cot = upstream.astype(jnp.bfloat16)
    shared_down_term = jnp.dot(shared_hidden.T, shared_cot, preferred_element_type=jnp.float32)
    dshared_hidden = jnp.dot(shared_cot, full_sdown.T, preferred_element_type=jnp.float32)
    dshared_pre = swiglu_back(shared_pre, dshared_hidden, shared_width).astype(jnp.bfloat16)
    shared_up_term = jnp.dot(ffn_low.T, dshared_pre, preferred_element_type=jnp.float32)
    dnormed_second = jnp.dot(dshared_pre, full_sup.T, preferred_element_type=jnp.float32)
    token_cot = (gates[:, :, None] * upstream[:, None, :]).astype(jnp.bfloat16)
    dgates = jnp.sum(upstream[:, None, :] * token_outputs, axis=2)
    padded_cot = jnp.concatenate(
        [token_cot.reshape(-1, model_width), jnp.zeros((1, model_width), jnp.bfloat16)], axis=0
    )
    send_cot = padded_cot[send_table].reshape(local_experts, groups, capacity, model_width)
    received_cot = lax.all_to_all(
        send_cot, "expert", split_axis=1, concat_axis=1, tiled=True
    ).reshape(local_experts, groups * capacity, model_width)
    down_term = jnp.einsum(
        "erf,erd->efd", expert_hidden, received_cot, preferred_element_type=jnp.float32
    )
    dexpert_hidden = jnp.einsum(
        "erd,efd->erf", received_cot, experts_down, preferred_element_type=jnp.float32
    )
    dexpert_pre = swiglu_back(expert_pre, dexpert_hidden, hidden_width).astype(jnp.bfloat16)
    up_term = jnp.einsum(
        "erd,erf->edf", expert_rows, dexpert_pre, preferred_element_type=jnp.float32
    )
    drows = jnp.einsum(
        "erf,edf->erd", dexpert_pre, experts_up, preferred_element_type=jnp.float32
    ).astype(jnp.bfloat16)
    returned_grad = lax.all_to_all(
        drows.reshape(local_experts, groups, capacity, model_width),
        "expert",
        split_axis=1,
        concat_axis=1,
        tiled=True,
    )
    row_grads = returned_grad.reshape(-1, model_width)[return_pos].reshape(
        tokens_dev, TOP, model_width
    )
    dnormed_second = dnormed_second + jnp.sum(row_grads, axis=1, dtype=jnp.float32)
    expert_up_grad, expert_down_grad = (
        lax.psum_scatter(
            up_term.astype(jnp.bfloat16), "batch", scatter_dimension=1, tiled=True
        ).astype(jnp.float32),
        lax.psum_scatter(
            down_term.astype(jnp.bfloat16), "batch", scatter_dimension=1, tiled=True
        ).astype(jnp.float32),
    )
    dchosen = (dgates - jnp.sum(dgates * gates, axis=1, keepdims=True)) / chosen_sum
    dprobs = jnp.sum(jnp.where(route_hot, dchosen[:, :, None], 0.0), axis=1)
    dlogits = (probs * (dprobs - jnp.sum(probs * dprobs, axis=1, keepdims=True))).astype(
        jnp.bfloat16
    )
    router_term = jnp.dot(ffn_low.T, dlogits, preferred_element_type=jnp.float32)
    dnormed_second = dnormed_second + jnp.dot(
        dlogits, full_router.T, preferred_element_type=jnp.float32
    )
    dresid_norm, gain_ffn_term = norm_back(dnormed_second, normed_second, inv_second, gain_second)
    dresid = upstream + dresid_norm
    dproj = dresid.astype(jnp.bfloat16)
    out_term = jnp.dot(attn_low.T, dproj, preferred_element_type=jnp.float32)
    dattn = (
        jnp.dot(dproj, full_out.T, preferred_element_type=jnp.float32)
        .astype(jnp.bfloat16)
        .reshape(tokens_dev, heads_count, HEAD)
    )
    delta_rows = jnp.sum(dattn.astype(jnp.float32) * attn_full, axis=2)
    delta_heads = jnp.transpose(delta_rows)
    key_piece = lax.all_gather(keys, "expert", axis=0, tiled=True)
    value_piece = lax.all_gather(values, "expert", axis=0, tiled=True)
    allowed = key_mask(key_piece.shape[0])[None]
    scores = (
        jnp.einsum("qhd,khd->hqk", queries, key_piece, preferred_element_type=jnp.float32)
        * score_scale
    )
    attn_probs = jnp.where(allowed, jnp.exp(scores - logsum[:, :, None]), 0.0)
    dprob = jnp.einsum("qhd,khd->hqk", dattn, value_piece, preferred_element_type=jnp.float32)
    dscore = (attn_probs * (dprob - delta_heads[:, :, None])).astype(jnp.bfloat16)
    attn_probs, dscore = (attn_probs, dscore)
    dquery = jnp.einsum("hqk,khd->qhd", dscore, key_piece, preferred_element_type=jnp.float32)
    dkey_piece = jnp.einsum("hqk,qhd->khd", dscore, queries, preferred_element_type=jnp.float32)
    dvalue_piece = jnp.einsum(
        "hqk,qhd->khd", attn_probs.astype(jnp.bfloat16), dattn, preferred_element_type=jnp.float32
    )
    folded = (dquery, dkey_piece, dvalue_piece)
    dquery = folded[0]
    dkey, dvalue = (
        lax.psum_scatter(
            folded[1].astype(jnp.bfloat16), "expert", scatter_dimension=0, tiled=True
        ).astype(jnp.float32),
        lax.psum_scatter(
            folded[2].astype(jnp.bfloat16), "expert", scatter_dimension=0, tiled=True
        ).astype(jnp.float32),
    )
    dquery_raw = rotate(dquery * score_scale, positions, -1.0).reshape(tokens_dev, model_width)
    dkey_raw = rotate(dkey * score_scale, positions, -1.0).reshape(tokens_dev, model_width)
    dprojected = jnp.concatenate(
        [dquery_raw, dkey_raw, dvalue.reshape(tokens_dev, model_width)], axis=1
    ).astype(jnp.bfloat16)
    qkv_term = jnp.dot(input_low.T, dprojected, preferred_element_type=jnp.float32)
    dnormed_first = jnp.dot(dprojected, full_qkv.T, preferred_element_type=jnp.float32)
    dinput_norm, gain_attn_term = norm_back(dnormed_first, normed_first, inv_first, gain_first)
    input_grad = dresid + dinput_norm
    grads = (
        lax.psum_scatter(qkv_term, ("batch", "expert"), scatter_dimension=0, tiled=True),
        lax.psum_scatter(out_term, ("batch", "expert"), scatter_dimension=0, tiled=True),
        lax.psum_scatter(shared_up_term, ("batch", "expert"), scatter_dimension=0, tiled=True),
        lax.psum_scatter(shared_down_term, ("batch", "expert"), scatter_dimension=0, tiled=True),
        lax.psum_scatter(router_term, ("batch", "expert"), scatter_dimension=0, tiled=True),
        lax.psum_scatter(gain_attn_term, ("batch", "expert"), scatter_dimension=0, tiled=True),
        lax.psum_scatter(gain_ffn_term, ("batch", "expert"), scatter_dimension=0, tiled=True),
    )
    (
        qkv_grad,
        out_grad,
        shared_up_grad,
        shared_down_grad,
        router_grad,
        gain_attn_grad,
        gain_ffn_grad,
    ) = grads
    return (
        output_rows[None],
        input_grad[None],
        qkv_grad,
        out_grad,
        shared_up_grad,
        shared_down_grad,
        router_grad,
        gain_attn_grad,
        gain_ffn_grad,
        expert_up_grad,
        expert_down_grad,
    )


PAIR_OF = {0: 0, 2: 1, 4: 2, 6: 3, 3: 4}
F32 = jnp.float32
LOW = jnp.bfloat16
COST = 10**9


def low(values):
    return values.astype(LOW)


def dot(left, right, dims=((1,), (0,))):
    return lax.dot_general(left, right, (dims, ((), ())), preferred_element_type=F32)


MESH_ID = pl.DeviceIdType.MESH


def place():
    b = lax.axis_index("batch")
    e = lax.axis_index("expert")
    return b, e, e // 2, lax.rem(e, 2)


def greet(devices):
    barrier = pltpu.get_barrier_semaphore()
    for device in devices:
        pl.semaphore_signal(barrier, inc=1, device_id=device, device_id_type=MESH_ID)
    pl.semaphore_wait(barrier, len(devices))


def pack_mates():
    b, e, _, _ = place()
    return [(b, lax.rem(e + i, 8)) for i in range(1, 8)]


def send(src, dst, send_sem, recv_sem, device):
    return pltpu.make_async_remote_copy(
        src_ref=src,
        dst_ref=dst,
        send_sem=send_sem,
        recv_sem=recv_sem,
        device_id=device,
        device_id_type=MESH_ID,
    )


GATHER_SEMS = [pltpu.SemaphoreType.DMA((3,))] * 4 + [pltpu.SemaphoreType.DMA((4,))] * 2


def line_stages(buf, up_send, up_recv, down_send, down_recv, core_send, core_recv):
    b, e, z, core = place()

    def to_core(owner_z):
        block = buf.at[2 * owner_z + core]
        return send(block, block, core_send.at[owner_z], core_recv.at[owner_z], (b, e ^ 1))

    def up(step):
        block = buf.at[jnp.maximum(2 * (z - step), 0) + core]
        return send(block, block, up_send.at[step], up_recv.at[step], (b, jnp.minimum(e + 2, 7)))

    def down(step):
        block = buf.at[jnp.minimum(2 * (z + step), 6) + core]
        return send(
            block, block, down_send.at[step], down_recv.at[step], (b, jnp.maximum(e - 2, 0))
        )

    def start(step):
        @pl.when((z >= step) & (z < 3))
        def _():
            up(step).start()

        @pl.when((z + step <= 3) & (z > 0))
        def _():
            down(step).start()

        if step == 0:
            to_core(z).start()

    def arrive(step):
        @pl.when(z - 1 - step >= 0)
        def _():
            up(step).wait_recv()

        @pl.when(z + 1 + step <= 3)
        def _():
            down(step).wait_recv()

        if step < 2:
            start(step + 1)

        @pl.when(z - 1 - step >= 0)
        def _():
            to_core(z - 1 - step).start()

        @pl.when(z + 1 + step <= 3)
        def _():
            to_core(z + 1 + step).start()

    def finish():
        for owner_z in range(4):
            to_core(owner_z).wait()
        for step in range(3):

            @pl.when((z >= step) & (z < 3))
            def _():
                up(step).wait_send()

            @pl.when((z + step <= 3) & (z > 0))
            def _():
                down(step).wait_send()

    return [lambda: start(0)] + [functools.partial(arrive, i) for i in range(3)] + [finish]


def line_gather(buf, *sems):
    for stage in line_stages(buf, *sems):
        stage()


def scatter_scratch(tokens, width):
    return [pltpu.VMEM((4, tokens, width), LOW)] + [
        pltpu.VMEM((3, tokens, width), LOW) for _ in range(4)
    ]


SCATTER_SEMS = [pltpu.SemaphoreType.DMA((3,))] * 4 + [pltpu.SemaphoreType.DMA((4,))] * 2


def line_sum_stages(
    part,
    from_core,
    up_out,
    up_in,
    down_out,
    down_in,
    up_send,
    up_recv,
    down_send,
    down_recv,
    core_send,
    core_recv,
):
    b, e, z, core = place()

    def to_core(target):
        return send(
            part.at[2 * target + 1 - core],
            from_core.at[target],
            core_send.at[target],
            core_recv.at[target],
            (b, e ^ 1),
        )

    def up(step):
        return send(
            up_out.at[step],
            up_in.at[step],
            up_send.at[step],
            up_recv.at[step],
            (b, jnp.minimum(e + 2, 7)),
        )

    def down(step):
        return send(
            down_out.at[step],
            down_in.at[step],
            down_send.at[step],
            down_recv.at[step],
            (b, jnp.maximum(e - 2, 0)),
        )

    def chip_sum(target):
        return part[2 * target + core].astype(F32) + from_core[target].astype(F32)

    def start():
        for target in (3, 0, 2, 1):
            to_core(target).start()

    def advance(step):
        top = 3 - step
        if step == 0:
            for target in range(4):
                to_core(target).wait()

        @pl.when(z < top)
        def _():
            @pl.when(z > 0)
            def _():
                up(step).wait_recv()
                up_out[step] = low(chip_sum(top) + up_in[step].astype(F32))

            @pl.when(z == 0)
            def _():
                up_out[step] = low(chip_sum(top))

            up(step).start()

        @pl.when(z > step)
        def _():
            @pl.when(z < 3)
            def _():
                down(step).wait_recv()
                down_out[step] = low(chip_sum(step) + down_in[step].astype(F32))

            @pl.when(z == 3)
            def _():
                down_out[step] = low(chip_sum(step))

            down(step).start()

    def finish():
        @pl.when(z == 0)
        def _():
            up_in[0] = jnp.zeros_like(up_in[0])

        @pl.when(z == 3)
        def _():
            down_in[0] = jnp.zeros_like(down_in[0])

        last_up = lax.rem(3 - z, 3)
        last_down = lax.rem(z, 3)

        @pl.when(z > 0)
        def _():
            up(last_up).wait_recv()

        @pl.when(z < 3)
        def _():
            down(last_down).wait_recv()

        total = chip_sum(z) + up_in[last_up].astype(F32) + down_in[last_down].astype(F32)
        for step in range(3):

            @pl.when(z < 3 - step)
            def _():
                up(step).wait_send()

            @pl.when(z > step)
            def _():
                down(step).wait_send()

        return total

    return [start] + [functools.partial(advance, i) for i in range(3)] + [finish]


def sum_into(out, *terms):
    if len(out.shape) == 2:

        @pl.loop(0, out.shape[0] // 16)
        def _(i):
            here = pl.ds(pl.multiple_of(i * 16, 16), 16)
            total = terms[0][here, :].astype(F32)
            for term in terms[1:]:
                total = total + term[here, :].astype(F32)
            out[here, :] = total.astype(out.dtype)

    else:
        for i in range(out.shape[0]):
            total = terms[0][i].astype(F32)
            for term in terms[1:]:
                total = total + term[i].astype(F32)
            out[i] = total.astype(out.dtype)


REDUCE_COUNT = 8


def reduce_scratch(half_shape, far=False):
    kept = (4, *half_shape) if far else (1, 8, 128)
    return [
        pltpu.VMEM((6, *half_shape), LOW),
        pltpu.VMEM((2, *half_shape), LOW),
        pltpu.VMEM(kept, LOW if far else F32),
    ] + [pltpu.SemaphoreType.DMA((size,)) for size in (3, 3, 3, 3, 4)]


def reduce_stages(
    block, out, received, sums, kept, x_send, x_recv, y_send, y_recv, local_sem
):
    b, e, _, _ = place()
    x_device, y_device = (b ^ 1, e), (b ^ 2, e)

    def over_x(slot):
        src = (block(b ^ 3, 0), block(b ^ 1, 0), sums.at[1])[slot]
        return send(src, received.at[slot], x_send.at[slot], x_recv.at[slot], x_device)

    def over_y(slot):
        src = (block(b ^ 3, 1), block(b ^ 2, 1), sums.at[0])[slot]
        return send(src, received.at[3 + slot], y_send.at[slot], y_recv.at[slot], y_device)

    far = kept.shape[0] == 4

    def mine(i):
        return (block(b ^ 2, 0), block(b ^ 1, 1), block(b, 0), block(b, 1))[i]

    def keep(i):
        return pltpu.make_async_copy(mine(i), kept.at[i], local_sem.at[i])

    def held(i):
        if not far:
            return mine(i)
        keep(i).wait()
        return kept.at[i]

    def start():
        for slot in range(2):
            over_x(slot).start()
            over_y(slot).start()
        for i in range(4 if far else 0):
            keep(i).start()

    def forward():
        over_x(0).wait_recv()
        sum_into(sums.at[0], held(0), received.at[0])
        over_y(2).start()
        over_y(0).wait_recv()
        sum_into(sums.at[1], held(1), received.at[3])
        over_x(2).start()

    def finish():
        for slot in (1, 2):
            over_x(slot).wait_recv()
            over_y(slot).wait_recv()
        sum_into(out(0), held(2), received.at[1], received.at[5])
        sum_into(out(1), held(3), received.at[4], received.at[2])
        for slot in range(3):
            over_x(slot).wait_send()
            over_y(slot).wait_send()

    return start, forward, finish


def reduce_rows(term, out, scratch):
    half_rows = out.shape[0] // 2

    def block(owner, half):
        return term.at[pl.ds((2 * owner + half) * half_rows, half_rows)]

    def out_half(half):
        return out.at[pl.ds(half * half_rows, half_rows)]

    return reduce_stages(block, out_half, *scratch)


def kernel_call(body, outs, args, scratch, collective_id, far_outs=(), far_args=()):
    near = pl.BlockSpec(memory_space=pltpu.VMEM)
    far = pl.BlockSpec(memory_space=pl.ANY)
    return pl.pallas_call(
        body,
        cost_estimate=pl.CostEstimate(flops=COST, bytes_accessed=COST, transcendentals=0),
        out_shape=[jax.ShapeDtypeStruct(shape, dtype) for shape, dtype in outs],
        in_specs=[far if i in far_args else near for i in range(len(args))],
        out_specs=[far if i in far_outs else near for i in range(len(outs))],
        scratch_shapes=scratch,
        compiler_params=pltpu.CompilerParams(
            collective_id=collective_id, has_side_effects=True, vmem_limit_bytes=56 * 2**20
        ),
    )(*args)


SPREAD_SEMS = [pltpu.SemaphoreType.DMA((2,))] + [pltpu.SemaphoreType.DMA((3,))] * 4


def spread_stages(own, whole, local_sem, x_send, x_recv, y_send, y_recv):
    b, e, _, _ = place()
    x_device, y_device = (b ^ 1, e), (b ^ 2, e)

    def over_x(slot):
        src, dst = (
            (own(0), whole(b, 0)),
            (own(1), whole(b, 1)),
            (whole(b ^ 2, 1), whole(b ^ 2, 1)),
        )[slot]
        return send(src, dst, x_send.at[slot], x_recv.at[slot], x_device)

    def over_y(slot):
        src, dst = (
            (own(1), whole(b, 1)),
            (own(0), whole(b, 0)),
            (whole(b ^ 1, 0), whole(b ^ 1, 0)),
        )[slot]
        return send(src, dst, y_send.at[slot], y_recv.at[slot], y_device)

    def keep(half):
        return pltpu.make_async_copy(own(half), whole(b, half), local_sem.at[half])

    def start():
        for slot in range(2):
            over_x(slot).start()
            over_y(slot).start()
        for half in range(2):
            keep(half).start()

    def forward():
        over_x(0).wait_recv()
        over_y(2).start()
        over_y(0).wait_recv()
        over_x(2).start()
    def finish():
        for slot in range(3):
            for over in (over_x, over_y):
                if slot > 0:
                    over(slot).wait_recv()
                over(slot).wait_send()
        for half in range(2):
            keep(half).wait()

    return start, forward, finish


def spread_rows(own_ref, whole_ref, rows, sems):
    half_rows = rows // 2

    def own(half):
        return own_ref.at[pl.ds(half * half_rows, half_rows)]

    def whole(owner, half):
        return whole_ref.at[pl.ds(owner * rows + half * half_rows, half_rows)]

    return spread_stages(own, whole, *sems)


def opening_kernel(
    rows, small, marks, columns, w_out, up_own, n1_all, gains, small_all, marks_all, columns_all,
    out_all, up_all, *sems,
):
    (
        b_send, b_recv, s_send, s_recv, m_send, m_recv, c_send, c_recv,
        x_send, x_recv, y_send, y_recv, z_send, z_recv, o_send, o_recv, p_send, p_recv,
    ) = sems[:18]
    b, e, z, core = place()
    over = [(b ^ bit, e) for bit in (1, 2, 3)]
    mates = pack_mates()
    up_start, up_forward, up_finish = spread_rows(
        up_own.at[0], up_all, up_own.shape[1], sems[18:23]
    )
    greet(over + mates)
    small_all[e, b] = small[...]
    marks_all[e] = marks[...]
    columns_all[b, e] = columns[e]
    out_all[b, z, core] = w_out[...]
    first = []
    for i, device in enumerate(over):
        first.append(send(small, small_all.at[e, b], b_send.at[i], b_recv.at[i], device))
        first[-1].start()
    across = []
    for i, device in enumerate(mates):
        across.append(
            send(columns.at[device[1]], columns_all.at[b, e], c_send.at[i], c_recv.at[i], device)
        )
        across[-1].start()
    along = []
    for i in range(3):
        device = (b, lax.rem(e + 2 * i + 2, 8))
        along.append(
            send(w_out, out_all.at[b, z, core], z_send.at[i], z_recv.at[i], device)
        )
        along[-1].start()
    rest = []
    for i, device in enumerate(mates):
        rest.append(send(marks, marks_all.at[e], m_send.at[i], m_recv.at[i], device))
        rest[-1].start()
    up_start()
    values = rows[...]
    inv = lax.rsqrt(jnp.mean(values * values, axis=1, keepdims=True) + EPSILON)
    for copy in first:
        copy.wait()
    second = []
    for i, device in enumerate(mates):
        second.append(send(small_all.at[e], small_all.at[e], s_send.at[i], s_recv.at[i], device))
        second[-1].start()
    for copy in second:
        copy.wait()

    width = rows.shape[1]
    piece = width // 32
    lane = lax.broadcasted_iota(jnp.int32, (128, width), 1)
    spread = low(jnp.where(lax.rem(lane, piece) == lax.broadcasted_iota(jnp.int32, (128, width), 0), 1.0, 0.0))
    row = lax.broadcasted_iota(jnp.int32, (32, width), 0)
    owner = lax.rem(row, 4) * 8 + row // 4
    mine = lax.broadcasted_iota(jnp.int32, (32, width), 1) // piece == owner
    for i, index in enumerate((5, 6)):
        pieces = jnp.concatenate([small_all[j, :, index, :] for j in range(8)], axis=0)
        spread_out = dot(low(pieces), spread)
        gains[i : i + 1, :] = jnp.sum(jnp.where(mine, spread_out, 0.0), axis=0, keepdims=True)
    n1_all[e] = low(values * inv * gains[0:1, :])
    stages = line_stages(n1_all, *sems[23:])
    stages[0]()

    def hop(owner, half, sems_out, sems_in, slot, device):
        block = columns_all.at[owner, pl.ds(4 * half, 4)]
        return send(block, block, sems_out.at[slot], sems_in.at[slot], device)

    def over_x(slot):
        owner, half = ((b, 0), (b, 1), (b ^ 2, 1))[slot]
        return hop(owner, half, x_send, x_recv, slot, over[0])

    def over_y(slot):
        owner, half = ((b, 1), (b, 0), (b ^ 1, 0))[slot]
        return hop(owner, half, y_send, y_recv, slot, over[1])

    def out_block(owner):
        return out_all.at[owner, :, core]

    for copy in across:
        copy.wait()
    for slot in range(2):
        over_x(slot).start()
        over_y(slot).start()
    for copy in along:
        copy.wait()
    beyond = []
    for i, device in enumerate(over):
        beyond.append(send(out_block(b), out_block(b), o_send.at[i], o_recv.at[i], device))
        beyond[-1].start()

    def out_pair(slot):
        block = out_block(b ^ slot)
        return send(block, block, p_send.at[slot], p_recv.at[slot], (b, e ^ 1))

    out_pair(0).start()
    stages[1]()
    over_x(0).wait_recv()
    over_y(2).start()
    over_y(0).wait_recv()
    over_x(2).start()
    stages[2]()
    up_forward()
    stages[3]()
    for i, copy in enumerate(beyond):
        copy.wait()
        out_pair(i + 1).start()
    stages[4]()
    for slot in range(3):
        for over_one in (over_x, over_y):
            if slot > 0:
                over_one(slot).wait_recv()
            over_one(slot).wait_send()
    for copy in rest:
        copy.wait()
    for slot in range(4):
        out_pair(slot).wait()
    up_finish()


def opening(rows, small, marks, columns, w_out, up_own):
    tokens, width = rows.shape
    sizes = (3, 3, 7, 7, 7, 7, 7, 7, 3, 3, 3, 3, 3, 3, 3, 3, 4, 4)
    return kernel_call(
        opening_kernel,
        [
            ((8, tokens, width), LOW),
            ((2, width), F32),
            ((8, 4, 8, 128), F32),
            ((8, 8, 128), F32),
            ((4, *columns.shape), LOW),
            ((4, 4, 2, *w_out.shape), LOW),
            ((4 * up_own.shape[1], up_own.shape[2]), LOW),
        ],
        (rows, small, marks, columns, w_out, up_own),
        [pltpu.SemaphoreType.DMA((size,)) for size in sizes] + SPREAD_SEMS + GATHER_SEMS,
        0,
        far_outs=(6,),
        far_args=(5,),
    )


def holder(e):
    return (lax.rem(e, 2) == 0) | (e == 3), jnp.where(e == 3, 4, e // 2)


BLOCK = 256


def turned(values, cosine, sine):
    return values * cosine + pltpu.roll(values, HEAD // 2, 1) * sine


def middle_kernel(
    n1, weights, cosine, sine, ids_row, ids_column, w_out, rows, gain, cot, up_own, down_own, sdown_own,
    qkv, logsum, attn, resid, n2_all, cot_all, up_all, down_all, sdown_all,
    attended, a_send, a_recv, *sems,
):
    b, e, z, core = place()
    tokens = rows.shape[0]
    mates = pack_mates()
    count = len(SPREAD_SEMS)
    spreads = [
        spread_rows(up_own.at[1], up_all, up_own.shape[1], sems[:count]),
        spread_rows(down_own.at[0], down_all.at[0], down_own.shape[1], sems[count : 2 * count]),
        spread_rows(down_own.at[1], down_all.at[1], down_own.shape[1], sems[2 * count : 3 * count]),
        spread_rows(sdown_own, sdown_all, sdown_own.shape[0], sems[3 * count : 4 * count]),
    ]
    sems = sems[4 * count :]
    cot_stages = line_stages(cot_all, *sems[: len(GATHER_SEMS)])
    n2_stages = line_stages(n2_all, *sems[len(GATHER_SEMS) :])
    greet([(b ^ 1, e), (b ^ 2, e), *mates])
    cot_all[e] = cot[...]
    for start, _, _ in spreads:
        start()
    cot_stages[0]()
    holds, pair = holder(e)

    @pl.when(jnp.logical_not(holds))
    def _():
        qkv[...] = jnp.zeros_like(qkv)
        logsum[...] = jnp.zeros_like(logsum)

    @pl.when(holds)
    def _():
        @pl.loop(0, n1.shape[0] // BLOCK)
        def _(i):
            here = pl.ds(pl.multiple_of(i * BLOCK, BLOCK), BLOCK)
            projected = dot(n1[here, :], weights[:, : 6 * HEAD])
            cos_here, sin_here = cosine[here, :], sine[here, :]
            for part in range(6):
                piece = projected[:, part * HEAD : (part + 1) * HEAD]
                if part < 4:
                    piece = turned(piece, cos_here, sin_here)
                qkv[part, here, :] = low(piece)

    cot_stages[1]()
    for head in range(2):

        @pl.when(holds)
        def _():
            for i in range(n1.shape[0] // BLOCK):
                here = pl.ds(i * BLOCK, BLOCK)
                keys = (i + 1) * BLOCK
                scores = dot(qkv[head, here, :], qkv[2 + head, :keys, :], ((1,), (1,)))
                scores = jnp.where(
                    allowed_here(ids_column, ids_row, i, keys), scores * HEAD ** (-0.5), NEGATIVE
                )
                top = jnp.max(scores, axis=1, keepdims=True)
                weight = jnp.exp(scores - top)
                total = jnp.sum(weight, axis=1, keepdims=True)
                out = dot(low(weight / total), qkv[4 + head, :keys, :])
                logsum[head, here, :] = jnp.broadcast_to(top + jnp.log(total), (BLOCK, HEAD))
                for j in range(BLOCK // tokens):
                    attended[i * (BLOCK // tokens) + j, :, head * HEAD : (head + 1) * HEAD] = low(
                        out[j * tokens : (j + 1) * tokens]
                    )

        cot_stages[2 + head]()
        spreads[head][1]()

    def give(i):
        other = lax.rem(e + i, 8)
        return send(
            attended.at[other], attn.at[pair], a_send.at[i - 1], a_recv.at[pair], (b, other)
        )

    @pl.when(holds)
    def _():
        for i in range(1, 8):
            give(i).start()
        attn[pair] = attended[e]

    total = rows[...]
    for source, index in PAIR_OF.items():

        @pl.when(e != source)
        def _():
            block = attn.at[index]
            send(block, block, a_send.at[0], a_recv.at[index], (b, source)).wait_recv()

        size = attn.shape[2]
        total = total + dot(attn[index], w_out[index * size : (index + 1) * size, :])
    resid[...] = total
    inv = lax.rsqrt(jnp.mean(total * total, axis=1, keepdims=True) + EPSILON)
    n2_all[e] = low(total * inv * gain[...])
    n2_stages[0]()
    spreads[2][1]()
    spreads[3][1]()
    for stage in n2_stages[1:]:
        stage()
    cot_stages[4]()

    @pl.when(holds)
    def _():
        for i in range(1, 8):
            give(i).wait_send()

    for _, _, finish in spreads:
        finish()


def allowed_here(ids_column, ids_row, i, keys):
    query = i * BLOCK + lax.broadcasted_iota(jnp.int32, (BLOCK, keys), 0)
    key = lax.broadcasted_iota(jnp.int32, (BLOCK, keys), 1)
    same = ids_column[i * BLOCK : (i + 1) * BLOCK, :] == ids_row[:, :keys]
    return (key <= query) & same


def middle(n1, weights, cosine, sine, ids_row, ids_column, w_out, rows, gain, cot, up_own, down_own, sdown_own):
    tokens, width = rows.shape
    length = n1.shape[0]
    pair = 2 * HEAD
    count = len(PAIR_OF)
    return kernel_call(
        middle_kernel,
        [
            ((6, length, HEAD), LOW),
            ((2, length, HEAD), F32),
            ((count, tokens, pair), LOW),
            ((tokens, width), F32),
            ((8, tokens, width), LOW),
            ((8, tokens, width), LOW),
            ((4 * up_own.shape[1], up_own.shape[2]), LOW),
            ((2, 4 * down_own.shape[1], width), LOW),
            ((4 * sdown_own.shape[0], width), LOW),
        ],
        (n1, weights, cosine, sine, ids_row, ids_column, w_out, rows, gain, cot, up_own, down_own, sdown_own),
        [
            pltpu.VMEM((8, tokens, pair), LOW),
            pltpu.SemaphoreType.DMA((7,)),
            pltpu.SemaphoreType.DMA((count,)),
        ]
        + SPREAD_SEMS * 4
        + GATHER_SEMS * 2,
        1,
        far_outs=(6, 7, 8),
        far_args=(10, 11, 12),
    )


def turn_kernel(
    part, out_part, upstream, gates, w_router, resid, gain, w_out, up_term, down_term,
    dresid, dlogits, gain_term, darrived, output_rows, up_grad, down_grad,
    dattn, a_send, a_recv, *scratch,
):
    b, e, z, core = place()
    greet([(b ^ 1, e), (b ^ 2, e), *pack_mates()])
    reduces = [
        reduce_rows(up_term, up_grad, scratch[:REDUCE_COUNT]),
        reduce_rows(down_term, down_grad, scratch[REDUCE_COUNT : 2 * REDUCE_COUNT]),
    ]
    scratch = scratch[2 * REDUCE_COUNT :]
    count = len(scratch) // 2
    row_stages = line_sum_stages(part, *scratch[:count])
    out_stages = line_sum_stages(out_part, *scratch[count:])
    row_stages[0]()
    for start, _, _ in reduces:
        start()
    holds, pair = holder(e)
    row_stages[1]()
    out_stages[0]()
    row_stages[2]()
    reduces[0][1]()
    row_stages[3]()
    total = row_stages[4]()
    width = upstream.shape[1]
    experts = gates.shape[1]
    dgate = total[:, width : width + experts] + total[:, width + experts : width + 2 * experts]
    own = gates[...]
    dlog = low(own * (dgate - jnp.sum(own * dgate, axis=1, keepdims=True)))
    dlogits[...] = dlog
    dn2 = total[:, :width] + dot(dlog, w_router[...])
    rows = resid[...]
    inv = lax.rsqrt(jnp.mean(rows * rows, axis=1, keepdims=True) + EPSILON)
    xhat = rows * inv
    gain_term[...] = jnp.sum(dn2 * xhat, axis=0, keepdims=True)
    scaled = dn2 * gain[...]
    grad = upstream[...] + inv * (scaled - xhat * jnp.mean(scaled * xhat, axis=1, keepdims=True))
    dresid[...] = grad
    back = low(dot(low(grad), w_out[...], ((1,), (1,))))
    size = dattn.shape[2]

    def give(source, index):
        return send(dattn.at[index], darrived.at[e], a_send.at[index], a_recv.at[e], (b, source))

    for source, index in PAIR_OF.items():
        dattn[index] = back[:, index * size : (index + 1) * size]

        @pl.when(e != source)
        def _():
            give(source, index).start()

    out_stages[1]()
    reduces[1][1]()
    out_stages[2]()
    out_stages[3]()

    @pl.when(jnp.logical_not(holds))
    def _():
        darrived[...] = jnp.zeros_like(darrived)

    @pl.when(holds)
    def _():
        darrived[e] = dattn[pair]
        for i in range(1, 8):
            other = lax.rem(e + i, 8)
            block = darrived.at[other]
            send(block, block, a_send.at[0], a_recv.at[other], (b, other)).wait_recv()

    output_rows[...] = resid[...] + out_stages[4]()
    for _, _, finish in reduces:
        finish()
    for source, index in PAIR_OF.items():

        @pl.when(e != source)
        def _():
            give(source, index).wait_send()


def turn(part, out_part, upstream, gates, w_router, resid, gain, w_out, up_term, down_term):
    tokens, width = upstream.shape
    pair = 2 * HEAD
    count = len(PAIR_OF)
    up_rows, down_rows = up_term.shape[0] // 4, down_term.shape[0] // 4
    return kernel_call(
        turn_kernel,
        [
            ((tokens, width), F32),
            (gates.shape, LOW),
            ((1, width), F32),
            ((8, tokens, pair), LOW),
            ((tokens, width), F32),
            ((up_rows, up_term.shape[1]), F32),
            ((down_rows, down_term.shape[1]), F32),
        ],
        (part, out_part, upstream, gates, w_router, resid, gain, w_out, up_term, down_term),
        [
            pltpu.VMEM((count, tokens, pair), LOW),
            pltpu.SemaphoreType.DMA((count,)),
            pltpu.SemaphoreType.DMA((8,)),
        ]
        + reduce_scratch((up_rows // 2, up_term.shape[1]), True)
        + reduce_scratch((down_rows // 2, down_term.shape[1]), True)
        + scatter_scratch(tokens, part.shape[2])
        + SCATTER_SEMS
        + scatter_scratch(tokens, width)
        + SCATTER_SEMS,
        2,
        far_args=(8, 9),
    )


PARTNERS = ((0, 1), (1, 0), (2, 0), (0, 2), (0, 4))


def closing_kernel(
    dattn, qkv, logsum, n1, weights, cosine, sine, ids_row, ids_column, rows, gain, dresid,
    up_term, down_term, sdown_term, sup_term, out_term, small,
    input_grad, columns, out_grad, up_grad, down_grad, sdown_grad, small_sum,
    dkey, dvalue, dprojected, part, column_term, column_sum, column_low,
    out_near, out_sum, out_low, out_half, out_got, small_got, small_step,
    n_send, n_recv, o_send, o_recv, c_send, c_recv, s_send, s_recv, *scratch,
):
    b, e, z, core = place()
    length = n1.shape[0]
    tokens = rows.shape[0]
    mates = pack_mates()
    greet([(b ^ 1, e), (b ^ 2, e), *mates])
    holds, pair = holder(e)

    def cut():
        nonlocal scratch
        mine, scratch = scratch[:REDUCE_COUNT], scratch[REDUCE_COUNT:]
        return mine

    up = reduce_rows(up_term, up_grad, cut())
    down = reduce_rows(down_term, down_grad, cut())
    sdown = reduce_rows(sdown_term, sdown_grad, cut())
    column = reduce_rows(column_term, column_sum, cut())
    out = reduce_stages(
        lambda owner, half: out_sum.at[owner, pl.ds(2 * half, 2)],
        lambda half: out_half.at[pl.ds(2 * half, 2)],
        *cut(),
    )
    stages = line_sum_stages(part, *scratch)

    def partner(i):
        batch_bit, expert_bit = PARTNERS[i]
        src = small if i == 0 else small_step.at[i - 1]
        device = (b ^ batch_bit, e ^ expert_bit)
        return send(src, small_got.at[i], s_send.at[i], s_recv.at[i], device)

    def small_round(i):
        partner(i).wait_recv()
        before = small[...] if i == 0 else small_step[i - 1]
        if i < len(PARTNERS) - 1:
            small_step[i] = before + small_got[i]
            partner(i + 1).start()
        else:
            small_sum[...] = before + small_got[i]

    near = send(
        out_term.at[:, :, 1 - core], out_near, n_send.at[0], n_recv.at[0], (b, e ^ 1)
    )
    near.start()
    own = pltpu.make_async_copy(out_term.at[:, :, core], out_sum, n_send.at[1])
    own.start()
    partner(0).start()
    up[0]()
    down[0]()
    sdown[0]()

    def attend(head):
        dkey[...] = jnp.zeros_like(dkey)
        dvalue[...] = jnp.zeros_like(dvalue)
        lanes = pl.ds(head * HEAD, HEAD)
        for i in range(length // BLOCK):
            here = pl.ds(i * BLOCK, BLOCK)
            keys = (i + 1) * BLOCK
            count = BLOCK // tokens
            back = jnp.concatenate(
                [dattn[count * i + j, :, lanes] for j in range(count)], axis=0
            )
            query = qkv[head, here, :]
            scores = dot(query, qkv[2 + head, :keys, :], ((1,), (1,))) * HEAD ** (-0.5)
            weight = jnp.where(
                allowed_here(ids_column, ids_row, i, keys),
                jnp.exp(scores - logsum[head, here, 0:1]),
                0.0,
            )
            dprob = dot(back, qkv[4 + head, :keys, :], ((1,), (1,)))
            delta = jnp.sum(weight * dprob, axis=1, keepdims=True)
            dscore = low(weight * (dprob - delta))
            dquery = dot(dscore, qkv[2 + head, :keys, :]) * HEAD ** (-0.5)
            dkey[:keys, :] += dot(dscore, query, ((0,), (0,)))
            dvalue[:keys, :] += dot(low(weight), back, ((0,), (0,)))
            dprojected[here, lanes] = low(turned(dquery, cosine[here, :], -sine[here, :]))
        dprojected[:, (2 + head) * HEAD : (3 + head) * HEAD] = low(
            turned(dkey[...] * HEAD ** (-0.5), cosine[...], -sine[...])
        )
        dprojected[:, (4 + head) * HEAD : (5 + head) * HEAD] = low(dvalue[...])

    @pl.when(holds)
    def _():
        attend(0)

    near.wait()
    own.wait()
    for owner in range(4):
        for owner_z in range(4):
            out_sum[owner, owner_z] = low(
                out_sum[owner, owner_z].astype(F32) + out_near[owner, owner_z].astype(F32)
            )
    out[0]()
    small_round(0)
    up[1]()

    @pl.when(holds)
    def _():
        attend(1)
        for i in range(8):
            part[i] = low(
                dot(
                    dprojected[i * tokens : (i + 1) * tokens, :],
                    weights[:, : 6 * HEAD],
                    ((1,), (1,)),
                )
            )

    @pl.when(jnp.logical_not(holds))
    def _():
        part[...] = jnp.zeros_like(part)

    stages[0]()
    column_term[:, 6 * HEAD :] = sup_term[...]

    @pl.when(holds)
    def _():
        for i in range(n1.shape[1] // BLOCK):
            here = pl.ds(i * BLOCK, BLOCK)
            column_term[here, : 6 * HEAD] = low(dot(n1[:, here], dprojected[...], ((0,), (0,))))

    @pl.when(jnp.logical_not(holds))
    def _():
        column_term[:, : 6 * HEAD] = jnp.zeros((n1.shape[1], 6 * HEAD), LOW)

    column[0]()
    stages[1]()
    small_round(1)
    down[1]()
    sdown[1]()
    stages[2]()
    small_round(2)
    out[1]()
    stages[3]()
    small_round(3)
    values = rows[...]
    inv = lax.rsqrt(jnp.mean(values * values, axis=1, keepdims=True) + EPSILON)
    xhat = values * inv
    scaled = stages[4]() * gain[...]
    input_grad[...] = dresid[...] + inv * (
        scaled - xhat * jnp.mean(scaled * xhat, axis=1, keepdims=True)
    )
    column[1]()
    out[2]()
    for owner_z in range(4):
        out_low[owner_z] = low(out_half[owner_z])
    along = []
    for i in range(3):
        device = (b, lax.rem(e + 2 * i + 2, 8))
        along.append(
            send(
                out_low.at[device[1] // 2], out_got.at[i], o_send.at[i], o_recv.at[i], device
            )
        )
        along[-1].start()
    small_round(4)
    for i in range(len(PARTNERS)):
        partner(i).wait_send()
    up[2]()
    down[2]()
    sdown[2]()
    for copy in along:
        copy.wait()
    out_grad[...] = (
        out_half[z]
        + out_got[0].astype(F32)
        + out_got[1].astype(F32)
        + out_got[2].astype(F32)
    )
    column[2]()
    piece = column_low.shape[1]
    for i in range(0, 8, 2):
        two = column_sum[i * piece : (i + 2) * piece, :].astype(F32)
        column_low[i] = low(two[:piece])
        column_low[i + 1] = low(two[piece:])
    columns[e] = column_low[e]
    across = []
    for i, device in enumerate(mates):
        across.append(
            send(column_low.at[device[1]], columns.at[e], c_send.at[i], c_recv.at[i], device)
        )
        across[-1].start()
    for copy in across:
        copy.wait()


def closing(
    dattn, qkv, logsum, n1, weights, cosine, sine, ids_row, ids_column, rows, gain, dresid,
    up_term, down_term, sdown_term, sup_term, out_term, small,
):
    tokens, width = rows.shape
    length = n1.shape[0]
    rows_w = out_term.shape[3]
    wide = weights.shape[1]
    up_rows, down_rows, sdown_rows = (
        term.shape[0] // 4 for term in (up_term, down_term, sdown_term)
    )
    dma = pltpu.SemaphoreType.DMA
    return kernel_call(
        closing_kernel,
        [
            ((tokens, width), F32),
            ((8, rows_w, wide), LOW),
            ((rows_w, width), F32),
            ((up_rows, up_term.shape[1]), F32),
            ((down_rows, width), F32),
            ((sdown_rows, width), F32),
            (small.shape, F32),
        ],
        (
            dattn, qkv, logsum, n1, weights, cosine, sine, ids_row, ids_column, rows, gain, dresid,
            up_term, down_term, sdown_term, sup_term, out_term, small,
        ),
        [
            pltpu.VMEM((length, HEAD), F32),
            pltpu.VMEM((length, HEAD), F32),
            pltpu.VMEM((length, 6 * HEAD), LOW),
            pltpu.VMEM((8, tokens, width), LOW),
            pltpu.VMEM((width, wide), LOW),
            pltpu.VMEM((width // 4, wide), LOW),
            pltpu.VMEM((8, rows_w, wide), LOW),
            pltpu.VMEM((4, 4, rows_w, width), LOW),
            pltpu.VMEM((4, 4, rows_w, width), LOW),
            pltpu.VMEM((4, rows_w, width), LOW),
            pltpu.VMEM((4, rows_w, width), F32),
            pltpu.VMEM((3, rows_w, width), LOW),
            pltpu.VMEM((5, *small.shape), F32),
            pltpu.VMEM((4, *small.shape), F32),
            dma((2,)), dma((1,)), dma((3,)), dma((3,)), dma((7,)), dma((7,)), dma((5,)), dma((5,)),
        ]
        + reduce_scratch((up_rows // 2, up_term.shape[1]), True)
        + reduce_scratch((down_rows // 2, width), True)
        + reduce_scratch((sdown_rows // 2, width))
        + reduce_scratch((width // 8, wide))
        + reduce_scratch((2, rows_w, width))
        + scatter_scratch(tokens, width)
        + SCATTER_SEMS,
        3,
        far_args=(12, 13, 16),
    )


def silu_parts(gate, up):
    sigma = jax.nn.sigmoid(gate)
    return gate * sigma, up * sigma * (1.0 + gate * (1.0 - sigma))


def pack_device(
    block_input,
    seq_ids,
    routes,
    cotangent,
    qkv_weight,
    out_weight,
    shared_up,
    shared_down,
    router_weight,
    gain_attn,
    gain_ffn,
    expert_up,
    expert_down,
):
    b = lax.axis_index("batch")
    e = lax.axis_index("expert")
    rows_in = block_input[0]
    upstream = cotangent[0]
    tokens, width = rows_in.shape
    length = tokens * 8
    rows_w = qkv_weight.shape[0]
    pair = 2 * HEAD
    pairs_of_heads = width // pair
    hidden = expert_up.shape[2] // 2
    experts = expert_up.shape[0] * 8
    s_rows = shared_down.shape[0]
    s_each = -(-s_rows // 32) * 32
    s_pad = 4 * s_each

    qkv_low = low(qkv_weight).reshape(rows_w, 3, pairs_of_heads, pair)
    nothing = jnp.zeros((rows_w, 3, pair), LOW)
    columns = [qkv_low[:, :, PAIR_OF[i]] if i in PAIR_OF else nothing for i in range(8)]
    columns = jnp.stack(columns).reshape(8, rows_w, 3 * pair)
    sup_low = low(shared_up).reshape(rows_w, 2, 4, 8, s_rows)
    sup_low = jnp.pad(sup_low, ((0, 0),) * 4 + ((0, s_each - s_rows),)).transpose(3, 0, 1, 2, 4)
    columns = jnp.concatenate([columns, sup_low.reshape(8, rows_w, 2 * s_pad)], axis=2)
    up_own = low(expert_up)
    down_own = low(expert_down)
    sdown_own = jnp.pad(low(shared_down), ((0, s_each - s_rows), (0, 0)))
    core = lax.rem(e, 2)

    small = jnp.concatenate(
        [
            router_weight.reshape(-1, 128),
            jnp.pad(gain_attn[None], ((0, 0), (0, 128 - rows_w))),
            jnp.pad(gain_ffn[None], ((0, 0), (0, 128 - rows_w))),
            jnp.zeros((1, 128), F32),
        ]
    )
    small = low(small).astype(F32)
    marks = jnp.concatenate([routes[0].T, seq_ids], axis=0).astype(F32)
    marks = jnp.pad(marks, ((0, 7 - TOP), (0, 0)))
    n1_all, gains, small, marks, columns, w_out, up_first = opening(
        rows_in, small, marks, columns, low(out_weight), up_own
    )
    n1_all = n1_all.reshape(length, width)
    columns = columns.reshape(width, 3 * pair + 2 * s_pad)
    w_qkv = columns[:, : 3 * pair]
    w_sup = columns[:, 3 * pair :]
    w_out = w_out.reshape(width, width)
    router_rows = rows_w * experts // 128
    w_router = low(small[:, :, :router_rows].transpose(1, 0, 2, 3).reshape(width, experts))
    gain_first = gains[0:1]
    gain_second = gains[1:2]
    marks = marks.astype(jnp.int32).transpose(0, 2, 1).reshape(length, 8)
    route_all = marks[:, :TOP]
    ids_all = marks[:, TOP]
    positions = jnp.arange(length, dtype=jnp.int32)
    ids_row = ids_all[None, :]
    ids_column = ids_all[:, None]
    frequency = 10000.0 ** (-jnp.arange(HEAD // 2, dtype=jnp.float32) / (HEAD // 2))
    angle = positions.astype(F32)[:, None] * frequency[None, :]
    cosine = jnp.concatenate([jnp.cos(angle)] * 2, axis=1)
    sine = jnp.concatenate([-jnp.sin(angle), jnp.sin(angle)], axis=1)
    qkv, logsum, attn, resid, n2_all, cot_all, up_second, down_low, w_sdown = middle(
        n1_all,
        columns,
        cosine,
        sine,
        ids_row,
        ids_column,
        w_out,
        rows_in,
        gain_second,
        low(upstream),
        up_own,
        down_own,
        sdown_own,
    )
    up_low = (up_first, up_second)
    attn = attn.transpose(1, 0, 2).reshape(tokens, width)
    cot_all = cot_all.reshape(length, width)

    n2 = lax.dynamic_index_in_dim(n2_all, e, 0, False)
    n2_all = n2_all.reshape(length, width)
    logits = dot(n2_all, w_router)
    hot = route_all[:, :, None] == jnp.arange(experts, dtype=jnp.int32)[None, None, :]
    routed_to = jnp.any(hot, axis=1)
    logits = jnp.where(routed_to, logits, NEGATIVE)
    gates = jnp.where(routed_to, jnp.exp(logits - jnp.max(logits, axis=1, keepdims=True)), 0.0)
    gates = gates / jnp.sum(gates, axis=1, keepdims=True)
    mine = lax.dynamic_slice_in_dim(gates, 2 * e, 2, 1)

    output_part = 0.0
    drow_part = 0.0
    dgates = []
    up_terms = []
    down_terms = []
    for k in range(2):
        gate = mine[:, k : k + 1]
        pre = dot(n2_all, up_low[k])
        silu, slope = silu_parts(pre[:, :hidden], pre[:, hidden:])
        hid = silu * pre[:, hidden:]
        back = dot(cot_all, down_low[k], ((1,), (1,)))
        dgates.append(jnp.sum(back * hid, axis=1, keepdims=True))
        hid_low = low(hid * gate)
        output_part = output_part + dot(hid_low, down_low[k])
        down_terms.append(dot(hid_low, cot_all, ((0,), (0,))))
        back = back * gate
        dpre = low(jnp.concatenate([back * slope, back * silu], axis=1))
        up_terms.append(dot(n2_all, dpre, ((0,), (0,))))
        drow_part = drow_part + dot(dpre, up_low[k], ((1,), (1,)))
    pre = dot(n2_all, w_sup)
    silu, slope = silu_parts(pre[:, :s_pad], pre[:, s_pad:])
    hid_low = low(silu * pre[:, s_pad:])
    back = dot(cot_all, w_sdown, ((1,), (1,)))
    output_part = output_part + dot(hid_low, w_sdown)
    sdown_term = dot(hid_low, cot_all, ((0,), (0,)))
    dpre = low(jnp.concatenate([back * slope, back * silu], axis=1))
    sup_term = dot(n2_all, dpre, ((0,), (0,)))
    drow_part = drow_part + dot(dpre, w_sup, ((1,), (1,)))
    lane = jnp.arange(experts, dtype=jnp.int32)[None, :] - 2 * e
    dgate = jnp.where(lane == 0, dgates[0], 0.0) + jnp.where(lane == 1, dgates[1], 0.0)
    dgate_high = low(dgate)
    dgate_rest = low(dgate - dgate_high.astype(F32))
    spare = jnp.zeros((length, 128 - 2 * experts), LOW)
    part = jnp.concatenate([low(drow_part), dgate_high, dgate_rest, spare], axis=1)
    up_terms = [low(term) for term in up_terms]
    down_terms = [low(term) for term in down_terms]
    own_gates = lax.dynamic_slice_in_dim(gates, e * tokens, tokens, 0)
    dresid, dlogits, gain_ffn_term, dattn, output_rows, up_grad_first, down_grad_first = turn(
        part.reshape(8, tokens, part.shape[1]),
        low(output_part).reshape(8, tokens, width),
        upstream,
        own_gates,
        w_router.T,
        resid,
        gain_second,
        w_out,
        up_terms[0],
        down_terms[0],
    )
    router_term = dot(dlogits, n2, ((0,), (0,)))
    small = jnp.concatenate(
        [router_term, gain_ffn_term, jnp.zeros((7, width), F32)], axis=0
    )
    out_term = low(dot(attn, low(dresid), ((0,), (0,)))).reshape(4, 4, 2, rows_w, width)
    input_grad, columns, out_grad, up_grad_second, down_grad_second, sdown_grad, small = closing(
        dattn,
        qkv,
        logsum,
        n1_all,
        columns,
        cosine,
        sine,
        ids_row,
        ids_column,
        rows_in,
        gain_first,
        dresid,
        up_terms[1],
        down_terms[1],
        low(sdown_term),
        low(sup_term),
        out_term,
        small,
    )
    expert_up_grad = jnp.stack([up_grad_first, up_grad_second])
    expert_down_grad = jnp.stack([down_grad_first, down_grad_second])
    shared_down_grad = sdown_grad[:s_rows]
    small = lax.dynamic_slice_in_dim(small, (b * 8 + e) * rows_w, rows_w, 1)
    columns = columns.astype(F32)
    qkv_grad = jnp.stack([columns[i, :, : 3 * pair] for i in PAIR_OF])
    qkv_grad = qkv_grad.reshape(pairs_of_heads, rows_w, 3, pair).transpose(1, 2, 0, 3)
    qkv_grad = qkv_grad.reshape(rows_w, 3 * width)
    sup_grad = columns[:, :, 3 * pair :].reshape(8, rows_w, 2, 4, s_each)[..., :s_rows]
    sup_grad = sup_grad.transpose(1, 2, 3, 0, 4)
    sup_grad = sup_grad.reshape(rows_w, shared_up.shape[1])
    own_first = low(gain_attn).astype(F32)
    gain_attn_grad = jnp.sum(low(qkv_weight).astype(F32) * qkv_grad, axis=1) / own_first
    return (
        output_rows[None],
        input_grad[None],
        qkv_grad,
        out_grad,
        sup_grad,
        shared_down_grad,
        small[:experts].T,
        gain_attn_grad,
        small[experts],
        expert_up_grad,
        expert_down_grad,
    )


def solution(mesh):
    in_specs = (
        P("batch", "expert", None),
        P("batch", "expert"),
        P("batch", "expert", None),
        P("batch", "expert", None),
        P(("batch", "expert"), None),
        P(("batch", "expert"), None),
        P(("batch", "expert"), None),
        P(("batch", "expert"), None),
        P(("batch", "expert"), None),
        P(("batch", "expert")),
        P(("batch", "expert")),
        P("expert", "batch", None),
        P("expert", "batch", None),
    )
    out_specs = (
        P("batch", "expert", None),
        P("batch", "expert", None),
        P(("batch", "expert"), None),
        P(("batch", "expert"), None),
        P(("batch", "expert"), None),
        P(("batch", "expert"), None),
        P(("batch", "expert"), None),
        P(("batch", "expert")),
        P(("batch", "expert")),
        P("expert", "batch", None),
        P("expert", "batch", None),
    )
    sizes = dict(mesh.shape)
    body = pack_device if sizes == {"batch": 4, "expert": 8} else per_device
    return jax.shard_map(
        body, mesh=mesh, in_specs=in_specs, out_specs=out_specs, check_vma=False
    )
```

```python
import functools

import jax
import jax.numpy as jnp
import numpy as np
from jax import lax
from jax.experimental import pallas as pl
from jax.experimental.pallas import tpu as pltpu
from jax.sharding import PartitionSpec as P

HEAD = 128
TOP = 6


EPSILON = 1e-06
NEGATIVE = -1e30


def rotate(values, positions, sign):
    half = values.shape[-1] // 2
    frequency = 10000.0 ** (-jnp.arange(half, dtype=jnp.float32) / half)
    angle = positions.astype(jnp.float32)[:, None] * frequency[None, :]
    cosine = jnp.cos(angle)[:, None, :]
    sine = sign * jnp.sin(angle)[:, None, :]
    first = values[..., :half]
    second = values[..., half:]
    return jnp.concatenate(
        [first * cosine - second * sine, first * sine + second * cosine], axis=-1
    )


def swiglu(pre, hidden_width):
    return jax.nn.silu(pre[..., :hidden_width]) * pre[..., hidden_width:]


def swiglu_back(pre, dhidden, hidden_width):
    gate_part = pre[..., :hidden_width]
    up_part = pre[..., hidden_width:]
    sigma = jax.nn.sigmoid(gate_part)
    dgate = dhidden * up_part * sigma * (1.0 + gate_part * (1.0 - sigma))
    dupper = dhidden * gate_part * sigma
    return jnp.concatenate([dgate, dupper], axis=-1)


def norm_back(dnormed, normed, inv_rms, gain):
    dscaled = dnormed * gain
    dinputs = inv_rms * (dscaled - normed * jnp.mean(dscaled * normed, axis=1, keepdims=True))
    return (dinputs, jnp.sum(dnormed * normed, axis=0))


def per_device(
    block_input,
    seq_ids,
    routes,
    cotangent,
    qkv_weight,
    out_weight,
    shared_up,
    shared_down,
    router_weight,
    gain_attn,
    gain_ffn,
    expert_up,
    expert_down,
):
    dense = (
        lax.all_gather(qkv_weight.astype(jnp.bfloat16), ("batch", "expert"), axis=0, tiled=True),
        lax.all_gather(out_weight.astype(jnp.bfloat16), ("batch", "expert"), axis=0, tiled=True),
        lax.all_gather(shared_up.astype(jnp.bfloat16), ("batch", "expert"), axis=0, tiled=True),
        lax.all_gather(shared_down.astype(jnp.bfloat16), ("batch", "expert"), axis=0, tiled=True),
        lax.all_gather(router_weight.astype(jnp.bfloat16), ("batch", "expert"), axis=0, tiled=True),
        lax.all_gather(gain_attn.astype(jnp.bfloat16), ("batch", "expert"), axis=0, tiled=True),
        lax.all_gather(gain_ffn.astype(jnp.bfloat16), ("batch", "expert"), axis=0, tiled=True),
    )
    full_qkv, full_out, full_sup, full_sdown, full_router, low_gain_a, low_gain_f = dense
    gain_first = low_gain_a.astype(jnp.float32)
    gain_second = low_gain_f.astype(jnp.float32)
    experts_up, experts_down = (
        lax.all_gather(expert_up.astype(jnp.bfloat16), "batch", axis=1, tiled=True),
        lax.all_gather(expert_down.astype(jnp.bfloat16), "batch", axis=1, tiled=True),
    )
    rows_in = block_input[0]
    ids_local = seq_ids[0]
    route_local = routes[0]
    upstream = cotangent[0]
    tokens_dev = rows_in.shape[0]
    model_width = rows_in.shape[1]
    heads_count = model_width // HEAD
    groups = lax.axis_size("expert")
    local_experts = experts_up.shape[0]
    experts_all = local_experts * groups
    shared_width = full_sdown.shape[0]
    hidden_width = experts_down.shape[1]
    capacity = max(2, tokens_dev * TOP * 3 // (experts_all * 2))
    score_scale = HEAD ** (-0.5)
    positions = lax.axis_index("expert") * tokens_dev + jnp.arange(tokens_dev, dtype=jnp.int32)
    key_ids = lax.all_gather(ids_local, "expert", axis=0, tiled=True)
    inv_first = lax.rsqrt(jnp.mean(rows_in * rows_in, axis=1, keepdims=True) + EPSILON)
    normed_first = rows_in * inv_first
    input_low = (normed_first * gain_first).astype(jnp.bfloat16)
    projected = jnp.dot(input_low, full_qkv, preferred_element_type=jnp.float32)
    queries = rotate(
        projected[:, :model_width].reshape(tokens_dev, heads_count, HEAD), positions, 1.0
    ).astype(jnp.bfloat16)
    keys = rotate(
        projected[:, model_width : 2 * model_width].reshape(tokens_dev, heads_count, HEAD),
        positions,
        1.0,
    ).astype(jnp.bfloat16)
    values = (
        projected[:, 2 * model_width :].reshape(tokens_dev, heads_count, HEAD).astype(jnp.bfloat16)
    )

    def key_mask(key_count):
        key_pos = jnp.arange(key_count, dtype=jnp.int32)
        return (key_pos[None, :] <= positions[:, None]) & (key_ids[None, :] == ids_local[:, None])

    run_max = jnp.full((heads_count, tokens_dev), NEGATIVE, jnp.float32)
    key_piece = lax.all_gather(keys, "expert", axis=0, tiled=True)
    value_piece = lax.all_gather(values, "expert", axis=0, tiled=True)
    allowed = key_mask(key_piece.shape[0])[None]
    scores = (
        jnp.einsum("qhd,khd->hqk", queries, key_piece, preferred_element_type=jnp.float32)
        * score_scale
    )
    scores = jnp.where(allowed, scores, NEGATIVE)
    new_max = jnp.maximum(run_max, jnp.max(scores, axis=2))
    weights = jnp.where(allowed, jnp.exp(scores - new_max[:, :, None]), 0.0)
    run_sum = jnp.sum(weights, axis=2)
    update = jnp.einsum(
        "hqk,khd->qhd",
        weights.astype(jnp.bfloat16),
        value_piece,
        preferred_element_type=jnp.float32,
    )
    run_acc = update
    run_max, run_sum, run_acc = (new_max, run_sum, run_acc)
    attn_full = run_acc / jnp.transpose(run_sum)[:, :, None]
    logsum = run_max + jnp.log(run_sum)
    attn_low = attn_full.reshape(tokens_dev, model_width).astype(jnp.bfloat16)
    resid = rows_in + jnp.dot(attn_low, full_out, preferred_element_type=jnp.float32)
    inv_second = lax.rsqrt(jnp.mean(resid * resid, axis=1, keepdims=True) + EPSILON)
    normed_second = resid * inv_second
    ffn_low = (normed_second * gain_second).astype(jnp.bfloat16)
    logits = jnp.dot(ffn_low, full_router, preferred_element_type=jnp.float32)
    probs = jax.nn.softmax(logits, axis=1)
    route_hot = route_local[:, :, None] == jnp.arange(experts_all, dtype=jnp.int32)[None, None, :]
    chosen = jnp.sum(jnp.where(route_hot, probs[:, None, :], 0.0), axis=2)
    chosen_sum = jnp.sum(chosen, axis=1, keepdims=True)
    gates = chosen / chosen_sum
    shared_pre = jnp.dot(ffn_low, full_sup, preferred_element_type=jnp.float32)
    shared_hidden = swiglu(shared_pre, shared_width).astype(jnp.bfloat16)
    shared_result = jnp.dot(shared_hidden, full_sdown, preferred_element_type=jnp.float32)
    flat_route = route_local.reshape(-1)
    flat_hot = (flat_route[:, None] == jnp.arange(experts_all, dtype=jnp.int32)[None, :]).astype(
        jnp.bfloat16
    )
    pair_count = tokens_dev * TOP
    pair_index = jnp.arange(pair_count, dtype=jnp.int32)
    earlier = (pair_index[None, :] < pair_index[:, None]).astype(jnp.bfloat16)
    counts = jnp.dot(earlier, flat_hot, preferred_element_type=jnp.float32)
    slots = jnp.sum(counts * flat_hot, axis=1).astype(jnp.int32)
    source_table = (
        jnp.full((experts_all * capacity,), pair_count, jnp.int32)
        .at[flat_route * capacity + slots]
        .set(jnp.arange(pair_count, dtype=jnp.int32))
    )
    send_table = jnp.transpose(
        source_table.reshape(groups, local_experts, capacity), (1, 0, 2)
    ).reshape(-1)
    return_pos = (
        flat_route % local_experts * (groups * capacity)
        + flat_route // local_experts * capacity
        + slots
    )
    padded_rows = jnp.concatenate([ffn_low, jnp.zeros((1, model_width), jnp.bfloat16)], axis=0)
    send_rows = padded_rows[send_table // TOP].reshape(local_experts, groups, capacity, model_width)
    received = lax.all_to_all(send_rows, "expert", split_axis=1, concat_axis=1, tiled=True)
    expert_rows = received.reshape(local_experts, groups * capacity, model_width)
    expert_pre = jnp.einsum(
        "erd,edf->erf", expert_rows, experts_up, preferred_element_type=jnp.float32
    )
    expert_hidden = swiglu(expert_pre, hidden_width).astype(jnp.bfloat16)
    expert_result = jnp.einsum(
        "erf,efd->erd", expert_hidden, experts_down, preferred_element_type=jnp.float32
    ).astype(jnp.bfloat16)
    returned = lax.all_to_all(
        expert_result.reshape(local_experts, groups, capacity, model_width),
        "expert",
        split_axis=1,
        concat_axis=1,
        tiled=True,
    )
    token_outputs = returned.reshape(-1, model_width)[return_pos].reshape(
        tokens_dev, TOP, model_width
    )
    routed = jnp.sum(gates[:, :, None] * token_outputs, axis=1)
    output_rows = resid + shared_result + routed
    shared_cot = upstream.astype(jnp.bfloat16)
    shared_down_term = jnp.dot(shared_hidden.T, shared_cot, preferred_element_type=jnp.float32)
    dshared_hidden = jnp.dot(shared_cot, full_sdown.T, preferred_element_type=jnp.float32)
    dshared_pre = swiglu_back(shared_pre, dshared_hidden, shared_width).astype(jnp.bfloat16)
    shared_up_term = jnp.dot(ffn_low.T, dshared_pre, preferred_element_type=jnp.float32)
    dnormed_second = jnp.dot(dshared_pre, full_sup.T, preferred_element_type=jnp.float32)
    token_cot = (gates[:, :, None] * upstream[:, None, :]).astype(jnp.bfloat16)
    dgates = jnp.sum(upstream[:, None, :] * token_outputs, axis=2)
    padded_cot = jnp.concatenate(
        [token_cot.reshape(-1, model_width), jnp.zeros((1, model_width), jnp.bfloat16)], axis=0
    )
    send_cot = padded_cot[send_table].reshape(local_experts, groups, capacity, model_width)
    received_cot = lax.all_to_all(
        send_cot, "expert", split_axis=1, concat_axis=1, tiled=True
    ).reshape(local_experts, groups * capacity, model_width)
    down_term = jnp.einsum(
        "erf,erd->efd", expert_hidden, received_cot, preferred_element_type=jnp.float32
    )
    dexpert_hidden = jnp.einsum(
        "erd,efd->erf", received_cot, experts_down, preferred_element_type=jnp.float32
    )
    dexpert_pre = swiglu_back(expert_pre, dexpert_hidden, hidden_width).astype(jnp.bfloat16)
    up_term = jnp.einsum(
        "erd,erf->edf", expert_rows, dexpert_pre, preferred_element_type=jnp.float32
    )
    drows = jnp.einsum(
        "erf,edf->erd", dexpert_pre, experts_up, preferred_element_type=jnp.float32
    ).astype(jnp.bfloat16)
    returned_grad = lax.all_to_all(
        drows.reshape(local_experts, groups, capacity, model_width),
        "expert",
        split_axis=1,
        concat_axis=1,
        tiled=True,
    )
    row_grads = returned_grad.reshape(-1, model_width)[return_pos].reshape(
        tokens_dev, TOP, model_width
    )
    dnormed_second = dnormed_second + jnp.sum(row_grads, axis=1, dtype=jnp.float32)
    expert_up_grad, expert_down_grad = (
        lax.psum_scatter(
            up_term.astype(jnp.bfloat16), "batch", scatter_dimension=1, tiled=True
        ).astype(jnp.float32),
        lax.psum_scatter(
            down_term.astype(jnp.bfloat16), "batch", scatter_dimension=1, tiled=True
        ).astype(jnp.float32),
    )
    dchosen = (dgates - jnp.sum(dgates * gates, axis=1, keepdims=True)) / chosen_sum
    dprobs = jnp.sum(jnp.where(route_hot, dchosen[:, :, None], 0.0), axis=1)
    dlogits = (probs * (dprobs - jnp.sum(probs * dprobs, axis=1, keepdims=True))).astype(
        jnp.bfloat16
    )
    router_term = jnp.dot(ffn_low.T, dlogits, preferred_element_type=jnp.float32)
    dnormed_second = dnormed_second + jnp.dot(
        dlogits, full_router.T, preferred_element_type=jnp.float32
    )
    dresid_norm, gain_ffn_term = norm_back(dnormed_second, normed_second, inv_second, gain_second)
    dresid = upstream + dresid_norm
    dproj = dresid.astype(jnp.bfloat16)
    out_term = jnp.dot(attn_low.T, dproj, preferred_element_type=jnp.float32)
    dattn = (
        jnp.dot(dproj, full_out.T, preferred_element_type=jnp.float32)
        .astype(jnp.bfloat16)
        .reshape(tokens_dev, heads_count, HEAD)
    )
    delta_rows = jnp.sum(dattn.astype(jnp.float32) * attn_full, axis=2)
    delta_heads = jnp.transpose(delta_rows)
    key_piece = lax.all_gather(keys, "expert", axis=0, tiled=True)
    value_piece = lax.all_gather(values, "expert", axis=0, tiled=True)
    allowed = key_mask(key_piece.shape[0])[None]
    scores = (
        jnp.einsum("qhd,khd->hqk", queries, key_piece, preferred_element_type=jnp.float32)
        * score_scale
    )
    attn_probs = jnp.where(allowed, jnp.exp(scores - logsum[:, :, None]), 0.0)
    dprob = jnp.einsum("qhd,khd->hqk", dattn, value_piece, preferred_element_type=jnp.float32)
    dscore = (attn_probs * (dprob - delta_heads[:, :, None])).astype(jnp.bfloat16)
    attn_probs, dscore = (attn_probs, dscore)
    dquery = jnp.einsum("hqk,khd->qhd", dscore, key_piece, preferred_element_type=jnp.float32)
    dkey_piece = jnp.einsum("hqk,qhd->khd", dscore, queries, preferred_element_type=jnp.float32)
    dvalue_piece = jnp.einsum(
        "hqk,qhd->khd", attn_probs.astype(jnp.bfloat16), dattn, preferred_element_type=jnp.float32
    )
    folded = (dquery, dkey_piece, dvalue_piece)
    dquery = folded[0]
    dkey, dvalue = (
        lax.psum_scatter(
            folded[1].astype(jnp.bfloat16), "expert", scatter_dimension=0, tiled=True
        ).astype(jnp.float32),
        lax.psum_scatter(
            folded[2].astype(jnp.bfloat16), "expert", scatter_dimension=0, tiled=True
        ).astype(jnp.float32),
    )
    dquery_raw = rotate(dquery * score_scale, positions, -1.0).reshape(tokens_dev, model_width)
    dkey_raw = rotate(dkey * score_scale, positions, -1.0).reshape(tokens_dev, model_width)
    dprojected = jnp.concatenate(
        [dquery_raw, dkey_raw, dvalue.reshape(tokens_dev, model_width)], axis=1
    ).astype(jnp.bfloat16)
    qkv_term = jnp.dot(input_low.T, dprojected, preferred_element_type=jnp.float32)
    dnormed_first = jnp.dot(dprojected, full_qkv.T, preferred_element_type=jnp.float32)
    dinput_norm, gain_attn_term = norm_back(dnormed_first, normed_first, inv_first, gain_first)
    input_grad = dresid + dinput_norm
    grads = (
        lax.psum_scatter(qkv_term, ("batch", "expert"), scatter_dimension=0, tiled=True),
        lax.psum_scatter(out_term, ("batch", "expert"), scatter_dimension=0, tiled=True),
        lax.psum_scatter(shared_up_term, ("batch", "expert"), scatter_dimension=0, tiled=True),
        lax.psum_scatter(shared_down_term, ("batch", "expert"), scatter_dimension=0, tiled=True),
        lax.psum_scatter(router_term, ("batch", "expert"), scatter_dimension=0, tiled=True),
        lax.psum_scatter(gain_attn_term, ("batch", "expert"), scatter_dimension=0, tiled=True),
        lax.psum_scatter(gain_ffn_term, ("batch", "expert"), scatter_dimension=0, tiled=True),
    )
    (
        qkv_grad,
        out_grad,
        shared_up_grad,
        shared_down_grad,
        router_grad,
        gain_attn_grad,
        gain_ffn_grad,
    ) = grads
    return (
        output_rows[None],
        input_grad[None],
        qkv_grad,
        out_grad,
        shared_up_grad,
        shared_down_grad,
        router_grad,
        gain_attn_grad,
        gain_ffn_grad,
        expert_up_grad,
        expert_down_grad,
    )


PAIR_OF = {0: 0, 2: 1, 4: 2, 6: 3, 3: 4}
F32 = jnp.float32
LOW = jnp.bfloat16
COST = 10**9


def low(values):
    return values.astype(LOW)


def dot(left, right, dims=((1,), (0,))):
    return lax.dot_general(left, right, (dims, ((), ())), preferred_element_type=F32)


MESH_ID = pl.DeviceIdType.MESH


def place():
    b = lax.axis_index("batch")
    e = lax.axis_index("expert")
    return b, e, e // 2, lax.rem(e, 2)


def greet_line():
    b, e, z, core = place()
    barrier = pltpu.get_barrier_semaphore()
    pl.semaphore_signal(barrier, inc=1, device_id=(b, e ^ 1), device_id_type=MESH_ID)

    @pl.when(z > 0)
    def _():
        pl.semaphore_signal(barrier, inc=1, device_id=(b, e - 2), device_id_type=MESH_ID)

    @pl.when(z < 3)
    def _():
        pl.semaphore_signal(barrier, inc=1, device_id=(b, e + 2), device_id_type=MESH_ID)

    ends = jnp.where((z == 0) | (z == 3), 1, 0)
    pl.semaphore_wait(barrier, 3 - ends)


def greet(devices):
    barrier = pltpu.get_barrier_semaphore()
    for device in devices:
        pl.semaphore_signal(barrier, inc=1, device_id=device, device_id_type=MESH_ID)
    pl.semaphore_wait(barrier, len(devices))


def pack_mates():
    b, e, _, _ = place()
    return [(b, lax.rem(e + i, 8)) for i in range(1, 8)]


def send(src, dst, send_sem, recv_sem, device):
    return pltpu.make_async_remote_copy(
        src_ref=src,
        dst_ref=dst,
        send_sem=send_sem,
        recv_sem=recv_sem,
        device_id=device,
        device_id_type=MESH_ID,
    )


GATHER_SEMS = [pltpu.SemaphoreType.DMA((3,))] * 4 + [pltpu.SemaphoreType.DMA((4,))] * 2


def line_stages(buf, up_send, up_recv, down_send, down_recv, core_send, core_recv):
    b, e, z, core = place()

    def to_core(owner_z):
        block = buf.at[2 * owner_z + core]
        return send(block, block, core_send.at[owner_z], core_recv.at[owner_z], (b, e ^ 1))

    def up(step):
        block = buf.at[jnp.maximum(2 * (z - step), 0) + core]
        return send(block, block, up_send.at[step], up_recv.at[step], (b, jnp.minimum(e + 2, 7)))

    def down(step):
        block = buf.at[jnp.minimum(2 * (z + step), 6) + core]
        return send(
            block, block, down_send.at[step], down_recv.at[step], (b, jnp.maximum(e - 2, 0))
        )

    def start(step):
        @pl.when((z >= step) & (z < 3))
        def _():
            up(step).start()

        @pl.when((z + step <= 3) & (z > 0))
        def _():
            down(step).start()

        if step == 0:
            to_core(z).start()

    def arrive(step):
        @pl.when(z - 1 - step >= 0)
        def _():
            up(step).wait_recv()

        @pl.when(z + 1 + step <= 3)
        def _():
            down(step).wait_recv()

        if step < 2:
            start(step + 1)

        @pl.when(z - 1 - step >= 0)
        def _():
            to_core(z - 1 - step).start()

        @pl.when(z + 1 + step <= 3)
        def _():
            to_core(z + 1 + step).start()

    def finish():
        for owner_z in range(4):
            to_core(owner_z).wait()
        for step in range(3):

            @pl.when((z >= step) & (z < 3))
            def _():
                up(step).wait_send()

            @pl.when((z + step <= 3) & (z > 0))
            def _():
                down(step).wait_send()

    return [lambda: start(0)] + [functools.partial(arrive, i) for i in range(3)] + [finish]


def line_gather(buf, *sems):
    for stage in line_stages(buf, *sems):
        stage()


def scatter_scratch(tokens, width):
    return [pltpu.VMEM((4, tokens, width), LOW)] + [
        pltpu.VMEM((3, tokens, width), LOW) for _ in range(4)
    ]


SCATTER_SEMS = [pltpu.SemaphoreType.DMA((3,))] * 4 + [pltpu.SemaphoreType.DMA((4,))] * 2


def line_sum_stages(
    part,
    from_core,
    up_out,
    up_in,
    down_out,
    down_in,
    up_send,
    up_recv,
    down_send,
    down_recv,
    core_send,
    core_recv,
):
    b, e, z, core = place()

    def to_core(target):
        return send(
            part.at[2 * target + 1 - core],
            from_core.at[target],
            core_send.at[target],
            core_recv.at[target],
            (b, e ^ 1),
        )

    def up(step):
        return send(
            up_out.at[step],
            up_in.at[step],
            up_send.at[step],
            up_recv.at[step],
            (b, jnp.minimum(e + 2, 7)),
        )

    def down(step):
        return send(
            down_out.at[step],
            down_in.at[step],
            down_send.at[step],
            down_recv.at[step],
            (b, jnp.maximum(e - 2, 0)),
        )

    def chip_sum(target):
        return part[2 * target + core].astype(F32) + from_core[target].astype(F32)

    def start():
        for target in (3, 0, 2, 1):
            to_core(target).start()

    def send_up(step):
        up_out[step] = low(chip_sum(3 - step))
        up(step).start()

    def send_down(step):
        down_out[step] = low(chip_sum(step))
        down(step).start()

    def pass_up(step):
        up(step).wait_recv()
        up_out[step] = low(chip_sum(3 - step) + up_in[step].astype(F32))
        up(step).start()

    def pass_down(step):
        down(step).wait_recv()
        down_out[step] = low(chip_sum(step) + down_in[step].astype(F32))
        down(step).start()

    def ends():
        for target in range(4):
            to_core(target).wait()

        @pl.when(z == 0)
        def _():
            for step in range(3):
                send_up(step)

        @pl.when(z == 3)
        def _():
            for step in range(3):
                send_down(step)

    def near():
        @pl.when(z == 1)
        def _():
            pass_up(0)

        @pl.when(z == 2)
        def _():
            pass_down(0)

    def far():
        @pl.when(z == 1)
        def _():
            pass_up(1)
            pass_down(0)

        @pl.when(z == 2)
        def _():
            pass_down(1)
            pass_up(0)

    def finish():
        @pl.when(z == 0)
        def _():
            up_in[0] = jnp.zeros_like(up_in[0])

        @pl.when(z == 3)
        def _():
            down_in[0] = jnp.zeros_like(down_in[0])

        last_up = lax.rem(3 - z, 3)
        last_down = lax.rem(z, 3)

        @pl.when(z > 0)
        def _():
            up(last_up).wait_recv()

        @pl.when(z < 3)
        def _():
            down(last_down).wait_recv()

        total = chip_sum(z) + up_in[last_up].astype(F32) + down_in[last_down].astype(F32)
        for step in range(3):

            @pl.when(z < 3 - step)
            def _():
                up(step).wait_send()

            @pl.when(z > step)
            def _():
                down(step).wait_send()

        return total

    return [start, ends, near, far, finish]


def sum_into(out, *terms):
    if len(out.shape) == 2:

        @pl.loop(0, out.shape[0] // 16)
        def _(i):
            here = pl.ds(pl.multiple_of(i * 16, 16), 16)
            total = terms[0][here, :].astype(F32)
            for term in terms[1:]:
                total = total + term[here, :].astype(F32)
            out[here, :] = total.astype(out.dtype)

    else:
        for i in range(out.shape[0]):
            total = terms[0][i].astype(F32)
            for term in terms[1:]:
                total = total + term[i].astype(F32)
            out[i] = total.astype(out.dtype)


REDUCE_COUNT = 8


def reduce_scratch(half_shape, far=False):
    kept = (4, *half_shape) if far else (1, 8, 128)
    return [
        pltpu.VMEM((6, *half_shape), LOW),
        pltpu.VMEM((2, *half_shape), LOW),
        pltpu.VMEM(kept, LOW if far else F32),
    ] + [pltpu.SemaphoreType.DMA((size,)) for size in (3, 3, 3, 3, 4)]


def reduce_stages(
    block, out, received, sums, kept, x_send, x_recv, y_send, y_recv, local_sem
):
    b, e, _, _ = place()
    x_device, y_device = (b ^ 1, e), (b ^ 2, e)

    def over_x(slot):
        src = (block(b ^ 3, 0), block(b ^ 1, 0), sums.at[1])[slot]
        return send(src, received.at[slot], x_send.at[slot], x_recv.at[slot], x_device)

    def over_y(slot):
        src = (block(b ^ 3, 1), block(b ^ 2, 1), sums.at[0])[slot]
        return send(src, received.at[3 + slot], y_send.at[slot], y_recv.at[slot], y_device)

    far = kept.shape[0] == 4

    def mine(i):
        return (block(b ^ 2, 0), block(b ^ 1, 1), block(b, 0), block(b, 1))[i]

    def keep(i):
        return pltpu.make_async_copy(mine(i), kept.at[i], local_sem.at[i])

    def held(i):
        if not far:
            return mine(i)
        keep(i).wait()
        return kept.at[i]

    def start():
        over_x(0).start()
        over_y(0).start()
        for i in range(4 if far else 0):
            keep(i).start()

    def forward():
        over_x(0).wait_recv()
        over_x(1).start()
        sum_into(sums.at[0], held(0), received.at[0])
        over_y(2).start()
        over_y(0).wait_recv()
        over_y(1).start()
        sum_into(sums.at[1], held(1), received.at[3])
        over_x(2).start()

    def finish():
        for slot in (1, 2):
            over_x(slot).wait_recv()
            over_y(slot).wait_recv()
        sum_into(out(0), held(2), received.at[1], received.at[5])
        sum_into(out(1), held(3), received.at[4], received.at[2])
        for slot in range(3):
            over_x(slot).wait_send()
            over_y(slot).wait_send()

    return start, forward, finish


def reduce_rows(term, out, scratch):
    half_rows = out.shape[0] // 2

    def block(owner, half):
        return term.at[pl.ds((2 * owner + half) * half_rows, half_rows)]

    def out_half(half):
        return out.at[pl.ds(half * half_rows, half_rows)]

    return reduce_stages(block, out_half, *scratch)


def kernel_call(body, outs, args, scratch, collective_id, far_outs=(), far_args=()):
    near = pl.BlockSpec(memory_space=pltpu.VMEM)
    far = pl.BlockSpec(memory_space=pl.ANY)
    return pl.pallas_call(
        body,
        cost_estimate=pl.CostEstimate(flops=COST, bytes_accessed=COST, transcendentals=0),
        out_shape=[jax.ShapeDtypeStruct(shape, dtype) for shape, dtype in outs],
        in_specs=[far if i in far_args else near for i in range(len(args))],
        out_specs=[far if i in far_outs else near for i in range(len(outs))],
        scratch_shapes=scratch,
        compiler_params=pltpu.CompilerParams(
            collective_id=collective_id, has_side_effects=True, vmem_limit_bytes=56 * 2**20
        ),
    )(*args)


SPREAD_SEMS = [pltpu.SemaphoreType.DMA((2,))] + [pltpu.SemaphoreType.DMA((3,))] * 4


def spread_stages(own, whole, local_sem, x_send, x_recv, y_send, y_recv):
    b, e, _, _ = place()
    x_device, y_device = (b ^ 1, e), (b ^ 2, e)

    def over_x(slot):
        src, dst = (
            (own(0), whole(b, 0)),
            (own(1), whole(b, 1)),
            (whole(b ^ 2, 1), whole(b ^ 2, 1)),
        )[slot]
        return send(src, dst, x_send.at[slot], x_recv.at[slot], x_device)

    def over_y(slot):
        src, dst = (
            (own(1), whole(b, 1)),
            (own(0), whole(b, 0)),
            (whole(b ^ 1, 0), whole(b ^ 1, 0)),
        )[slot]
        return send(src, dst, y_send.at[slot], y_recv.at[slot], y_device)

    def keep(half):
        return pltpu.make_async_copy(own(half), whole(b, half), local_sem.at[half])

    def start():
        over_x(0).start()
        over_y(0).start()
        for half in range(2):
            keep(half).start()

    def forward():
        over_x(0).wait_recv()
        over_y(2).start()
        over_x(1).start()
        over_y(0).wait_recv()
        over_x(2).start()
        over_y(1).start()
    def finish():
        for slot in range(3):
            for over in (over_x, over_y):
                if slot > 0:
                    over(slot).wait_recv()
                over(slot).wait_send()
        for half in range(2):
            keep(half).wait()

    return start, forward, finish


def spread_rows(own_ref, whole_ref, rows, sems):
    half_rows = rows // 2

    def own(half):
        return own_ref.at[pl.ds(half * half_rows, half_rows)]

    def whole(owner, half):
        return whole_ref.at[pl.ds(owner * rows + half * half_rows, half_rows)]

    return spread_stages(own, whole, *sems)


def opening_kernel(
    rows, router, first_gain, second_gain, routes, ids, qkv, sup, out_weight, up_weight,
    n1_all, gains, small_all, marks_all, columns_all, out_all, up_all,
    small, marks, columns, w_out, up_own, up_wide, up_sem, *sems,
):
    (
        b_send, b_recv, s_send, s_recv, m_send, m_recv, c_send, c_recv,
        x_send, x_recv, y_send, y_recv, z_send, z_recv, o_send, o_recv, p_send, p_recv,
    ) = sems[:18]
    b, e, z, core = place()
    over = [(b ^ bit, e) for bit in (1, 2, 3)]
    mates = pack_mates()
    up_start, up_forward, up_finish = spread_rows(up_own, up_all, up_own.shape[0], sems[18:23])
    bring = pltpu.make_async_copy(up_weight.at[0], up_wide, up_sem.at[0])
    bring.start()
    greet(over + mates)
    bring.wait()
    up_own[...] = low(up_wide[...])
    up_start()
    rows_w = router.shape[0]
    small[...] = jnp.zeros_like(small)
    small[:rows_w] = router[...]
    small[rows_w : rows_w + 1, : first_gain.shape[1]] = first_gain[...]
    small[rows_w + 1 : rows_w + 2, : second_gain.shape[1]] = second_gain[...]
    chosen = routes[0].astype(F32)
    chosen = jnp.concatenate([chosen, jnp.zeros((128, 128 - TOP), F32)], axis=1).T
    marks[...] = jnp.concatenate(
        [chosen[:TOP], ids[...].astype(F32), jnp.zeros((7 - TOP, 128), F32)], axis=0
    )
    pair = 2 * HEAD
    width = rows.shape[1]
    for i in range(8):
        for part in range(3):
            lanes = slice(part * pair, (part + 1) * pair)
            if i in PAIR_OF:
                start = part * width + PAIR_OF[i] * pair
                columns[i, :, lanes] = low(qkv[:, start : start + pair])
            else:
                columns[i, :, lanes] = jnp.zeros((columns.shape[1], pair), LOW)
        columns[i, :, 3 * pair :] = sup[i]
    w_out[...] = low(out_weight[...])
    small_all[e, b] = small[...]
    marks_all[e] = marks[...]
    columns_all[b, e] = columns[e]
    out_all[b, z, core] = w_out[...]
    first = []
    for i, device in enumerate(over):
        first.append(send(small, small_all.at[e, b], b_send.at[i], b_recv.at[i], device))
        first[-1].start()
    across = []
    for i, device in enumerate(mates):
        across.append(
            send(columns.at[device[1]], columns_all.at[b, e], c_send.at[i], c_recv.at[i], device)
        )
        across[-1].start()
    beyond = []
    for i, device in enumerate(over):
        beyond.append(
            send(w_out, out_all.at[b, z, core], o_send.at[i], o_recv.at[i], device)
        )
        beyond[-1].start()
    rest = []
    for i, device in enumerate(mates):
        rest.append(send(marks, marks_all.at[e], m_send.at[i], m_recv.at[i], device))
        rest[-1].start()
    values = rows[...]
    inv = lax.rsqrt(jnp.mean(values * values, axis=1, keepdims=True) + EPSILON)
    for copy in first:
        copy.wait()
    second = []
    for i, device in enumerate(mates):
        second.append(send(small_all.at[e], small_all.at[e], s_send.at[i], s_recv.at[i], device))
        second[-1].start()
    for copy in second:
        copy.wait()

    piece = width // 32
    lane = lax.broadcasted_iota(jnp.int32, (128, width), 1)
    spread = low(jnp.where(lax.rem(lane, piece) == lax.broadcasted_iota(jnp.int32, (128, width), 0), 1.0, 0.0))
    row = lax.broadcasted_iota(jnp.int32, (32, width), 0)
    owner = lax.rem(row, 4) * 8 + row // 4
    mine = lax.broadcasted_iota(jnp.int32, (32, width), 1) // piece == owner
    for i, index in enumerate((5, 6)):
        pieces = jnp.concatenate([small_all[j, :, index, :] for j in range(8)], axis=0)
        spread_out = dot(low(pieces), spread)
        gains[i : i + 1, :] = jnp.sum(jnp.where(mine, spread_out, 0.0), axis=0, keepdims=True)
    n1_all[e] = low(values * inv * gains[0:1, :])
    stages = line_stages(n1_all, *sems[23:])
    stages[0]()

    def hop(owner, half, sems_out, sems_in, slot, device):
        block = columns_all.at[owner, pl.ds(4 * half, 4)]
        return send(block, block, sems_out.at[slot], sems_in.at[slot], device)

    def over_x(slot):
        owner, half = ((b, 0), (b, 1), (b ^ 2, 1))[slot]
        return hop(owner, half, x_send, x_recv, slot, over[0])

    def over_y(slot):
        owner, half = ((b, 1), (b, 0), (b ^ 1, 0))[slot]
        return hop(owner, half, y_send, y_recv, slot, over[1])

    def out_block(owner_z):
        return out_all.at[:, owner_z, core]

    def out_pair(slot):
        block = out_block(lax.rem(z + 4 - slot, 4))
        return send(block, block, p_send.at[slot], p_recv.at[slot], (b, e ^ 1))

    for copy in across:
        copy.wait()
    over_x(0).start()
    over_y(0).start()
    up_forward()
    over_x(1).start()
    over_y(1).start()
    stages[1]()
    over_x(0).wait_recv()
    over_y(2).start()
    over_y(0).wait_recv()
    over_x(2).start()
    stages[2]()
    for copy in beyond:
        copy.wait()
    along = []
    for i in range(3):
        device = (b, lax.rem(e + 2 * i + 2, 8))
        along.append(send(out_block(z), out_block(z), z_send.at[i], z_recv.at[i], device))
        along[-1].start()
    out_pair(0).start()
    stages[3]()
    for i, copy in enumerate(along):
        copy.wait()
        out_pair(i + 1).start()
    stages[4]()
    for slot in range(3):
        for over_one in (over_x, over_y):
            if slot > 0:
                over_one(slot).wait_recv()
            over_one(slot).wait_send()
    for copy in rest:
        copy.wait()
    for slot in range(4):
        out_pair(slot).wait()
    up_finish()


def opening(rows, router, first_gain, second_gain, routes, ids, qkv, sup, out_weight, up_weight):
    tokens, width = rows.shape
    _, up_rows, up_width = up_weight.shape
    rows_w = out_weight.shape[0]
    wide = 6 * HEAD + sup.shape[2]
    sizes = (3, 3, 7, 7, 7, 7, 7, 7, 3, 3, 3, 3, 3, 3, 3, 3, 4, 4)
    return kernel_call(
        opening_kernel,
        [
            ((8, tokens, width), LOW),
            ((2, width), F32),
            ((8, 4, 8, 128), F32),
            ((8, 8, 128), F32),
            ((4, 8, rows_w, wide), LOW),
            ((4, 4, 2, rows_w, width), LOW),
            ((4 * up_rows, up_width), LOW),
        ],
        (rows, router, first_gain, second_gain, routes, ids, qkv, sup, out_weight, up_weight),
        [
            pltpu.VMEM((8, 128), F32),
            pltpu.VMEM((8, 128), F32),
            pltpu.VMEM((8, rows_w, wide), LOW),
            pltpu.VMEM((rows_w, width), LOW),
            pltpu.VMEM((up_rows, up_width), LOW),
            pltpu.VMEM((up_rows, up_width), F32),
            pltpu.SemaphoreType.DMA((1,)),
        ]
        + [pltpu.SemaphoreType.DMA((size,)) for size in sizes]
        + SPREAD_SEMS
        + GATHER_SEMS,
        0,
        far_outs=(6,),
        far_args=(9,),
    )


def holder(e):
    return (lax.rem(e, 2) == 0) | (e == 3), jnp.where(e == 3, 4, e // 2)


BLOCK = 256


def turned(values, cosine, sine):
    return values * cosine + pltpu.roll(values, HEAD // 2, 1) * sine


def middle_kernel(
    n1, weights, cosine, sine, ids_row, ids_column, w_out, rows, gain, cot, up_weight, down_weight, sdown_weight,
    qkv, logsum, attn, resid, n2_all, cot_all, up_all, down_all, sdown_all,
    attended, up_own, up_wide, down_own, sdown_own, up_sem, a_send, a_recv, *sems,
):
    b, e, z, core = place()
    tokens = rows.shape[0]
    mates = pack_mates()
    count = len(SPREAD_SEMS)
    spreads = [
        spread_rows(up_own, up_all, up_own.shape[0], sems[:count]),
        spread_rows(down_own.at[0], down_all.at[0], down_own.shape[1], sems[count : 2 * count]),
        spread_rows(down_own.at[1], down_all.at[1], down_own.shape[1], sems[2 * count : 3 * count]),
        spread_rows(sdown_own, sdown_all, sdown_own.shape[0], sems[3 * count : 4 * count]),
    ]
    sems = sems[4 * count :]
    cot_stages = line_stages(cot_all, *sems[: len(GATHER_SEMS)])
    n2_stages = line_stages(n2_all, *sems[len(GATHER_SEMS) :])
    cot_all[e] = low(cot[0])
    bring = pltpu.make_async_copy(up_weight.at[1], up_wide, up_sem.at[0])
    bring.start()
    greet([(b ^ 1, e), (b ^ 2, e), *mates])
    bring.wait()
    up_own[...] = low(up_wide[...])
    spreads[0][0]()
    cot_stages[0]()
    down_own[...] = low(down_weight[...])
    short = sdown_own.shape[0] - sdown_weight.shape[0]
    sdown_own[...] = low(
        jnp.concatenate([sdown_weight[...], jnp.zeros((short, cot.shape[2]), F32)], axis=0)
    )
    for start, _, _ in spreads[1:]:
        start()
    holds, pair = holder(e)

    @pl.when(jnp.logical_not(holds))
    def _():
        qkv[...] = jnp.zeros_like(qkv)
        logsum[...] = jnp.zeros_like(logsum)

    @pl.when(holds)
    def _():
        @pl.loop(0, n1.shape[0] // BLOCK)
        def _(i):
            here = pl.ds(pl.multiple_of(i * BLOCK, BLOCK), BLOCK)
            projected = dot(n1[here, :], weights[:, : 6 * HEAD])
            cos_here, sin_here = cosine[here, :], sine[here, :]
            for part in range(6):
                piece = projected[:, part * HEAD : (part + 1) * HEAD]
                if part < 4:
                    piece = turned(piece, cos_here, sin_here)
                qkv[part, here, :] = low(piece)

    cot_stages[1]()
    for head in range(2):

        @pl.when(holds)
        def _():
            for i in range(n1.shape[0] // BLOCK):
                here = pl.ds(i * BLOCK, BLOCK)
                keys = (i + 1) * BLOCK
                scores = dot(qkv[head, here, :], qkv[2 + head, :keys, :], ((1,), (1,)))
                scores = jnp.where(
                    allowed_here(ids_column, ids_row, i, keys), scores * HEAD ** (-0.5), NEGATIVE
                )
                top = jnp.max(scores, axis=1, keepdims=True)
                weight = jnp.exp(scores - top)
                total = jnp.sum(weight, axis=1, keepdims=True)
                out = dot(low(weight / total), qkv[4 + head, :keys, :])
                logsum[head, here, :] = jnp.broadcast_to(top + jnp.log(total), (BLOCK, HEAD))
                for j in range(BLOCK // tokens):
                    attended[i * (BLOCK // tokens) + j, :, head * HEAD : (head + 1) * HEAD] = low(
                        out[j * tokens : (j + 1) * tokens]
                    )

        cot_stages[2 + head]()
        spreads[head][1]()

    def give(i):
        other = lax.rem(e + i, 8)
        return send(
            attended.at[other], attn.at[pair], a_send.at[i - 1], a_recv.at[pair], (b, other)
        )

    @pl.when(holds)
    def _():
        for i in range(1, 8):
            give(i).start()
        attn[pair] = attended[e]

    total = rows[...]
    for source, index in PAIR_OF.items():

        @pl.when(e != source)
        def _():
            block = attn.at[index]
            send(block, block, a_send.at[0], a_recv.at[index], (b, source)).wait_recv()

        size = attn.shape[2]
        total = total + dot(attn[index], w_out[index * size : (index + 1) * size, :])
    resid[...] = total
    inv = lax.rsqrt(jnp.mean(total * total, axis=1, keepdims=True) + EPSILON)
    n2_all[e] = low(total * inv * gain[...])
    n2_stages[0]()
    spreads[2][1]()
    spreads[3][1]()
    for stage in n2_stages[1:]:
        stage()
    cot_stages[4]()

    @pl.when(holds)
    def _():
        for i in range(1, 8):
            give(i).wait_send()

    for _, _, finish in spreads:
        finish()


def allowed_here(ids_column, ids_row, i, keys):
    query = i * BLOCK + lax.broadcasted_iota(jnp.int32, (BLOCK, keys), 0)
    key = lax.broadcasted_iota(jnp.int32, (BLOCK, keys), 1)
    same = ids_column[i * BLOCK : (i + 1) * BLOCK, :] == ids_row[:, :keys]
    return (key <= query) & same


def middle(n1, weights, cosine, sine, ids_row, ids_column, w_out, rows, gain, cot, up_weight, down_weight, sdown_weight):
    tokens, width = rows.shape
    length = n1.shape[0]
    pair = 2 * HEAD
    count = len(PAIR_OF)
    _, up_rows, up_width = up_weight.shape
    down_rows = down_weight.shape[1]
    sdown_rows = -(-sdown_weight.shape[0] // 32) * 32
    return kernel_call(
        middle_kernel,
        [
            ((6, length, HEAD), LOW),
            ((2, length, HEAD), F32),
            ((count, tokens, pair), LOW),
            ((tokens, width), F32),
            ((8, tokens, width), LOW),
            ((8, tokens, width), LOW),
            ((4 * up_rows, up_width), LOW),
            ((2, 4 * down_rows, width), LOW),
            ((4 * sdown_rows, width), LOW),
        ],
        (n1, weights, cosine, sine, ids_row, ids_column, w_out, rows, gain, cot, up_weight, down_weight, sdown_weight),
        [
            pltpu.VMEM((8, tokens, pair), LOW),
            pltpu.VMEM((up_rows, up_width), LOW),
            pltpu.VMEM((up_rows, up_width), F32),
            pltpu.VMEM((2, down_rows, width), LOW),
            pltpu.VMEM((sdown_rows, width), LOW),
            pltpu.SemaphoreType.DMA((1,)),
            pltpu.SemaphoreType.DMA((7,)),
            pltpu.SemaphoreType.DMA((count,)),
        ]
        + SPREAD_SEMS * 4
        + GATHER_SEMS * 2,
        1,
        far_outs=(6, 7, 8),
        far_args=(10,),
    )


def experts_kernel(
    n2, cot, w_sup, w_sdown, gates, up_first, up_second, w_down,
    out_part, row_sum, sdown_term, sup_term, up_term_first, up_term_second, down_term_first, down_term_second,
    part, up_w, down_w, hid, dpre, hid_shared, dpre_shared, load_sem, store_sem, *scratch,
):
    e = lax.axis_index("expert")
    greet_line()
    stages = line_sum_stages(part, *scratch)
    tokens = part.shape[1]
    length, width = n2.shape
    hidden = down_w.shape[1]
    pad = w_sdown.shape[0]
    loads = []
    for k, up_ref in enumerate((up_first, up_second)):
        loads.append(pltpu.make_async_copy(up_ref, up_w.at[k], load_sem.at[2 * k]))
        loads.append(pltpu.make_async_copy(w_down.at[k], down_w.at[k], load_sem.at[2 * k + 1]))
    for copy in loads:
        copy.start()
    for copy in loads:
        copy.wait()
    lane = lax.broadcasted_iota(jnp.int32, (ROWS, 128), 1)

    @pl.loop(0, length // ROWS)
    def _(i):
        here = pl.ds(pl.multiple_of(i * ROWS, ROWS), ROWS)
        x = n2[here, :]
        c = cot[here, :]
        marks = jnp.zeros((ROWS, 128), F32)
        gate_part = dot(x, w_sup[:, :pad])
        up_part = dot(x, w_sup[:, pad:])
        back = dot(c, w_sdown[...], ((1,), (1,)))
        silu, slope = silu_parts(gate_part, up_part)
        hid_shared[here, :] = low(silu * up_part)
        dpre_shared[here, :pad] = low(back * slope)
        dpre_shared[here, pad:] = low(back * silu)
        out = dot(hid_shared[here, :], w_sdown[...])
        drow = dot(dpre_shared[here, :], w_sup[...], ((1,), (1,)))
        for k in range(2):
            gate = gates[here, k : k + 1]
            gate_part = dot(x, up_w[k, :, :hidden])
            up_part = dot(x, up_w[k, :, hidden:])
            back = dot(c, down_w[k], ((1,), (1,)))
            silu, slope = silu_parts(gate_part, up_part)
            value = silu * up_part
            dgate = jnp.sum(back * value, axis=1, keepdims=True)
            hid[k, here, :] = low(value * gate)
            back = back * gate
            dpre[k, here, :hidden] = low(back * slope)
            dpre[k, here, hidden:] = low(back * silu)
            out = out + dot(hid[k, here, :], down_w[k])
            drow = drow + dot(dpre[k, here, :], up_w[k], ((1,), (1,)))
            high = low(dgate).astype(F32)
            marks = jnp.where(lane == 2 * e + k, high, marks)
            marks = jnp.where(lane == 2 * e + k + 16, dgate - high, marks)
        out_part[here, :] = low(out)
        for j in range(ROWS // tokens):
            rows = slice(j * tokens, (j + 1) * tokens)
            part[i * (ROWS // tokens) + j, :, :width] = low(drow[rows])
            part[i * (ROWS // tokens) + j, :, width:] = low(marks[rows])

    stages[0]()
    stores = []
    for k, (up_ref, down_ref) in enumerate(
        ((up_term_first, down_term_first), (up_term_second, down_term_second))
    ):

        if k == 0:
            stages[1]()

        @pl.loop(0, width // COLS)
        def _(i):
            here = pl.ds(pl.multiple_of(i * COLS, COLS), COLS)
            up_w[k, here, :] = low(dot(n2[:, here], dpre[k], ((0,), (0,))))

        if k == 0:
            stages[2]()

        stores.append(pltpu.make_async_copy(up_w.at[k], up_ref, store_sem.at[2 * k]))
        stores[-1].start()

        @pl.loop(0, hidden // 128)
        def _(i):
            here = pl.ds(pl.multiple_of(i * 128, 128), 128)
            down_w[k, here, :] = low(dot(hid[k, :, here], cot[...], ((0,), (0,))))

        stores.append(pltpu.make_async_copy(down_w.at[k], down_ref, store_sem.at[2 * k + 1]))
        stores[-1].start()
        if k == 0:
            stages[3]()

    sdown_term[...] = low(dot(hid_shared[...], cot[...], ((0,), (0,))))

    @pl.loop(0, width // COLS)
    def _(i):
        here = pl.ds(pl.multiple_of(i * COLS, COLS), COLS)
        sup_term[here, :] = low(dot(n2[:, here], dpre_shared[...], ((0,), (0,))))

    row_sum[...] = stages[4]()
    for copy in stores:
        copy.wait()


ROWS = 256
COLS = 256


def experts_phase(n2, cot, w_sup, w_sdown, gates, up_first, up_second, w_down):
    length, width = n2.shape
    _, hidden, _ = w_down.shape
    pad = w_sdown.shape[0]
    tokens = length // 8
    wide = width + 128
    return kernel_call(
        experts_kernel,
        [
            ((length, width), LOW),
            ((tokens, wide), F32),
            ((pad, width), LOW),
            ((width, 2 * pad), LOW),
            (up_first.shape, LOW),
            (up_first.shape, LOW),
            ((hidden, width), LOW),
            ((hidden, width), LOW),
        ],
        (n2, cot, w_sup, w_sdown, gates, up_first, up_second, w_down),
        [
            pltpu.VMEM((8, tokens, wide), LOW),
            pltpu.VMEM((2, *up_first.shape), LOW),
            pltpu.VMEM(w_down.shape, LOW),
            pltpu.VMEM((2, length, hidden), LOW),
            pltpu.VMEM((2, length, 2 * hidden), LOW),
            pltpu.VMEM((length, pad), LOW),
            pltpu.VMEM((length, 2 * pad), LOW),
            pltpu.SemaphoreType.DMA((4,)),
            pltpu.SemaphoreType.DMA((4,)),
        ]
        + scatter_scratch(tokens, wide)
        + SCATTER_SEMS,
        4,
        far_outs=(4, 5, 6, 7),
        far_args=(5, 6, 7),
    )


def turn_kernel(
    row_sum, out_part, upstream, gates, w_router, resid, gain, w_out, up_term, down_term,
    dresid, dlogits, gain_term, darrived, output_rows, up_grad, down_grad,
    dattn, a_send, a_recv, *scratch,
):
    b, e, z, core = place()
    greet([(b ^ 1, e), (b ^ 2, e), *pack_mates()])
    reduces = [
        reduce_rows(up_term, up_grad, scratch[:REDUCE_COUNT]),
        reduce_rows(down_term, down_grad, scratch[REDUCE_COUNT : 2 * REDUCE_COUNT]),
    ]
    scratch = scratch[2 * REDUCE_COUNT :]
    out_stages = line_sum_stages(out_part, *scratch)
    out_stages[0]()
    for start, _, _ in reduces:
        start()
    holds, pair = holder(e)
    total = row_sum[...]
    width = upstream.shape[1]
    experts = gates.shape[1]
    dgate = total[:, width : width + experts] + total[:, width + experts : width + 2 * experts]
    own = gates[...]
    dlog = low(own * (dgate - jnp.sum(own * dgate, axis=1, keepdims=True)))
    dlogits[...] = dlog
    dn2 = total[:, :width] + dot(dlog, w_router[...])
    rows = resid[...]
    inv = lax.rsqrt(jnp.mean(rows * rows, axis=1, keepdims=True) + EPSILON)
    xhat = rows * inv
    gain_term[...] = jnp.sum(dn2 * xhat, axis=0, keepdims=True)
    scaled = dn2 * gain[...]
    grad = upstream[...] + inv * (scaled - xhat * jnp.mean(scaled * xhat, axis=1, keepdims=True))
    dresid[...] = grad
    back = low(dot(low(grad), w_out[...], ((1,), (1,))))
    size = dattn.shape[2]

    def give(source, index):
        return send(dattn.at[index], darrived.at[e], a_send.at[index], a_recv.at[e], (b, source))

    for source, index in PAIR_OF.items():
        dattn[index] = back[:, index * size : (index + 1) * size]

        @pl.when(e != source)
        def _():
            give(source, index).start()

    out_stages[1]()
    reduces[0][1]()
    out_stages[2]()
    reduces[1][1]()
    out_stages[3]()

    @pl.when(jnp.logical_not(holds))
    def _():
        darrived[...] = jnp.zeros_like(darrived)

    @pl.when(holds)
    def _():
        darrived[e] = dattn[pair]
        for i in range(1, 8):
            other = lax.rem(e + i, 8)
            block = darrived.at[other]
            send(block, block, a_send.at[0], a_recv.at[other], (b, other)).wait_recv()

    output_rows[...] = resid[...] + out_stages[4]()
    for _, _, finish in reduces:
        finish()
    for source, index in PAIR_OF.items():

        @pl.when(e != source)
        def _():
            give(source, index).wait_send()


def turn(row_sum, out_part, upstream, gates, w_router, resid, gain, w_out, up_term, down_term):
    tokens, width = upstream.shape
    pair = 2 * HEAD
    count = len(PAIR_OF)
    up_rows, down_rows = up_term.shape[0] // 4, down_term.shape[0] // 4
    return kernel_call(
        turn_kernel,
        [
            ((tokens, width), F32),
            (gates.shape, LOW),
            ((1, width), F32),
            ((8, tokens, pair), LOW),
            ((tokens, width), F32),
            ((up_rows, up_term.shape[1]), F32),
            ((down_rows, down_term.shape[1]), F32),
        ],
        (row_sum, out_part, upstream, gates, w_router, resid, gain, w_out, up_term, down_term),
        [
            pltpu.VMEM((count, tokens, pair), LOW),
            pltpu.SemaphoreType.DMA((count,)),
            pltpu.SemaphoreType.DMA((8,)),
        ]
        + reduce_scratch((up_rows // 2, up_term.shape[1]), True)
        + reduce_scratch((down_rows // 2, down_term.shape[1]), True)
        + scatter_scratch(tokens, width)
        + SCATTER_SEMS,
        2,
        far_args=(8, 9),
    )


PARTNERS = ((0, 1), (1, 0), (2, 0), (0, 2), (0, 4))


def closing_kernel(
    dattn, qkv, logsum, n1, weights, cosine, sine, ids_row, ids_column, rows, gain, dresid,
    up_term, down_term, sdown_term, sup_term, out_term, small,
    input_grad, columns, out_grad, up_grad, down_grad, sdown_grad, small_sum,
    dkey, dvalue, dprojected, part, column_term, column_sum, column_low,
    out_near, out_sum, out_low, out_half, out_got, small_got, small_step,
    n_send, n_recv, o_send, o_recv, c_send, c_recv, s_send, s_recv, *scratch,
):
    b, e, z, core = place()
    length = n1.shape[0]
    tokens = rows.shape[0]
    mates = pack_mates()
    greet([(b ^ 1, e), (b ^ 2, e), *mates])
    holds, pair = holder(e)

    def cut():
        nonlocal scratch
        mine, scratch = scratch[:REDUCE_COUNT], scratch[REDUCE_COUNT:]
        return mine

    up = reduce_rows(up_term, up_grad, cut())
    down = reduce_rows(down_term, down_grad, cut())
    sdown = reduce_rows(sdown_term, sdown_grad, cut())
    column = reduce_rows(column_term, column_sum, cut())
    out = reduce_stages(
        lambda owner, half: out_sum.at[owner, pl.ds(2 * half, 2)],
        lambda half: out_half.at[pl.ds(2 * half, 2)],
        *cut(),
    )
    stages = line_sum_stages(part, *scratch)

    def partner(i):
        batch_bit, expert_bit = PARTNERS[i]
        src = small if i == 0 else small_step.at[i - 1]
        device = (b ^ batch_bit, e ^ expert_bit)
        return send(src, small_got.at[i], s_send.at[i], s_recv.at[i], device)

    def small_round(i):
        partner(i).wait_recv()
        before = small[...] if i == 0 else small_step[i - 1]
        if i < len(PARTNERS) - 1:
            small_step[i] = before + small_got[i]
            partner(i + 1).start()
        else:
            small_sum[...] = before + small_got[i]

    near = send(
        out_term.at[:, :, 1 - core], out_near, n_send.at[0], n_recv.at[0], (b, e ^ 1)
    )
    near.start()
    own = pltpu.make_async_copy(out_term.at[:, :, core], out_sum, n_send.at[1])
    own.start()
    partner(0).start()
    up[0]()

    def attend(head):
        dkey[...] = jnp.zeros_like(dkey)
        dvalue[...] = jnp.zeros_like(dvalue)
        lanes = pl.ds(head * HEAD, HEAD)
        for i in range(length // BLOCK):
            here = pl.ds(i * BLOCK, BLOCK)
            keys = (i + 1) * BLOCK
            count = BLOCK // tokens
            back = jnp.concatenate(
                [dattn[count * i + j, :, lanes] for j in range(count)], axis=0
            )
            query = qkv[head, here, :]
            scores = dot(query, qkv[2 + head, :keys, :], ((1,), (1,))) * HEAD ** (-0.5)
            weight = jnp.where(
                allowed_here(ids_column, ids_row, i, keys),
                jnp.exp(scores - logsum[head, here, 0:1]),
                0.0,
            )
            dprob = dot(back, qkv[4 + head, :keys, :], ((1,), (1,)))
            delta = jnp.sum(weight * dprob, axis=1, keepdims=True)
            dscore = low(weight * (dprob - delta))
            dquery = dot(dscore, qkv[2 + head, :keys, :]) * HEAD ** (-0.5)
            dkey[:keys, :] += dot(dscore, query, ((0,), (0,)))
            dvalue[:keys, :] += dot(low(weight), back, ((0,), (0,)))
            dprojected[here, lanes] = low(turned(dquery, cosine[here, :], -sine[here, :]))
        dprojected[:, (2 + head) * HEAD : (3 + head) * HEAD] = low(
            turned(dkey[...] * HEAD ** (-0.5), cosine[...], -sine[...])
        )
        dprojected[:, (4 + head) * HEAD : (5 + head) * HEAD] = low(dvalue[...])

    @pl.when(holds)
    def _():
        attend(0)

    near.wait()
    own.wait()
    for owner in range(4):
        for owner_z in range(4):
            out_sum[owner, owner_z] = low(
                out_sum[owner, owner_z].astype(F32) + out_near[owner, owner_z].astype(F32)
            )
    small_round(0)
    up[1]()

    @pl.when(holds)
    def _():
        attend(1)
        for i in range(8):
            part[i] = low(
                dot(
                    dprojected[i * tokens : (i + 1) * tokens, :],
                    weights[:, : 6 * HEAD],
                    ((1,), (1,)),
                )
            )

    @pl.when(jnp.logical_not(holds))
    def _():
        part[...] = jnp.zeros_like(part)

    stages[0]()
    column_term[:, 6 * HEAD :] = sup_term[...]

    @pl.when(holds)
    def _():
        for i in range(n1.shape[1] // BLOCK):
            here = pl.ds(i * BLOCK, BLOCK)
            column_term[here, : 6 * HEAD] = low(dot(n1[:, here], dprojected[...], ((0,), (0,))))

    @pl.when(jnp.logical_not(holds))
    def _():
        column_term[:, : 6 * HEAD] = jnp.zeros((n1.shape[1], 6 * HEAD), LOW)

    column[0]()
    stages[1]()
    out[0]()
    small_round(1)
    stages[2]()
    column[1]()
    down[0]()
    sdown[0]()
    stages[3]()
    small_round(2)
    out[1]()
    small_round(3)
    values = rows[...]
    inv = lax.rsqrt(jnp.mean(values * values, axis=1, keepdims=True) + EPSILON)
    xhat = values * inv
    scaled = stages[4]() * gain[...]
    input_grad[...] = dresid[...] + inv * (
        scaled - xhat * jnp.mean(scaled * xhat, axis=1, keepdims=True)
    )
    column[2]()
    piece = column_low.shape[1]
    for i in range(0, 8, 2):
        two = column_sum[i * piece : (i + 2) * piece, :].astype(F32)
        column_low[i] = low(two[:piece])
        column_low[i + 1] = low(two[piece:])
    columns[e] = column_low[e]
    across = []
    for i, device in enumerate(mates):
        across.append(
            send(column_low.at[device[1]], columns.at[e], c_send.at[i], c_recv.at[i], device)
        )
        across[-1].start()
    down[1]()
    sdown[1]()
    small_round(4)
    for i in range(len(PARTNERS)):
        partner(i).wait_send()
    out[2]()
    for owner_z in range(4):
        out_low[owner_z] = low(out_half[owner_z])
    along = []
    for i in range(3):
        device = (b, lax.rem(e + 2 * i + 2, 8))
        along.append(
            send(
                out_low.at[device[1] // 2], out_got.at[i], o_send.at[i], o_recv.at[i], device
            )
        )
        along[-1].start()
    up[2]()
    for copy in along:
        copy.wait()
    out_grad[...] = (
        out_half[z]
        + out_got[0].astype(F32)
        + out_got[1].astype(F32)
        + out_got[2].astype(F32)
    )
    down[2]()
    sdown[2]()
    for copy in across:
        copy.wait()


def closing(
    dattn, qkv, logsum, n1, weights, cosine, sine, ids_row, ids_column, rows, gain, dresid,
    up_term, down_term, sdown_term, sup_term, out_term, small,
):
    tokens, width = rows.shape
    length = n1.shape[0]
    rows_w = out_term.shape[3]
    wide = weights.shape[1]
    up_rows, down_rows, sdown_rows = (
        term.shape[0] // 4 for term in (up_term, down_term, sdown_term)
    )
    dma = pltpu.SemaphoreType.DMA
    return kernel_call(
        closing_kernel,
        [
            ((tokens, width), F32),
            ((8, rows_w, wide), LOW),
            ((rows_w, width), F32),
            ((up_rows, up_term.shape[1]), F32),
            ((down_rows, width), F32),
            ((sdown_rows, width), F32),
            (small.shape, F32),
        ],
        (
            dattn, qkv, logsum, n1, weights, cosine, sine, ids_row, ids_column, rows, gain, dresid,
            up_term, down_term, sdown_term, sup_term, out_term, small,
        ),
        [
            pltpu.VMEM((length, HEAD), F32),
            pltpu.VMEM((length, HEAD), F32),
            pltpu.VMEM((length, 6 * HEAD), LOW),
            pltpu.VMEM((8, tokens, width), LOW),
            pltpu.VMEM((width, wide), LOW),
            pltpu.VMEM((width // 4, wide), LOW),
            pltpu.VMEM((8, rows_w, wide), LOW),
            pltpu.VMEM((4, 4, rows_w, width), LOW),
            pltpu.VMEM((4, 4, rows_w, width), LOW),
            pltpu.VMEM((4, rows_w, width), LOW),
            pltpu.VMEM((4, rows_w, width), F32),
            pltpu.VMEM((3, rows_w, width), LOW),
            pltpu.VMEM((5, *small.shape), F32),
            pltpu.VMEM((4, *small.shape), F32),
            dma((2,)), dma((1,)), dma((3,)), dma((3,)), dma((7,)), dma((7,)), dma((5,)), dma((5,)),
        ]
        + reduce_scratch((up_rows // 2, up_term.shape[1]), True)
        + reduce_scratch((down_rows // 2, width), True)
        + reduce_scratch((sdown_rows // 2, width))
        + reduce_scratch((width // 8, wide))
        + reduce_scratch((2, rows_w, width))
        + scatter_scratch(tokens, width)
        + SCATTER_SEMS,
        3,
        far_args=(12, 13, 16),
    )


def silu_parts(gate, up):
    sigma = jax.nn.sigmoid(gate)
    return gate * sigma, up * sigma * (1.0 + gate * (1.0 - sigma))


def rotary_angles(length):
    half = HEAD // 2
    frequency = np.float32(10000.0) ** (-np.arange(half, dtype=np.float32) / np.float32(half))
    return np.arange(length, dtype=np.float32)[:, None] * frequency[None, :]


def pack_device(
    block_input,
    seq_ids,
    routes,
    cotangent,
    qkv_weight,
    out_weight,
    shared_up,
    shared_down,
    router_weight,
    gain_attn,
    gain_ffn,
    expert_up,
    expert_down,
):
    b = lax.axis_index("batch")
    e = lax.axis_index("expert")
    rows_in = block_input[0]
    upstream = cotangent[0]
    tokens, width = rows_in.shape
    length = tokens * 8
    rows_w = qkv_weight.shape[0]
    pair = 2 * HEAD
    pairs_of_heads = width // pair
    hidden = expert_up.shape[2] // 2
    experts = expert_up.shape[0] * 8
    s_rows = shared_down.shape[0]
    s_each = -(-s_rows // 32) * 32
    s_pad = 4 * s_each

    sup_low = low(shared_up).reshape(rows_w, 2, 4, 8, s_rows)
    sup_low = jnp.pad(sup_low, ((0, 0),) * 4 + ((0, s_each - s_rows),)).transpose(3, 0, 1, 2, 4)
    n1_all, gains, small, marks, columns, w_out, up_first = opening(
        rows_in,
        router_weight.reshape(-1, 128),
        gain_attn[None],
        gain_ffn[None],
        routes,
        seq_ids,
        qkv_weight,
        sup_low.reshape(8, rows_w, 2 * s_pad),
        out_weight,
        expert_up,
    )
    n1_all = n1_all.reshape(length, width)
    columns = columns.reshape(width, 3 * pair + 2 * s_pad)
    w_out = w_out.reshape(width, width)
    router_rows = rows_w * experts // 128
    w_router = low(small[:, :, :router_rows].transpose(1, 0, 2, 3).reshape(width, experts))
    gain_first = gains[0:1]
    gain_second = gains[1:2]
    marks = marks.astype(jnp.int32).transpose(0, 2, 1).reshape(length, 8)
    route_all = marks[:, :TOP]
    ids_all = marks[:, TOP]
    positions = jnp.arange(length, dtype=jnp.int32)
    ids_row = ids_all[None, :]
    ids_column = ids_all[:, None]
    angle = rotary_angles(length)
    cosine = np.concatenate([np.cos(angle)] * 2, axis=1)
    sine = np.concatenate([-np.sin(angle), np.sin(angle)], axis=1)
    qkv, logsum, attn, resid, n2_all, cot_all, up_second, down_low, w_sdown = middle(
        n1_all,
        columns,
        jnp.asarray(cosine),
        jnp.asarray(sine),
        ids_row,
        ids_column,
        w_out,
        rows_in,
        gain_second,
        cotangent,
        expert_up,
        expert_down,
        shared_down,
    )
    attn = attn.transpose(1, 0, 2).reshape(tokens, width)
    cot_all = cot_all.reshape(length, width)

    n2 = lax.dynamic_index_in_dim(n2_all, e, 0, False)
    n2_all = n2_all.reshape(length, width)
    logits = dot(n2_all, w_router)
    hot = route_all[:, :, None] == jnp.arange(experts, dtype=jnp.int32)[None, None, :]
    routed_to = jnp.any(hot, axis=1)
    logits = jnp.where(routed_to, logits, NEGATIVE)
    gates = jnp.where(routed_to, jnp.exp(logits - jnp.max(logits, axis=1, keepdims=True)), 0.0)
    gates = gates / jnp.sum(gates, axis=1, keepdims=True)
    mine = lax.dynamic_slice_in_dim(gates, 2 * e, 2, 1)

    output_part, row_sum, sdown_term, sup_term, *terms = experts_phase(
        n2_all,
        cot_all,
        columns[:, 3 * pair :],
        w_sdown,
        mine,
        up_first,
        up_second,
        down_low,
    )
    up_terms, down_terms = terms[:2], terms[2:]
    own_gates = lax.dynamic_slice_in_dim(gates, e * tokens, tokens, 0)
    dresid, dlogits, gain_ffn_term, dattn, output_rows, up_grad_first, down_grad_first = turn(
        row_sum,
        output_part.reshape(8, tokens, width),
        upstream,
        own_gates,
        w_router.T,
        resid,
        gain_second,
        w_out,
        up_terms[0],
        down_terms[0],
    )
    router_term = dot(dlogits, n2, ((0,), (0,)))
    small = jnp.concatenate(
        [router_term, gain_ffn_term, jnp.zeros((7, width), F32)], axis=0
    )
    out_term = low(dot(attn, low(dresid), ((0,), (0,)))).reshape(4, 4, 2, rows_w, width)
    input_grad, columns, out_grad, up_grad_second, down_grad_second, sdown_grad, small = closing(
        dattn,
        qkv,
        logsum,
        n1_all,
        columns,
        jnp.asarray(cosine),
        jnp.asarray(sine),
        ids_row,
        ids_column,
        rows_in,
        gain_first,
        dresid,
        up_terms[1],
        down_terms[1],
        sdown_term,
        sup_term,
        out_term,
        small,
    )
    expert_up_grad = jnp.stack([up_grad_first, up_grad_second])
    expert_down_grad = jnp.stack([down_grad_first, down_grad_second])
    shared_down_grad = sdown_grad[:s_rows]
    small = lax.dynamic_slice_in_dim(small, (b * 8 + e) * rows_w, rows_w, 1)
    columns = columns.astype(F32)
    qkv_grad = jnp.stack([columns[i, :, : 3 * pair] for i in PAIR_OF])
    qkv_grad = qkv_grad.reshape(pairs_of_heads, rows_w, 3, pair).transpose(1, 2, 0, 3)
    qkv_grad = qkv_grad.reshape(rows_w, 3 * width)
    sup_grad = columns[:, :, 3 * pair :].reshape(8, rows_w, 2, 4, s_each)[..., :s_rows]
    sup_grad = sup_grad.transpose(1, 2, 3, 0, 4)
    sup_grad = sup_grad.reshape(rows_w, shared_up.shape[1])
    own_first = low(gain_attn).astype(F32)
    gain_attn_grad = jnp.sum(low(qkv_weight).astype(F32) * qkv_grad, axis=1) / own_first
    return (
        output_rows[None],
        input_grad[None],
        qkv_grad,
        out_grad,
        sup_grad,
        shared_down_grad,
        small[:experts].T,
        gain_attn_grad,
        small[experts],
        expert_up_grad,
        expert_down_grad,
    )


def solution(mesh):
    in_specs = (
        P("batch", "expert", None),
        P("batch", "expert"),
        P("batch", "expert", None),
        P("batch", "expert", None),
        P(("batch", "expert"), None),
        P(("batch", "expert"), None),
        P(("batch", "expert"), None),
        P(("batch", "expert"), None),
        P(("batch", "expert"), None),
        P(("batch", "expert")),
        P(("batch", "expert")),
        P("expert", "batch", None),
        P("expert", "batch", None),
    )
    out_specs = (
        P("batch", "expert", None),
        P("batch", "expert", None),
        P(("batch", "expert"), None),
        P(("batch", "expert"), None),
        P(("batch", "expert"), None),
        P(("batch", "expert"), None),
        P(("batch", "expert"), None),
        P(("batch", "expert")),
        P(("batch", "expert")),
        P("expert", "batch", None),
        P("expert", "batch", None),
    )
    sizes = dict(mesh.shape)
    body = pack_device if sizes == {"batch": 4, "expert": 8} else per_device
    return jax.shard_map(
        body, mesh=mesh, in_specs=in_specs, out_specs=out_specs, check_vma=False
    )
```

```python
import functools

import jax
import jax.numpy as jnp
import numpy as np
from jax import lax
from jax.experimental import pallas as pl
from jax.experimental.pallas import tpu as pltpu
from jax.sharding import PartitionSpec as P

HEAD = 128
TOP = 6


EPSILON = 1e-06
NEGATIVE = -1e30


def rotate(values, positions, sign):
    half = values.shape[-1] // 2
    frequency = 10000.0 ** (-jnp.arange(half, dtype=jnp.float32) / half)
    angle = positions.astype(jnp.float32)[:, None] * frequency[None, :]
    cosine = jnp.cos(angle)[:, None, :]
    sine = sign * jnp.sin(angle)[:, None, :]
    first = values[..., :half]
    second = values[..., half:]
    return jnp.concatenate(
        [first * cosine - second * sine, first * sine + second * cosine], axis=-1
    )


def swiglu(pre, hidden_width):
    return jax.nn.silu(pre[..., :hidden_width]) * pre[..., hidden_width:]


def swiglu_back(pre, dhidden, hidden_width):
    gate_part = pre[..., :hidden_width]
    up_part = pre[..., hidden_width:]
    sigma = jax.nn.sigmoid(gate_part)
    dgate = dhidden * up_part * sigma * (1.0 + gate_part * (1.0 - sigma))
    dupper = dhidden * gate_part * sigma
    return jnp.concatenate([dgate, dupper], axis=-1)


def norm_back(dnormed, normed, inv_rms, gain):
    dscaled = dnormed * gain
    dinputs = inv_rms * (dscaled - normed * jnp.mean(dscaled * normed, axis=1, keepdims=True))
    return (dinputs, jnp.sum(dnormed * normed, axis=0))


def per_device(
    block_input,
    seq_ids,
    routes,
    cotangent,
    qkv_weight,
    out_weight,
    shared_up,
    shared_down,
    router_weight,
    gain_attn,
    gain_ffn,
    expert_up,
    expert_down,
):
    dense = (
        lax.all_gather(qkv_weight.astype(jnp.bfloat16), ("batch", "expert"), axis=0, tiled=True),
        lax.all_gather(out_weight.astype(jnp.bfloat16), ("batch", "expert"), axis=0, tiled=True),
        lax.all_gather(shared_up.astype(jnp.bfloat16), ("batch", "expert"), axis=0, tiled=True),
        lax.all_gather(shared_down.astype(jnp.bfloat16), ("batch", "expert"), axis=0, tiled=True),
        lax.all_gather(router_weight.astype(jnp.bfloat16), ("batch", "expert"), axis=0, tiled=True),
        lax.all_gather(gain_attn.astype(jnp.bfloat16), ("batch", "expert"), axis=0, tiled=True),
        lax.all_gather(gain_ffn.astype(jnp.bfloat16), ("batch", "expert"), axis=0, tiled=True),
    )
    full_qkv, full_out, full_sup, full_sdown, full_router, low_gain_a, low_gain_f = dense
    gain_first = low_gain_a.astype(jnp.float32)
    gain_second = low_gain_f.astype(jnp.float32)
    experts_up, experts_down = (
        lax.all_gather(expert_up.astype(jnp.bfloat16), "batch", axis=1, tiled=True),
        lax.all_gather(expert_down.astype(jnp.bfloat16), "batch", axis=1, tiled=True),
    )
    rows_in = block_input[0]
    ids_local = seq_ids[0]
    route_local = routes[0]
    upstream = cotangent[0]
    tokens_dev = rows_in.shape[0]
    model_width = rows_in.shape[1]
    heads_count = model_width // HEAD
    groups = lax.axis_size("expert")
    local_experts = experts_up.shape[0]
    experts_all = local_experts * groups
    shared_width = full_sdown.shape[0]
    hidden_width = experts_down.shape[1]
    capacity = max(2, tokens_dev * TOP * 3 // (experts_all * 2))
    score_scale = HEAD ** (-0.5)
    positions = lax.axis_index("expert") * tokens_dev + jnp.arange(tokens_dev, dtype=jnp.int32)
    key_ids = lax.all_gather(ids_local, "expert", axis=0, tiled=True)
    inv_first = lax.rsqrt(jnp.mean(rows_in * rows_in, axis=1, keepdims=True) + EPSILON)
    normed_first = rows_in * inv_first
    input_low = (normed_first * gain_first).astype(jnp.bfloat16)
    projected = jnp.dot(input_low, full_qkv, preferred_element_type=jnp.float32)
    queries = rotate(
        projected[:, :model_width].reshape(tokens_dev, heads_count, HEAD), positions, 1.0
    ).astype(jnp.bfloat16)
    keys = rotate(
        projected[:, model_width : 2 * model_width].reshape(tokens_dev, heads_count, HEAD),
        positions,
        1.0,
    ).astype(jnp.bfloat16)
    values = (
        projected[:, 2 * model_width :].reshape(tokens_dev, heads_count, HEAD).astype(jnp.bfloat16)
    )

    def key_mask(key_count):
        key_pos = jnp.arange(key_count, dtype=jnp.int32)
        return (key_pos[None, :] <= positions[:, None]) & (key_ids[None, :] == ids_local[:, None])

    run_max = jnp.full((heads_count, tokens_dev), NEGATIVE, jnp.float32)
    key_piece = lax.all_gather(keys, "expert", axis=0, tiled=True)
    value_piece = lax.all_gather(values, "expert", axis=0, tiled=True)
    allowed = key_mask(key_piece.shape[0])[None]
    scores = (
        jnp.einsum("qhd,khd->hqk", queries, key_piece, preferred_element_type=jnp.float32)
        * score_scale
    )
    scores = jnp.where(allowed, scores, NEGATIVE)
    new_max = jnp.maximum(run_max, jnp.max(scores, axis=2))
    weights = jnp.where(allowed, jnp.exp(scores - new_max[:, :, None]), 0.0)
    run_sum = jnp.sum(weights, axis=2)
    update = jnp.einsum(
        "hqk,khd->qhd",
        weights.astype(jnp.bfloat16),
        value_piece,
        preferred_element_type=jnp.float32,
    )
    run_acc = update
    run_max, run_sum, run_acc = (new_max, run_sum, run_acc)
    attn_full = run_acc / jnp.transpose(run_sum)[:, :, None]
    logsum = run_max + jnp.log(run_sum)
    attn_low = attn_full.reshape(tokens_dev, model_width).astype(jnp.bfloat16)
    resid = rows_in + jnp.dot(attn_low, full_out, preferred_element_type=jnp.float32)
    inv_second = lax.rsqrt(jnp.mean(resid * resid, axis=1, keepdims=True) + EPSILON)
    normed_second = resid * inv_second
    ffn_low = (normed_second * gain_second).astype(jnp.bfloat16)
    logits = jnp.dot(ffn_low, full_router, preferred_element_type=jnp.float32)
    probs = jax.nn.softmax(logits, axis=1)
    route_hot = route_local[:, :, None] == jnp.arange(experts_all, dtype=jnp.int32)[None, None, :]
    chosen = jnp.sum(jnp.where(route_hot, probs[:, None, :], 0.0), axis=2)
    chosen_sum = jnp.sum(chosen, axis=1, keepdims=True)
    gates = chosen / chosen_sum
    shared_pre = jnp.dot(ffn_low, full_sup, preferred_element_type=jnp.float32)
    shared_hidden = swiglu(shared_pre, shared_width).astype(jnp.bfloat16)
    shared_result = jnp.dot(shared_hidden, full_sdown, preferred_element_type=jnp.float32)
    flat_route = route_local.reshape(-1)
    flat_hot = (flat_route[:, None] == jnp.arange(experts_all, dtype=jnp.int32)[None, :]).astype(
        jnp.bfloat16
    )
    pair_count = tokens_dev * TOP
    pair_index = jnp.arange(pair_count, dtype=jnp.int32)
    earlier = (pair_index[None, :] < pair_index[:, None]).astype(jnp.bfloat16)
    counts = jnp.dot(earlier, flat_hot, preferred_element_type=jnp.float32)
    slots = jnp.sum(counts * flat_hot, axis=1).astype(jnp.int32)
    source_table = (
        jnp.full((experts_all * capacity,), pair_count, jnp.int32)
        .at[flat_route * capacity + slots]
        .set(jnp.arange(pair_count, dtype=jnp.int32))
    )
    send_table = jnp.transpose(
        source_table.reshape(groups, local_experts, capacity), (1, 0, 2)
    ).reshape(-1)
    return_pos = (
        flat_route % local_experts * (groups * capacity)
        + flat_route // local_experts * capacity
        + slots
    )
    padded_rows = jnp.concatenate([ffn_low, jnp.zeros((1, model_width), jnp.bfloat16)], axis=0)
    send_rows = padded_rows[send_table // TOP].reshape(local_experts, groups, capacity, model_width)
    received = lax.all_to_all(send_rows, "expert", split_axis=1, concat_axis=1, tiled=True)
    expert_rows = received.reshape(local_experts, groups * capacity, model_width)
    expert_pre = jnp.einsum(
        "erd,edf->erf", expert_rows, experts_up, preferred_element_type=jnp.float32
    )
    expert_hidden = swiglu(expert_pre, hidden_width).astype(jnp.bfloat16)
    expert_result = jnp.einsum(
        "erf,efd->erd", expert_hidden, experts_down, preferred_element_type=jnp.float32
    ).astype(jnp.bfloat16)
    returned = lax.all_to_all(
        expert_result.reshape(local_experts, groups, capacity, model_width),
        "expert",
        split_axis=1,
        concat_axis=1,
        tiled=True,
    )
    token_outputs = returned.reshape(-1, model_width)[return_pos].reshape(
        tokens_dev, TOP, model_width
    )
    routed = jnp.sum(gates[:, :, None] * token_outputs, axis=1)
    output_rows = resid + shared_result + routed
    shared_cot = upstream.astype(jnp.bfloat16)
    shared_down_term = jnp.dot(shared_hidden.T, shared_cot, preferred_element_type=jnp.float32)
    dshared_hidden = jnp.dot(shared_cot, full_sdown.T, preferred_element_type=jnp.float32)
    dshared_pre = swiglu_back(shared_pre, dshared_hidden, shared_width).astype(jnp.bfloat16)
    shared_up_term = jnp.dot(ffn_low.T, dshared_pre, preferred_element_type=jnp.float32)
    dnormed_second = jnp.dot(dshared_pre, full_sup.T, preferred_element_type=jnp.float32)
    token_cot = (gates[:, :, None] * upstream[:, None, :]).astype(jnp.bfloat16)
    dgates = jnp.sum(upstream[:, None, :] * token_outputs, axis=2)
    padded_cot = jnp.concatenate(
        [token_cot.reshape(-1, model_width), jnp.zeros((1, model_width), jnp.bfloat16)], axis=0
    )
    send_cot = padded_cot[send_table].reshape(local_experts, groups, capacity, model_width)
    received_cot = lax.all_to_all(
        send_cot, "expert", split_axis=1, concat_axis=1, tiled=True
    ).reshape(local_experts, groups * capacity, model_width)
    down_term = jnp.einsum(
        "erf,erd->efd", expert_hidden, received_cot, preferred_element_type=jnp.float32
    )
    dexpert_hidden = jnp.einsum(
        "erd,efd->erf", received_cot, experts_down, preferred_element_type=jnp.float32
    )
    dexpert_pre = swiglu_back(expert_pre, dexpert_hidden, hidden_width).astype(jnp.bfloat16)
    up_term = jnp.einsum(
        "erd,erf->edf", expert_rows, dexpert_pre, preferred_element_type=jnp.float32
    )
    drows = jnp.einsum(
        "erf,edf->erd", dexpert_pre, experts_up, preferred_element_type=jnp.float32
    ).astype(jnp.bfloat16)
    returned_grad = lax.all_to_all(
        drows.reshape(local_experts, groups, capacity, model_width),
        "expert",
        split_axis=1,
        concat_axis=1,
        tiled=True,
    )
    row_grads = returned_grad.reshape(-1, model_width)[return_pos].reshape(
        tokens_dev, TOP, model_width
    )
    dnormed_second = dnormed_second + jnp.sum(row_grads, axis=1, dtype=jnp.float32)
    expert_up_grad, expert_down_grad = (
        lax.psum_scatter(
            up_term.astype(jnp.bfloat16), "batch", scatter_dimension=1, tiled=True
        ).astype(jnp.float32),
        lax.psum_scatter(
            down_term.astype(jnp.bfloat16), "batch", scatter_dimension=1, tiled=True
        ).astype(jnp.float32),
    )
    dchosen = (dgates - jnp.sum(dgates * gates, axis=1, keepdims=True)) / chosen_sum
    dprobs = jnp.sum(jnp.where(route_hot, dchosen[:, :, None], 0.0), axis=1)
    dlogits = (probs * (dprobs - jnp.sum(probs * dprobs, axis=1, keepdims=True))).astype(
        jnp.bfloat16
    )
    router_term = jnp.dot(ffn_low.T, dlogits, preferred_element_type=jnp.float32)
    dnormed_second = dnormed_second + jnp.dot(
        dlogits, full_router.T, preferred_element_type=jnp.float32
    )
    dresid_norm, gain_ffn_term = norm_back(dnormed_second, normed_second, inv_second, gain_second)
    dresid = upstream + dresid_norm
    dproj = dresid.astype(jnp.bfloat16)
    out_term = jnp.dot(attn_low.T, dproj, preferred_element_type=jnp.float32)
    dattn = (
        jnp.dot(dproj, full_out.T, preferred_element_type=jnp.float32)
        .astype(jnp.bfloat16)
        .reshape(tokens_dev, heads_count, HEAD)
    )
    delta_rows = jnp.sum(dattn.astype(jnp.float32) * attn_full, axis=2)
    delta_heads = jnp.transpose(delta_rows)
    key_piece = lax.all_gather(keys, "expert", axis=0, tiled=True)
    value_piece = lax.all_gather(values, "expert", axis=0, tiled=True)
    allowed = key_mask(key_piece.shape[0])[None]
    scores = (
        jnp.einsum("qhd,khd->hqk", queries, key_piece, preferred_element_type=jnp.float32)
        * score_scale
    )
    attn_probs = jnp.where(allowed, jnp.exp(scores - logsum[:, :, None]), 0.0)
    dprob = jnp.einsum("qhd,khd->hqk", dattn, value_piece, preferred_element_type=jnp.float32)
    dscore = (attn_probs * (dprob - delta_heads[:, :, None])).astype(jnp.bfloat16)
    attn_probs, dscore = (attn_probs, dscore)
    dquery = jnp.einsum("hqk,khd->qhd", dscore, key_piece, preferred_element_type=jnp.float32)
    dkey_piece = jnp.einsum("hqk,qhd->khd", dscore, queries, preferred_element_type=jnp.float32)
    dvalue_piece = jnp.einsum(
        "hqk,qhd->khd", attn_probs.astype(jnp.bfloat16), dattn, preferred_element_type=jnp.float32
    )
    folded = (dquery, dkey_piece, dvalue_piece)
    dquery = folded[0]
    dkey, dvalue = (
        lax.psum_scatter(
            folded[1].astype(jnp.bfloat16), "expert", scatter_dimension=0, tiled=True
        ).astype(jnp.float32),
        lax.psum_scatter(
            folded[2].astype(jnp.bfloat16), "expert", scatter_dimension=0, tiled=True
        ).astype(jnp.float32),
    )
    dquery_raw = rotate(dquery * score_scale, positions, -1.0).reshape(tokens_dev, model_width)
    dkey_raw = rotate(dkey * score_scale, positions, -1.0).reshape(tokens_dev, model_width)
    dprojected = jnp.concatenate(
        [dquery_raw, dkey_raw, dvalue.reshape(tokens_dev, model_width)], axis=1
    ).astype(jnp.bfloat16)
    qkv_term = jnp.dot(input_low.T, dprojected, preferred_element_type=jnp.float32)
    dnormed_first = jnp.dot(dprojected, full_qkv.T, preferred_element_type=jnp.float32)
    dinput_norm, gain_attn_term = norm_back(dnormed_first, normed_first, inv_first, gain_first)
    input_grad = dresid + dinput_norm
    grads = (
        lax.psum_scatter(qkv_term, ("batch", "expert"), scatter_dimension=0, tiled=True),
        lax.psum_scatter(out_term, ("batch", "expert"), scatter_dimension=0, tiled=True),
        lax.psum_scatter(shared_up_term, ("batch", "expert"), scatter_dimension=0, tiled=True),
        lax.psum_scatter(shared_down_term, ("batch", "expert"), scatter_dimension=0, tiled=True),
        lax.psum_scatter(router_term, ("batch", "expert"), scatter_dimension=0, tiled=True),
        lax.psum_scatter(gain_attn_term, ("batch", "expert"), scatter_dimension=0, tiled=True),
        lax.psum_scatter(gain_ffn_term, ("batch", "expert"), scatter_dimension=0, tiled=True),
    )
    (
        qkv_grad,
        out_grad,
        shared_up_grad,
        shared_down_grad,
        router_grad,
        gain_attn_grad,
        gain_ffn_grad,
    ) = grads
    return (
        output_rows[None],
        input_grad[None],
        qkv_grad,
        out_grad,
        shared_up_grad,
        shared_down_grad,
        router_grad,
        gain_attn_grad,
        gain_ffn_grad,
        expert_up_grad,
        expert_down_grad,
    )


PAIR_OF = {0: 0, 2: 1, 4: 2, 6: 3, 3: 4}
F32 = jnp.float32
LOW = jnp.bfloat16
COST = 10**9


def low(values):
    return values.astype(LOW)


def dot(left, right, dims=((1,), (0,))):
    return lax.dot_general(left, right, (dims, ((), ())), preferred_element_type=F32)


MESH_ID = pl.DeviceIdType.MESH


def place():
    b = lax.axis_index("batch")
    e = lax.axis_index("expert")
    return b, e, e // 2, lax.rem(e, 2)


def greet_near():
    b, e, z, core = place()
    barrier = pltpu.get_barrier_semaphore()
    for device in ((b ^ 1, e), (b ^ 2, e), (b, e ^ 1)):
        pl.semaphore_signal(barrier, inc=1, device_id=device, device_id_type=MESH_ID)

    @pl.when(z > 0)
    def _():
        pl.semaphore_signal(barrier, inc=1, device_id=(b, e - 2), device_id_type=MESH_ID)

    @pl.when(z < 3)
    def _():
        pl.semaphore_signal(barrier, inc=1, device_id=(b, e + 2), device_id_type=MESH_ID)

    ends = jnp.where((z == 0) | (z == 3), 1, 0)
    pl.semaphore_wait(barrier, 5 - ends)


def greet(devices):
    barrier = pltpu.get_barrier_semaphore()
    for device in devices:
        pl.semaphore_signal(barrier, inc=1, device_id=device, device_id_type=MESH_ID)
    pl.semaphore_wait(barrier, len(devices))


def pack_mates():
    b, e, _, _ = place()
    return [(b, lax.rem(e + i, 8)) for i in range(1, 8)]


def send(src, dst, send_sem, recv_sem, device):
    return pltpu.make_async_remote_copy(
        src_ref=src,
        dst_ref=dst,
        send_sem=send_sem,
        recv_sem=recv_sem,
        device_id=device,
        device_id_type=MESH_ID,
    )


GATHER_SEMS = [pltpu.SemaphoreType.DMA((3,))] * 4 + [pltpu.SemaphoreType.DMA((4,))] * 2


def line_stages(buf, up_send, up_recv, down_send, down_recv, core_send, core_recv):
    b, e, z, core = place()

    def to_core(owner_z):
        block = buf.at[2 * owner_z + core]
        return send(block, block, core_send.at[owner_z], core_recv.at[owner_z], (b, e ^ 1))

    def up(step):
        block = buf.at[jnp.maximum(2 * (z - step), 0) + core]
        return send(block, block, up_send.at[step], up_recv.at[step], (b, jnp.minimum(e + 2, 7)))

    def down(step):
        block = buf.at[jnp.minimum(2 * (z + step), 6) + core]
        return send(
            block, block, down_send.at[step], down_recv.at[step], (b, jnp.maximum(e - 2, 0))
        )

    def start(step):
        @pl.when((z >= step) & (z < 3))
        def _():
            up(step).start()

        @pl.when((z + step <= 3) & (z > 0))
        def _():
            down(step).start()

        if step == 0:
            to_core(z).start()

    def arrive(step):
        @pl.when(z - 1 - step >= 0)
        def _():
            up(step).wait_recv()

        @pl.when(z + 1 + step <= 3)
        def _():
            down(step).wait_recv()

        if step < 2:
            start(step + 1)

        @pl.when(z - 1 - step >= 0)
        def _():
            to_core(z - 1 - step).start()

        @pl.when(z + 1 + step <= 3)
        def _():
            to_core(z + 1 + step).start()

    def finish():
        for owner_z in range(4):
            to_core(owner_z).wait()
        for step in range(3):

            @pl.when((z >= step) & (z < 3))
            def _():
                up(step).wait_send()

            @pl.when((z + step <= 3) & (z > 0))
            def _():
                down(step).wait_send()

    return [lambda: start(0)] + [functools.partial(arrive, i) for i in range(3)] + [finish]


def line_gather(buf, *sems):
    for stage in line_stages(buf, *sems):
        stage()


def scatter_scratch(tokens, width):
    return [pltpu.VMEM((4, tokens, width), LOW)] + [
        pltpu.VMEM((3, tokens, width), LOW) for _ in range(4)
    ]


SCATTER_SEMS = [pltpu.SemaphoreType.DMA((3,))] * 4 + [pltpu.SemaphoreType.DMA((4,))] * 2


def line_sum_stages(
    part,
    from_core,
    up_out,
    up_in,
    down_out,
    down_in,
    up_send,
    up_recv,
    down_send,
    down_recv,
    core_send,
    core_recv,
):
    b, e, z, core = place()

    def to_core(target):
        return send(
            part.at[2 * target + 1 - core],
            from_core.at[target],
            core_send.at[target],
            core_recv.at[target],
            (b, e ^ 1),
        )

    def up(step):
        return send(
            up_out.at[step],
            up_in.at[step],
            up_send.at[step],
            up_recv.at[step],
            (b, jnp.minimum(e + 2, 7)),
        )

    def down(step):
        return send(
            down_out.at[step],
            down_in.at[step],
            down_send.at[step],
            down_recv.at[step],
            (b, jnp.maximum(e - 2, 0)),
        )

    def chip_sum(target):
        return part[2 * target + core].astype(F32) + from_core[target].astype(F32)

    def start():
        for target in (3, 0, 2, 1):
            to_core(target).start()

    def send_up(step):
        up_out[step] = low(chip_sum(3 - step))
        up(step).start()

    def send_down(step):
        down_out[step] = low(chip_sum(step))
        down(step).start()

    def pass_up(step):
        up(step).wait_recv()
        up_out[step] = low(chip_sum(3 - step) + up_in[step].astype(F32))
        up(step).start()

    def pass_down(step):
        down(step).wait_recv()
        down_out[step] = low(chip_sum(step) + down_in[step].astype(F32))
        down(step).start()

    def ends():
        for target in range(4):
            to_core(target).wait()

        @pl.when(z == 0)
        def _():
            for step in range(3):
                send_up(step)

        @pl.when(z == 3)
        def _():
            for step in range(3):
                send_down(step)

    def near():
        @pl.when(z == 1)
        def _():
            pass_up(0)

        @pl.when(z == 2)
        def _():
            pass_down(0)

    def far():
        @pl.when(z == 1)
        def _():
            pass_up(1)
            pass_down(0)

        @pl.when(z == 2)
        def _():
            pass_down(1)
            pass_up(0)

    def finish():
        @pl.when(z == 0)
        def _():
            up_in[0] = jnp.zeros_like(up_in[0])

        @pl.when(z == 3)
        def _():
            down_in[0] = jnp.zeros_like(down_in[0])

        last_up = lax.rem(3 - z, 3)
        last_down = lax.rem(z, 3)

        @pl.when(z > 0)
        def _():
            up(last_up).wait_recv()

        @pl.when(z < 3)
        def _():
            down(last_down).wait_recv()

        total = chip_sum(z) + up_in[last_up].astype(F32) + down_in[last_down].astype(F32)
        for step in range(3):

            @pl.when(z < 3 - step)
            def _():
                up(step).wait_send()

            @pl.when(z > step)
            def _():
                down(step).wait_send()

        return total

    return [start, ends, near, far, finish]


def sum_into(out, *terms):
    if len(out.shape) == 2:

        @pl.loop(0, out.shape[0] // 16)
        def _(i):
            here = pl.ds(pl.multiple_of(i * 16, 16), 16)
            total = terms[0][here, :].astype(F32)
            for term in terms[1:]:
                total = total + term[here, :].astype(F32)
            out[here, :] = total.astype(out.dtype)

    else:
        for i in range(out.shape[0]):
            total = terms[0][i].astype(F32)
            for term in terms[1:]:
                total = total + term[i].astype(F32)
            out[i] = total.astype(out.dtype)


REDUCE_COUNT = 8


def reduce_scratch(half_shape, far=False):
    kept = (4, *half_shape) if far else (1, 8, 128)
    return [
        pltpu.VMEM((6, *half_shape), LOW),
        pltpu.VMEM((2, *half_shape), LOW),
        pltpu.VMEM(kept, LOW if far else F32),
    ] + [pltpu.SemaphoreType.DMA((size,)) for size in (3, 3, 3, 3, 4)]


def reduce_stages(
    block, out, received, sums, kept, x_send, x_recv, y_send, y_recv, local_sem
):
    b, e, _, _ = place()
    x_device, y_device = (b ^ 1, e), (b ^ 2, e)

    def over_x(slot):
        src = (block(b ^ 3, 0), block(b ^ 1, 0), sums.at[1])[slot]
        return send(src, received.at[slot], x_send.at[slot], x_recv.at[slot], x_device)

    def over_y(slot):
        src = (block(b ^ 3, 1), block(b ^ 2, 1), sums.at[0])[slot]
        return send(src, received.at[3 + slot], y_send.at[slot], y_recv.at[slot], y_device)

    far = kept.shape[0] == 4

    def mine(i):
        return (block(b ^ 2, 0), block(b ^ 1, 1), block(b, 0), block(b, 1))[i]

    def keep(i):
        return pltpu.make_async_copy(mine(i), kept.at[i], local_sem.at[i])

    def held(i):
        if not far:
            return mine(i)
        keep(i).wait()
        return kept.at[i]

    def start():
        over_x(0).start()
        over_y(0).start()
        for i in range(4 if far else 0):
            keep(i).start()

    def forward():
        over_x(0).wait_recv()
        over_x(1).start()
        sum_into(sums.at[0], held(0), received.at[0])
        over_y(2).start()
        over_y(0).wait_recv()
        over_y(1).start()
        sum_into(sums.at[1], held(1), received.at[3])
        over_x(2).start()

    def finish():
        for slot in (1, 2):
            over_x(slot).wait_recv()
            over_y(slot).wait_recv()
        sum_into(out(0), held(2), received.at[1], received.at[5])
        sum_into(out(1), held(3), received.at[4], received.at[2])
        for slot in range(3):
            over_x(slot).wait_send()
            over_y(slot).wait_send()

    return start, forward, finish


def reduce_rows(term, out, scratch):
    half_rows = out.shape[0] // 2

    def block(owner, half):
        return term.at[pl.ds((2 * owner + half) * half_rows, half_rows)]

    def out_half(half):
        return out.at[pl.ds(half * half_rows, half_rows)]

    return reduce_stages(block, out_half, *scratch)


def kernel_call(body, outs, args, scratch, collective_id, far_outs=(), far_args=()):
    near = pl.BlockSpec(memory_space=pltpu.VMEM)
    far = pl.BlockSpec(memory_space=pl.ANY)
    return pl.pallas_call(
        body,
        cost_estimate=pl.CostEstimate(flops=COST, bytes_accessed=COST, transcendentals=0),
        out_shape=[jax.ShapeDtypeStruct(shape, dtype) for shape, dtype in outs],
        in_specs=[far if i in far_args else near for i in range(len(args))],
        out_specs=[far if i in far_outs else near for i in range(len(outs))],
        scratch_shapes=scratch,
        compiler_params=pltpu.CompilerParams(
            collective_id=collective_id, has_side_effects=True, vmem_limit_bytes=56 * 2**20
        ),
    )(*args)


SPREAD_SEMS = [pltpu.SemaphoreType.DMA((2,))] + [pltpu.SemaphoreType.DMA((3,))] * 4


def spread_stages(own, whole, local_sem, x_send, x_recv, y_send, y_recv):
    b, e, _, _ = place()
    x_device, y_device = (b ^ 1, e), (b ^ 2, e)

    def over_x(slot):
        src, dst = (
            (own(0), whole(b, 0)),
            (own(1), whole(b, 1)),
            (whole(b ^ 2, 1), whole(b ^ 2, 1)),
        )[slot]
        return send(src, dst, x_send.at[slot], x_recv.at[slot], x_device)

    def over_y(slot):
        src, dst = (
            (own(1), whole(b, 1)),
            (own(0), whole(b, 0)),
            (whole(b ^ 1, 0), whole(b ^ 1, 0)),
        )[slot]
        return send(src, dst, y_send.at[slot], y_recv.at[slot], y_device)

    def keep(half):
        return pltpu.make_async_copy(own(half), whole(b, half), local_sem.at[half])

    def start():
        over_x(0).start()
        over_y(0).start()
        for half in range(2):
            keep(half).start()

    def forward():
        over_x(0).wait_recv()
        over_y(2).start()
        over_x(1).start()
        over_y(0).wait_recv()
        over_x(2).start()
        over_y(1).start()
    def finish():
        for slot in range(3):
            for over in (over_x, over_y):
                if slot > 0:
                    over(slot).wait_recv()
                over(slot).wait_send()
        for half in range(2):
            keep(half).wait()

    return start, forward, finish


def spread_rows(own_ref, whole_ref, rows, sems):
    half_rows = rows // 2

    def own(half):
        return own_ref.at[pl.ds(half * half_rows, half_rows)]

    def whole(owner, half):
        return whole_ref.at[pl.ds(owner * rows + half * half_rows, half_rows)]

    return spread_stages(own, whole, *sems)


def opening_kernel(
    rows, router, first_gain, second_gain, routes, ids, qkv, sup, out_weight, up_weight,
    n1_all, gains, small_all, marks_all, columns_all, out_all, up_all,
    small, marks, columns, w_out, up_own, up_wide, up_sem, *sems,
):
    (
        b_send, b_recv, s_send, s_recv, m_send, m_recv, c_send, c_recv,
        x_send, x_recv, y_send, y_recv, z_send, z_recv, o_send, o_recv, p_send, p_recv,
    ) = sems[:18]
    b, e, z, core = place()
    over = [(b ^ bit, e) for bit in (1, 2, 3)]
    mates = pack_mates()
    up_start, up_forward, up_finish = spread_rows(up_own, up_all, up_own.shape[0], sems[18:23])
    bring = pltpu.make_async_copy(up_weight.at[0], up_wide, up_sem.at[0])
    bring.start()
    greet(over + mates)
    bring.wait()
    up_own[...] = low(up_wide[...])
    up_start()
    rows_w = router.shape[0]
    small[...] = jnp.zeros_like(small)
    small[:rows_w] = router[...]
    small[rows_w : rows_w + 1, : first_gain.shape[1]] = first_gain[...]
    small[rows_w + 1 : rows_w + 2, : second_gain.shape[1]] = second_gain[...]
    chosen = routes[0].astype(F32)
    chosen = jnp.concatenate([chosen, jnp.zeros((128, 128 - TOP), F32)], axis=1).T
    marks[...] = jnp.concatenate(
        [chosen[:TOP], ids[...].astype(F32), jnp.zeros((7 - TOP, 128), F32)], axis=0
    )
    pair = 2 * HEAD
    width = rows.shape[1]
    for i in range(8):
        for part in range(3):
            lanes = slice(part * pair, (part + 1) * pair)
            if i in PAIR_OF:
                start = part * width + PAIR_OF[i] * pair
                columns[i, :, lanes] = low(qkv[:, start : start + pair])
            else:
                columns[i, :, lanes] = jnp.zeros((columns.shape[1], pair), LOW)
        columns[i, :, 3 * pair :] = sup[i]
    w_out[...] = low(out_weight[...])
    small_all[e, b] = small[...]
    marks_all[e] = marks[...]
    columns_all[b, e] = columns[e]
    out_all[b, z, core] = w_out[...]
    first = []
    for i, device in enumerate(over):
        first.append(send(small, small_all.at[e, b], b_send.at[i], b_recv.at[i], device))
        first[-1].start()
    across = []
    for i, device in enumerate(mates):
        across.append(
            send(columns.at[device[1]], columns_all.at[b, e], c_send.at[i], c_recv.at[i], device)
        )
        across[-1].start()
    beyond = []
    for i, device in enumerate(over):
        beyond.append(
            send(w_out, out_all.at[b, z, core], o_send.at[i], o_recv.at[i], device)
        )
        beyond[-1].start()
    rest = []
    for i, device in enumerate(mates):
        rest.append(send(marks, marks_all.at[e], m_send.at[i], m_recv.at[i], device))
        rest[-1].start()
    values = rows[...]
    inv = lax.rsqrt(jnp.mean(values * values, axis=1, keepdims=True) + EPSILON)
    for copy in first:
        copy.wait()
    second = []
    for i, device in enumerate(mates):
        second.append(send(small_all.at[e], small_all.at[e], s_send.at[i], s_recv.at[i], device))
        second[-1].start()
    for copy in second:
        copy.wait()

    piece = width // 32
    lane = lax.broadcasted_iota(jnp.int32, (128, width), 1)
    spread = low(jnp.where(lax.rem(lane, piece) == lax.broadcasted_iota(jnp.int32, (128, width), 0), 1.0, 0.0))
    row = lax.broadcasted_iota(jnp.int32, (32, width), 0)
    owner = lax.rem(row, 4) * 8 + row // 4
    mine = lax.broadcasted_iota(jnp.int32, (32, width), 1) // piece == owner
    for i, index in enumerate((5, 6)):
        pieces = jnp.concatenate([small_all[j, :, index, :] for j in range(8)], axis=0)
        spread_out = dot(low(pieces), spread)
        gains[i : i + 1, :] = jnp.sum(jnp.where(mine, spread_out, 0.0), axis=0, keepdims=True)
    n1_all[e] = low(values * inv * gains[0:1, :])
    stages = line_stages(n1_all, *sems[23:])
    stages[0]()

    def hop(owner, half, sems_out, sems_in, slot, device):
        block = columns_all.at[owner, pl.ds(4 * half, 4)]
        return send(block, block, sems_out.at[slot], sems_in.at[slot], device)

    def over_x(slot):
        owner, half = ((b, 0), (b, 1), (b ^ 2, 1))[slot]
        return hop(owner, half, x_send, x_recv, slot, over[0])

    def over_y(slot):
        owner, half = ((b, 1), (b, 0), (b ^ 1, 0))[slot]
        return hop(owner, half, y_send, y_recv, slot, over[1])

    def out_block(owner_z):
        return out_all.at[:, owner_z, core]

    def out_pair(slot):
        block = out_block(lax.rem(z + 4 - slot, 4))
        return send(block, block, p_send.at[slot], p_recv.at[slot], (b, e ^ 1))

    for copy in across:
        copy.wait()
    over_x(0).start()
    over_y(0).start()
    up_forward()
    over_x(1).start()
    over_y(1).start()
    stages[1]()
    over_x(0).wait_recv()
    over_y(2).start()
    over_y(0).wait_recv()
    over_x(2).start()
    stages[2]()
    for copy in beyond:
        copy.wait()
    along = []
    for i in range(3):
        device = (b, lax.rem(e + 2 * i + 2, 8))
        along.append(send(out_block(z), out_block(z), z_send.at[i], z_recv.at[i], device))
        along[-1].start()
    out_pair(0).start()
    stages[3]()
    for i, copy in enumerate(along):
        copy.wait()
        out_pair(i + 1).start()
    stages[4]()
    for slot in range(3):
        for over_one in (over_x, over_y):
            if slot > 0:
                over_one(slot).wait_recv()
            over_one(slot).wait_send()
    for copy in rest:
        copy.wait()
    for slot in range(4):
        out_pair(slot).wait()
    up_finish()


def opening(rows, router, first_gain, second_gain, routes, ids, qkv, sup, out_weight, up_weight):
    tokens, width = rows.shape
    _, up_rows, up_width = up_weight.shape
    rows_w = out_weight.shape[0]
    wide = 6 * HEAD + sup.shape[2]
    sizes = (3, 3, 7, 7, 7, 7, 7, 7, 3, 3, 3, 3, 3, 3, 3, 3, 4, 4)
    return kernel_call(
        opening_kernel,
        [
            ((8, tokens, width), LOW),
            ((2, width), F32),
            ((8, 4, 8, 128), F32),
            ((8, 8, 128), F32),
            ((4, 8, rows_w, wide), LOW),
            ((4, 4, 2, rows_w, width), LOW),
            ((4 * up_rows, up_width), LOW),
        ],
        (rows, router, first_gain, second_gain, routes, ids, qkv, sup, out_weight, up_weight),
        [
            pltpu.VMEM((8, 128), F32),
            pltpu.VMEM((8, 128), F32),
            pltpu.VMEM((8, rows_w, wide), LOW),
            pltpu.VMEM((rows_w, width), LOW),
            pltpu.VMEM((up_rows, up_width), LOW),
            pltpu.VMEM((up_rows, up_width), F32),
            pltpu.SemaphoreType.DMA((1,)),
        ]
        + [pltpu.SemaphoreType.DMA((size,)) for size in sizes]
        + SPREAD_SEMS
        + GATHER_SEMS,
        0,
        far_outs=(6,),
        far_args=(9,),
    )


def holder(e):
    return (lax.rem(e, 2) == 0) | (e == 3), jnp.where(e == 3, 4, e // 2)


BLOCK = 256


def turned(values, cosine, sine):
    return values * cosine + pltpu.roll(values, HEAD // 2, 1) * sine


def middle_kernel(
    n1, weights, cosine, sine, ids_row, ids_column, w_out, rows, gain, cot, up_weight, down_weight, sdown_weight,
    qkv, logsum, attn, resid, n2_all, cot_all, up_all, down_all, sdown_all, down_second,
    attended, up_own, up_wide, down_own, sdown_own, up_sem, a_send, a_recv, *sems,
):
    b, e, z, core = place()
    tokens = rows.shape[0]
    mates = pack_mates()
    count = len(SPREAD_SEMS)
    spreads = [
        spread_rows(up_own, up_all, up_own.shape[0], sems[:count]),
        spread_rows(down_own, down_all, down_own.shape[0], sems[count : 2 * count]),
        spread_rows(sdown_own, sdown_all, sdown_own.shape[0], sems[2 * count : 3 * count]),
    ]
    sems = sems[3 * count :]
    cot_stages = line_stages(cot_all, *sems[: len(GATHER_SEMS)])
    n2_stages = line_stages(n2_all, *sems[len(GATHER_SEMS) :])
    cot_all[e] = low(cot[0])
    bring = pltpu.make_async_copy(up_weight.at[1], up_wide, up_sem.at[0])
    bring.start()
    greet([(b ^ 1, e), (b ^ 2, e), *mates])
    bring.wait()
    up_own[...] = low(up_wide[...])
    spreads[0][0]()
    cot_stages[0]()
    down_own[...] = low(down_weight[0])
    down_second[...] = low(down_weight[1])
    short = sdown_own.shape[0] - sdown_weight.shape[0]
    sdown_own[...] = low(
        jnp.concatenate([sdown_weight[...], jnp.zeros((short, cot.shape[2]), F32)], axis=0)
    )
    for start, _, _ in spreads[1:]:
        start()
    holds, pair = holder(e)

    @pl.when(jnp.logical_not(holds))
    def _():
        qkv[...] = jnp.zeros_like(qkv)
        logsum[...] = jnp.zeros_like(logsum)

    @pl.when(holds)
    def _():
        @pl.loop(0, n1.shape[0] // BLOCK)
        def _(i):
            here = pl.ds(pl.multiple_of(i * BLOCK, BLOCK), BLOCK)
            projected = dot(n1[here, :], weights[:, : 6 * HEAD])
            cos_here, sin_here = cosine[here, :], sine[here, :]
            for part in range(6):
                piece = projected[:, part * HEAD : (part + 1) * HEAD]
                if part < 4:
                    piece = turned(piece, cos_here, sin_here)
                qkv[part, here, :] = low(piece)

    cot_stages[1]()
    for head in range(2):

        @pl.when(holds)
        def _():
            for i in range(n1.shape[0] // BLOCK):
                here = pl.ds(i * BLOCK, BLOCK)
                keys = (i + 1) * BLOCK
                scores = dot(qkv[head, here, :], qkv[2 + head, :keys, :], ((1,), (1,)))
                scores = jnp.where(
                    allowed_here(ids_column, ids_row, i, keys), scores * HEAD ** (-0.5), NEGATIVE
                )
                top = jnp.max(scores, axis=1, keepdims=True)
                weight = jnp.exp(scores - top)
                total = jnp.sum(weight, axis=1, keepdims=True)
                out = dot(low(weight / total), qkv[4 + head, :keys, :])
                logsum[head, here, :] = jnp.broadcast_to(top + jnp.log(total), (BLOCK, HEAD))
                for j in range(BLOCK // tokens):
                    attended[i * (BLOCK // tokens) + j, :, head * HEAD : (head + 1) * HEAD] = low(
                        out[j * tokens : (j + 1) * tokens]
                    )

        if head == 0:
            cot_stages[2]()
        spreads[head][1]()

    def give(i):
        other = lax.rem(e + i, 8)
        return send(
            attended.at[other], attn.at[pair], a_send.at[i - 1], a_recv.at[pair], (b, other)
        )

    @pl.when(holds)
    def _():
        for i in range(1, 8):
            give(i).start()
        attn[pair] = attended[e]

    total = rows[...]
    for source, index in PAIR_OF.items():

        @pl.when(e != source)
        def _():
            block = attn.at[index]
            send(block, block, a_send.at[0], a_recv.at[index], (b, source)).wait_recv()

        size = attn.shape[2]
        total = total + dot(attn[index], w_out[index * size : (index + 1) * size, :])
    resid[...] = total
    inv = lax.rsqrt(jnp.mean(total * total, axis=1, keepdims=True) + EPSILON)
    n2_all[e] = low(total * inv * gain[...])
    n2_stages[0]()
    cot_stages[3]()
    spreads[2][1]()
    for stage in n2_stages[1:]:
        stage()
    cot_stages[4]()

    @pl.when(holds)
    def _():
        for i in range(1, 8):
            give(i).wait_send()

    for _, _, finish in spreads:
        finish()


def allowed_here(ids_column, ids_row, i, keys):
    query = i * BLOCK + lax.broadcasted_iota(jnp.int32, (BLOCK, keys), 0)
    key = lax.broadcasted_iota(jnp.int32, (BLOCK, keys), 1)
    same = ids_column[i * BLOCK : (i + 1) * BLOCK, :] == ids_row[:, :keys]
    return (key <= query) & same


def middle(n1, weights, cosine, sine, ids_row, ids_column, w_out, rows, gain, cot, up_weight, down_weight, sdown_weight):
    tokens, width = rows.shape
    length = n1.shape[0]
    pair = 2 * HEAD
    count = len(PAIR_OF)
    _, up_rows, up_width = up_weight.shape
    down_rows = down_weight.shape[1]
    sdown_rows = -(-sdown_weight.shape[0] // 32) * 32
    return kernel_call(
        middle_kernel,
        [
            ((6, length, HEAD), LOW),
            ((2, length, HEAD), F32),
            ((count, tokens, pair), LOW),
            ((tokens, width), F32),
            ((8, tokens, width), LOW),
            ((8, tokens, width), LOW),
            ((4 * up_rows, up_width), LOW),
            ((4 * down_rows, width), LOW),
            ((4 * sdown_rows, width), LOW),
            ((down_rows, width), LOW),
        ],
        (n1, weights, cosine, sine, ids_row, ids_column, w_out, rows, gain, cot, up_weight, down_weight, sdown_weight),
        [
            pltpu.VMEM((8, tokens, pair), LOW),
            pltpu.VMEM((up_rows, up_width), LOW),
            pltpu.VMEM((up_rows, up_width), F32),
            pltpu.VMEM((down_rows, width), LOW),
            pltpu.VMEM((sdown_rows, width), LOW),
            pltpu.SemaphoreType.DMA((1,)),
            pltpu.SemaphoreType.DMA((7,)),
            pltpu.SemaphoreType.DMA((count,)),
        ]
        + SPREAD_SEMS * 3
        + GATHER_SEMS * 2,
        1,
        far_outs=(6, 7, 8),
        far_args=(10,),
    )


def experts_kernel(
    n2, cot, w_sup, w_sdown, gates, down_second, up_first, up_second, down_first,
    out_part, row_sum, sdown_term, sup_term, down_grad, up_term_first, up_term_second, down_term_second,
    part, up_w, down_w, hid, dpre, hid_shared, dpre_shared, load_sem, store_sem, *scratch,
):
    e = lax.axis_index("expert")
    length, width = n2.shape
    hidden = down_w.shape[1]
    pad = w_sdown.shape[0]
    loads = [
        pltpu.make_async_copy(up_first, up_w.at[0], load_sem.at[0]),
        pltpu.make_async_copy(down_first, down_w.at[0], load_sem.at[1]),
        pltpu.make_async_copy(up_second, up_w.at[1], load_sem.at[2]),
    ]
    for copy in loads:
        copy.start()
    count = len(SPREAD_SEMS)
    arrive = spread_rows(down_second, down_w.at[1], down_second.shape[0], scratch[:count])
    reduce = reduce_rows(down_w.at[0], down_grad, scratch[count : count + REDUCE_COUNT])
    stages = line_sum_stages(part, *scratch[count + REDUCE_COUNT :])
    tokens = part.shape[1]
    greet_near()
    arrive[0]()
    for copy in loads[:2]:
        copy.wait()
    lane = lax.broadcasted_iota(jnp.int32, (ROWS, 128), 1)

    def routed(k, here, x, c):
        gate = gates[here, k : k + 1]
        gate_part = dot(x, up_w[k, :, :hidden])
        up_part = dot(x, up_w[k, :, hidden:])
        back = dot(c, down_w[k], ((1,), (1,)))
        silu, slope = silu_parts(gate_part, up_part)
        value = silu * up_part
        dgate = jnp.sum(back * value, axis=1, keepdims=True)
        hid[k, here, :] = low(value * gate)
        back = back * gate
        dpre[k, here, :hidden] = low(back * slope)
        dpre[k, here, hidden:] = low(back * silu)
        out = dot(hid[k, here, :], down_w[k])
        drow = dot(dpre[k, here, :], up_w[k], ((1,), (1,)))
        return out, drow, dgate

    def mark(k, dgate, marks):
        high = low(dgate).astype(F32)
        marks = jnp.where(lane == 2 * e + k, high, marks)
        return jnp.where(lane == 2 * e + k + 16, dgate - high, marks)

    def first_pass(i):
        here = pl.ds(pl.multiple_of(i * ROWS, ROWS), ROWS)
        x = n2[here, :]
        c = cot[here, :]
        gate_part = dot(x, w_sup[:, :pad])
        up_part = dot(x, w_sup[:, pad:])
        back = dot(c, w_sdown[...], ((1,), (1,)))
        silu, slope = silu_parts(gate_part, up_part)
        hid_shared[here, :] = low(silu * up_part)
        dpre_shared[here, :pad] = low(back * slope)
        dpre_shared[here, pad:] = low(back * silu)
        out, drow, dgate = routed(0, here, x, c)
        out = out + dot(hid_shared[here, :], w_sdown[...])
        drow = drow + dot(dpre_shared[here, :], w_sup[...], ((1,), (1,)))
        marks = mark(0, dgate, jnp.zeros((ROWS, 128), F32))
        out_part[here, :] = low(out)
        for j in range(ROWS // tokens):
            rows = slice(j * tokens, (j + 1) * tokens)
            part[i * (ROWS // tokens) + j, :, :width] = low(drow[rows])
            part[i * (ROWS // tokens) + j, :, width:] = low(marks[rows])

    half = length // ROWS // 2

    @pl.loop(0, half)
    def _(i):
        first_pass(i)

    arrive[1]()

    @pl.loop(half, 2 * half)
    def _(i):
        first_pass(i)

    loads[2].wait()
    arrive[2]()

    @pl.loop(0, length // ROWS)
    def _(i):
        here = pl.ds(pl.multiple_of(i * ROWS, ROWS), ROWS)
        out, drow, dgate = routed(1, here, n2[here, :], cot[here, :])
        out_part[here, :] = low(out_part[here, :].astype(F32) + out)
        for j in range(ROWS // tokens):
            rows = slice(j * tokens, (j + 1) * tokens)
            block = i * (ROWS // tokens) + j
            part[block, :, :width] = low(part[block, :, :width].astype(F32) + drow[rows])
            marks = part[block, :, width:].astype(F32)
            high = low(dgate[rows]).astype(F32)
            marks = jnp.where(lane[rows] == 2 * e + 1, high, marks)
            marks = jnp.where(lane[rows] == 2 * e + 17, dgate[rows] - high, marks)
            part[block, :, width:] = low(marks)

    stages[0]()

    def up_gradient(k, up_ref):
        @pl.loop(0, width // COLS)
        def _(i):
            here = pl.ds(pl.multiple_of(i * COLS, COLS), COLS)
            up_w[k, here, :] = low(dot(n2[:, here], dpre[k], ((0,), (0,))))

        store = pltpu.make_async_copy(up_w.at[k], up_ref, store_sem.at[k])
        store.start()
        return store

    def down_gradient(k):
        @pl.loop(0, hidden // 128)
        def _(i):
            here = pl.ds(pl.multiple_of(i * 128, 128), 128)
            down_w[k, here, :] = low(dot(hid[k, :, here], cot[...], ((0,), (0,))))

    down_gradient(0)
    reduce[0]()
    stages[1]()
    stores = [up_gradient(0, up_term_first)]
    stages[2]()
    reduce[1]()
    down_gradient(1)
    stores.append(pltpu.make_async_copy(down_w.at[1], down_term_second, store_sem.at[2]))
    stores[-1].start()
    stages[3]()
    stores.append(up_gradient(1, up_term_second))
    sdown_term[...] = low(dot(hid_shared[...], cot[...], ((0,), (0,))))

    @pl.loop(0, width // COLS)
    def _(i):
        here = pl.ds(pl.multiple_of(i * COLS, COLS), COLS)
        sup_term[here, :] = low(dot(n2[:, here], dpre_shared[...], ((0,), (0,))))

    row_sum[...] = stages[4]()
    reduce[2]()
    for copy in stores:
        copy.wait()


ROWS = 256
COLS = 256


def experts_phase(n2, cot, w_sup, w_sdown, gates, down_second, up_first, up_second, down_first):
    length, width = n2.shape
    hidden = down_first.shape[0]
    pad = w_sdown.shape[0]
    tokens = length // 8
    wide = width + 128
    return kernel_call(
        experts_kernel,
        [
            ((length, width), LOW),
            ((tokens, wide), F32),
            ((pad, width), LOW),
            ((width, 2 * pad), LOW),
            ((hidden // 4, width), F32),
            (up_first.shape, LOW),
            (up_first.shape, LOW),
            ((hidden, width), LOW),
        ],
        (n2, cot, w_sup, w_sdown, gates, down_second, up_first, up_second, down_first),
        [
            pltpu.VMEM((8, tokens, wide), LOW),
            pltpu.VMEM((2, *up_first.shape), LOW),
            pltpu.VMEM((2, hidden, width), LOW),
            pltpu.VMEM((2, length, hidden), LOW),
            pltpu.VMEM((2, length, 2 * hidden), LOW),
            pltpu.VMEM((length, pad), LOW),
            pltpu.VMEM((length, 2 * pad), LOW),
            pltpu.SemaphoreType.DMA((3,)),
            pltpu.SemaphoreType.DMA((3,)),
        ]
        + SPREAD_SEMS
        + reduce_scratch((hidden // 8, width))
        + scatter_scratch(tokens, wide)
        + SCATTER_SEMS,
        4,
        far_outs=(5, 6, 7),
        far_args=(6, 7, 8),
    )


def turn_kernel(
    row_sum, out_part, upstream, gates, w_router, resid, gain, w_out, attn, n2, up_term, down_term,
    dresid, small, out_term, darrived, output_rows, up_grad, down_grad,
    dattn, a_send, a_recv, *scratch,
):
    b, e, z, core = place()
    greet([(b ^ 1, e), (b ^ 2, e), *pack_mates()])
    reduces = [
        reduce_rows(up_term, up_grad, scratch[:REDUCE_COUNT]),
        reduce_rows(down_term, down_grad, scratch[REDUCE_COUNT : 2 * REDUCE_COUNT]),
    ]
    scratch = scratch[2 * REDUCE_COUNT :]
    out_stages = line_sum_stages(out_part, *scratch)
    out_stages[0]()
    for start, _, _ in reduces:
        start()
    holds, pair = holder(e)
    total = row_sum[...]
    width = upstream.shape[1]
    experts = gates.shape[1]
    dgate = total[:, width : width + experts] + total[:, width + experts : width + 2 * experts]
    own = gates[...]
    dlog = low(own * (dgate - jnp.sum(own * dgate, axis=1, keepdims=True)))
    dn2 = total[:, :width] + dot(dlog, w_router[...])
    rows = resid[...]
    inv = lax.rsqrt(jnp.mean(rows * rows, axis=1, keepdims=True) + EPSILON)
    xhat = rows * inv
    small[experts : experts + 1, :] = jnp.sum(dn2 * xhat, axis=0, keepdims=True)
    scaled = dn2 * gain[...]
    grad = upstream[...] + inv * (scaled - xhat * jnp.mean(scaled * xhat, axis=1, keepdims=True))
    dresid[...] = grad
    back = low(dot(low(grad), w_out[...], ((1,), (1,))))
    size = dattn.shape[2]

    def give(source, index):
        return send(dattn.at[index], darrived.at[e], a_send.at[index], a_recv.at[e], (b, source))

    for source, index in PAIR_OF.items():
        dattn[index] = back[:, index * size : (index + 1) * size]

        @pl.when(e != source)
        def _():
            give(source, index).start()

    out_stages[1]()
    reduces[0][1]()
    small[:experts, :] = dot(dlog, n2[...], ((0,), (0,)))
    small[experts + 1 :, :] = jnp.zeros((small.shape[0] - experts - 1, width), F32)
    out_stages[2]()
    grad_low = low(dresid[...])
    for index in range(len(PAIR_OF)):
        out_term[index * size : (index + 1) * size, :] = low(
            dot(attn[index], grad_low, ((0,), (0,)))
        )
    reduces[1][1]()
    out_stages[3]()

    @pl.when(jnp.logical_not(holds))
    def _():
        darrived[...] = jnp.zeros_like(darrived)

    @pl.when(holds)
    def _():
        darrived[e] = dattn[pair]
        for i in range(1, 8):
            other = lax.rem(e + i, 8)
            block = darrived.at[other]
            send(block, block, a_send.at[0], a_recv.at[other], (b, other)).wait_recv()

    output_rows[...] = resid[...] + out_stages[4]()
    for _, _, finish in reduces:
        finish()
    for source, index in PAIR_OF.items():

        @pl.when(e != source)
        def _():
            give(source, index).wait_send()


def turn(row_sum, out_part, upstream, gates, w_router, resid, gain, w_out, attn, n2, up_term, down_term):
    tokens, width = upstream.shape
    pair = 2 * HEAD
    count = len(PAIR_OF)
    up_rows, down_rows = up_term.shape[0] // 4, down_term.shape[0] // 4
    return kernel_call(
        turn_kernel,
        [
            ((tokens, width), F32),
            ((gates.shape[1] + 8, width), F32),
            ((width, width), LOW),
            ((8, tokens, pair), LOW),
            ((tokens, width), F32),
            ((up_rows, up_term.shape[1]), F32),
            ((down_rows, down_term.shape[1]), F32),
        ],
        (row_sum, out_part, upstream, gates, w_router, resid, gain, w_out, attn, n2, up_term, down_term),
        [
            pltpu.VMEM((count, tokens, pair), LOW),
            pltpu.SemaphoreType.DMA((count,)),
            pltpu.SemaphoreType.DMA((8,)),
        ]
        + reduce_scratch((up_rows // 2, up_term.shape[1]), True)
        + reduce_scratch((down_rows // 2, down_term.shape[1]), True)
        + scatter_scratch(tokens, width)
        + SCATTER_SEMS,
        2,
        far_args=(10, 11),
    )


PARTNERS = ((0, 1), (1, 0), (2, 0), (0, 2), (0, 4))


def closing_kernel(
    dattn, qkv, logsum, n1, weights, cosine, sine, ids_row, ids_column, rows, gain, dresid,
    up_term, sdown_term, sup_term, out_term, small,
    input_grad, columns, out_grad, up_grad, sdown_grad, small_sum,
    dkey, dvalue, dprojected, part, column_term, column_sum, column_low,
    out_near, out_sum, out_low, out_half, out_got, small_got, small_step,
    n_send, n_recv, o_send, o_recv, c_send, c_recv, s_send, s_recv, *scratch,
):
    b, e, z, core = place()
    length = n1.shape[0]
    tokens = rows.shape[0]
    mates = pack_mates()
    greet([(b ^ 1, e), (b ^ 2, e), *mates])
    holds, pair = holder(e)

    def cut():
        nonlocal scratch
        mine, scratch = scratch[:REDUCE_COUNT], scratch[REDUCE_COUNT:]
        return mine

    up = reduce_rows(up_term, up_grad, cut())
    sdown = reduce_rows(sdown_term, sdown_grad, cut())
    column = reduce_rows(column_term, column_sum, cut())
    out = reduce_stages(
        lambda owner, half: out_sum.at[owner, pl.ds(2 * half, 2)],
        lambda half: out_half.at[pl.ds(2 * half, 2)],
        *cut(),
    )
    stages = line_sum_stages(part, *scratch)

    def partner(i):
        batch_bit, expert_bit = PARTNERS[i]
        src = small if i == 0 else small_step.at[i - 1]
        device = (b ^ batch_bit, e ^ expert_bit)
        return send(src, small_got.at[i], s_send.at[i], s_recv.at[i], device)

    def small_round(i):
        partner(i).wait_recv()
        before = small[...] if i == 0 else small_step[i - 1]
        if i < len(PARTNERS) - 1:
            small_step[i] = before + small_got[i]
            partner(i + 1).start()
        else:
            small_sum[...] = before + small_got[i]

    near = send(
        out_term.at[:, :, 1 - core], out_near, n_send.at[0], n_recv.at[0], (b, e ^ 1)
    )
    near.start()
    own = pltpu.make_async_copy(out_term.at[:, :, core], out_sum, n_send.at[1])
    own.start()
    partner(0).start()
    up[0]()

    def attend(head):
        dkey[...] = jnp.zeros_like(dkey)
        dvalue[...] = jnp.zeros_like(dvalue)
        lanes = pl.ds(head * HEAD, HEAD)
        for i in range(length // BLOCK):
            here = pl.ds(i * BLOCK, BLOCK)
            keys = (i + 1) * BLOCK
            count = BLOCK // tokens
            back = jnp.concatenate(
                [dattn[count * i + j, :, lanes] for j in range(count)], axis=0
            )
            query = qkv[head, here, :]
            scores = dot(query, qkv[2 + head, :keys, :], ((1,), (1,))) * HEAD ** (-0.5)
            weight = jnp.where(
                allowed_here(ids_column, ids_row, i, keys),
                jnp.exp(scores - logsum[head, here, 0:1]),
                0.0,
            )
            dprob = dot(back, qkv[4 + head, :keys, :], ((1,), (1,)))
            delta = jnp.sum(weight * dprob, axis=1, keepdims=True)
            dscore = low(weight * (dprob - delta))
            dquery = dot(dscore, qkv[2 + head, :keys, :]) * HEAD ** (-0.5)
            dkey[:keys, :] += dot(dscore, query, ((0,), (0,)))
            dvalue[:keys, :] += dot(low(weight), back, ((0,), (0,)))
            dprojected[here, lanes] = low(turned(dquery, cosine[here, :], -sine[here, :]))
        dprojected[:, (2 + head) * HEAD : (3 + head) * HEAD] = low(
            turned(dkey[...] * HEAD ** (-0.5), cosine[...], -sine[...])
        )
        dprojected[:, (4 + head) * HEAD : (5 + head) * HEAD] = low(dvalue[...])

    @pl.when(holds)
    def _():
        attend(0)

    near.wait()
    own.wait()
    for owner in range(4):
        for owner_z in range(4):
            out_sum[owner, owner_z] = low(
                out_sum[owner, owner_z].astype(F32) + out_near[owner, owner_z].astype(F32)
            )
    small_round(0)
    up[1]()

    @pl.when(holds)
    def _():
        attend(1)
        for i in range(8):
            part[i] = low(
                dot(
                    dprojected[i * tokens : (i + 1) * tokens, :],
                    weights[:, : 6 * HEAD],
                    ((1,), (1,)),
                )
            )

    @pl.when(jnp.logical_not(holds))
    def _():
        part[...] = jnp.zeros_like(part)

    stages[0]()
    column_term[:, 6 * HEAD :] = sup_term[...]

    @pl.when(holds)
    def _():
        for i in range(n1.shape[1] // BLOCK):
            here = pl.ds(i * BLOCK, BLOCK)
            column_term[here, : 6 * HEAD] = low(dot(n1[:, here], dprojected[...], ((0,), (0,))))

    @pl.when(jnp.logical_not(holds))
    def _():
        column_term[:, : 6 * HEAD] = jnp.zeros((n1.shape[1], 6 * HEAD), LOW)

    column[0]()
    stages[1]()
    out[0]()
    small_round(1)
    stages[2]()
    column[1]()
    sdown[0]()
    stages[3]()
    small_round(2)
    out[1]()
    small_round(3)
    values = rows[...]
    inv = lax.rsqrt(jnp.mean(values * values, axis=1, keepdims=True) + EPSILON)
    xhat = values * inv
    scaled = stages[4]() * gain[...]
    input_grad[...] = dresid[...] + inv * (
        scaled - xhat * jnp.mean(scaled * xhat, axis=1, keepdims=True)
    )
    column[2]()
    piece = column_low.shape[1]
    for i in range(0, 8, 2):
        two = column_sum[i * piece : (i + 2) * piece, :].astype(F32)
        column_low[i] = low(two[:piece])
        column_low[i + 1] = low(two[piece:])
    columns[e] = column_low[e]
    across = []
    for i, device in enumerate(mates):
        across.append(
            send(column_low.at[device[1]], columns.at[e], c_send.at[i], c_recv.at[i], device)
        )
        across[-1].start()
    sdown[1]()
    small_round(4)
    for i in range(len(PARTNERS)):
        partner(i).wait_send()
    out[2]()
    for owner_z in range(4):
        out_low[owner_z] = low(out_half[owner_z])
    along = []
    for i in range(3):
        device = (b, lax.rem(e + 2 * i + 2, 8))
        along.append(
            send(
                out_low.at[device[1] // 2], out_got.at[i], o_send.at[i], o_recv.at[i], device
            )
        )
        along[-1].start()
    up[2]()
    for copy in along:
        copy.wait()
    out_grad[...] = (
        out_half[z]
        + out_got[0].astype(F32)
        + out_got[1].astype(F32)
        + out_got[2].astype(F32)
    )
    sdown[2]()
    for copy in across:
        copy.wait()


def closing(
    dattn, qkv, logsum, n1, weights, cosine, sine, ids_row, ids_column, rows, gain, dresid,
    up_term, sdown_term, sup_term, out_term, small,
):
    tokens, width = rows.shape
    length = n1.shape[0]
    rows_w = out_term.shape[3]
    wide = weights.shape[1]
    up_rows, sdown_rows = up_term.shape[0] // 4, sdown_term.shape[0] // 4
    dma = pltpu.SemaphoreType.DMA
    return kernel_call(
        closing_kernel,
        [
            ((tokens, width), F32),
            ((8, rows_w, wide), LOW),
            ((rows_w, width), F32),
            ((up_rows, up_term.shape[1]), F32),
            ((sdown_rows, width), F32),
            (small.shape, F32),
        ],
        (
            dattn, qkv, logsum, n1, weights, cosine, sine, ids_row, ids_column, rows, gain, dresid,
            up_term, sdown_term, sup_term, out_term, small,
        ),
        [
            pltpu.VMEM((length, HEAD), F32),
            pltpu.VMEM((length, HEAD), F32),
            pltpu.VMEM((length, 6 * HEAD), LOW),
            pltpu.VMEM((8, tokens, width), LOW),
            pltpu.VMEM((width, wide), LOW),
            pltpu.VMEM((width // 4, wide), LOW),
            pltpu.VMEM((8, rows_w, wide), LOW),
            pltpu.VMEM((4, 4, rows_w, width), LOW),
            pltpu.VMEM((4, 4, rows_w, width), LOW),
            pltpu.VMEM((4, rows_w, width), LOW),
            pltpu.VMEM((4, rows_w, width), F32),
            pltpu.VMEM((3, rows_w, width), LOW),
            pltpu.VMEM((5, *small.shape), F32),
            pltpu.VMEM((4, *small.shape), F32),
            dma((2,)), dma((1,)), dma((3,)), dma((3,)), dma((7,)), dma((7,)), dma((5,)), dma((5,)),
        ]
        + reduce_scratch((up_rows // 2, up_term.shape[1]), True)
        + reduce_scratch((sdown_rows // 2, width))
        + reduce_scratch((width // 8, wide))
        + reduce_scratch((2, rows_w, width))
        + scatter_scratch(tokens, width)
        + SCATTER_SEMS,
        3,
        far_args=(12, 15),
    )


def silu_parts(gate, up):
    sigma = jax.nn.sigmoid(gate)
    return gate * sigma, up * sigma * (1.0 + gate * (1.0 - sigma))


def rotary_angles(length):
    half = HEAD // 2
    frequency = np.float32(10000.0) ** (-np.arange(half, dtype=np.float32) / np.float32(half))
    return np.arange(length, dtype=np.float32)[:, None] * frequency[None, :]


def pack_device(
    block_input,
    seq_ids,
    routes,
    cotangent,
    qkv_weight,
    out_weight,
    shared_up,
    shared_down,
    router_weight,
    gain_attn,
    gain_ffn,
    expert_up,
    expert_down,
):
    b = lax.axis_index("batch")
    e = lax.axis_index("expert")
    rows_in = block_input[0]
    upstream = cotangent[0]
    tokens, width = rows_in.shape
    length = tokens * 8
    rows_w = qkv_weight.shape[0]
    pair = 2 * HEAD
    pairs_of_heads = width // pair
    hidden = expert_up.shape[2] // 2
    experts = expert_up.shape[0] * 8
    s_rows = shared_down.shape[0]
    s_each = -(-s_rows // 32) * 32
    s_pad = 4 * s_each

    sup_low = low(shared_up).reshape(rows_w, 2, 4, 8, s_rows)
    sup_low = jnp.pad(sup_low, ((0, 0),) * 4 + ((0, s_each - s_rows),)).transpose(3, 0, 1, 2, 4)
    n1_all, gains, small, marks, columns, w_out, up_first = opening(
        rows_in,
        router_weight.reshape(-1, 128),
        gain_attn[None],
        gain_ffn[None],
        routes,
        seq_ids,
        qkv_weight,
        sup_low.reshape(8, rows_w, 2 * s_pad),
        out_weight,
        expert_up,
    )
    n1_all = n1_all.reshape(length, width)
    columns = columns.reshape(width, 3 * pair + 2 * s_pad)
    w_out = w_out.reshape(width, width)
    router_rows = rows_w * experts // 128
    w_router = low(small[:, :, :router_rows].transpose(1, 0, 2, 3).reshape(width, experts))
    gain_first = gains[0:1]
    gain_second = gains[1:2]
    marks = marks.astype(jnp.int32).transpose(0, 2, 1).reshape(length, 8)
    route_all = marks[:, :TOP]
    ids_all = marks[:, TOP]
    positions = jnp.arange(length, dtype=jnp.int32)
    ids_row = ids_all[None, :]
    ids_column = ids_all[:, None]
    angle = rotary_angles(length)
    cosine = np.concatenate([np.cos(angle)] * 2, axis=1)
    sine = np.concatenate([-np.sin(angle), np.sin(angle)], axis=1)
    qkv, logsum, attn, resid, n2_all, cot_all, up_second, down_low, w_sdown, down_second = middle(
        n1_all,
        columns,
        jnp.asarray(cosine),
        jnp.asarray(sine),
        ids_row,
        ids_column,
        w_out,
        rows_in,
        gain_second,
        cotangent,
        expert_up,
        expert_down,
        shared_down,
    )
    cot_all = cot_all.reshape(length, width)

    n2 = lax.dynamic_index_in_dim(n2_all, e, 0, False)
    n2_all = n2_all.reshape(length, width)
    logits = dot(n2_all, w_router)
    hot = route_all[:, :, None] == jnp.arange(experts, dtype=jnp.int32)[None, None, :]
    routed_to = jnp.any(hot, axis=1)
    logits = jnp.where(routed_to, logits, NEGATIVE)
    gates = jnp.where(routed_to, jnp.exp(logits - jnp.max(logits, axis=1, keepdims=True)), 0.0)
    gates = gates / jnp.sum(gates, axis=1, keepdims=True)
    mine = lax.dynamic_slice_in_dim(gates, 2 * e, 2, 1)

    output_part, row_sum, sdown_term, sup_term, down_grad_first, *terms = experts_phase(
        n2_all,
        cot_all,
        columns[:, 3 * pair :],
        w_sdown,
        mine,
        down_second,
        up_first,
        up_second,
        down_low,
    )
    up_terms, down_term_second = terms[:2], terms[2]
    own_gates = lax.dynamic_slice_in_dim(gates, e * tokens, tokens, 0)
    dresid, small, out_term, dattn, output_rows, up_grad_first, down_grad_second = turn(
        row_sum,
        output_part.reshape(8, tokens, width),
        upstream,
        own_gates,
        w_router.T,
        resid,
        gain_second,
        w_out,
        attn,
        n2,
        up_terms[0],
        down_term_second,
    )
    out_term = out_term.reshape(4, 4, 2, rows_w, width)
    input_grad, columns, out_grad, up_grad_second, sdown_grad, small = closing(
        dattn,
        qkv,
        logsum,
        n1_all,
        columns,
        jnp.asarray(cosine),
        jnp.asarray(sine),
        ids_row,
        ids_column,
        rows_in,
        gain_first,
        dresid,
        up_terms[1],
        sdown_term,
        sup_term,
        out_term,
        small,
    )
    expert_up_grad = jnp.stack([up_grad_first, up_grad_second])
    expert_down_grad = jnp.stack([down_grad_first, down_grad_second])
    shared_down_grad = sdown_grad[:s_rows]
    small = lax.dynamic_slice_in_dim(small, (b * 8 + e) * rows_w, rows_w, 1)
    columns = columns.astype(F32)
    qkv_grad = jnp.stack([columns[i, :, : 3 * pair] for i in PAIR_OF])
    qkv_grad = qkv_grad.reshape(pairs_of_heads, rows_w, 3, pair).transpose(1, 2, 0, 3)
    qkv_grad = qkv_grad.reshape(rows_w, 3 * width)
    sup_grad = columns[:, :, 3 * pair :].reshape(8, rows_w, 2, 4, s_each)[..., :s_rows]
    sup_grad = sup_grad.transpose(1, 2, 3, 0, 4)
    sup_grad = sup_grad.reshape(rows_w, shared_up.shape[1])
    own_first = low(gain_attn).astype(F32)
    gain_attn_grad = jnp.sum(low(qkv_weight).astype(F32) * qkv_grad, axis=1) / own_first
    return (
        output_rows[None],
        input_grad[None],
        qkv_grad,
        out_grad,
        sup_grad,
        shared_down_grad,
        small[:experts].T,
        gain_attn_grad,
        small[experts],
        expert_up_grad,
        expert_down_grad,
    )


def solution(mesh):
    in_specs = (
        P("batch", "expert", None),
        P("batch", "expert"),
        P("batch", "expert", None),
        P("batch", "expert", None),
        P(("batch", "expert"), None),
        P(("batch", "expert"), None),
        P(("batch", "expert"), None),
        P(("batch", "expert"), None),
        P(("batch", "expert"), None),
        P(("batch", "expert")),
        P(("batch", "expert")),
        P("expert", "batch", None),
        P("expert", "batch", None),
    )
    out_specs = (
        P("batch", "expert", None),
        P("batch", "expert", None),
        P(("batch", "expert"), None),
        P(("batch", "expert"), None),
        P(("batch", "expert"), None),
        P(("batch", "expert"), None),
        P(("batch", "expert"), None),
        P(("batch", "expert")),
        P(("batch", "expert")),
        P("expert", "batch", None),
        P("expert", "batch", None),
    )
    sizes = dict(mesh.shape)
    body = pack_device if sizes == {"batch": 4, "expert": 8} else per_device
    return jax.shard_map(
        body, mesh=mesh, in_specs=in_specs, out_specs=out_specs, check_vma=False
    )
```

```python
import functools

import jax
import jax.numpy as jnp
import numpy as np
from jax import lax
from jax.experimental import pallas as pl
from jax.experimental.pallas import tpu as pltpu
from jax.sharding import PartitionSpec as P

HEAD = 128
TOP = 6


EPSILON = 1e-06
NEGATIVE = -1e30


def rotate(values, positions, sign):
    half = values.shape[-1] // 2
    frequency = 10000.0 ** (-jnp.arange(half, dtype=jnp.float32) / half)
    angle = positions.astype(jnp.float32)[:, None] * frequency[None, :]
    cosine = jnp.cos(angle)[:, None, :]
    sine = sign * jnp.sin(angle)[:, None, :]
    first = values[..., :half]
    second = values[..., half:]
    return jnp.concatenate(
        [first * cosine - second * sine, first * sine + second * cosine], axis=-1
    )


def swiglu(pre, hidden_width):
    return jax.nn.silu(pre[..., :hidden_width]) * pre[..., hidden_width:]


def swiglu_back(pre, dhidden, hidden_width):
    gate_part = pre[..., :hidden_width]
    up_part = pre[..., hidden_width:]
    sigma = jax.nn.sigmoid(gate_part)
    dgate = dhidden * up_part * sigma * (1.0 + gate_part * (1.0 - sigma))
    dupper = dhidden * gate_part * sigma
    return jnp.concatenate([dgate, dupper], axis=-1)


def norm_back(dnormed, normed, inv_rms, gain):
    dscaled = dnormed * gain
    dinputs = inv_rms * (dscaled - normed * jnp.mean(dscaled * normed, axis=1, keepdims=True))
    return (dinputs, jnp.sum(dnormed * normed, axis=0))


def per_device(
    block_input,
    seq_ids,
    routes,
    cotangent,
    qkv_weight,
    out_weight,
    shared_up,
    shared_down,
    router_weight,
    gain_attn,
    gain_ffn,
    expert_up,
    expert_down,
):
    dense = (
        lax.all_gather(qkv_weight.astype(jnp.bfloat16), ("batch", "expert"), axis=0, tiled=True),
        lax.all_gather(out_weight.astype(jnp.bfloat16), ("batch", "expert"), axis=0, tiled=True),
        lax.all_gather(shared_up.astype(jnp.bfloat16), ("batch", "expert"), axis=0, tiled=True),
        lax.all_gather(shared_down.astype(jnp.bfloat16), ("batch", "expert"), axis=0, tiled=True),
        lax.all_gather(router_weight.astype(jnp.bfloat16), ("batch", "expert"), axis=0, tiled=True),
        lax.all_gather(gain_attn.astype(jnp.bfloat16), ("batch", "expert"), axis=0, tiled=True),
        lax.all_gather(gain_ffn.astype(jnp.bfloat16), ("batch", "expert"), axis=0, tiled=True),
    )
    full_qkv, full_out, full_sup, full_sdown, full_router, low_gain_a, low_gain_f = dense
    gain_first = low_gain_a.astype(jnp.float32)
    gain_second = low_gain_f.astype(jnp.float32)
    experts_up, experts_down = (
        lax.all_gather(expert_up.astype(jnp.bfloat16), "batch", axis=1, tiled=True),
        lax.all_gather(expert_down.astype(jnp.bfloat16), "batch", axis=1, tiled=True),
    )
    rows_in = block_input[0]
    ids_local = seq_ids[0]
    route_local = routes[0]
    upstream = cotangent[0]
    tokens_dev = rows_in.shape[0]
    model_width = rows_in.shape[1]
    heads_count = model_width // HEAD
    groups = lax.axis_size("expert")
    local_experts = experts_up.shape[0]
    experts_all = local_experts * groups
    shared_width = full_sdown.shape[0]
    hidden_width = experts_down.shape[1]
    capacity = max(2, tokens_dev * TOP * 3 // (experts_all * 2))
    score_scale = HEAD ** (-0.5)
    positions = lax.axis_index("expert") * tokens_dev + jnp.arange(tokens_dev, dtype=jnp.int32)
    key_ids = lax.all_gather(ids_local, "expert", axis=0, tiled=True)
    inv_first = lax.rsqrt(jnp.mean(rows_in * rows_in, axis=1, keepdims=True) + EPSILON)
    normed_first = rows_in * inv_first
    input_low = (normed_first * gain_first).astype(jnp.bfloat16)
    projected = jnp.dot(input_low, full_qkv, preferred_element_type=jnp.float32)
    queries = rotate(
        projected[:, :model_width].reshape(tokens_dev, heads_count, HEAD), positions, 1.0
    ).astype(jnp.bfloat16)
    keys = rotate(
        projected[:, model_width : 2 * model_width].reshape(tokens_dev, heads_count, HEAD),
        positions,
        1.0,
    ).astype(jnp.bfloat16)
    values = (
        projected[:, 2 * model_width :].reshape(tokens_dev, heads_count, HEAD).astype(jnp.bfloat16)
    )

    def key_mask(key_count):
        key_pos = jnp.arange(key_count, dtype=jnp.int32)
        return (key_pos[None, :] <= positions[:, None]) & (key_ids[None, :] == ids_local[:, None])

    run_max = jnp.full((heads_count, tokens_dev), NEGATIVE, jnp.float32)
    key_piece = lax.all_gather(keys, "expert", axis=0, tiled=True)
    value_piece = lax.all_gather(values, "expert", axis=0, tiled=True)
    allowed = key_mask(key_piece.shape[0])[None]
    scores = (
        jnp.einsum("qhd,khd->hqk", queries, key_piece, preferred_element_type=jnp.float32)
        * score_scale
    )
    scores = jnp.where(allowed, scores, NEGATIVE)
    new_max = jnp.maximum(run_max, jnp.max(scores, axis=2))
    weights = jnp.where(allowed, jnp.exp(scores - new_max[:, :, None]), 0.0)
    run_sum = jnp.sum(weights, axis=2)
    update = jnp.einsum(
        "hqk,khd->qhd",
        weights.astype(jnp.bfloat16),
        value_piece,
        preferred_element_type=jnp.float32,
    )
    run_acc = update
    run_max, run_sum, run_acc = (new_max, run_sum, run_acc)
    attn_full = run_acc / jnp.transpose(run_sum)[:, :, None]
    logsum = run_max + jnp.log(run_sum)
    attn_low = attn_full.reshape(tokens_dev, model_width).astype(jnp.bfloat16)
    resid = rows_in + jnp.dot(attn_low, full_out, preferred_element_type=jnp.float32)
    inv_second = lax.rsqrt(jnp.mean(resid * resid, axis=1, keepdims=True) + EPSILON)
    normed_second = resid * inv_second
    ffn_low = (normed_second * gain_second).astype(jnp.bfloat16)
    logits = jnp.dot(ffn_low, full_router, preferred_element_type=jnp.float32)
    probs = jax.nn.softmax(logits, axis=1)
    route_hot = route_local[:, :, None] == jnp.arange(experts_all, dtype=jnp.int32)[None, None, :]
    chosen = jnp.sum(jnp.where(route_hot, probs[:, None, :], 0.0), axis=2)
    chosen_sum = jnp.sum(chosen, axis=1, keepdims=True)
    gates = chosen / chosen_sum
    shared_pre = jnp.dot(ffn_low, full_sup, preferred_element_type=jnp.float32)
    shared_hidden = swiglu(shared_pre, shared_width).astype(jnp.bfloat16)
    shared_result = jnp.dot(shared_hidden, full_sdown, preferred_element_type=jnp.float32)
    flat_route = route_local.reshape(-1)
    flat_hot = (flat_route[:, None] == jnp.arange(experts_all, dtype=jnp.int32)[None, :]).astype(
        jnp.bfloat16
    )
    pair_count = tokens_dev * TOP
    pair_index = jnp.arange(pair_count, dtype=jnp.int32)
    earlier = (pair_index[None, :] < pair_index[:, None]).astype(jnp.bfloat16)
    counts = jnp.dot(earlier, flat_hot, preferred_element_type=jnp.float32)
    slots = jnp.sum(counts * flat_hot, axis=1).astype(jnp.int32)
    source_table = (
        jnp.full((experts_all * capacity,), pair_count, jnp.int32)
        .at[flat_route * capacity + slots]
        .set(jnp.arange(pair_count, dtype=jnp.int32))
    )
    send_table = jnp.transpose(
        source_table.reshape(groups, local_experts, capacity), (1, 0, 2)
    ).reshape(-1)
    return_pos = (
        flat_route % local_experts * (groups * capacity)
        + flat_route // local_experts * capacity
        + slots
    )
    padded_rows = jnp.concatenate([ffn_low, jnp.zeros((1, model_width), jnp.bfloat16)], axis=0)
    send_rows = padded_rows[send_table // TOP].reshape(local_experts, groups, capacity, model_width)
    received = lax.all_to_all(send_rows, "expert", split_axis=1, concat_axis=1, tiled=True)
    expert_rows = received.reshape(local_experts, groups * capacity, model_width)
    expert_pre = jnp.einsum(
        "erd,edf->erf", expert_rows, experts_up, preferred_element_type=jnp.float32
    )
    expert_hidden = swiglu(expert_pre, hidden_width).astype(jnp.bfloat16)
    expert_result = jnp.einsum(
        "erf,efd->erd", expert_hidden, experts_down, preferred_element_type=jnp.float32
    ).astype(jnp.bfloat16)
    returned = lax.all_to_all(
        expert_result.reshape(local_experts, groups, capacity, model_width),
        "expert",
        split_axis=1,
        concat_axis=1,
        tiled=True,
    )
    token_outputs = returned.reshape(-1, model_width)[return_pos].reshape(
        tokens_dev, TOP, model_width
    )
    routed = jnp.sum(gates[:, :, None] * token_outputs, axis=1)
    output_rows = resid + shared_result + routed
    shared_cot = upstream.astype(jnp.bfloat16)
    shared_down_term = jnp.dot(shared_hidden.T, shared_cot, preferred_element_type=jnp.float32)
    dshared_hidden = jnp.dot(shared_cot, full_sdown.T, preferred_element_type=jnp.float32)
    dshared_pre = swiglu_back(shared_pre, dshared_hidden, shared_width).astype(jnp.bfloat16)
    shared_up_term = jnp.dot(ffn_low.T, dshared_pre, preferred_element_type=jnp.float32)
    dnormed_second = jnp.dot(dshared_pre, full_sup.T, preferred_element_type=jnp.float32)
    token_cot = (gates[:, :, None] * upstream[:, None, :]).astype(jnp.bfloat16)
    dgates = jnp.sum(upstream[:, None, :] * token_outputs, axis=2)
    padded_cot = jnp.concatenate(
        [token_cot.reshape(-1, model_width), jnp.zeros((1, model_width), jnp.bfloat16)], axis=0
    )
    send_cot = padded_cot[send_table].reshape(local_experts, groups, capacity, model_width)
    received_cot = lax.all_to_all(
        send_cot, "expert", split_axis=1, concat_axis=1, tiled=True
    ).reshape(local_experts, groups * capacity, model_width)
    down_term = jnp.einsum(
        "erf,erd->efd", expert_hidden, received_cot, preferred_element_type=jnp.float32
    )
    dexpert_hidden = jnp.einsum(
        "erd,efd->erf", received_cot, experts_down, preferred_element_type=jnp.float32
    )
    dexpert_pre = swiglu_back(expert_pre, dexpert_hidden, hidden_width).astype(jnp.bfloat16)
    up_term = jnp.einsum(
        "erd,erf->edf", expert_rows, dexpert_pre, preferred_element_type=jnp.float32
    )
    drows = jnp.einsum(
        "erf,edf->erd", dexpert_pre, experts_up, preferred_element_type=jnp.float32
    ).astype(jnp.bfloat16)
    returned_grad = lax.all_to_all(
        drows.reshape(local_experts, groups, capacity, model_width),
        "expert",
        split_axis=1,
        concat_axis=1,
        tiled=True,
    )
    row_grads = returned_grad.reshape(-1, model_width)[return_pos].reshape(
        tokens_dev, TOP, model_width
    )
    dnormed_second = dnormed_second + jnp.sum(row_grads, axis=1, dtype=jnp.float32)
    expert_up_grad, expert_down_grad = (
        lax.psum_scatter(
            up_term.astype(jnp.bfloat16), "batch", scatter_dimension=1, tiled=True
        ).astype(jnp.float32),
        lax.psum_scatter(
            down_term.astype(jnp.bfloat16), "batch", scatter_dimension=1, tiled=True
        ).astype(jnp.float32),
    )
    dchosen = (dgates - jnp.sum(dgates * gates, axis=1, keepdims=True)) / chosen_sum
    dprobs = jnp.sum(jnp.where(route_hot, dchosen[:, :, None], 0.0), axis=1)
    dlogits = (probs * (dprobs - jnp.sum(probs * dprobs, axis=1, keepdims=True))).astype(
        jnp.bfloat16
    )
    router_term = jnp.dot(ffn_low.T, dlogits, preferred_element_type=jnp.float32)
    dnormed_second = dnormed_second + jnp.dot(
        dlogits, full_router.T, preferred_element_type=jnp.float32
    )
    dresid_norm, gain_ffn_term = norm_back(dnormed_second, normed_second, inv_second, gain_second)
    dresid = upstream + dresid_norm
    dproj = dresid.astype(jnp.bfloat16)
    out_term = jnp.dot(attn_low.T, dproj, preferred_element_type=jnp.float32)
    dattn = (
        jnp.dot(dproj, full_out.T, preferred_element_type=jnp.float32)
        .astype(jnp.bfloat16)
        .reshape(tokens_dev, heads_count, HEAD)
    )
    delta_rows = jnp.sum(dattn.astype(jnp.float32) * attn_full, axis=2)
    delta_heads = jnp.transpose(delta_rows)
    key_piece = lax.all_gather(keys, "expert", axis=0, tiled=True)
    value_piece = lax.all_gather(values, "expert", axis=0, tiled=True)
    allowed = key_mask(key_piece.shape[0])[None]
    scores = (
        jnp.einsum("qhd,khd->hqk", queries, key_piece, preferred_element_type=jnp.float32)
        * score_scale
    )
    attn_probs = jnp.where(allowed, jnp.exp(scores - logsum[:, :, None]), 0.0)
    dprob = jnp.einsum("qhd,khd->hqk", dattn, value_piece, preferred_element_type=jnp.float32)
    dscore = (attn_probs * (dprob - delta_heads[:, :, None])).astype(jnp.bfloat16)
    attn_probs, dscore = (attn_probs, dscore)
    dquery = jnp.einsum("hqk,khd->qhd", dscore, key_piece, preferred_element_type=jnp.float32)
    dkey_piece = jnp.einsum("hqk,qhd->khd", dscore, queries, preferred_element_type=jnp.float32)
    dvalue_piece = jnp.einsum(
        "hqk,qhd->khd", attn_probs.astype(jnp.bfloat16), dattn, preferred_element_type=jnp.float32
    )
    folded = (dquery, dkey_piece, dvalue_piece)
    dquery = folded[0]
    dkey, dvalue = (
        lax.psum_scatter(
            folded[1].astype(jnp.bfloat16), "expert", scatter_dimension=0, tiled=True
        ).astype(jnp.float32),
        lax.psum_scatter(
            folded[2].astype(jnp.bfloat16), "expert", scatter_dimension=0, tiled=True
        ).astype(jnp.float32),
    )
    dquery_raw = rotate(dquery * score_scale, positions, -1.0).reshape(tokens_dev, model_width)
    dkey_raw = rotate(dkey * score_scale, positions, -1.0).reshape(tokens_dev, model_width)
    dprojected = jnp.concatenate(
        [dquery_raw, dkey_raw, dvalue.reshape(tokens_dev, model_width)], axis=1
    ).astype(jnp.bfloat16)
    qkv_term = jnp.dot(input_low.T, dprojected, preferred_element_type=jnp.float32)
    dnormed_first = jnp.dot(dprojected, full_qkv.T, preferred_element_type=jnp.float32)
    dinput_norm, gain_attn_term = norm_back(dnormed_first, normed_first, inv_first, gain_first)
    input_grad = dresid + dinput_norm
    grads = (
        lax.psum_scatter(qkv_term, ("batch", "expert"), scatter_dimension=0, tiled=True),
        lax.psum_scatter(out_term, ("batch", "expert"), scatter_dimension=0, tiled=True),
        lax.psum_scatter(shared_up_term, ("batch", "expert"), scatter_dimension=0, tiled=True),
        lax.psum_scatter(shared_down_term, ("batch", "expert"), scatter_dimension=0, tiled=True),
        lax.psum_scatter(router_term, ("batch", "expert"), scatter_dimension=0, tiled=True),
        lax.psum_scatter(gain_attn_term, ("batch", "expert"), scatter_dimension=0, tiled=True),
        lax.psum_scatter(gain_ffn_term, ("batch", "expert"), scatter_dimension=0, tiled=True),
    )
    (
        qkv_grad,
        out_grad,
        shared_up_grad,
        shared_down_grad,
        router_grad,
        gain_attn_grad,
        gain_ffn_grad,
    ) = grads
    return (
        output_rows[None],
        input_grad[None],
        qkv_grad,
        out_grad,
        shared_up_grad,
        shared_down_grad,
        router_grad,
        gain_attn_grad,
        gain_ffn_grad,
        expert_up_grad,
        expert_down_grad,
    )


PAIR_OF = {0: 0, 2: 1, 4: 2, 6: 3, 3: 4}
F32 = jnp.float32
LOW = jnp.bfloat16
COST = 10**9


def low(values):
    return values.astype(LOW)


def dot(left, right, dims=((1,), (0,))):
    return lax.dot_general(left, right, (dims, ((), ())), preferred_element_type=F32)


MESH_ID = pl.DeviceIdType.MESH


def place():
    b = lax.axis_index("batch")
    e = lax.axis_index("expert")
    return b, e, e // 2, lax.rem(e, 2)


def greet_near():
    b, e, z, core = place()
    barrier = pltpu.get_barrier_semaphore()
    for device in ((b ^ 1, e), (b ^ 2, e), (b, e ^ 1)):
        pl.semaphore_signal(barrier, inc=1, device_id=device, device_id_type=MESH_ID)

    @pl.when(z > 0)
    def _():
        pl.semaphore_signal(barrier, inc=1, device_id=(b, e - 2), device_id_type=MESH_ID)

    @pl.when(z < 3)
    def _():
        pl.semaphore_signal(barrier, inc=1, device_id=(b, e + 2), device_id_type=MESH_ID)

    ends = jnp.where((z == 0) | (z == 3), 1, 0)
    pl.semaphore_wait(barrier, 5 - ends)


def greet(devices):
    barrier = pltpu.get_barrier_semaphore()
    for device in devices:
        pl.semaphore_signal(barrier, inc=1, device_id=device, device_id_type=MESH_ID)
    pl.semaphore_wait(barrier, len(devices))


def pack_mates():
    b, e, _, _ = place()
    return [(b, lax.rem(e + i, 8)) for i in range(1, 8)]


def send(src, dst, send_sem, recv_sem, device):
    return pltpu.make_async_remote_copy(
        src_ref=src,
        dst_ref=dst,
        send_sem=send_sem,
        recv_sem=recv_sem,
        device_id=device,
        device_id_type=MESH_ID,
    )


GATHER_SEMS = [pltpu.SemaphoreType.DMA((3,))] * 4 + [pltpu.SemaphoreType.DMA((4,))] * 2


def line_stages(buf, up_send, up_recv, down_send, down_recv, core_send, core_recv):
    b, e, z, core = place()

    def to_core(owner_z):
        block = buf.at[2 * owner_z + core]
        return send(block, block, core_send.at[owner_z], core_recv.at[owner_z], (b, e ^ 1))

    def up(step):
        block = buf.at[jnp.maximum(2 * (z - step), 0) + core]
        return send(block, block, up_send.at[step], up_recv.at[step], (b, jnp.minimum(e + 2, 7)))

    def down(step):
        block = buf.at[jnp.minimum(2 * (z + step), 6) + core]
        return send(
            block, block, down_send.at[step], down_recv.at[step], (b, jnp.maximum(e - 2, 0))
        )

    def start(step):
        @pl.when((z >= step) & (z < 3))
        def _():
            up(step).start()

        @pl.when((z + step <= 3) & (z > 0))
        def _():
            down(step).start()

        if step == 0:
            to_core(z).start()

    def arrive(step):
        @pl.when(z - 1 - step >= 0)
        def _():
            up(step).wait_recv()

        @pl.when(z + 1 + step <= 3)
        def _():
            down(step).wait_recv()

        if step < 2:
            start(step + 1)

        @pl.when(z - 1 - step >= 0)
        def _():
            to_core(z - 1 - step).start()

        @pl.when(z + 1 + step <= 3)
        def _():
            to_core(z + 1 + step).start()

    def finish():
        for owner_z in range(4):
            to_core(owner_z).wait()
        for step in range(3):

            @pl.when((z >= step) & (z < 3))
            def _():
                up(step).wait_send()

            @pl.when((z + step <= 3) & (z > 0))
            def _():
                down(step).wait_send()

    return [lambda: start(0)] + [functools.partial(arrive, i) for i in range(3)] + [finish]


def line_gather(buf, *sems):
    for stage in line_stages(buf, *sems):
        stage()


def scatter_scratch(tokens, width):
    return [pltpu.VMEM((4, tokens, width), LOW)] + [
        pltpu.VMEM((3, tokens, width), LOW) for _ in range(4)
    ]


SCATTER_SEMS = [pltpu.SemaphoreType.DMA((3,))] * 4 + [pltpu.SemaphoreType.DMA((4,))] * 2


def line_sum_stages(
    part,
    from_core,
    up_out,
    up_in,
    down_out,
    down_in,
    up_send,
    up_recv,
    down_send,
    down_recv,
    core_send,
    core_recv,
):
    b, e, z, core = place()

    def to_core(target):
        return send(
            part.at[2 * target + 1 - core],
            from_core.at[target],
            core_send.at[target],
            core_recv.at[target],
            (b, e ^ 1),
        )

    def up(step):
        return send(
            up_out.at[step],
            up_in.at[step],
            up_send.at[step],
            up_recv.at[step],
            (b, jnp.minimum(e + 2, 7)),
        )

    def down(step):
        return send(
            down_out.at[step],
            down_in.at[step],
            down_send.at[step],
            down_recv.at[step],
            (b, jnp.maximum(e - 2, 0)),
        )

    def chip_sum(target):
        return part[2 * target + core].astype(F32) + from_core[target].astype(F32)

    def start():
        for target in (3, 0, 2, 1):
            to_core(target).start()

    def send_up(step):
        up_out[step] = low(chip_sum(3 - step))
        up(step).start()

    def send_down(step):
        down_out[step] = low(chip_sum(step))
        down(step).start()

    def pass_up(step):
        up(step).wait_recv()
        up_out[step] = low(chip_sum(3 - step) + up_in[step].astype(F32))
        up(step).start()

    def pass_down(step):
        down(step).wait_recv()
        down_out[step] = low(chip_sum(step) + down_in[step].astype(F32))
        down(step).start()

    def ends():
        for target in range(4):
            to_core(target).wait()

        @pl.when(z == 0)
        def _():
            for step in range(3):
                send_up(step)

        @pl.when(z == 3)
        def _():
            for step in range(3):
                send_down(step)

    def near():
        @pl.when(z == 1)
        def _():
            pass_up(0)

        @pl.when(z == 2)
        def _():
            pass_down(0)

    def far():
        @pl.when(z == 1)
        def _():
            pass_up(1)
            pass_down(0)

        @pl.when(z == 2)
        def _():
            pass_down(1)
            pass_up(0)

    def finish():
        @pl.when(z == 0)
        def _():
            up_in[0] = jnp.zeros_like(up_in[0])

        @pl.when(z == 3)
        def _():
            down_in[0] = jnp.zeros_like(down_in[0])

        last_up = lax.rem(3 - z, 3)
        last_down = lax.rem(z, 3)

        @pl.when(z > 0)
        def _():
            up(last_up).wait_recv()

        @pl.when(z < 3)
        def _():
            down(last_down).wait_recv()

        total = chip_sum(z) + up_in[last_up].astype(F32) + down_in[last_down].astype(F32)
        for step in range(3):

            @pl.when(z < 3 - step)
            def _():
                up(step).wait_send()

            @pl.when(z > step)
            def _():
                down(step).wait_send()

        return total

    return [start, ends, near, far, finish]


def sum_into(out, *terms):
    if len(out.shape) == 2:

        @pl.loop(0, out.shape[0] // 16)
        def _(i):
            here = pl.ds(pl.multiple_of(i * 16, 16), 16)
            total = terms[0][here, :].astype(F32)
            for term in terms[1:]:
                total = total + term[here, :].astype(F32)
            out[here, :] = total.astype(out.dtype)

    else:
        for i in range(out.shape[0]):
            total = terms[0][i].astype(F32)
            for term in terms[1:]:
                total = total + term[i].astype(F32)
            out[i] = total.astype(out.dtype)


REDUCE_COUNT = 8


def reduce_scratch(half_shape, far=False):
    kept = (4, *half_shape) if far else (1, 8, 128)
    return [
        pltpu.VMEM((6, *half_shape), LOW),
        pltpu.VMEM((2, *half_shape), LOW),
        pltpu.VMEM(kept, LOW if far else F32),
    ] + [pltpu.SemaphoreType.DMA((size,)) for size in (3, 3, 3, 3, 4)]


def reduce_stages(
    block, out, received, sums, kept, x_send, x_recv, y_send, y_recv, local_sem
):
    b, e, _, _ = place()
    x_device, y_device = (b ^ 1, e), (b ^ 2, e)

    def over_x(slot):
        src = (block(b ^ 3, 0), block(b ^ 1, 0), sums.at[1])[slot]
        return send(src, received.at[slot], x_send.at[slot], x_recv.at[slot], x_device)

    def over_y(slot):
        src = (block(b ^ 3, 1), block(b ^ 2, 1), sums.at[0])[slot]
        return send(src, received.at[3 + slot], y_send.at[slot], y_recv.at[slot], y_device)

    far = kept.shape[0] == 4

    def mine(i):
        return (block(b ^ 2, 0), block(b ^ 1, 1), block(b, 0), block(b, 1))[i]

    def keep(i):
        return pltpu.make_async_copy(mine(i), kept.at[i], local_sem.at[i])

    def held(i):
        if not far:
            return mine(i)
        keep(i).wait()
        return kept.at[i]

    def start():
        over_x(0).start()
        over_y(0).start()
        for i in range(4 if far else 0):
            keep(i).start()

    def forward():
        over_x(0).wait_recv()
        over_x(1).start()
        sum_into(sums.at[0], held(0), received.at[0])
        over_y(2).start()
        over_y(0).wait_recv()
        over_y(1).start()
        sum_into(sums.at[1], held(1), received.at[3])
        over_x(2).start()

    def finish():
        for slot in (1, 2):
            over_x(slot).wait_recv()
            over_y(slot).wait_recv()
        sum_into(out(0), held(2), received.at[1], received.at[5])
        sum_into(out(1), held(3), received.at[4], received.at[2])
        for slot in range(3):
            over_x(slot).wait_send()
            over_y(slot).wait_send()

    return start, forward, finish


def reduce_rows(term, out, scratch):
    half_rows = out.shape[0] // 2

    def block(owner, half):
        return term.at[pl.ds((2 * owner + half) * half_rows, half_rows)]

    def out_half(half):
        return out.at[pl.ds(half * half_rows, half_rows)]

    return reduce_stages(block, out_half, *scratch)


def bring_all(far_refs, near_refs, sem):
    copies = [
        pltpu.make_async_copy(far, near, sem.at[i])
        for i, (far, near) in enumerate(zip(far_refs, near_refs))
    ]
    for copy in copies:
        copy.start()
    return copies


def kernel_call(body, outs, args, scratch, collective_id, far_outs=(), far_args=()):
    near = pl.BlockSpec(memory_space=pltpu.VMEM)
    far = pl.BlockSpec(memory_space=pl.ANY)
    return pl.pallas_call(
        body,
        cost_estimate=pl.CostEstimate(flops=COST, bytes_accessed=COST, transcendentals=0),
        out_shape=[jax.ShapeDtypeStruct(shape, dtype) for shape, dtype in outs],
        in_specs=[far if i in far_args else near for i in range(len(args))],
        out_specs=[far if i in far_outs else near for i in range(len(outs))],
        scratch_shapes=scratch,
        compiler_params=pltpu.CompilerParams(
            collective_id=collective_id, has_side_effects=True, vmem_limit_bytes=56 * 2**20
        ),
    )(*args)


SPREAD_SEMS = [pltpu.SemaphoreType.DMA((2,))] + [pltpu.SemaphoreType.DMA((3,))] * 4


def spread_stages(own, whole, local_sem, x_send, x_recv, y_send, y_recv):
    b, e, _, _ = place()
    x_device, y_device = (b ^ 1, e), (b ^ 2, e)

    def over_x(slot):
        src, dst = (
            (own(0), whole(b, 0)),
            (own(1), whole(b, 1)),
            (whole(b ^ 2, 1), whole(b ^ 2, 1)),
        )[slot]
        return send(src, dst, x_send.at[slot], x_recv.at[slot], x_device)

    def over_y(slot):
        src, dst = (
            (own(1), whole(b, 1)),
            (own(0), whole(b, 0)),
            (whole(b ^ 1, 0), whole(b ^ 1, 0)),
        )[slot]
        return send(src, dst, y_send.at[slot], y_recv.at[slot], y_device)

    def keep(half):
        return pltpu.make_async_copy(own(half), whole(b, half), local_sem.at[half])

    def start():
        over_x(0).start()
        over_y(0).start()
        for half in range(2):
            keep(half).start()

    def forward():
        over_x(0).wait_recv()
        over_y(2).start()
        over_x(1).start()
        over_y(0).wait_recv()
        over_x(2).start()
        over_y(1).start()
    def finish():
        for slot in range(3):
            for over in (over_x, over_y):
                if slot > 0:
                    over(slot).wait_recv()
                over(slot).wait_send()
        for half in range(2):
            keep(half).wait()

    return start, forward, finish


def spread_rows(own_ref, whole_ref, rows, sems):
    half_rows = rows // 2

    def own(half):
        return own_ref.at[pl.ds(half * half_rows, half_rows)]

    def whole(owner, half):
        return whole_ref.at[pl.ds(owner * rows + half * half_rows, half_rows)]

    return spread_stages(own, whole, *sems)


def opening_kernel(
    rows, router, first_gain, second_gain, routes, ids, qkv, sup, out_weight, up_weight,
    n1_all, gains, small_all, marks_all, columns_all, out_all, up_all,
    small, marks, columns, w_out, up_own, up_wide, up_sem, *sems,
):
    (
        b_send, b_recv, s_send, s_recv, m_send, m_recv, c_send, c_recv,
        x_send, x_recv, y_send, y_recv, z_send, z_recv, o_send, o_recv, p_send, p_recv,
    ) = sems[:18]
    b, e, z, core = place()
    over = [(b ^ bit, e) for bit in (1, 2, 3)]
    mates = pack_mates()
    up_start, up_forward, up_finish = spread_rows(up_own, up_all, up_own.shape[0], sems[18:23])
    bring = pltpu.make_async_copy(up_weight.at[0], up_wide, up_sem.at[0])
    bring.start()
    greet(over + mates)
    bring.wait()
    up_own[...] = low(up_wide[...])
    up_start()
    rows_w = router.shape[0]
    small[...] = jnp.zeros_like(small)
    small[:rows_w] = router[...]
    small[rows_w : rows_w + 1, : first_gain.shape[1]] = first_gain[...]
    small[rows_w + 1 : rows_w + 2, : second_gain.shape[1]] = second_gain[...]
    chosen = routes[0].astype(F32)
    chosen = jnp.concatenate([chosen, jnp.zeros((128, 128 - TOP), F32)], axis=1).T
    marks[...] = jnp.concatenate(
        [chosen[:TOP], ids[...].astype(F32), jnp.zeros((7 - TOP, 128), F32)], axis=0
    )
    pair = 2 * HEAD
    width = rows.shape[1]
    for i in range(8):
        for part in range(3):
            lanes = slice(part * pair, (part + 1) * pair)
            if i in PAIR_OF:
                start = part * width + PAIR_OF[i] * pair
                columns[i, :, lanes] = low(qkv[:, start : start + pair])
            else:
                columns[i, :, lanes] = jnp.zeros((columns.shape[1], pair), LOW)
        columns[i, :, 3 * pair :] = sup[i]
    w_out[...] = low(out_weight[...])
    small_all[e, b] = small[...]
    marks_all[e] = marks[...]
    columns_all[b, e] = columns[e]
    out_all[b, z, core] = w_out[...]
    first = []
    for i, device in enumerate(over):
        first.append(send(small, small_all.at[e, b], b_send.at[i], b_recv.at[i], device))
        first[-1].start()
    across = []
    for i, device in enumerate(mates):
        across.append(
            send(columns.at[device[1]], columns_all.at[b, e], c_send.at[i], c_recv.at[i], device)
        )
        across[-1].start()
    beyond = []
    for i, device in enumerate(over):
        beyond.append(
            send(w_out, out_all.at[b, z, core], o_send.at[i], o_recv.at[i], device)
        )
        beyond[-1].start()
    rest = []
    for i, device in enumerate(mates):
        rest.append(send(marks, marks_all.at[e], m_send.at[i], m_recv.at[i], device))
        rest[-1].start()
    values = rows[...]
    inv = lax.rsqrt(jnp.mean(values * values, axis=1, keepdims=True) + EPSILON)
    for copy in first:
        copy.wait()
    second = []
    for i, device in enumerate(mates):
        second.append(send(small_all.at[e], small_all.at[e], s_send.at[i], s_recv.at[i], device))
        second[-1].start()
    for copy in second:
        copy.wait()

    piece = width // 32
    lane = lax.broadcasted_iota(jnp.int32, (128, width), 1)
    spread = low(jnp.where(lax.rem(lane, piece) == lax.broadcasted_iota(jnp.int32, (128, width), 0), 1.0, 0.0))
    row = lax.broadcasted_iota(jnp.int32, (32, width), 0)
    owner = lax.rem(row, 4) * 8 + row // 4
    mine = lax.broadcasted_iota(jnp.int32, (32, width), 1) // piece == owner
    for i, index in enumerate((5, 6)):
        pieces = jnp.concatenate([small_all[j, :, index, :] for j in range(8)], axis=0)
        spread_out = dot(low(pieces), spread)
        gains[i : i + 1, :] = jnp.sum(jnp.where(mine, spread_out, 0.0), axis=0, keepdims=True)
    n1_all[e] = low(values * inv * gains[0:1, :])
    stages = line_stages(n1_all, *sems[23:])
    stages[0]()

    def hop(owner, half, sems_out, sems_in, slot, device):
        block = columns_all.at[owner, pl.ds(4 * half, 4)]
        return send(block, block, sems_out.at[slot], sems_in.at[slot], device)

    def over_x(slot):
        owner, half = ((b, 0), (b, 1), (b ^ 2, 1))[slot]
        return hop(owner, half, x_send, x_recv, slot, over[0])

    def over_y(slot):
        owner, half = ((b, 1), (b, 0), (b ^ 1, 0))[slot]
        return hop(owner, half, y_send, y_recv, slot, over[1])

    def out_block(owner_z):
        return out_all.at[:, owner_z, core]

    def out_pair(slot):
        block = out_block(lax.rem(z + 4 - slot, 4))
        return send(block, block, p_send.at[slot], p_recv.at[slot], (b, e ^ 1))

    for copy in across:
        copy.wait()
    over_x(0).start()
    over_y(0).start()
    up_forward()
    over_x(1).start()
    over_y(1).start()
    stages[1]()
    over_x(0).wait_recv()
    over_y(2).start()
    over_y(0).wait_recv()
    over_x(2).start()
    stages[2]()
    for copy in beyond:
        copy.wait()
    along = []
    for i in range(3):
        device = (b, lax.rem(e + 2 * i + 2, 8))
        along.append(send(out_block(z), out_block(z), z_send.at[i], z_recv.at[i], device))
        along[-1].start()
    out_pair(0).start()
    stages[3]()
    for i, copy in enumerate(along):
        copy.wait()
        out_pair(i + 1).start()
    stages[4]()
    for slot in range(3):
        for over_one in (over_x, over_y):
            if slot > 0:
                over_one(slot).wait_recv()
            over_one(slot).wait_send()
    for copy in rest:
        copy.wait()
    for slot in range(4):
        out_pair(slot).wait()
    up_finish()


def opening(rows, router, first_gain, second_gain, routes, ids, qkv, sup, out_weight, up_weight):
    tokens, width = rows.shape
    _, up_rows, up_width = up_weight.shape
    rows_w = out_weight.shape[0]
    wide = 6 * HEAD + sup.shape[2]
    sizes = (3, 3, 7, 7, 7, 7, 7, 7, 3, 3, 3, 3, 3, 3, 3, 3, 4, 4)
    return kernel_call(
        opening_kernel,
        [
            ((8, tokens, width), LOW),
            ((2, width), F32),
            ((8, 4, 8, 128), F32),
            ((8, 8, 128), F32),
            ((4, 8, rows_w, wide), LOW),
            ((4, 4, 2, rows_w, width), LOW),
            ((4 * up_rows, up_width), LOW),
        ],
        (rows, router, first_gain, second_gain, routes, ids, qkv, sup, out_weight, up_weight),
        [
            pltpu.VMEM((8, 128), F32),
            pltpu.VMEM((8, 128), F32),
            pltpu.VMEM((8, rows_w, wide), LOW),
            pltpu.VMEM((rows_w, width), LOW),
            pltpu.VMEM((up_rows, up_width), LOW),
            pltpu.VMEM((up_rows, up_width), F32),
            pltpu.SemaphoreType.DMA((1,)),
        ]
        + [pltpu.SemaphoreType.DMA((size,)) for size in sizes]
        + SPREAD_SEMS
        + GATHER_SEMS,
        0,
        far_outs=(6,),
        far_args=(9,),
    )


def holder(e):
    return (lax.rem(e, 2) == 0) | (e == 3), jnp.where(e == 3, 4, e // 2)


BLOCK = 256


def turned(values, cosine, sine):
    return values * cosine + pltpu.roll(values, HEAD // 2, 1) * sine


def middle_kernel(
    n1_far, weights_far, cosine_far, sine_far, ids_row, ids_column, w_out_far, rows, gain, cot, up_weight, down_weight,
    sdown_weight,
    qkv, logsum, attn, resid, n2_all, cot_all, up_all, down_all, sdown_all, down_second, n2_own,
    n1, weights, cosine, sine, w_out, bring_sem,
    attended, up_own, up_wide, down_own, sdown_own, up_sem, a_send, a_recv, *sems,
):
    b, e, z, core = place()
    tokens = rows.shape[0]
    mates = pack_mates()
    count = len(SPREAD_SEMS)
    spreads = [
        spread_rows(up_own, up_all, up_own.shape[0], sems[:count]),
        spread_rows(down_own, down_all, down_own.shape[0], sems[count : 2 * count]),
        spread_rows(sdown_own, sdown_all, sdown_own.shape[0], sems[2 * count : 3 * count]),
    ]
    sems = sems[3 * count :]
    cot_stages = line_stages(cot_all, *sems[: len(GATHER_SEMS)])
    n2_stages = line_stages(n2_all, *sems[len(GATHER_SEMS) :])
    cot_all[e] = low(cot[0])
    bring = pltpu.make_async_copy(up_weight.at[1], up_wide, up_sem.at[0])
    bring.start()
    brought = bring_all(
        (n1_far, weights_far, cosine_far, sine_far, w_out_far),
        (n1, weights, cosine, sine, w_out),
        bring_sem,
    )
    greet([(b ^ 1, e), (b ^ 2, e), *mates])
    bring.wait()
    up_own[...] = low(up_wide[...])
    spreads[0][0]()
    cot_stages[0]()
    down_own[...] = low(down_weight[0])
    down_second[...] = low(down_weight[1])
    short = sdown_own.shape[0] - sdown_weight.shape[0]
    sdown_own[...] = low(
        jnp.concatenate([sdown_weight[...], jnp.zeros((short, cot.shape[2]), F32)], axis=0)
    )
    for start, _, _ in spreads[1:]:
        start()
    holds, pair = holder(e)
    for copy in brought:
        copy.wait()

    @pl.when(jnp.logical_not(holds))
    def _():
        qkv[...] = jnp.zeros_like(qkv)
        logsum[...] = jnp.zeros_like(logsum)

    @pl.when(holds)
    def _():
        @pl.loop(0, n1.shape[0] // BLOCK)
        def _(i):
            here = pl.ds(pl.multiple_of(i * BLOCK, BLOCK), BLOCK)
            projected = dot(n1[here, :], weights[:, : 6 * HEAD])
            cos_here, sin_here = cosine[here, :], sine[here, :]
            for part in range(6):
                piece = projected[:, part * HEAD : (part + 1) * HEAD]
                if part < 4:
                    piece = turned(piece, cos_here, sin_here)
                qkv[part, here, :] = low(piece)

    cot_stages[1]()
    for head in range(2):

        @pl.when(holds)
        def _():
            for i in range(n1.shape[0] // BLOCK):
                here = pl.ds(i * BLOCK, BLOCK)
                keys = (i + 1) * BLOCK
                scores = dot(qkv[head, here, :], qkv[2 + head, :keys, :], ((1,), (1,)))
                scores = jnp.where(
                    allowed_here(ids_column, ids_row, i, keys), scores * HEAD ** (-0.5), NEGATIVE
                )
                top = jnp.max(scores, axis=1, keepdims=True)
                weight = jnp.exp(scores - top)
                total = jnp.sum(weight, axis=1, keepdims=True)
                out = dot(low(weight / total), qkv[4 + head, :keys, :])
                logsum[head, here, :] = jnp.broadcast_to(top + jnp.log(total), (BLOCK, HEAD))
                for j in range(BLOCK // tokens):
                    attended[i * (BLOCK // tokens) + j, :, head * HEAD : (head + 1) * HEAD] = low(
                        out[j * tokens : (j + 1) * tokens]
                    )

        if head == 0:
            cot_stages[2]()
        spreads[head][1]()

    def give(i):
        other = lax.rem(e + i, 8)
        return send(
            attended.at[other], attn.at[pair], a_send.at[i - 1], a_recv.at[pair], (b, other)
        )

    @pl.when(holds)
    def _():
        for i in range(1, 8):
            give(i).start()
        attn[pair] = attended[e]

    total = rows[...]
    for source, index in PAIR_OF.items():

        @pl.when(e != source)
        def _():
            block = attn.at[index]
            send(block, block, a_send.at[0], a_recv.at[index], (b, source)).wait_recv()

        size = attn.shape[2]
        total = total + dot(attn[index], w_out[index * size : (index + 1) * size, :])
    resid[...] = total
    inv = lax.rsqrt(jnp.mean(total * total, axis=1, keepdims=True) + EPSILON)
    n2_all[e] = low(total * inv * gain[...])
    n2_own[...] = n2_all[e]
    n2_stages[0]()
    cot_stages[3]()
    spreads[2][1]()
    for stage in n2_stages[1:]:
        stage()
    cot_stages[4]()

    @pl.when(holds)
    def _():
        for i in range(1, 8):
            give(i).wait_send()

    for _, _, finish in spreads:
        finish()


def allowed_here(ids_column, ids_row, i, keys):
    query = i * BLOCK + lax.broadcasted_iota(jnp.int32, (BLOCK, keys), 0)
    key = lax.broadcasted_iota(jnp.int32, (BLOCK, keys), 1)
    same = ids_column[i * BLOCK : (i + 1) * BLOCK, :] == ids_row[:, :keys]
    return (key <= query) & same


def middle(n1, weights, cosine, sine, ids_row, ids_column, w_out, rows, gain, cot, up_weight, down_weight, sdown_weight):
    tokens, width = rows.shape
    length = n1.shape[0]
    pair = 2 * HEAD
    count = len(PAIR_OF)
    _, up_rows, up_width = up_weight.shape
    down_rows = down_weight.shape[1]
    sdown_rows = -(-sdown_weight.shape[0] // 32) * 32
    return kernel_call(
        middle_kernel,
        [
            ((6, length, HEAD), LOW),
            ((2, length, HEAD), F32),
            ((count, tokens, pair), LOW),
            ((tokens, width), F32),
            ((8, tokens, width), LOW),
            ((8, tokens, width), LOW),
            ((4 * up_rows, up_width), LOW),
            ((4 * down_rows, width), LOW),
            ((4 * sdown_rows, width), LOW),
            ((down_rows, width), LOW),
            ((tokens, width), LOW),
        ],
        (n1, weights, cosine, sine, ids_row, ids_column, w_out, rows, gain, cot, up_weight, down_weight, sdown_weight),
        [
            pltpu.VMEM(n1.shape, LOW),
            pltpu.VMEM(weights.shape, LOW),
            pltpu.VMEM(cosine.shape, F32),
            pltpu.VMEM(sine.shape, F32),
            pltpu.VMEM(w_out.shape, LOW),
            pltpu.SemaphoreType.DMA((5,)),
            pltpu.VMEM((8, tokens, pair), LOW),
            pltpu.VMEM((up_rows, up_width), LOW),
            pltpu.VMEM((up_rows, up_width), F32),
            pltpu.VMEM((down_rows, width), LOW),
            pltpu.VMEM((sdown_rows, width), LOW),
            pltpu.SemaphoreType.DMA((1,)),
            pltpu.SemaphoreType.DMA((7,)),
            pltpu.SemaphoreType.DMA((count,)),
        ]
        + SPREAD_SEMS * 3
        + GATHER_SEMS * 2,
        1,
        far_outs=(6, 7, 8),
        far_args=(0, 1, 2, 3, 6, 10),
    )


def experts_kernel(
    n2, cot, columns, w_sdown, gates, down_second, up_first, up_second, down_first,
    out_part, row_sum, sdown_term, sup_term, down_grad, up_term_first, up_term_second, down_term_second,
    part, w_sup, up_w, down_w, hid, dpre, hid_shared, dpre_shared, load_sem, store_sem, *scratch,
):
    e = lax.axis_index("expert")
    length, width = n2.shape
    hidden = down_w.shape[1]
    pad = w_sdown.shape[0]
    loads = [
        pltpu.make_async_copy(up_first, up_w.at[0], load_sem.at[0]),
        pltpu.make_async_copy(down_first, down_w.at[0], load_sem.at[1]),
        pltpu.make_async_copy(columns.at[:, pl.ds(6 * HEAD, 2 * pad)], w_sup, load_sem.at[3]),
        pltpu.make_async_copy(up_second, up_w.at[1], load_sem.at[2]),
    ]
    for copy in loads:
        copy.start()
    count = len(SPREAD_SEMS)
    arrive = spread_rows(down_second, down_w.at[1], down_second.shape[0], scratch[:count])
    reduce = reduce_rows(down_w.at[0], down_grad, scratch[count : count + REDUCE_COUNT])
    stages = line_sum_stages(part, *scratch[count + REDUCE_COUNT :])
    tokens = part.shape[1]
    greet_near()
    arrive[0]()
    for copy in loads[:3]:
        copy.wait()
    lane = lax.broadcasted_iota(jnp.int32, (ROWS, 128), 1)

    def routed(k, here, x, c):
        gate = gates[here, k : k + 1]
        gate_part = dot(x, up_w[k, :, :hidden])
        up_part = dot(x, up_w[k, :, hidden:])
        back = dot(c, down_w[k], ((1,), (1,)))
        silu, slope = silu_parts(gate_part, up_part)
        value = silu * up_part
        dgate = jnp.sum(back * value, axis=1, keepdims=True)
        hid[k, here, :] = low(value * gate)
        back = back * gate
        dpre[k, here, :hidden] = low(back * slope)
        dpre[k, here, hidden:] = low(back * silu)
        out = dot(hid[k, here, :], down_w[k])
        drow = dot(dpre[k, here, :], up_w[k], ((1,), (1,)))
        return out, drow, dgate

    def mark(k, dgate, marks):
        high = low(dgate).astype(F32)
        marks = jnp.where(lane == 2 * e + k, high, marks)
        return jnp.where(lane == 2 * e + k + 16, dgate - high, marks)

    def first_pass(i):
        here = pl.ds(pl.multiple_of(i * ROWS, ROWS), ROWS)
        x = n2[here, :]
        c = cot[here, :]
        gate_part = dot(x, w_sup[:, :pad])
        up_part = dot(x, w_sup[:, pad:])
        back = dot(c, w_sdown[...], ((1,), (1,)))
        silu, slope = silu_parts(gate_part, up_part)
        hid_shared[here, :] = low(silu * up_part)
        dpre_shared[here, :pad] = low(back * slope)
        dpre_shared[here, pad:] = low(back * silu)
        out, drow, dgate = routed(0, here, x, c)
        out = out + dot(hid_shared[here, :], w_sdown[...])
        drow = drow + dot(dpre_shared[here, :], w_sup[...], ((1,), (1,)))
        marks = mark(0, dgate, jnp.zeros((ROWS, 128), F32))
        out_part[here, :] = low(out)
        for j in range(ROWS // tokens):
            rows = slice(j * tokens, (j + 1) * tokens)
            part[i * (ROWS // tokens) + j, :, :width] = low(drow[rows])
            part[i * (ROWS // tokens) + j, :, width:] = low(marks[rows])

    half = length // ROWS // 2

    @pl.loop(0, half)
    def _(i):
        first_pass(i)

    arrive[1]()

    @pl.loop(half, 2 * half)
    def _(i):
        first_pass(i)

    loads[3].wait()
    arrive[2]()

    @pl.loop(0, length // ROWS)
    def _(i):
        here = pl.ds(pl.multiple_of(i * ROWS, ROWS), ROWS)
        out, drow, dgate = routed(1, here, n2[here, :], cot[here, :])
        out_part[here, :] = low(out_part[here, :].astype(F32) + out)
        for j in range(ROWS // tokens):
            rows = slice(j * tokens, (j + 1) * tokens)
            block = i * (ROWS // tokens) + j
            part[block, :, :width] = low(part[block, :, :width].astype(F32) + drow[rows])
            marks = part[block, :, width:].astype(F32)
            high = low(dgate[rows]).astype(F32)
            marks = jnp.where(lane[rows] == 2 * e + 1, high, marks)
            marks = jnp.where(lane[rows] == 2 * e + 17, dgate[rows] - high, marks)
            part[block, :, width:] = low(marks)

    stages[0]()

    def up_gradient(k, up_ref):
        @pl.loop(0, width // COLS)
        def _(i):
            here = pl.ds(pl.multiple_of(i * COLS, COLS), COLS)
            up_w[k, here, :] = low(dot(n2[:, here], dpre[k], ((0,), (0,))))

        store = pltpu.make_async_copy(up_w.at[k], up_ref, store_sem.at[k])
        store.start()
        return store

    def down_gradient(k):
        @pl.loop(0, hidden // 128)
        def _(i):
            here = pl.ds(pl.multiple_of(i * 128, 128), 128)
            down_w[k, here, :] = low(dot(hid[k, :, here], cot[...], ((0,), (0,))))

    down_gradient(0)
    reduce[0]()
    stages[1]()
    stores = [up_gradient(0, up_term_first)]
    stages[2]()
    reduce[1]()
    down_gradient(1)
    stores.append(pltpu.make_async_copy(down_w.at[1], down_term_second, store_sem.at[2]))
    stores[-1].start()
    stages[3]()
    stores.append(up_gradient(1, up_term_second))
    sdown_term[...] = low(dot(hid_shared[...], cot[...], ((0,), (0,))))

    @pl.loop(0, width // COLS)
    def _(i):
        here = pl.ds(pl.multiple_of(i * COLS, COLS), COLS)
        sup_term[here, :] = low(dot(n2[:, here], dpre_shared[...], ((0,), (0,))))

    row_sum[...] = stages[4]()
    reduce[2]()
    for copy in stores:
        copy.wait()


ROWS = 256
COLS = 256


def experts_phase(n2, cot, columns, w_sdown, gates, down_second, up_first, up_second, down_first):
    length, width = n2.shape
    hidden = down_first.shape[0]
    pad = w_sdown.shape[0]
    tokens = length // 8
    wide = width + 128
    return kernel_call(
        experts_kernel,
        [
            ((length, width), LOW),
            ((tokens, wide), F32),
            ((pad, width), LOW),
            ((width, 2 * pad), LOW),
            ((hidden // 4, width), F32),
            (up_first.shape, LOW),
            (up_first.shape, LOW),
            ((hidden, width), LOW),
        ],
        (n2, cot, columns, w_sdown, gates, down_second, up_first, up_second, down_first),
        [
            pltpu.VMEM((8, tokens, wide), LOW),
            pltpu.VMEM((width, 2 * pad), LOW),
            pltpu.VMEM((2, *up_first.shape), LOW),
            pltpu.VMEM((2, hidden, width), LOW),
            pltpu.VMEM((2, length, hidden), LOW),
            pltpu.VMEM((2, length, 2 * hidden), LOW),
            pltpu.VMEM((length, pad), LOW),
            pltpu.VMEM((length, 2 * pad), LOW),
            pltpu.SemaphoreType.DMA((4,)),
            pltpu.SemaphoreType.DMA((3,)),
        ]
        + SPREAD_SEMS
        + reduce_scratch((hidden // 8, width))
        + scatter_scratch(tokens, wide)
        + SCATTER_SEMS,
        4,
        far_outs=(5, 6, 7),
        far_args=(2, 6, 7, 8),
    )


def turn_kernel(
    row_sum, out_part, upstream, gates, w_router, resid, gain, w_out, attn, n2, up_term, down_term,
    dresid, small, out_term, darrived, output_rows, up_grad, down_grad,
    dattn, a_send, a_recv, *scratch,
):
    b, e, z, core = place()
    greet([(b ^ 1, e), (b ^ 2, e), *pack_mates()])
    reduces = [
        reduce_rows(up_term, up_grad, scratch[:REDUCE_COUNT]),
        reduce_rows(down_term, down_grad, scratch[REDUCE_COUNT : 2 * REDUCE_COUNT]),
    ]
    scratch = scratch[2 * REDUCE_COUNT :]
    out_stages = line_sum_stages(out_part, *scratch)
    out_stages[0]()
    for start, _, _ in reduces:
        start()
    holds, pair = holder(e)
    total = row_sum[...]
    width = upstream.shape[1]
    experts = gates.shape[1]
    dgate = total[:, width : width + experts] + total[:, width + experts : width + 2 * experts]
    own = gates[...]
    dlog = low(own * (dgate - jnp.sum(own * dgate, axis=1, keepdims=True)))
    dn2 = total[:, :width] + dot(dlog, w_router[...])
    rows = resid[...]
    inv = lax.rsqrt(jnp.mean(rows * rows, axis=1, keepdims=True) + EPSILON)
    xhat = rows * inv
    small[experts : experts + 1, :] = jnp.sum(dn2 * xhat, axis=0, keepdims=True)
    scaled = dn2 * gain[...]
    grad = upstream[...] + inv * (scaled - xhat * jnp.mean(scaled * xhat, axis=1, keepdims=True))
    dresid[...] = grad
    back = low(dot(low(grad), w_out[...], ((1,), (1,))))
    size = dattn.shape[2]

    def give(source, index):
        return send(dattn.at[index], darrived.at[e], a_send.at[index], a_recv.at[e], (b, source))

    for source, index in PAIR_OF.items():
        dattn[index] = back[:, index * size : (index + 1) * size]

        @pl.when(e != source)
        def _():
            give(source, index).start()

    out_stages[1]()
    reduces[0][1]()
    small[:experts, :] = dot(dlog, n2[...], ((0,), (0,)))
    small[experts + 1 :, :] = jnp.zeros((small.shape[0] - experts - 1, width), F32)
    out_stages[2]()
    grad_low = low(dresid[...])
    for index in range(len(PAIR_OF)):
        out_term[index * size : (index + 1) * size, :] = low(
            dot(attn[index], grad_low, ((0,), (0,)))
        )
    reduces[1][1]()
    out_stages[3]()

    @pl.when(jnp.logical_not(holds))
    def _():
        darrived[...] = jnp.zeros_like(darrived)

    @pl.when(holds)
    def _():
        darrived[e] = dattn[pair]
        for i in range(1, 8):
            other = lax.rem(e + i, 8)
            block = darrived.at[other]
            send(block, block, a_send.at[0], a_recv.at[other], (b, other)).wait_recv()

    output_rows[...] = resid[...] + out_stages[4]()
    for _, _, finish in reduces:
        finish()
    for source, index in PAIR_OF.items():

        @pl.when(e != source)
        def _():
            give(source, index).wait_send()


def turn(row_sum, out_part, upstream, gates, w_router, resid, gain, w_out, attn, n2, up_term, down_term):
    tokens, width = upstream.shape
    pair = 2 * HEAD
    count = len(PAIR_OF)
    up_rows, down_rows = up_term.shape[0] // 4, down_term.shape[0] // 4
    return kernel_call(
        turn_kernel,
        [
            ((tokens, width), F32),
            ((gates.shape[1] + 8, width), F32),
            ((width, width), LOW),
            ((8, tokens, pair), LOW),
            ((tokens, width), F32),
            ((up_rows, up_term.shape[1]), F32),
            ((down_rows, down_term.shape[1]), F32),
        ],
        (row_sum, out_part, upstream, gates, w_router, resid, gain, w_out, attn, n2, up_term, down_term),
        [
            pltpu.VMEM((count, tokens, pair), LOW),
            pltpu.SemaphoreType.DMA((count,)),
            pltpu.SemaphoreType.DMA((8,)),
        ]
        + reduce_scratch((up_rows // 2, up_term.shape[1]), True)
        + reduce_scratch((down_rows // 2, down_term.shape[1]), True)
        + scatter_scratch(tokens, width)
        + SCATTER_SEMS,
        2,
        far_args=(10, 11),
    )


PARTNERS = ((0, 1), (1, 0), (2, 0), (0, 2), (0, 4))


def closing_kernel(
    dattn, qkv_far, logsum_far, n1_far, weights_far, cosine_far, sine_far, ids_row, ids_column, rows, gain, dresid,
    up_term, sdown_term, sup_term, out_term, small,
    input_grad, columns, out_grad, up_grad, sdown_grad, small_sum,
    qkv, logsum, n1, weights, cosine, sine, bring_sem,
    dkey, dvalue, dprojected, part, column_term, column_sum, column_low,
    out_near, out_sum, out_low, out_half, out_got, small_got, small_step,
    n_send, n_recv, o_send, o_recv, c_send, c_recv, s_send, s_recv, *scratch,
):
    b, e, z, core = place()
    length = n1.shape[0]
    tokens = rows.shape[0]
    mates = pack_mates()
    greet([(b ^ 1, e), (b ^ 2, e), *mates])
    holds, pair = holder(e)

    def cut():
        nonlocal scratch
        mine, scratch = scratch[:REDUCE_COUNT], scratch[REDUCE_COUNT:]
        return mine

    up = reduce_rows(up_term, up_grad, cut())
    sdown = reduce_rows(sdown_term, sdown_grad, cut())
    column = reduce_rows(column_term, column_sum, cut())
    out = reduce_stages(
        lambda owner, half: out_sum.at[owner, pl.ds(2 * half, 2)],
        lambda half: out_half.at[pl.ds(2 * half, 2)],
        *cut(),
    )
    stages = line_sum_stages(part, *scratch)

    def partner(i):
        batch_bit, expert_bit = PARTNERS[i]
        src = small if i == 0 else small_step.at[i - 1]
        device = (b ^ batch_bit, e ^ expert_bit)
        return send(src, small_got.at[i], s_send.at[i], s_recv.at[i], device)

    def small_round(i):
        partner(i).wait_recv()
        before = small[...] if i == 0 else small_step[i - 1]
        if i < len(PARTNERS) - 1:
            small_step[i] = before + small_got[i]
            partner(i + 1).start()
        else:
            small_sum[...] = before + small_got[i]

    near = send(
        out_term.at[:, :, 1 - core], out_near, n_send.at[0], n_recv.at[0], (b, e ^ 1)
    )
    up[0]()
    near.start()
    brought = bring_all(
        (qkv_far, logsum_far, n1_far, weights_far, cosine_far, sine_far),
        (qkv, logsum, n1, weights, cosine, sine),
        bring_sem,
    )
    own = pltpu.make_async_copy(out_term.at[:, :, core], out_sum, n_send.at[1])
    own.start()
    partner(0).start()

    def attend(head):
        dkey[...] = jnp.zeros_like(dkey)
        dvalue[...] = jnp.zeros_like(dvalue)
        lanes = pl.ds(head * HEAD, HEAD)
        for i in range(length // BLOCK):
            here = pl.ds(i * BLOCK, BLOCK)
            keys = (i + 1) * BLOCK
            count = BLOCK // tokens
            back = jnp.concatenate(
                [dattn[count * i + j, :, lanes] for j in range(count)], axis=0
            )
            query = qkv[head, here, :]
            scores = dot(query, qkv[2 + head, :keys, :], ((1,), (1,))) * HEAD ** (-0.5)
            weight = jnp.where(
                allowed_here(ids_column, ids_row, i, keys),
                jnp.exp(scores - logsum[head, here, 0:1]),
                0.0,
            )
            dprob = dot(back, qkv[4 + head, :keys, :], ((1,), (1,)))
            delta = jnp.sum(weight * dprob, axis=1, keepdims=True)
            dscore = low(weight * (dprob - delta))
            dquery = dot(dscore, qkv[2 + head, :keys, :]) * HEAD ** (-0.5)
            dkey[:keys, :] += dot(dscore, query, ((0,), (0,)))
            dvalue[:keys, :] += dot(low(weight), back, ((0,), (0,)))
            dprojected[here, lanes] = low(turned(dquery, cosine[here, :], -sine[here, :]))
        dprojected[:, (2 + head) * HEAD : (3 + head) * HEAD] = low(
            turned(dkey[...] * HEAD ** (-0.5), cosine[...], -sine[...])
        )
        dprojected[:, (4 + head) * HEAD : (5 + head) * HEAD] = low(dvalue[...])

    for copy in brought:
        copy.wait()

    @pl.when(holds)
    def _():
        attend(0)

    near.wait()
    own.wait()
    for owner in range(4):
        for owner_z in range(4):
            out_sum[owner, owner_z] = low(
                out_sum[owner, owner_z].astype(F32) + out_near[owner, owner_z].astype(F32)
            )
    small_round(0)
    up[1]()

    @pl.when(holds)
    def _():
        attend(1)
        for i in range(8):
            part[i] = low(
                dot(
                    dprojected[i * tokens : (i + 1) * tokens, :],
                    weights[:, : 6 * HEAD],
                    ((1,), (1,)),
                )
            )

    @pl.when(jnp.logical_not(holds))
    def _():
        part[...] = jnp.zeros_like(part)

    stages[0]()
    column_term[:, 6 * HEAD :] = sup_term[...]

    @pl.when(holds)
    def _():
        for i in range(n1.shape[1] // BLOCK):
            here = pl.ds(i * BLOCK, BLOCK)
            column_term[here, : 6 * HEAD] = low(dot(n1[:, here], dprojected[...], ((0,), (0,))))

    @pl.when(jnp.logical_not(holds))
    def _():
        column_term[:, : 6 * HEAD] = jnp.zeros((n1.shape[1], 6 * HEAD), LOW)

    column[0]()
    stages[1]()
    out[0]()
    small_round(1)
    stages[2]()
    column[1]()
    sdown[0]()
    stages[3]()
    small_round(2)
    out[1]()
    small_round(3)
    values = rows[...]
    inv = lax.rsqrt(jnp.mean(values * values, axis=1, keepdims=True) + EPSILON)
    xhat = values * inv
    scaled = stages[4]() * gain[...]
    input_grad[...] = dresid[...] + inv * (
        scaled - xhat * jnp.mean(scaled * xhat, axis=1, keepdims=True)
    )
    column[2]()
    piece = column_low.shape[1]
    for i in range(0, 8, 2):
        two = column_sum[i * piece : (i + 2) * piece, :].astype(F32)
        column_low[i] = low(two[:piece])
        column_low[i + 1] = low(two[piece:])
    columns[e] = column_low[e]
    across = []
    for i, device in enumerate(mates):
        across.append(
            send(column_low.at[device[1]], columns.at[e], c_send.at[i], c_recv.at[i], device)
        )
        across[-1].start()
    sdown[1]()
    small_round(4)
    for i in range(len(PARTNERS)):
        partner(i).wait_send()
    out[2]()
    for owner_z in range(4):
        out_low[owner_z] = low(out_half[owner_z])
    along = []
    for i in range(3):
        device = (b, lax.rem(e + 2 * i + 2, 8))
        along.append(
            send(
                out_low.at[device[1] // 2], out_got.at[i], o_send.at[i], o_recv.at[i], device
            )
        )
        along[-1].start()
    up[2]()
    for copy in along:
        copy.wait()
    out_grad[...] = (
        out_half[z]
        + out_got[0].astype(F32)
        + out_got[1].astype(F32)
        + out_got[2].astype(F32)
    )
    sdown[2]()
    for copy in across:
        copy.wait()


def closing(
    dattn, qkv, logsum, n1, weights, cosine, sine, ids_row, ids_column, rows, gain, dresid,
    up_term, sdown_term, sup_term, out_term, small,
):
    tokens, width = rows.shape
    length = n1.shape[0]
    rows_w = out_term.shape[3]
    wide = weights.shape[1]
    up_rows, sdown_rows = up_term.shape[0] // 4, sdown_term.shape[0] // 4
    dma = pltpu.SemaphoreType.DMA
    return kernel_call(
        closing_kernel,
        [
            ((tokens, width), F32),
            ((8, rows_w, wide), LOW),
            ((rows_w, width), F32),
            ((up_rows, up_term.shape[1]), F32),
            ((sdown_rows, width), F32),
            (small.shape, F32),
        ],
        (
            dattn, qkv, logsum, n1, weights, cosine, sine, ids_row, ids_column, rows, gain, dresid,
            up_term, sdown_term, sup_term, out_term, small,
        ),
        [
            pltpu.VMEM(qkv.shape, LOW),
            pltpu.VMEM(logsum.shape, F32),
            pltpu.VMEM(n1.shape, LOW),
            pltpu.VMEM(weights.shape, LOW),
            pltpu.VMEM(cosine.shape, F32),
            pltpu.VMEM(sine.shape, F32),
            pltpu.SemaphoreType.DMA((6,)),
            pltpu.VMEM((length, HEAD), F32),
            pltpu.VMEM((length, HEAD), F32),
            pltpu.VMEM((length, 6 * HEAD), LOW),
            pltpu.VMEM((8, tokens, width), LOW),
            pltpu.VMEM((width, wide), LOW),
            pltpu.VMEM((width // 4, wide), LOW),
            pltpu.VMEM((8, rows_w, wide), LOW),
            pltpu.VMEM((4, 4, rows_w, width), LOW),
            pltpu.VMEM((4, 4, rows_w, width), LOW),
            pltpu.VMEM((4, rows_w, width), LOW),
            pltpu.VMEM((4, rows_w, width), F32),
            pltpu.VMEM((3, rows_w, width), LOW),
            pltpu.VMEM((5, *small.shape), F32),
            pltpu.VMEM((4, *small.shape), F32),
            dma((2,)), dma((1,)), dma((3,)), dma((3,)), dma((7,)), dma((7,)), dma((5,)), dma((5,)),
        ]
        + reduce_scratch((up_rows // 2, up_term.shape[1]), True)
        + reduce_scratch((sdown_rows // 2, width))
        + reduce_scratch((width // 8, wide))
        + reduce_scratch((2, rows_w, width))
        + scatter_scratch(tokens, width)
        + SCATTER_SEMS,
        3,
        far_args=(1, 2, 3, 4, 5, 6, 12, 15),
    )


def silu_parts(gate, up):
    sigma = jax.nn.sigmoid(gate)
    return gate * sigma, up * sigma * (1.0 + gate * (1.0 - sigma))


def rotary_angles(length):
    half = HEAD // 2
    frequency = np.float32(10000.0) ** (-np.arange(half, dtype=np.float32) / np.float32(half))
    return np.arange(length, dtype=np.float32)[:, None] * frequency[None, :]


def pack_device(
    block_input,
    seq_ids,
    routes,
    cotangent,
    qkv_weight,
    out_weight,
    shared_up,
    shared_down,
    router_weight,
    gain_attn,
    gain_ffn,
    expert_up,
    expert_down,
):
    b = lax.axis_index("batch")
    e = lax.axis_index("expert")
    rows_in = block_input[0]
    upstream = cotangent[0]
    tokens, width = rows_in.shape
    length = tokens * 8
    rows_w = qkv_weight.shape[0]
    pair = 2 * HEAD
    pairs_of_heads = width // pair
    hidden = expert_up.shape[2] // 2
    experts = expert_up.shape[0] * 8
    s_rows = shared_down.shape[0]
    s_each = -(-s_rows // 32) * 32
    s_pad = 4 * s_each

    sup_low = low(shared_up).reshape(rows_w, 2, 4, 8, s_rows)
    sup_low = jnp.pad(sup_low, ((0, 0),) * 4 + ((0, s_each - s_rows),)).transpose(3, 0, 1, 2, 4)
    n1_all, gains, small, marks, columns, w_out, up_first = opening(
        rows_in,
        router_weight.reshape(-1, 128),
        gain_attn[None],
        gain_ffn[None],
        routes,
        seq_ids,
        qkv_weight,
        sup_low.reshape(8, rows_w, 2 * s_pad),
        out_weight,
        expert_up,
    )
    n1_all = n1_all.reshape(length, width)
    columns = columns.reshape(width, 3 * pair + 2 * s_pad)
    w_out = w_out.reshape(width, width)
    router_rows = rows_w * experts // 128
    w_router = low(small[:, :, :router_rows].transpose(1, 0, 2, 3).reshape(width, experts))
    gain_first = gains[0:1]
    gain_second = gains[1:2]
    marks = marks.astype(jnp.int32).transpose(0, 2, 1).reshape(length, 8)
    route_all = marks[:, :TOP]
    ids_all = marks[:, TOP]
    positions = jnp.arange(length, dtype=jnp.int32)
    ids_row = ids_all[None, :]
    ids_column = ids_all[:, None]
    angle = rotary_angles(length)
    cosine = np.concatenate([np.cos(angle)] * 2, axis=1)
    sine = np.concatenate([-np.sin(angle), np.sin(angle)], axis=1)
    qkv, logsum, attn, resid, n2_all, cot_all, up_second, down_low, w_sdown, down_second, n2 = middle(
        n1_all,
        columns,
        jnp.asarray(cosine),
        jnp.asarray(sine),
        ids_row,
        ids_column,
        w_out,
        rows_in,
        gain_second,
        cotangent,
        expert_up,
        expert_down,
        shared_down,
    )
    cot_all = cot_all.reshape(length, width)

    n2_all = n2_all.reshape(length, width)
    logits = dot(n2_all, w_router)
    hot = route_all[:, :, None] == jnp.arange(experts, dtype=jnp.int32)[None, None, :]
    routed_to = jnp.any(hot, axis=1)
    logits = jnp.where(routed_to, logits, NEGATIVE)
    gates = jnp.where(routed_to, jnp.exp(logits - jnp.max(logits, axis=1, keepdims=True)), 0.0)
    gates = gates / jnp.sum(gates, axis=1, keepdims=True)
    mine = lax.dynamic_slice_in_dim(gates, 2 * e, 2, 1)

    output_part, row_sum, sdown_term, sup_term, down_grad_first, *terms = experts_phase(
        n2_all,
        cot_all,
        columns,
        w_sdown,
        mine,
        down_second,
        up_first,
        up_second,
        down_low,
    )
    up_terms, down_term_second = terms[:2], terms[2]
    own_gates = lax.dynamic_slice_in_dim(gates, e * tokens, tokens, 0)
    dresid, small, out_term, dattn, output_rows, up_grad_first, down_grad_second = turn(
        row_sum,
        output_part.reshape(8, tokens, width),
        upstream,
        own_gates,
        w_router.T,
        resid,
        gain_second,
        w_out,
        attn,
        n2,
        up_terms[0],
        down_term_second,
    )
    out_term = out_term.reshape(4, 4, 2, rows_w, width)
    input_grad, columns, out_grad, up_grad_second, sdown_grad, small = closing(
        dattn,
        qkv,
        logsum,
        n1_all,
        columns,
        jnp.asarray(cosine),
        jnp.asarray(sine),
        ids_row,
        ids_column,
        rows_in,
        gain_first,
        dresid,
        up_terms[1],
        sdown_term,
        sup_term,
        out_term,
        small,
    )
    expert_up_grad = jnp.stack([up_grad_first, up_grad_second])
    expert_down_grad = jnp.stack([down_grad_first, down_grad_second])
    shared_down_grad = sdown_grad[:s_rows]
    small = lax.dynamic_slice_in_dim(small, (b * 8 + e) * rows_w, rows_w, 1)
    columns = columns.astype(F32)
    qkv_grad = jnp.stack([columns[i, :, : 3 * pair] for i in PAIR_OF])
    qkv_grad = qkv_grad.reshape(pairs_of_heads, rows_w, 3, pair).transpose(1, 2, 0, 3)
    qkv_grad = qkv_grad.reshape(rows_w, 3 * width)
    sup_grad = columns[:, :, 3 * pair :].reshape(8, rows_w, 2, 4, s_each)[..., :s_rows]
    sup_grad = sup_grad.transpose(1, 2, 3, 0, 4)
    sup_grad = sup_grad.reshape(rows_w, shared_up.shape[1])
    own_first = low(gain_attn).astype(F32)
    gain_attn_grad = jnp.sum(low(qkv_weight).astype(F32) * qkv_grad, axis=1) / own_first
    return (
        output_rows[None],
        input_grad[None],
        qkv_grad,
        out_grad,
        sup_grad,
        shared_down_grad,
        small[:experts].T,
        gain_attn_grad,
        small[experts],
        expert_up_grad,
        expert_down_grad,
    )


def solution(mesh):
    in_specs = (
        P("batch", "expert", None),
        P("batch", "expert"),
        P("batch", "expert", None),
        P("batch", "expert", None),
        P(("batch", "expert"), None),
        P(("batch", "expert"), None),
        P(("batch", "expert"), None),
        P(("batch", "expert"), None),
        P(("batch", "expert"), None),
        P(("batch", "expert")),
        P(("batch", "expert")),
        P("expert", "batch", None),
        P("expert", "batch", None),
    )
    out_specs = (
        P("batch", "expert", None),
        P("batch", "expert", None),
        P(("batch", "expert"), None),
        P(("batch", "expert"), None),
        P(("batch", "expert"), None),
        P(("batch", "expert"), None),
        P(("batch", "expert"), None),
        P(("batch", "expert")),
        P(("batch", "expert")),
        P("expert", "batch", None),
        P("expert", "batch", None),
    )
    sizes = dict(mesh.shape)
    body = pack_device if sizes == {"batch": 4, "expert": 8} else per_device
    return jax.shard_map(
        body, mesh=mesh, in_specs=in_specs, out_specs=out_specs, check_vma=False
    )
```

```python
import functools

import jax
import jax.numpy as jnp
import numpy as np
from jax import lax
from jax.experimental import pallas as pl
from jax.experimental.pallas import tpu as pltpu
from jax.sharding import PartitionSpec as P

HEAD = 128
TOP = 6


EPSILON = 1e-06
NEGATIVE = -1e30


def rotate(values, positions, sign):
    half = values.shape[-1] // 2
    frequency = 10000.0 ** (-jnp.arange(half, dtype=jnp.float32) / half)
    angle = positions.astype(jnp.float32)[:, None] * frequency[None, :]
    cosine = jnp.cos(angle)[:, None, :]
    sine = sign * jnp.sin(angle)[:, None, :]
    first = values[..., :half]
    second = values[..., half:]
    return jnp.concatenate(
        [first * cosine - second * sine, first * sine + second * cosine], axis=-1
    )


def swiglu(pre, hidden_width):
    return jax.nn.silu(pre[..., :hidden_width]) * pre[..., hidden_width:]


def swiglu_back(pre, dhidden, hidden_width):
    gate_part = pre[..., :hidden_width]
    up_part = pre[..., hidden_width:]
    sigma = jax.nn.sigmoid(gate_part)
    dgate = dhidden * up_part * sigma * (1.0 + gate_part * (1.0 - sigma))
    dupper = dhidden * gate_part * sigma
    return jnp.concatenate([dgate, dupper], axis=-1)


def norm_back(dnormed, normed, inv_rms, gain):
    dscaled = dnormed * gain
    dinputs = inv_rms * (dscaled - normed * jnp.mean(dscaled * normed, axis=1, keepdims=True))
    return (dinputs, jnp.sum(dnormed * normed, axis=0))


def per_device(
    block_input,
    seq_ids,
    routes,
    cotangent,
    qkv_weight,
    out_weight,
    shared_up,
    shared_down,
    router_weight,
    gain_attn,
    gain_ffn,
    expert_up,
    expert_down,
):
    dense = (
        lax.all_gather(qkv_weight.astype(jnp.bfloat16), ("batch", "expert"), axis=0, tiled=True),
        lax.all_gather(out_weight.astype(jnp.bfloat16), ("batch", "expert"), axis=0, tiled=True),
        lax.all_gather(shared_up.astype(jnp.bfloat16), ("batch", "expert"), axis=0, tiled=True),
        lax.all_gather(shared_down.astype(jnp.bfloat16), ("batch", "expert"), axis=0, tiled=True),
        lax.all_gather(router_weight.astype(jnp.bfloat16), ("batch", "expert"), axis=0, tiled=True),
        lax.all_gather(gain_attn.astype(jnp.bfloat16), ("batch", "expert"), axis=0, tiled=True),
        lax.all_gather(gain_ffn.astype(jnp.bfloat16), ("batch", "expert"), axis=0, tiled=True),
    )
    full_qkv, full_out, full_sup, full_sdown, full_router, low_gain_a, low_gain_f = dense
    gain_first = low_gain_a.astype(jnp.float32)
    gain_second = low_gain_f.astype(jnp.float32)
    experts_up, experts_down = (
        lax.all_gather(expert_up.astype(jnp.bfloat16), "batch", axis=1, tiled=True),
        lax.all_gather(expert_down.astype(jnp.bfloat16), "batch", axis=1, tiled=True),
    )
    rows_in = block_input[0]
    ids_local = seq_ids[0]
    route_local = routes[0]
    upstream = cotangent[0]
    tokens_dev = rows_in.shape[0]
    model_width = rows_in.shape[1]
    heads_count = model_width // HEAD
    groups = lax.axis_size("expert")
    local_experts = experts_up.shape[0]
    experts_all = local_experts * groups
    shared_width = full_sdown.shape[0]
    hidden_width = experts_down.shape[1]
    capacity = max(2, tokens_dev * TOP * 3 // (experts_all * 2))
    score_scale = HEAD ** (-0.5)
    positions = lax.axis_index("expert") * tokens_dev + jnp.arange(tokens_dev, dtype=jnp.int32)
    key_ids = lax.all_gather(ids_local, "expert", axis=0, tiled=True)
    inv_first = lax.rsqrt(jnp.mean(rows_in * rows_in, axis=1, keepdims=True) + EPSILON)
    normed_first = rows_in * inv_first
    input_low = (normed_first * gain_first).astype(jnp.bfloat16)
    projected = jnp.dot(input_low, full_qkv, preferred_element_type=jnp.float32)
    queries = rotate(
        projected[:, :model_width].reshape(tokens_dev, heads_count, HEAD), positions, 1.0
    ).astype(jnp.bfloat16)
    keys = rotate(
        projected[:, model_width : 2 * model_width].reshape(tokens_dev, heads_count, HEAD),
        positions,
        1.0,
    ).astype(jnp.bfloat16)
    values = (
        projected[:, 2 * model_width :].reshape(tokens_dev, heads_count, HEAD).astype(jnp.bfloat16)
    )

    def key_mask(key_count):
        key_pos = jnp.arange(key_count, dtype=jnp.int32)
        return (key_pos[None, :] <= positions[:, None]) & (key_ids[None, :] == ids_local[:, None])

    run_max = jnp.full((heads_count, tokens_dev), NEGATIVE, jnp.float32)
    key_piece = lax.all_gather(keys, "expert", axis=0, tiled=True)
    value_piece = lax.all_gather(values, "expert", axis=0, tiled=True)
    allowed = key_mask(key_piece.shape[0])[None]
    scores = (
        jnp.einsum("qhd,khd->hqk", queries, key_piece, preferred_element_type=jnp.float32)
        * score_scale
    )
    scores = jnp.where(allowed, scores, NEGATIVE)
    new_max = jnp.maximum(run_max, jnp.max(scores, axis=2))
    weights = jnp.where(allowed, jnp.exp(scores - new_max[:, :, None]), 0.0)
    run_sum = jnp.sum(weights, axis=2)
    update = jnp.einsum(
        "hqk,khd->qhd",
        weights.astype(jnp.bfloat16),
        value_piece,
        preferred_element_type=jnp.float32,
    )
    run_acc = update
    run_max, run_sum, run_acc = (new_max, run_sum, run_acc)
    attn_full = run_acc / jnp.transpose(run_sum)[:, :, None]
    logsum = run_max + jnp.log(run_sum)
    attn_low = attn_full.reshape(tokens_dev, model_width).astype(jnp.bfloat16)
    resid = rows_in + jnp.dot(attn_low, full_out, preferred_element_type=jnp.float32)
    inv_second = lax.rsqrt(jnp.mean(resid * resid, axis=1, keepdims=True) + EPSILON)
    normed_second = resid * inv_second
    ffn_low = (normed_second * gain_second).astype(jnp.bfloat16)
    logits = jnp.dot(ffn_low, full_router, preferred_element_type=jnp.float32)
    probs = jax.nn.softmax(logits, axis=1)
    route_hot = route_local[:, :, None] == jnp.arange(experts_all, dtype=jnp.int32)[None, None, :]
    chosen = jnp.sum(jnp.where(route_hot, probs[:, None, :], 0.0), axis=2)
    chosen_sum = jnp.sum(chosen, axis=1, keepdims=True)
    gates = chosen / chosen_sum
    shared_pre = jnp.dot(ffn_low, full_sup, preferred_element_type=jnp.float32)
    shared_hidden = swiglu(shared_pre, shared_width).astype(jnp.bfloat16)
    shared_result = jnp.dot(shared_hidden, full_sdown, preferred_element_type=jnp.float32)
    flat_route = route_local.reshape(-1)
    flat_hot = (flat_route[:, None] == jnp.arange(experts_all, dtype=jnp.int32)[None, :]).astype(
        jnp.bfloat16
    )
    pair_count = tokens_dev * TOP
    pair_index = jnp.arange(pair_count, dtype=jnp.int32)
    earlier = (pair_index[None, :] < pair_index[:, None]).astype(jnp.bfloat16)
    counts = jnp.dot(earlier, flat_hot, preferred_element_type=jnp.float32)
    slots = jnp.sum(counts * flat_hot, axis=1).astype(jnp.int32)
    source_table = (
        jnp.full((experts_all * capacity,), pair_count, jnp.int32)
        .at[flat_route * capacity + slots]
        .set(jnp.arange(pair_count, dtype=jnp.int32))
    )
    send_table = jnp.transpose(
        source_table.reshape(groups, local_experts, capacity), (1, 0, 2)
    ).reshape(-1)
    return_pos = (
        flat_route % local_experts * (groups * capacity)
        + flat_route // local_experts * capacity
        + slots
    )
    padded_rows = jnp.concatenate([ffn_low, jnp.zeros((1, model_width), jnp.bfloat16)], axis=0)
    send_rows = padded_rows[send_table // TOP].reshape(local_experts, groups, capacity, model_width)
    received = lax.all_to_all(send_rows, "expert", split_axis=1, concat_axis=1, tiled=True)
    expert_rows = received.reshape(local_experts, groups * capacity, model_width)
    expert_pre = jnp.einsum(
        "erd,edf->erf", expert_rows, experts_up, preferred_element_type=jnp.float32
    )
    expert_hidden = swiglu(expert_pre, hidden_width).astype(jnp.bfloat16)
    expert_result = jnp.einsum(
        "erf,efd->erd", expert_hidden, experts_down, preferred_element_type=jnp.float32
    ).astype(jnp.bfloat16)
    returned = lax.all_to_all(
        expert_result.reshape(local_experts, groups, capacity, model_width),
        "expert",
        split_axis=1,
        concat_axis=1,
        tiled=True,
    )
    token_outputs = returned.reshape(-1, model_width)[return_pos].reshape(
        tokens_dev, TOP, model_width
    )
    routed = jnp.sum(gates[:, :, None] * token_outputs, axis=1)
    output_rows = resid + shared_result + routed
    shared_cot = upstream.astype(jnp.bfloat16)
    shared_down_term = jnp.dot(shared_hidden.T, shared_cot, preferred_element_type=jnp.float32)
    dshared_hidden = jnp.dot(shared_cot, full_sdown.T, preferred_element_type=jnp.float32)
    dshared_pre = swiglu_back(shared_pre, dshared_hidden, shared_width).astype(jnp.bfloat16)
    shared_up_term = jnp.dot(ffn_low.T, dshared_pre, preferred_element_type=jnp.float32)
    dnormed_second = jnp.dot(dshared_pre, full_sup.T, preferred_element_type=jnp.float32)
    token_cot = (gates[:, :, None] * upstream[:, None, :]).astype(jnp.bfloat16)
    dgates = jnp.sum(upstream[:, None, :] * token_outputs, axis=2)
    padded_cot = jnp.concatenate(
        [token_cot.reshape(-1, model_width), jnp.zeros((1, model_width), jnp.bfloat16)], axis=0
    )
    send_cot = padded_cot[send_table].reshape(local_experts, groups, capacity, model_width)
    received_cot = lax.all_to_all(
        send_cot, "expert", split_axis=1, concat_axis=1, tiled=True
    ).reshape(local_experts, groups * capacity, model_width)
    down_term = jnp.einsum(
        "erf,erd->efd", expert_hidden, received_cot, preferred_element_type=jnp.float32
    )
    dexpert_hidden = jnp.einsum(
        "erd,efd->erf", received_cot, experts_down, preferred_element_type=jnp.float32
    )
    dexpert_pre = swiglu_back(expert_pre, dexpert_hidden, hidden_width).astype(jnp.bfloat16)
    up_term = jnp.einsum(
        "erd,erf->edf", expert_rows, dexpert_pre, preferred_element_type=jnp.float32
    )
    drows = jnp.einsum(
        "erf,edf->erd", dexpert_pre, experts_up, preferred_element_type=jnp.float32
    ).astype(jnp.bfloat16)
    returned_grad = lax.all_to_all(
        drows.reshape(local_experts, groups, capacity, model_width),
        "expert",
        split_axis=1,
        concat_axis=1,
        tiled=True,
    )
    row_grads = returned_grad.reshape(-1, model_width)[return_pos].reshape(
        tokens_dev, TOP, model_width
    )
    dnormed_second = dnormed_second + jnp.sum(row_grads, axis=1, dtype=jnp.float32)
    expert_up_grad, expert_down_grad = (
        lax.psum_scatter(
            up_term.astype(jnp.bfloat16), "batch", scatter_dimension=1, tiled=True
        ).astype(jnp.float32),
        lax.psum_scatter(
            down_term.astype(jnp.bfloat16), "batch", scatter_dimension=1, tiled=True
        ).astype(jnp.float32),
    )
    dchosen = (dgates - jnp.sum(dgates * gates, axis=1, keepdims=True)) / chosen_sum
    dprobs = jnp.sum(jnp.where(route_hot, dchosen[:, :, None], 0.0), axis=1)
    dlogits = (probs * (dprobs - jnp.sum(probs * dprobs, axis=1, keepdims=True))).astype(
        jnp.bfloat16
    )
    router_term = jnp.dot(ffn_low.T, dlogits, preferred_element_type=jnp.float32)
    dnormed_second = dnormed_second + jnp.dot(
        dlogits, full_router.T, preferred_element_type=jnp.float32
    )
    dresid_norm, gain_ffn_term = norm_back(dnormed_second, normed_second, inv_second, gain_second)
    dresid = upstream + dresid_norm
    dproj = dresid.astype(jnp.bfloat16)
    out_term = jnp.dot(attn_low.T, dproj, preferred_element_type=jnp.float32)
    dattn = (
        jnp.dot(dproj, full_out.T, preferred_element_type=jnp.float32)
        .astype(jnp.bfloat16)
        .reshape(tokens_dev, heads_count, HEAD)
    )
    delta_rows = jnp.sum(dattn.astype(jnp.float32) * attn_full, axis=2)
    delta_heads = jnp.transpose(delta_rows)
    key_piece = lax.all_gather(keys, "expert", axis=0, tiled=True)
    value_piece = lax.all_gather(values, "expert", axis=0, tiled=True)
    allowed = key_mask(key_piece.shape[0])[None]
    scores = (
        jnp.einsum("qhd,khd->hqk", queries, key_piece, preferred_element_type=jnp.float32)
        * score_scale
    )
    attn_probs = jnp.where(allowed, jnp.exp(scores - logsum[:, :, None]), 0.0)
    dprob = jnp.einsum("qhd,khd->hqk", dattn, value_piece, preferred_element_type=jnp.float32)
    dscore = (attn_probs * (dprob - delta_heads[:, :, None])).astype(jnp.bfloat16)
    attn_probs, dscore = (attn_probs, dscore)
    dquery = jnp.einsum("hqk,khd->qhd", dscore, key_piece, preferred_element_type=jnp.float32)
    dkey_piece = jnp.einsum("hqk,qhd->khd", dscore, queries, preferred_element_type=jnp.float32)
    dvalue_piece = jnp.einsum(
        "hqk,qhd->khd", attn_probs.astype(jnp.bfloat16), dattn, preferred_element_type=jnp.float32
    )
    folded = (dquery, dkey_piece, dvalue_piece)
    dquery = folded[0]
    dkey, dvalue = (
        lax.psum_scatter(
            folded[1].astype(jnp.bfloat16), "expert", scatter_dimension=0, tiled=True
        ).astype(jnp.float32),
        lax.psum_scatter(
            folded[2].astype(jnp.bfloat16), "expert", scatter_dimension=0, tiled=True
        ).astype(jnp.float32),
    )
    dquery_raw = rotate(dquery * score_scale, positions, -1.0).reshape(tokens_dev, model_width)
    dkey_raw = rotate(dkey * score_scale, positions, -1.0).reshape(tokens_dev, model_width)
    dprojected = jnp.concatenate(
        [dquery_raw, dkey_raw, dvalue.reshape(tokens_dev, model_width)], axis=1
    ).astype(jnp.bfloat16)
    qkv_term = jnp.dot(input_low.T, dprojected, preferred_element_type=jnp.float32)
    dnormed_first = jnp.dot(dprojected, full_qkv.T, preferred_element_type=jnp.float32)
    dinput_norm, gain_attn_term = norm_back(dnormed_first, normed_first, inv_first, gain_first)
    input_grad = dresid + dinput_norm
    grads = (
        lax.psum_scatter(qkv_term, ("batch", "expert"), scatter_dimension=0, tiled=True),
        lax.psum_scatter(out_term, ("batch", "expert"), scatter_dimension=0, tiled=True),
        lax.psum_scatter(shared_up_term, ("batch", "expert"), scatter_dimension=0, tiled=True),
        lax.psum_scatter(shared_down_term, ("batch", "expert"), scatter_dimension=0, tiled=True),
        lax.psum_scatter(router_term, ("batch", "expert"), scatter_dimension=0, tiled=True),
        lax.psum_scatter(gain_attn_term, ("batch", "expert"), scatter_dimension=0, tiled=True),
        lax.psum_scatter(gain_ffn_term, ("batch", "expert"), scatter_dimension=0, tiled=True),
    )
    (
        qkv_grad,
        out_grad,
        shared_up_grad,
        shared_down_grad,
        router_grad,
        gain_attn_grad,
        gain_ffn_grad,
    ) = grads
    return (
        output_rows[None],
        input_grad[None],
        qkv_grad,
        out_grad,
        shared_up_grad,
        shared_down_grad,
        router_grad,
        gain_attn_grad,
        gain_ffn_grad,
        expert_up_grad,
        expert_down_grad,
    )


PAIR_OF = {0: 0, 2: 1, 4: 2, 6: 3, 3: 4}
F32 = jnp.float32
LOW = jnp.bfloat16
COST = 10**9


def low(values):
    return values.astype(LOW)


def dot(left, right, dims=((1,), (0,))):
    return lax.dot_general(left, right, (dims, ((), ())), preferred_element_type=F32)


MESH_ID = pl.DeviceIdType.MESH


def place():
    b = lax.axis_index("batch")
    e = lax.axis_index("expert")
    return b, e, e // 2, lax.rem(e, 2)


def greet_near():
    b, e, z, core = place()
    barrier = pltpu.get_barrier_semaphore()
    for device in ((b ^ 1, e), (b ^ 2, e), (b, e ^ 1)):
        pl.semaphore_signal(barrier, inc=1, device_id=device, device_id_type=MESH_ID)

    @pl.when(z > 0)
    def _():
        pl.semaphore_signal(barrier, inc=1, device_id=(b, e - 2), device_id_type=MESH_ID)

    @pl.when(z < 3)
    def _():
        pl.semaphore_signal(barrier, inc=1, device_id=(b, e + 2), device_id_type=MESH_ID)

    ends = jnp.where((z == 0) | (z == 3), 1, 0)
    pl.semaphore_wait(barrier, 5 - ends)


def greet(devices):
    barrier = pltpu.get_barrier_semaphore()
    for device in devices:
        pl.semaphore_signal(barrier, inc=1, device_id=device, device_id_type=MESH_ID)
    pl.semaphore_wait(barrier, len(devices))


def pack_mates():
    b, e, _, _ = place()
    return [(b, lax.rem(e + i, 8)) for i in range(1, 8)]


def send(src, dst, send_sem, recv_sem, device):
    return pltpu.make_async_remote_copy(
        src_ref=src,
        dst_ref=dst,
        send_sem=send_sem,
        recv_sem=recv_sem,
        device_id=device,
        device_id_type=MESH_ID,
    )


GATHER_SEMS = [pltpu.SemaphoreType.DMA((3,))] * 4 + [pltpu.SemaphoreType.DMA((4,))] * 2


def line_stages(buf, up_send, up_recv, down_send, down_recv, core_send, core_recv):
    b, e, z, core = place()

    def to_core(owner_z):
        block = buf.at[2 * owner_z + core]
        return send(block, block, core_send.at[owner_z], core_recv.at[owner_z], (b, e ^ 1))

    def up(step):
        block = buf.at[jnp.maximum(2 * (z - step), 0) + core]
        return send(block, block, up_send.at[step], up_recv.at[step], (b, jnp.minimum(e + 2, 7)))

    def down(step):
        block = buf.at[jnp.minimum(2 * (z + step), 6) + core]
        return send(
            block, block, down_send.at[step], down_recv.at[step], (b, jnp.maximum(e - 2, 0))
        )

    def start(step):
        @pl.when((z >= step) & (z < 3))
        def _():
            up(step).start()

        @pl.when((z + step <= 3) & (z > 0))
        def _():
            down(step).start()

        if step == 0:
            to_core(z).start()

    def arrive(step):
        @pl.when(z - 1 - step >= 0)
        def _():
            up(step).wait_recv()

        @pl.when(z + 1 + step <= 3)
        def _():
            down(step).wait_recv()

        if step < 2:
            start(step + 1)

        @pl.when(z - 1 - step >= 0)
        def _():
            to_core(z - 1 - step).start()

        @pl.when(z + 1 + step <= 3)
        def _():
            to_core(z + 1 + step).start()

    def finish():
        for owner_z in range(4):
            to_core(owner_z).wait()
        for step in range(3):

            @pl.when((z >= step) & (z < 3))
            def _():
                up(step).wait_send()

            @pl.when((z + step <= 3) & (z > 0))
            def _():
                down(step).wait_send()

    return [lambda: start(0)] + [functools.partial(arrive, i) for i in range(3)] + [finish]


def line_gather(buf, *sems):
    for stage in line_stages(buf, *sems):
        stage()


def scatter_scratch(tokens, width):
    return [pltpu.VMEM((4, tokens, width), LOW)] + [
        pltpu.VMEM((3, tokens, width), LOW) for _ in range(4)
    ]


SCATTER_SEMS = [pltpu.SemaphoreType.DMA((3,))] * 4 + [pltpu.SemaphoreType.DMA((4,))] * 2


def line_sum_stages(
    part,
    from_core,
    up_out,
    up_in,
    down_out,
    down_in,
    up_send,
    up_recv,
    down_send,
    down_recv,
    core_send,
    core_recv,
):
    b, e, z, core = place()

    def to_core(target):
        return send(
            part.at[2 * target + 1 - core],
            from_core.at[target],
            core_send.at[target],
            core_recv.at[target],
            (b, e ^ 1),
        )

    def up(step):
        return send(
            up_out.at[step],
            up_in.at[step],
            up_send.at[step],
            up_recv.at[step],
            (b, jnp.minimum(e + 2, 7)),
        )

    def down(step):
        return send(
            down_out.at[step],
            down_in.at[step],
            down_send.at[step],
            down_recv.at[step],
            (b, jnp.maximum(e - 2, 0)),
        )

    def chip_sum(target):
        return part[2 * target + core].astype(F32) + from_core[target].astype(F32)

    def start():
        for target in (3, 0, 2, 1):
            to_core(target).start()

    def send_up(step):
        up_out[step] = low(chip_sum(3 - step))
        up(step).start()

    def send_down(step):
        down_out[step] = low(chip_sum(step))
        down(step).start()

    def pass_up(step):
        up(step).wait_recv()
        up_out[step] = low(chip_sum(3 - step) + up_in[step].astype(F32))
        up(step).start()

    def pass_down(step):
        down(step).wait_recv()
        down_out[step] = low(chip_sum(step) + down_in[step].astype(F32))
        down(step).start()

    def ends():
        for target in range(4):
            to_core(target).wait()

        @pl.when(z == 0)
        def _():
            for step in range(3):
                send_up(step)

        @pl.when(z == 3)
        def _():
            for step in range(3):
                send_down(step)

    def near():
        @pl.when(z == 1)
        def _():
            pass_up(0)

        @pl.when(z == 2)
        def _():
            pass_down(0)

    def far():
        @pl.when(z == 1)
        def _():
            pass_up(1)
            pass_down(0)

        @pl.when(z == 2)
        def _():
            pass_down(1)
            pass_up(0)

    def finish():
        @pl.when(z == 0)
        def _():
            up_in[0] = jnp.zeros_like(up_in[0])

        @pl.when(z == 3)
        def _():
            down_in[0] = jnp.zeros_like(down_in[0])

        last_up = lax.rem(3 - z, 3)
        last_down = lax.rem(z, 3)

        @pl.when(z > 0)
        def _():
            up(last_up).wait_recv()

        @pl.when(z < 3)
        def _():
            down(last_down).wait_recv()

        total = chip_sum(z) + up_in[last_up].astype(F32) + down_in[last_down].astype(F32)
        for step in range(3):

            @pl.when(z < 3 - step)
            def _():
                up(step).wait_send()

            @pl.when(z > step)
            def _():
                down(step).wait_send()

        return total

    return [start, ends, near, far, finish]


def sum_into(out, *terms):
    if len(out.shape) == 2:

        @pl.loop(0, out.shape[0] // 16)
        def _(i):
            here = pl.ds(pl.multiple_of(i * 16, 16), 16)
            total = terms[0][here, :].astype(F32)
            for term in terms[1:]:
                total = total + term[here, :].astype(F32)
            out[here, :] = total.astype(out.dtype)

    else:
        for i in range(out.shape[0]):
            total = terms[0][i].astype(F32)
            for term in terms[1:]:
                total = total + term[i].astype(F32)
            out[i] = total.astype(out.dtype)


REDUCE_COUNT = 8


def reduce_scratch(half_shape, far=False):
    kept = (4, *half_shape) if far else (1, 8, 128)
    return [
        pltpu.VMEM((6, *half_shape), LOW),
        pltpu.VMEM((2, *half_shape), LOW),
        pltpu.VMEM(kept, LOW if far else F32),
    ] + [pltpu.SemaphoreType.DMA((size,)) for size in (3, 3, 3, 3, 4)]


def reduce_stages(
    block, out, received, sums, kept, x_send, x_recv, y_send, y_recv, local_sem
):
    b, e, _, _ = place()
    x_device, y_device = (b ^ 1, e), (b ^ 2, e)

    def over_x(slot):
        src = (block(b ^ 3, 0), block(b ^ 1, 0), sums.at[1])[slot]
        return send(src, received.at[slot], x_send.at[slot], x_recv.at[slot], x_device)

    def over_y(slot):
        src = (block(b ^ 3, 1), block(b ^ 2, 1), sums.at[0])[slot]
        return send(src, received.at[3 + slot], y_send.at[slot], y_recv.at[slot], y_device)

    far = kept.shape[0] == 4

    def mine(i):
        return (block(b ^ 2, 0), block(b ^ 1, 1), block(b, 0), block(b, 1))[i]

    def keep(i):
        return pltpu.make_async_copy(mine(i), kept.at[i], local_sem.at[i])

    def held(i):
        if not far:
            return mine(i)
        keep(i).wait()
        return kept.at[i]

    def start():
        over_x(0).start()
        over_y(0).start()
        for i in range(4 if far else 0):
            keep(i).start()

    def forward():
        over_x(0).wait_recv()
        over_x(1).start()
        sum_into(sums.at[0], held(0), received.at[0])
        over_y(2).start()
        over_y(0).wait_recv()
        over_y(1).start()
        sum_into(sums.at[1], held(1), received.at[3])
        over_x(2).start()

    def finish():
        for slot in (1, 2):
            over_x(slot).wait_recv()
            over_y(slot).wait_recv()
        sum_into(out(0), held(2), received.at[1], received.at[5])
        sum_into(out(1), held(3), received.at[4], received.at[2])
        for slot in range(3):
            over_x(slot).wait_send()
            over_y(slot).wait_send()

    return start, forward, finish


def reduce_rows(term, out, scratch):
    half_rows = out.shape[0] // 2

    def block(owner, half):
        return term.at[pl.ds((2 * owner + half) * half_rows, half_rows)]

    def out_half(half):
        return out.at[pl.ds(half * half_rows, half_rows)]

    return reduce_stages(block, out_half, *scratch)


def bring_all(far_refs, near_refs, sem):
    copies = [
        pltpu.make_async_copy(far, near, sem.at[i])
        for i, (far, near) in enumerate(zip(far_refs, near_refs))
    ]
    for copy in copies:
        copy.start()
    return copies


def kernel_call(body, outs, args, scratch, collective_id, far_outs=(), far_args=()):
    near = pl.BlockSpec(memory_space=pltpu.VMEM)
    far = pl.BlockSpec(memory_space=pl.ANY)
    return pl.pallas_call(
        body,
        cost_estimate=pl.CostEstimate(flops=COST, bytes_accessed=COST, transcendentals=0),
        out_shape=[jax.ShapeDtypeStruct(shape, dtype) for shape, dtype in outs],
        in_specs=[far if i in far_args else near for i in range(len(args))],
        out_specs=[far if i in far_outs else near for i in range(len(outs))],
        scratch_shapes=scratch,
        compiler_params=pltpu.CompilerParams(
            collective_id=collective_id, has_side_effects=True, vmem_limit_bytes=56 * 2**20
        ),
    )(*args)


SPREAD_SEMS = [pltpu.SemaphoreType.DMA((2,))] + [pltpu.SemaphoreType.DMA((3,))] * 4


def spread_stages(own, whole, local_sem, x_send, x_recv, y_send, y_recv):
    b, e, _, _ = place()
    x_device, y_device = (b ^ 1, e), (b ^ 2, e)

    def over_x(slot):
        src, dst = (
            (own(0), whole(b, 0)),
            (own(1), whole(b, 1)),
            (whole(b ^ 2, 1), whole(b ^ 2, 1)),
        )[slot]
        return send(src, dst, x_send.at[slot], x_recv.at[slot], x_device)

    def over_y(slot):
        src, dst = (
            (own(1), whole(b, 1)),
            (own(0), whole(b, 0)),
            (whole(b ^ 1, 0), whole(b ^ 1, 0)),
        )[slot]
        return send(src, dst, y_send.at[slot], y_recv.at[slot], y_device)

    def keep(half):
        return pltpu.make_async_copy(own(half), whole(b, half), local_sem.at[half])

    def start():
        over_x(0).start()
        over_y(0).start()
        for half in range(2):
            keep(half).start()

    def forward():
        over_x(0).wait_recv()
        over_y(2).start()
        over_x(1).start()
        over_y(0).wait_recv()
        over_x(2).start()
        over_y(1).start()
    def finish():
        for slot in range(3):
            for over in (over_x, over_y):
                if slot > 0:
                    over(slot).wait_recv()
                over(slot).wait_send()
        for half in range(2):
            keep(half).wait()

    return start, forward, finish


def spread_rows(own_ref, whole_ref, rows, sems):
    half_rows = rows // 2

    def own(half):
        return own_ref.at[pl.ds(half * half_rows, half_rows)]

    def whole(owner, half):
        return whole_ref.at[pl.ds(owner * rows + half * half_rows, half_rows)]

    return spread_stages(own, whole, *sems)


def opening_kernel(
    rows, router, first_gain, second_gain, routes, ids, qkv, sup, out_weight, up_weight,
    n1_all, gains, small_all, marks_all, columns_all, out_all, up_all,
    small, marks, columns, w_out, up_own, up_wide, up_sem, *sems,
):
    (
        b_send, b_recv, s_send, s_recv, m_send, m_recv, c_send, c_recv,
        x_send, x_recv, y_send, y_recv, z_send, z_recv, o_send, o_recv, p_send, p_recv,
    ) = sems[:18]
    b, e, z, core = place()
    over = [(b ^ bit, e) for bit in (1, 2, 3)]
    mates = pack_mates()
    up_start, up_forward, up_finish = spread_rows(up_own, up_all, up_own.shape[0], sems[18:23])
    bring = pltpu.make_async_copy(up_weight.at[0], up_wide, up_sem.at[0])
    bring.start()
    greet(over + mates)
    bring.wait()
    up_own[...] = low(up_wide[...])
    up_start()
    rows_w = router.shape[0]
    small[...] = jnp.zeros_like(small)
    small[:rows_w] = router[...]
    small[rows_w : rows_w + 1, : first_gain.shape[1]] = first_gain[...]
    small[rows_w + 1 : rows_w + 2, : second_gain.shape[1]] = second_gain[...]
    chosen = routes[0].astype(F32)
    chosen = jnp.concatenate([chosen, jnp.zeros((128, 128 - TOP), F32)], axis=1).T
    marks[...] = jnp.concatenate(
        [chosen[:TOP], ids[...].astype(F32), jnp.zeros((7 - TOP, 128), F32)], axis=0
    )
    pair = 2 * HEAD
    width = rows.shape[1]
    for i in range(8):
        for part in range(3):
            lanes = slice(part * pair, (part + 1) * pair)
            if i in PAIR_OF:
                start = part * width + PAIR_OF[i] * pair
                columns[i, :, lanes] = low(qkv[:, start : start + pair])
            else:
                columns[i, :, lanes] = jnp.zeros((columns.shape[1], pair), LOW)
        columns[i, :, 3 * pair :] = sup[i]
    w_out[...] = low(out_weight[...])
    small_all[e, b] = small[...]
    marks_all[e] = marks[...]
    columns_all[b, e] = columns[e]
    out_all[b, z, core] = w_out[...]
    first = []
    for i, device in enumerate(over):
        first.append(send(small, small_all.at[e, b], b_send.at[i], b_recv.at[i], device))
        first[-1].start()
    across = []
    for i, device in enumerate(mates):
        across.append(
            send(columns.at[device[1]], columns_all.at[b, e], c_send.at[i], c_recv.at[i], device)
        )
        across[-1].start()
    beyond = []
    for i, device in enumerate(over):
        beyond.append(
            send(w_out, out_all.at[b, z, core], o_send.at[i], o_recv.at[i], device)
        )
        beyond[-1].start()
    rest = []
    for i, device in enumerate(mates):
        rest.append(send(marks, marks_all.at[e], m_send.at[i], m_recv.at[i], device))
        rest[-1].start()
    values = rows[...]
    inv = lax.rsqrt(jnp.mean(values * values, axis=1, keepdims=True) + EPSILON)
    for copy in first:
        copy.wait()
    second = []
    for i, device in enumerate(mates):
        second.append(send(small_all.at[e], small_all.at[e], s_send.at[i], s_recv.at[i], device))
        second[-1].start()
    for copy in second:
        copy.wait()

    piece = width // 32
    lane = lax.broadcasted_iota(jnp.int32, (128, width), 1)
    spread = low(jnp.where(lax.rem(lane, piece) == lax.broadcasted_iota(jnp.int32, (128, width), 0), 1.0, 0.0))
    row = lax.broadcasted_iota(jnp.int32, (32, width), 0)
    owner = lax.rem(row, 4) * 8 + row // 4
    mine = lax.broadcasted_iota(jnp.int32, (32, width), 1) // piece == owner
    for i, index in enumerate((5, 6)):
        pieces = jnp.concatenate([small_all[j, :, index, :] for j in range(8)], axis=0)
        spread_out = dot(low(pieces), spread)
        gains[i : i + 1, :] = jnp.sum(jnp.where(mine, spread_out, 0.0), axis=0, keepdims=True)
    n1_all[e] = low(values * inv * gains[0:1, :])
    stages = line_stages(n1_all, *sems[23:])
    stages[0]()

    def hop(owner, half, sems_out, sems_in, slot, device):
        block = columns_all.at[owner, pl.ds(4 * half, 4)]
        return send(block, block, sems_out.at[slot], sems_in.at[slot], device)

    def over_x(slot):
        owner, half = ((b, 0), (b, 1), (b ^ 2, 1))[slot]
        return hop(owner, half, x_send, x_recv, slot, over[0])

    def over_y(slot):
        owner, half = ((b, 1), (b, 0), (b ^ 1, 0))[slot]
        return hop(owner, half, y_send, y_recv, slot, over[1])

    def out_block(owner_z):
        return out_all.at[:, owner_z, core]

    def out_pair(slot):
        block = out_block(lax.rem(z + 4 - slot, 4))
        return send(block, block, p_send.at[slot], p_recv.at[slot], (b, e ^ 1))

    for copy in across:
        copy.wait()
    over_x(0).start()
    over_y(0).start()
    up_forward()
    over_x(1).start()
    over_y(1).start()
    stages[1]()
    over_x(0).wait_recv()
    over_y(2).start()
    over_y(0).wait_recv()
    over_x(2).start()
    stages[2]()
    for copy in beyond:
        copy.wait()
    along = []
    for i in range(3):
        device = (b, lax.rem(e + 2 * i + 2, 8))
        along.append(send(out_block(z), out_block(z), z_send.at[i], z_recv.at[i], device))
        along[-1].start()
    out_pair(0).start()
    stages[3]()
    for i, copy in enumerate(along):
        copy.wait()
        out_pair(i + 1).start()
    stages[4]()
    for slot in range(3):
        for over_one in (over_x, over_y):
            if slot > 0:
                over_one(slot).wait_recv()
            over_one(slot).wait_send()
    for copy in rest:
        copy.wait()
    for slot in range(4):
        out_pair(slot).wait()
    up_finish()


def opening(rows, router, first_gain, second_gain, routes, ids, qkv, sup, out_weight, up_weight):
    tokens, width = rows.shape
    _, up_rows, up_width = up_weight.shape
    rows_w = out_weight.shape[0]
    wide = 6 * HEAD + sup.shape[2]
    sizes = (3, 3, 7, 7, 7, 7, 7, 7, 3, 3, 3, 3, 3, 3, 3, 3, 4, 4)
    return kernel_call(
        opening_kernel,
        [
            ((8, tokens, width), LOW),
            ((2, width), F32),
            ((8, 4, 8, 128), F32),
            ((8, 8, 128), F32),
            ((4, 8, rows_w, wide), LOW),
            ((4, 4, 2, rows_w, width), LOW),
            ((4 * up_rows, up_width), LOW),
        ],
        (rows, router, first_gain, second_gain, routes, ids, qkv, sup, out_weight, up_weight),
        [
            pltpu.VMEM((8, 128), F32),
            pltpu.VMEM((8, 128), F32),
            pltpu.VMEM((8, rows_w, wide), LOW),
            pltpu.VMEM((rows_w, width), LOW),
            pltpu.VMEM((up_rows, up_width), LOW),
            pltpu.VMEM((up_rows, up_width), F32),
            pltpu.SemaphoreType.DMA((1,)),
        ]
        + [pltpu.SemaphoreType.DMA((size,)) for size in sizes]
        + SPREAD_SEMS
        + GATHER_SEMS,
        0,
        far_outs=(6,),
        far_args=(9,),
    )


def holder(e):
    return (lax.rem(e, 2) == 0) | (e == 3), jnp.where(e == 3, 4, e // 2)


BLOCK = 256


def turned(values, cosine, sine):
    return values * cosine + pltpu.roll(values, HEAD // 2, 1) * sine


def middle_kernel(
    n1_far, weights_far, cosine_far, sine_far, ids_row, ids_column, w_out_far, rows, gain, cot, up_weight, down_weight,
    sdown_weight,
    qkv, logsum, attn, resid, n2_all, cot_all, up_all, down_all, sdown_all, down_second, n2_own,
    n1, weights, cosine, sine, w_out, bring_sem,
    attended, up_own, up_wide, down_own, sdown_own, up_sem, a_send, a_recv, *sems,
):
    b, e, z, core = place()
    tokens = rows.shape[0]
    mates = pack_mates()
    count = len(SPREAD_SEMS)
    spreads = [
        spread_rows(up_own, up_all, up_own.shape[0], sems[:count]),
        spread_rows(down_own, down_all, down_own.shape[0], sems[count : 2 * count]),
        spread_rows(sdown_own, sdown_all, sdown_own.shape[0], sems[2 * count : 3 * count]),
    ]
    sems = sems[3 * count :]
    cot_stages = line_stages(cot_all, *sems[: len(GATHER_SEMS)])
    n2_stages = line_stages(n2_all, *sems[len(GATHER_SEMS) :])
    cot_all[e] = low(cot[0])
    bring = pltpu.make_async_copy(up_weight.at[1], up_wide, up_sem.at[0])
    bring.start()
    brought = bring_all(
        (n1_far, weights_far, cosine_far, sine_far, w_out_far),
        (n1, weights, cosine, sine, w_out),
        bring_sem,
    )
    greet([(b ^ 1, e), (b ^ 2, e), *mates])
    bring.wait()
    up_own[...] = low(up_wide[...])
    spreads[0][0]()
    cot_stages[0]()
    down_own[...] = low(down_weight[0])
    down_second[...] = low(down_weight[1])
    short = sdown_own.shape[0] - sdown_weight.shape[0]
    sdown_own[...] = low(
        jnp.concatenate([sdown_weight[...], jnp.zeros((short, cot.shape[2]), F32)], axis=0)
    )
    for start, _, _ in spreads[1:]:
        start()
    holds, pair = holder(e)
    for copy in brought:
        copy.wait()

    @pl.when(jnp.logical_not(holds))
    def _():
        qkv[...] = jnp.zeros_like(qkv)
        logsum[...] = jnp.zeros_like(logsum)

    @pl.when(holds)
    def _():
        @pl.loop(0, n1.shape[0] // BLOCK)
        def _(i):
            here = pl.ds(pl.multiple_of(i * BLOCK, BLOCK), BLOCK)
            projected = dot(n1[here, :], weights[:, : 6 * HEAD])
            cos_here, sin_here = cosine[here, :], sine[here, :]
            for part in range(6):
                piece = projected[:, part * HEAD : (part + 1) * HEAD]
                if part < 4:
                    piece = turned(piece, cos_here, sin_here)
                qkv[part, here, :] = low(piece)

    cot_stages[1]()
    for head in range(2):

        @pl.when(holds)
        def _():
            for i in range(n1.shape[0] // BLOCK):
                here = pl.ds(i * BLOCK, BLOCK)
                keys = (i + 1) * BLOCK
                scores = dot(qkv[head, here, :], qkv[2 + head, :keys, :], ((1,), (1,)))
                scores = jnp.where(
                    allowed_here(ids_column, ids_row, i, keys), scores * HEAD ** (-0.5), NEGATIVE
                )
                top = jnp.max(scores, axis=1, keepdims=True)
                weight = jnp.exp(scores - top)
                total = jnp.sum(weight, axis=1, keepdims=True)
                out = dot(low(weight / total), qkv[4 + head, :keys, :])
                logsum[head, here, :] = jnp.broadcast_to(top + jnp.log(total), (BLOCK, HEAD))
                for j in range(BLOCK // tokens):
                    attended[i * (BLOCK // tokens) + j, :, head * HEAD : (head + 1) * HEAD] = low(
                        out[j * tokens : (j + 1) * tokens]
                    )

        if head == 0:
            cot_stages[2]()
        spreads[head][1]()

    def give(i):
        other = lax.rem(e + i, 8)
        return send(
            attended.at[other], attn.at[pair], a_send.at[i - 1], a_recv.at[pair], (b, other)
        )

    @pl.when(holds)
    def _():
        for i in range(1, 8):
            give(i).start()
        attn[pair] = attended[e]

    total = rows[...]
    for source, index in PAIR_OF.items():

        @pl.when(e != source)
        def _():
            block = attn.at[index]
            send(block, block, a_send.at[0], a_recv.at[index], (b, source)).wait_recv()

        size = attn.shape[2]
        total = total + dot(attn[index], w_out[index * size : (index + 1) * size, :])
    resid[...] = total
    inv = lax.rsqrt(jnp.mean(total * total, axis=1, keepdims=True) + EPSILON)
    n2_all[e] = low(total * inv * gain[...])
    n2_own[...] = n2_all[e]
    n2_stages[0]()
    cot_stages[3]()
    spreads[2][1]()
    for stage in n2_stages[1:]:
        stage()
    cot_stages[4]()

    @pl.when(holds)
    def _():
        for i in range(1, 8):
            give(i).wait_send()

    for _, _, finish in spreads:
        finish()


def allowed_here(ids_column, ids_row, i, keys):
    query = i * BLOCK + lax.broadcasted_iota(jnp.int32, (BLOCK, keys), 0)
    key = lax.broadcasted_iota(jnp.int32, (BLOCK, keys), 1)
    same = ids_column[i * BLOCK : (i + 1) * BLOCK, :] == ids_row[:, :keys]
    return (key <= query) & same


def middle(n1, weights, cosine, sine, ids_row, ids_column, w_out, rows, gain, cot, up_weight, down_weight, sdown_weight):
    tokens, width = rows.shape
    length = n1.shape[0]
    pair = 2 * HEAD
    count = len(PAIR_OF)
    _, up_rows, up_width = up_weight.shape
    down_rows = down_weight.shape[1]
    sdown_rows = -(-sdown_weight.shape[0] // 32) * 32
    return kernel_call(
        middle_kernel,
        [
            ((6, length, HEAD), LOW),
            ((2, length, HEAD), F32),
            ((count, tokens, pair), LOW),
            ((tokens, width), F32),
            ((8, tokens, width), LOW),
            ((8, tokens, width), LOW),
            ((4 * up_rows, up_width), LOW),
            ((4 * down_rows, width), LOW),
            ((4 * sdown_rows, width), LOW),
            ((down_rows, width), LOW),
            ((tokens, width), LOW),
        ],
        (n1, weights, cosine, sine, ids_row, ids_column, w_out, rows, gain, cot, up_weight, down_weight, sdown_weight),
        [
            pltpu.VMEM(n1.shape, LOW),
            pltpu.VMEM(weights.shape, LOW),
            pltpu.VMEM(cosine.shape, F32),
            pltpu.VMEM(sine.shape, F32),
            pltpu.VMEM(w_out.shape, LOW),
            pltpu.SemaphoreType.DMA((5,)),
            pltpu.VMEM((8, tokens, pair), LOW),
            pltpu.VMEM((up_rows, up_width), LOW),
            pltpu.VMEM((up_rows, up_width), F32),
            pltpu.VMEM((down_rows, width), LOW),
            pltpu.VMEM((sdown_rows, width), LOW),
            pltpu.SemaphoreType.DMA((1,)),
            pltpu.SemaphoreType.DMA((7,)),
            pltpu.SemaphoreType.DMA((count,)),
        ]
        + SPREAD_SEMS * 3
        + GATHER_SEMS * 2,
        1,
        far_outs=(6, 7, 8),
        far_args=(0, 1, 2, 3, 6, 10),
    )


def experts_kernel(
    n2, cot, columns, w_sdown, w_router, marks_all, down_second, up_first, up_second, down_first,
    gates, out_part, row_sum, sdown_term, sup_term, down_grad, up_term_first, up_term_second, down_term_second,
    part, w_sup, up_w, down_w, hid, dpre, hid_shared, dpre_shared, load_sem, store_sem, *scratch,
):
    e = lax.axis_index("expert")
    length, width = n2.shape
    hidden = down_w.shape[1]
    pad = w_sdown.shape[0]
    loads = [
        pltpu.make_async_copy(up_first, up_w.at[0], load_sem.at[0]),
        pltpu.make_async_copy(down_first, down_w.at[0], load_sem.at[1]),
        pltpu.make_async_copy(columns.at[:, pl.ds(6 * HEAD, 2 * pad)], w_sup, load_sem.at[3]),
        pltpu.make_async_copy(up_second, up_w.at[1], load_sem.at[2]),
    ]
    for copy in loads:
        copy.start()
    count = len(SPREAD_SEMS)
    arrive = spread_rows(down_second, down_w.at[1], down_second.shape[0], scratch[:count])
    reduce = reduce_rows(down_w.at[0], down_grad, scratch[count : count + REDUCE_COUNT])
    stages = line_sum_stages(part, *scratch[count + REDUCE_COUNT :])
    tokens = part.shape[1]
    greet_near()
    arrive[0]()
    for copy in loads[:3]:
        copy.wait()
    lane = lax.broadcasted_iota(jnp.int32, (ROWS, 128), 1)
    number = lax.broadcasted_iota(jnp.int32, (ROWS, w_router.shape[1]), 1)

    def weigh(here, x):
        chosen = number == marks_all[here, 0:1]
        for j in range(1, TOP):
            chosen = chosen | (number == marks_all[here, j : j + 1])
        logits = jnp.where(chosen, dot(x, w_router[...]), NEGATIVE)
        weight = jnp.exp(logits - jnp.max(logits, axis=1, keepdims=True))
        weight = jnp.where(chosen, weight, 0.0)
        gates[here, :] = weight / jnp.sum(weight, axis=1, keepdims=True)

    def routed(k, here, x, c):
        gate = jnp.sum(jnp.where(number == 2 * e + k, gates[here, :], 0.0), axis=1, keepdims=True)
        gate_part = dot(x, up_w[k, :, :hidden])
        up_part = dot(x, up_w[k, :, hidden:])
        back = dot(c, down_w[k], ((1,), (1,)))
        silu, slope = silu_parts(gate_part, up_part)
        value = silu * up_part
        dgate = jnp.sum(back * value, axis=1, keepdims=True)
        hid[k, here, :] = low(value * gate)
        back = back * gate
        dpre[k, here, :hidden] = low(back * slope)
        dpre[k, here, hidden:] = low(back * silu)
        out = dot(hid[k, here, :], down_w[k])
        drow = dot(dpre[k, here, :], up_w[k], ((1,), (1,)))
        return out, drow, dgate

    def mark(k, dgate, marks):
        high = low(dgate).astype(F32)
        marks = jnp.where(lane == 2 * e + k, high, marks)
        return jnp.where(lane == 2 * e + k + 16, dgate - high, marks)

    def first_pass(i):
        here = pl.ds(pl.multiple_of(i * ROWS, ROWS), ROWS)
        x = n2[here, :]
        c = cot[here, :]
        weigh(here, x)
        gate_part = dot(x, w_sup[:, :pad])
        up_part = dot(x, w_sup[:, pad:])
        back = dot(c, w_sdown[...], ((1,), (1,)))
        silu, slope = silu_parts(gate_part, up_part)
        hid_shared[here, :] = low(silu * up_part)
        dpre_shared[here, :pad] = low(back * slope)
        dpre_shared[here, pad:] = low(back * silu)
        out, drow, dgate = routed(0, here, x, c)
        out = out + dot(hid_shared[here, :], w_sdown[...])
        drow = drow + dot(dpre_shared[here, :], w_sup[...], ((1,), (1,)))
        marks = mark(0, dgate, jnp.zeros((ROWS, 128), F32))
        out_part[here, :] = low(out)
        for j in range(ROWS // tokens):
            rows = slice(j * tokens, (j + 1) * tokens)
            part[i * (ROWS // tokens) + j, :, :width] = low(drow[rows])
            part[i * (ROWS // tokens) + j, :, width:] = low(marks[rows])

    half = length // ROWS // 2

    @pl.loop(0, half)
    def _(i):
        first_pass(i)

    arrive[1]()

    @pl.loop(half, 2 * half)
    def _(i):
        first_pass(i)

    loads[3].wait()
    arrive[2]()

    @pl.loop(0, length // ROWS)
    def _(i):
        here = pl.ds(pl.multiple_of(i * ROWS, ROWS), ROWS)
        out, drow, dgate = routed(1, here, n2[here, :], cot[here, :])
        out_part[here, :] = low(out_part[here, :].astype(F32) + out)
        for j in range(ROWS // tokens):
            rows = slice(j * tokens, (j + 1) * tokens)
            block = i * (ROWS // tokens) + j
            part[block, :, :width] = low(part[block, :, :width].astype(F32) + drow[rows])
            marks = part[block, :, width:].astype(F32)
            high = low(dgate[rows]).astype(F32)
            marks = jnp.where(lane[rows] == 2 * e + 1, high, marks)
            marks = jnp.where(lane[rows] == 2 * e + 17, dgate[rows] - high, marks)
            part[block, :, width:] = low(marks)

    stages[0]()

    def up_gradient(k, up_ref):
        @pl.loop(0, width // COLS)
        def _(i):
            here = pl.ds(pl.multiple_of(i * COLS, COLS), COLS)
            up_w[k, here, :] = low(dot(n2[:, here], dpre[k], ((0,), (0,))))

        store = pltpu.make_async_copy(up_w.at[k], up_ref, store_sem.at[k])
        store.start()
        return store

    def down_gradient(k):
        @pl.loop(0, hidden // 128)
        def _(i):
            here = pl.ds(pl.multiple_of(i * 128, 128), 128)
            down_w[k, here, :] = low(dot(hid[k, :, here], cot[...], ((0,), (0,))))

    down_gradient(0)
    reduce[0]()
    stages[1]()
    stores = [up_gradient(0, up_term_first)]
    stages[2]()
    reduce[1]()
    down_gradient(1)
    stores.append(pltpu.make_async_copy(down_w.at[1], down_term_second, store_sem.at[2]))
    stores[-1].start()
    stages[3]()
    stores.append(up_gradient(1, up_term_second))
    sdown_term[...] = low(dot(hid_shared[...], cot[...], ((0,), (0,))))

    @pl.loop(0, width // COLS)
    def _(i):
        here = pl.ds(pl.multiple_of(i * COLS, COLS), COLS)
        sup_term[here, :] = low(dot(n2[:, here], dpre_shared[...], ((0,), (0,))))

    row_sum[...] = stages[4]()
    reduce[2]()
    for copy in stores:
        copy.wait()


ROWS = 256
COLS = 256


def experts_phase(
    n2, cot, columns, w_sdown, w_router, marks, down_second, up_first, up_second, down_first
):
    length, width = n2.shape
    hidden = down_first.shape[0]
    pad = w_sdown.shape[0]
    tokens = length // 8
    wide = width + 128
    return kernel_call(
        experts_kernel,
        [
            ((length, w_router.shape[1]), F32),
            ((length, width), LOW),
            ((tokens, wide), F32),
            ((pad, width), LOW),
            ((width, 2 * pad), LOW),
            ((hidden // 4, width), F32),
            (up_first.shape, LOW),
            (up_first.shape, LOW),
            ((hidden, width), LOW),
        ],
        (n2, cot, columns, w_sdown, w_router, marks, down_second, up_first, up_second, down_first),
        [
            pltpu.VMEM((8, tokens, wide), LOW),
            pltpu.VMEM((width, 2 * pad), LOW),
            pltpu.VMEM((2, *up_first.shape), LOW),
            pltpu.VMEM((2, hidden, width), LOW),
            pltpu.VMEM((2, length, hidden), LOW),
            pltpu.VMEM((2, length, 2 * hidden), LOW),
            pltpu.VMEM((length, pad), LOW),
            pltpu.VMEM((length, 2 * pad), LOW),
            pltpu.SemaphoreType.DMA((4,)),
            pltpu.SemaphoreType.DMA((3,)),
        ]
        + SPREAD_SEMS
        + reduce_scratch((hidden // 8, width))
        + scatter_scratch(tokens, wide)
        + SCATTER_SEMS,
        4,
        far_outs=(6, 7, 8),
        far_args=(2, 7, 8, 9),
    )


def turn_kernel(
    row_sum, out_part, upstream, gates, w_router, resid, gain, w_out, attn, n2, up_term, down_term,
    dresid, small, out_term, darrived, output_rows, up_grad, down_grad,
    dattn, a_send, a_recv, *scratch,
):
    b, e, z, core = place()
    greet([(b ^ 1, e), (b ^ 2, e), *pack_mates()])
    reduces = [
        reduce_rows(up_term, up_grad, scratch[:REDUCE_COUNT]),
        reduce_rows(down_term, down_grad, scratch[REDUCE_COUNT : 2 * REDUCE_COUNT]),
    ]
    scratch = scratch[2 * REDUCE_COUNT :]
    out_stages = line_sum_stages(out_part, *scratch)
    out_stages[0]()
    for start, _, _ in reduces:
        start()
    holds, pair = holder(e)
    total = row_sum[...]
    width = upstream.shape[1]
    experts = gates.shape[1]
    dgate = total[:, width : width + experts] + total[:, width + experts : width + 2 * experts]
    own = gates[pl.ds(pl.multiple_of(e * upstream.shape[0], 128), upstream.shape[0]), :]
    dlog = low(own * (dgate - jnp.sum(own * dgate, axis=1, keepdims=True)))
    dn2 = total[:, :width] + dot(dlog, w_router[...])
    rows = resid[...]
    inv = lax.rsqrt(jnp.mean(rows * rows, axis=1, keepdims=True) + EPSILON)
    xhat = rows * inv
    small[experts : experts + 1, :] = jnp.sum(dn2 * xhat, axis=0, keepdims=True)
    scaled = dn2 * gain[...]
    grad = upstream[...] + inv * (scaled - xhat * jnp.mean(scaled * xhat, axis=1, keepdims=True))
    dresid[...] = grad
    back = low(dot(low(grad), w_out[...], ((1,), (1,))))
    size = dattn.shape[2]

    def give(source, index):
        return send(dattn.at[index], darrived.at[e], a_send.at[index], a_recv.at[e], (b, source))

    for source, index in PAIR_OF.items():
        dattn[index] = back[:, index * size : (index + 1) * size]

        @pl.when(e != source)
        def _():
            give(source, index).start()

    out_stages[1]()
    reduces[0][1]()
    small[:experts, :] = dot(dlog, n2[...], ((0,), (0,)))
    small[experts + 1 :, :] = jnp.zeros((small.shape[0] - experts - 1, width), F32)
    out_stages[2]()
    grad_low = low(dresid[...])
    for index in range(len(PAIR_OF)):
        out_term[index * size : (index + 1) * size, :] = low(
            dot(attn[index], grad_low, ((0,), (0,)))
        )
    reduces[1][1]()
    out_stages[3]()

    @pl.when(jnp.logical_not(holds))
    def _():
        darrived[...] = jnp.zeros_like(darrived)

    @pl.when(holds)
    def _():
        darrived[e] = dattn[pair]
        for i in range(1, 8):
            other = lax.rem(e + i, 8)
            block = darrived.at[other]
            send(block, block, a_send.at[0], a_recv.at[other], (b, other)).wait_recv()

    output_rows[...] = resid[...] + out_stages[4]()
    for _, _, finish in reduces:
        finish()
    for source, index in PAIR_OF.items():

        @pl.when(e != source)
        def _():
            give(source, index).wait_send()


def turn(row_sum, out_part, upstream, gates, w_router, resid, gain, w_out, attn, n2, up_term, down_term):
    tokens, width = upstream.shape
    pair = 2 * HEAD
    count = len(PAIR_OF)
    up_rows, down_rows = up_term.shape[0] // 4, down_term.shape[0] // 4
    return kernel_call(
        turn_kernel,
        [
            ((tokens, width), F32),
            ((gates.shape[1] + 8, width), F32),
            ((width, width), LOW),
            ((8, tokens, pair), LOW),
            ((tokens, width), F32),
            ((up_rows, up_term.shape[1]), F32),
            ((down_rows, down_term.shape[1]), F32),
        ],
        (row_sum, out_part, upstream, gates, w_router, resid, gain, w_out, attn, n2, up_term, down_term),
        [
            pltpu.VMEM((count, tokens, pair), LOW),
            pltpu.SemaphoreType.DMA((count,)),
            pltpu.SemaphoreType.DMA((8,)),
        ]
        + reduce_scratch((up_rows // 2, up_term.shape[1]), True)
        + reduce_scratch((down_rows // 2, down_term.shape[1]), True)
        + scatter_scratch(tokens, width)
        + SCATTER_SEMS,
        2,
        far_args=(10, 11),
    )


PARTNERS = ((0, 1), (1, 0), (2, 0), (0, 2), (0, 4))


def closing_kernel(
    dattn, qkv_far, logsum_far, n1_far, weights_far, cosine_far, sine_far, ids_row, ids_column, rows, gain, dresid,
    up_term, sdown_term, sup_term, out_term, small,
    input_grad, columns, out_grad, up_grad, sdown_grad, small_sum,
    qkv, logsum, n1, weights, cosine, sine, bring_sem,
    dkey, dvalue, dprojected, part, column_term, column_sum, column_low,
    out_near, out_sum, out_low, out_half, out_got, small_got, small_step,
    n_send, n_recv, o_send, o_recv, c_send, c_recv, s_send, s_recv, *scratch,
):
    b, e, z, core = place()
    length = n1.shape[0]
    tokens = rows.shape[0]
    mates = pack_mates()
    greet([(b ^ 1, e), (b ^ 2, e), *mates])
    holds, pair = holder(e)

    def cut():
        nonlocal scratch
        mine, scratch = scratch[:REDUCE_COUNT], scratch[REDUCE_COUNT:]
        return mine

    up = reduce_rows(up_term, up_grad, cut())
    sdown = reduce_rows(sdown_term, sdown_grad, cut())
    column = reduce_rows(column_term, column_sum, cut())
    out = reduce_stages(
        lambda owner, half: out_sum.at[owner, pl.ds(2 * half, 2)],
        lambda half: out_half.at[pl.ds(2 * half, 2)],
        *cut(),
    )
    stages = line_sum_stages(part, *scratch)

    def partner(i):
        batch_bit, expert_bit = PARTNERS[i]
        src = small if i == 0 else small_step.at[i - 1]
        device = (b ^ batch_bit, e ^ expert_bit)
        return send(src, small_got.at[i], s_send.at[i], s_recv.at[i], device)

    def small_round(i):
        partner(i).wait_recv()
        before = small[...] if i == 0 else small_step[i - 1]
        if i < len(PARTNERS) - 1:
            small_step[i] = before + small_got[i]
            partner(i + 1).start()
        else:
            small_sum[...] = before + small_got[i]

    near = send(
        out_term.at[:, :, 1 - core], out_near, n_send.at[0], n_recv.at[0], (b, e ^ 1)
    )
    up[0]()
    near.start()
    brought = bring_all(
        (qkv_far, logsum_far, n1_far, weights_far, cosine_far, sine_far),
        (qkv, logsum, n1, weights, cosine, sine),
        bring_sem,
    )
    own = pltpu.make_async_copy(out_term.at[:, :, core], out_sum, n_send.at[1])
    own.start()
    partner(0).start()

    def attend(head):
        dkey[...] = jnp.zeros_like(dkey)
        dvalue[...] = jnp.zeros_like(dvalue)
        lanes = pl.ds(head * HEAD, HEAD)
        for i in range(length // BLOCK):
            here = pl.ds(i * BLOCK, BLOCK)
            keys = (i + 1) * BLOCK
            count = BLOCK // tokens
            back = jnp.concatenate(
                [dattn[count * i + j, :, lanes] for j in range(count)], axis=0
            )
            query = qkv[head, here, :]
            scores = dot(query, qkv[2 + head, :keys, :], ((1,), (1,))) * HEAD ** (-0.5)
            weight = jnp.where(
                allowed_here(ids_column, ids_row, i, keys),
                jnp.exp(scores - logsum[head, here, 0:1]),
                0.0,
            )
            dprob = dot(back, qkv[4 + head, :keys, :], ((1,), (1,)))
            delta = jnp.sum(weight * dprob, axis=1, keepdims=True)
            dscore = low(weight * (dprob - delta))
            dquery = dot(dscore, qkv[2 + head, :keys, :]) * HEAD ** (-0.5)
            dkey[:keys, :] += dot(dscore, query, ((0,), (0,)))
            dvalue[:keys, :] += dot(low(weight), back, ((0,), (0,)))
            dprojected[here, lanes] = low(turned(dquery, cosine[here, :], -sine[here, :]))
        dprojected[:, (2 + head) * HEAD : (3 + head) * HEAD] = low(
            turned(dkey[...] * HEAD ** (-0.5), cosine[...], -sine[...])
        )
        dprojected[:, (4 + head) * HEAD : (5 + head) * HEAD] = low(dvalue[...])

    for copy in brought:
        copy.wait()

    @pl.when(holds)
    def _():
        attend(0)

    near.wait()
    own.wait()
    for owner in range(4):
        for owner_z in range(4):
            out_sum[owner, owner_z] = low(
                out_sum[owner, owner_z].astype(F32) + out_near[owner, owner_z].astype(F32)
            )
    small_round(0)
    up[1]()

    @pl.when(holds)
    def _():
        attend(1)
        for i in range(8):
            part[i] = low(
                dot(
                    dprojected[i * tokens : (i + 1) * tokens, :],
                    weights[:, : 6 * HEAD],
                    ((1,), (1,)),
                )
            )

    @pl.when(jnp.logical_not(holds))
    def _():
        part[...] = jnp.zeros_like(part)

    stages[0]()
    column_term[:, 6 * HEAD :] = sup_term[...]

    @pl.when(holds)
    def _():
        for i in range(n1.shape[1] // BLOCK):
            here = pl.ds(i * BLOCK, BLOCK)
            column_term[here, : 6 * HEAD] = low(dot(n1[:, here], dprojected[...], ((0,), (0,))))

    @pl.when(jnp.logical_not(holds))
    def _():
        column_term[:, : 6 * HEAD] = jnp.zeros((n1.shape[1], 6 * HEAD), LOW)

    column[0]()
    stages[1]()
    out[0]()
    small_round(1)
    stages[2]()
    column[1]()
    sdown[0]()
    stages[3]()
    small_round(2)
    out[1]()
    small_round(3)
    values = rows[...]
    inv = lax.rsqrt(jnp.mean(values * values, axis=1, keepdims=True) + EPSILON)
    xhat = values * inv
    scaled = stages[4]() * gain[...]
    input_grad[...] = dresid[...] + inv * (
        scaled - xhat * jnp.mean(scaled * xhat, axis=1, keepdims=True)
    )
    column[2]()
    piece = column_low.shape[1]
    for i in range(0, 8, 2):
        two = column_sum[i * piece : (i + 2) * piece, :].astype(F32)
        column_low[i] = low(two[:piece])
        column_low[i + 1] = low(two[piece:])
    columns[e] = column_low[e]
    across = []
    for i, device in enumerate(mates):
        across.append(
            send(column_low.at[device[1]], columns.at[e], c_send.at[i], c_recv.at[i], device)
        )
        across[-1].start()
    sdown[1]()
    small_round(4)
    for i in range(len(PARTNERS)):
        partner(i).wait_send()
    out[2]()
    for owner_z in range(4):
        out_low[owner_z] = low(out_half[owner_z])
    along = []
    for i in range(3):
        device = (b, lax.rem(e + 2 * i + 2, 8))
        along.append(
            send(
                out_low.at[device[1] // 2], out_got.at[i], o_send.at[i], o_recv.at[i], device
            )
        )
        along[-1].start()
    up[2]()
    for copy in along:
        copy.wait()
    out_grad[...] = (
        out_half[z]
        + out_got[0].astype(F32)
        + out_got[1].astype(F32)
        + out_got[2].astype(F32)
    )
    sdown[2]()
    for copy in across:
        copy.wait()


def closing(
    dattn, qkv, logsum, n1, weights, cosine, sine, ids_row, ids_column, rows, gain, dresid,
    up_term, sdown_term, sup_term, out_term, small,
):
    tokens, width = rows.shape
    length = n1.shape[0]
    rows_w = out_term.shape[3]
    wide = weights.shape[1]
    up_rows, sdown_rows = up_term.shape[0] // 4, sdown_term.shape[0] // 4
    dma = pltpu.SemaphoreType.DMA
    return kernel_call(
        closing_kernel,
        [
            ((tokens, width), F32),
            ((8, rows_w, wide), LOW),
            ((rows_w, width), F32),
            ((up_rows, up_term.shape[1]), F32),
            ((sdown_rows, width), F32),
            (small.shape, F32),
        ],
        (
            dattn, qkv, logsum, n1, weights, cosine, sine, ids_row, ids_column, rows, gain, dresid,
            up_term, sdown_term, sup_term, out_term, small,
        ),
        [
            pltpu.VMEM(qkv.shape, LOW),
            pltpu.VMEM(logsum.shape, F32),
            pltpu.VMEM(n1.shape, LOW),
            pltpu.VMEM(weights.shape, LOW),
            pltpu.VMEM(cosine.shape, F32),
            pltpu.VMEM(sine.shape, F32),
            pltpu.SemaphoreType.DMA((6,)),
            pltpu.VMEM((length, HEAD), F32),
            pltpu.VMEM((length, HEAD), F32),
            pltpu.VMEM((length, 6 * HEAD), LOW),
            pltpu.VMEM((8, tokens, width), LOW),
            pltpu.VMEM((width, wide), LOW),
            pltpu.VMEM((width // 4, wide), LOW),
            pltpu.VMEM((8, rows_w, wide), LOW),
            pltpu.VMEM((4, 4, rows_w, width), LOW),
            pltpu.VMEM((4, 4, rows_w, width), LOW),
            pltpu.VMEM((4, rows_w, width), LOW),
            pltpu.VMEM((4, rows_w, width), F32),
            pltpu.VMEM((3, rows_w, width), LOW),
            pltpu.VMEM((5, *small.shape), F32),
            pltpu.VMEM((4, *small.shape), F32),
            dma((2,)), dma((1,)), dma((3,)), dma((3,)), dma((7,)), dma((7,)), dma((5,)), dma((5,)),
        ]
        + reduce_scratch((up_rows // 2, up_term.shape[1]), True)
        + reduce_scratch((sdown_rows // 2, width))
        + reduce_scratch((width // 8, wide))
        + reduce_scratch((2, rows_w, width))
        + scatter_scratch(tokens, width)
        + SCATTER_SEMS,
        3,
        far_args=(1, 2, 3, 4, 5, 6, 12, 15),
    )


def silu_parts(gate, up):
    sigma = jax.nn.sigmoid(gate)
    return gate * sigma, up * sigma * (1.0 + gate * (1.0 - sigma))


def rotary_angles(length):
    half = HEAD // 2
    frequency = np.float32(10000.0) ** (-np.arange(half, dtype=np.float32) / np.float32(half))
    return np.arange(length, dtype=np.float32)[:, None] * frequency[None, :]


def pack_device(
    block_input,
    seq_ids,
    routes,
    cotangent,
    qkv_weight,
    out_weight,
    shared_up,
    shared_down,
    router_weight,
    gain_attn,
    gain_ffn,
    expert_up,
    expert_down,
):
    b = lax.axis_index("batch")
    e = lax.axis_index("expert")
    rows_in = block_input[0]
    upstream = cotangent[0]
    tokens, width = rows_in.shape
    length = tokens * 8
    rows_w = qkv_weight.shape[0]
    pair = 2 * HEAD
    pairs_of_heads = width // pair
    hidden = expert_up.shape[2] // 2
    experts = expert_up.shape[0] * 8
    s_rows = shared_down.shape[0]
    s_each = -(-s_rows // 32) * 32
    s_pad = 4 * s_each

    sup_low = low(shared_up).reshape(rows_w, 2, 4, 8, s_rows)
    sup_low = jnp.pad(sup_low, ((0, 0),) * 4 + ((0, s_each - s_rows),)).transpose(3, 0, 1, 2, 4)
    n1_all, gains, small, marks, columns, w_out, up_first = opening(
        rows_in,
        router_weight.reshape(-1, 128),
        gain_attn[None],
        gain_ffn[None],
        routes,
        seq_ids,
        qkv_weight,
        sup_low.reshape(8, rows_w, 2 * s_pad),
        out_weight,
        expert_up,
    )
    n1_all = n1_all.reshape(length, width)
    columns = columns.reshape(width, 3 * pair + 2 * s_pad)
    w_out = w_out.reshape(width, width)
    router_rows = rows_w * experts // 128
    w_router = low(small[:, :, :router_rows].transpose(1, 0, 2, 3).reshape(width, experts))
    gain_first = gains[0:1]
    gain_second = gains[1:2]
    marks = marks.astype(jnp.int32).transpose(0, 2, 1).reshape(length, 8)
    ids_all = marks[:, TOP]
    positions = jnp.arange(length, dtype=jnp.int32)
    ids_row = ids_all[None, :]
    ids_column = ids_all[:, None]
    angle = rotary_angles(length)
    cosine = np.concatenate([np.cos(angle)] * 2, axis=1)
    sine = np.concatenate([-np.sin(angle), np.sin(angle)], axis=1)
    qkv, logsum, attn, resid, n2_all, cot_all, up_second, down_low, w_sdown, down_second, n2 = middle(
        n1_all,
        columns,
        jnp.asarray(cosine),
        jnp.asarray(sine),
        ids_row,
        ids_column,
        w_out,
        rows_in,
        gain_second,
        cotangent,
        expert_up,
        expert_down,
        shared_down,
    )
    cot_all = cot_all.reshape(length, width)

    n2_all = n2_all.reshape(length, width)
    gates, output_part, row_sum, sdown_term, sup_term, down_grad_first, *terms = experts_phase(
        n2_all,
        cot_all,
        columns,
        w_sdown,
        w_router,
        marks,
        down_second,
        up_first,
        up_second,
        down_low,
    )
    up_terms, down_term_second = terms[:2], terms[2]
    dresid, small, out_term, dattn, output_rows, up_grad_first, down_grad_second = turn(
        row_sum,
        output_part.reshape(8, tokens, width),
        upstream,
        gates,
        w_router.T,
        resid,
        gain_second,
        w_out,
        attn,
        n2,
        up_terms[0],
        down_term_second,
    )
    out_term = out_term.reshape(4, 4, 2, rows_w, width)
    input_grad, columns, out_grad, up_grad_second, sdown_grad, small = closing(
        dattn,
        qkv,
        logsum,
        n1_all,
        columns,
        jnp.asarray(cosine),
        jnp.asarray(sine),
        ids_row,
        ids_column,
        rows_in,
        gain_first,
        dresid,
        up_terms[1],
        sdown_term,
        sup_term,
        out_term,
        small,
    )
    expert_up_grad = jnp.stack([up_grad_first, up_grad_second])
    expert_down_grad = jnp.stack([down_grad_first, down_grad_second])
    shared_down_grad = sdown_grad[:s_rows]
    small = lax.dynamic_slice_in_dim(small, (b * 8 + e) * rows_w, rows_w, 1)
    columns = columns.astype(F32)
    qkv_grad = jnp.stack([columns[i, :, : 3 * pair] for i in PAIR_OF])
    qkv_grad = qkv_grad.reshape(pairs_of_heads, rows_w, 3, pair).transpose(1, 2, 0, 3)
    qkv_grad = qkv_grad.reshape(rows_w, 3 * width)
    sup_grad = columns[:, :, 3 * pair :].reshape(8, rows_w, 2, 4, s_each)[..., :s_rows]
    sup_grad = sup_grad.transpose(1, 2, 3, 0, 4)
    sup_grad = sup_grad.reshape(rows_w, shared_up.shape[1])
    own_first = low(gain_attn).astype(F32)
    gain_attn_grad = jnp.sum(low(qkv_weight).astype(F32) * qkv_grad, axis=1) / own_first
    return (
        output_rows[None],
        input_grad[None],
        qkv_grad,
        out_grad,
        sup_grad,
        shared_down_grad,
        small[:experts].T,
        gain_attn_grad,
        small[experts],
        expert_up_grad,
        expert_down_grad,
    )


def solution(mesh):
    in_specs = (
        P("batch", "expert", None),
        P("batch", "expert"),
        P("batch", "expert", None),
        P("batch", "expert", None),
        P(("batch", "expert"), None),
        P(("batch", "expert"), None),
        P(("batch", "expert"), None),
        P(("batch", "expert"), None),
        P(("batch", "expert"), None),
        P(("batch", "expert")),
        P(("batch", "expert")),
        P("expert", "batch", None),
        P("expert", "batch", None),
    )
    out_specs = (
        P("batch", "expert", None),
        P("batch", "expert", None),
        P(("batch", "expert"), None),
        P(("batch", "expert"), None),
        P(("batch", "expert"), None),
        P(("batch", "expert"), None),
        P(("batch", "expert"), None),
        P(("batch", "expert")),
        P(("batch", "expert")),
        P("expert", "batch", None),
        P("expert", "batch", None),
    )
    sizes = dict(mesh.shape)
    body = pack_device if sizes == {"batch": 4, "expert": 8} else per_device
    return jax.shard_map(
        body, mesh=mesh, in_specs=in_specs, out_specs=out_specs, check_vma=False
    )
```
